32 devices in a mesh: dom: 8 (over z, x), rows: 4 (over y, core).
Axes of the slice: x: 2, y: 2, z: 4, core: 2. Of those that a mesh axis runs over, the one named last changes fastest.
Arguments:
- features: bfloat16 [8192, 384], P(('dom', 'rows')), may hold values from -7 to 7
- out_grad: bfloat16 [8192, 384], P(('dom', 'rows')), may hold values from -6 to 6
- w_query: bfloat16 [384, 384], replicated, may hold values from -0.3125 to 0.3125
- w_keyval: bfloat16 [384, 768], replicated, may hold values from -0.3125 to 0.3125
- w_out: bfloat16 [384, 384], replicated, may hold values from -0.3125 to 0.3125
- virtual: bfloat16 [4, 384], replicated, may hold values from -6 to 6
- local_nbr: int32 [8192, 16], P(('dom', 'rows')), may hold values from 0 to 255
- expander: int32 [8192, 4], P(('dom', 'rows')), may hold values from 0 to 255
- send_rows: int32 [256, 32], P(('dom', 'rows')), may hold values from 0 to 255
Outputs:
- grad_features: float32 [8192, 384], P(('dom', 'rows'))
- grad_wq: float32 [384, 384], replicated
- grad_wkv: float32 [384, 768], replicated
- grad_wo: float32 [384, 384], replicated
- grad_virtual: float32 [4, 384], replicated
The draws below stay inside these ranges and needn't reach their ends.
Inputs may be any that keep to these rules, and one draw needn't show every extreme that they name: `local_nbr`: positions 0 to 127 name the previous tile of the partition's block order (cyclic within the partition), 128 to 255 the node's own tile. `expander`: slot s * 32 + k of a device holds the k-th row that the device of dom index s and the same rows index sends to it. `send_rows`: row g * 8 + a lists the 32 local rows that device g sends to dom index a; every device sends exactly 32 rows to every dom index, itself included.
All inputs are finite; a program needn't handle non-finite values.
Results may differ from the reference program's by a relative error of at most 0.008.
The reference program's roundings to bfloat16 on the way count: a program that leaves them out, or rounds other values in their place, can miss the bound.
Values may be sent and summed in bfloat16 or wider, within the bound.
No kernel may reach another device: no remote copies, remote signals or barrier semaphores. Data moves between devices by JAX's collectives and lax.ppermute only.
A program may use at most 64 MiB of HBM per device.

```python
import math
import jax
import jax.numpy as jnp
from jax import lax

D = 384
HEADS = 8
VIRTUAL = 4
EXP_DEG = 4
LOCAL = 16
TILE = 128
ROWS_DEV = 256
SLOTS_PEER = 32
NODES = 8192
SLOTS = 256
SEND_LISTS = 256
N_DOM = 8
N_ROWS = 4


def draw_features(key, part):
    base_key = jax.random.fold_in(key, 0)
    values = jax.random.truncated_normal(base_key, -6.0, 6.0, (NODES, D), jnp.float32)
    return values.astype(jnp.bfloat16)


def set_ends(entries, stream_key, least, largest):
    place = [jax.random.randint(jax.random.fold_in(stream_key, axis), (), 0, length) for axis, length in enumerate(entries.shape)]
    main_axis = entries.shape.index(max(entries.shape))
    beside = place[:main_axis] + [(place[main_axis] + 1) % entries.shape[main_axis]] + place[main_axis + 1:]
    return entries.at[tuple(place)].set(least).at[tuple(beside)].set(largest)


def level_of(own_key, extent, pieces, low, largest):
    def one(axis_at, shards_of):
        heights = jax.random.uniform(jax.random.fold_in(jax.random.fold_in(own_key, 6), axis_at), (shards_of,), jnp.float32, low / len(pieces), largest / len(pieces))
        return jnp.repeat(jnp.exp(heights), extent[axis_at] // shards_of).reshape((-1,) + (1,) * (len(extent) - axis_at - 1))

    level = one(*pieces[0])
    for cut in pieces[1:]:
        level = level * one(*cut)
    return level


def bell_draw(rng, dims, deviation, limit, cuts=(), held_as=jnp.bfloat16):
    level = level_of(rng, dims, cuts, -0.22, 0.18) if cuts else 1.0
    drawn = jax.random.normal(rng, dims, jnp.float32) * deviation * level
    return jnp.minimum(jnp.maximum(drawn, -limit), limit).astype(held_as)


def setup_inputs(seed: int = 0) -> dict:
    keys = jax.random.split(jax.random.key(seed), 10)
    features = draw_features(jax.random.fold_in(keys[9], 71), 0)
    out_grad = bell_draw(keys[1], (NODES, D), 1.0, 6.0, ((0, 32),))
    w_query = bell_draw(keys[2], (D, D), D ** -0.5, 0.3125)
    w_keyval = bell_draw(keys[3], (D, 2 * D), D ** -0.5, 0.3125)
    w_out = bell_draw(keys[4], (D, D), D ** -0.5, 0.3125)
    virtual = bell_draw(keys[5], (VIRTUAL, D), 1.0, 6.0)
    local_nbr = set_ends(jax.random.randint(keys[6], (NODES, LOCAL), 0, 2 * TILE), jax.random.fold_in(keys[6], 1), 0, (2 * TILE) - 1).astype(jnp.int32)
    expander = set_ends(jax.random.randint(keys[7], (NODES, EXP_DEG), 0, SLOTS), jax.random.fold_in(keys[7], 1), 0, SLOTS - 1).astype(jnp.int32)
    send_rows = set_ends(jax.random.randint(keys[8], (SEND_LISTS, SLOTS_PEER), 0, ROWS_DEV), jax.random.fold_in(keys[8], 1), 0, ROWS_DEV - 1).astype(jnp.int32)
    return dict(features=features, out_grad=out_grad, w_query=w_query, w_keyval=w_keyval, w_out=w_out, virtual=virtual, local_nbr=local_nbr, expander=expander, send_rows=send_rows)


NEGATIVE_FILL = -1e+30

def einsum_f32(spec, left, right):
    return jnp.einsum(spec, left.astype(jnp.float32), right.astype(jnp.float32))

def attend(queries, key_value, halo_kv, expand_kv, virtual_kv, local_nbr, out_delta):
    row_count, feat_width = queries.shape
    head_count = HEADS
    head_dim = feat_width // head_count
    tile_rows = TILE
    tile_count = row_count // tile_rows
    score_scale = 1.0 / math.sqrt(head_dim)
    extended = jnp.concatenate([halo_kv, key_value], axis=0)
    window = jnp.concatenate([extended[:row_count].reshape(tile_count, tile_rows, 2 * feat_width), key_value.reshape(tile_count, tile_rows, 2 * feat_width)], axis=1)
    win_keys = window[:, :, :feat_width].reshape(tile_count, 2 * tile_rows, head_count, head_dim)
    win_vals = window[:, :, feat_width:].reshape(tile_count, 2 * tile_rows, head_count, head_dim)
    exp_keys = expand_kv[:, :, :feat_width].reshape(row_count, -1, head_count, head_dim)
    exp_vals = expand_kv[:, :, feat_width:].reshape(row_count, -1, head_count, head_dim)
    virt_keys = virtual_kv[:, :feat_width].reshape(-1, head_count, head_dim)
    virt_vals = virtual_kv[:, feat_width:].reshape(-1, head_count, head_dim)
    q_heads = queries.reshape(row_count, head_count, head_dim)
    q_tiles = queries.reshape(tile_count, tile_rows, head_count, head_dim)
    d_heads = out_delta.reshape(row_count, head_count, head_dim)
    d_tiles = out_delta.reshape(tile_count, tile_rows, head_count, head_dim)
    positions = jnp.arange(2 * tile_rows, dtype=jnp.int32)
    local_mask = jnp.any(local_nbr[:, :, None] == positions[None, None, :], axis=1)[:, None, :]
    s_loc = einsum_f32('tqhd,tkhd->tqhk', q_tiles, win_keys).reshape(row_count, head_count, 2 * tile_rows) * score_scale
    s_loc = jnp.where(local_mask, s_loc, NEGATIVE_FILL)
    s_exp = einsum_f32('rhd,rkhd->rhk', q_heads, exp_keys) * score_scale
    s_virt = einsum_f32('rhd,khd->rhk', q_heads, virt_keys) * score_scale
    row_peak = jnp.maximum(jnp.maximum(s_loc.max(-1), s_exp.max(-1)), s_virt.max(-1))[..., None]
    e_loc = jnp.where(local_mask, jnp.exp(s_loc - row_peak), 0.0)
    e_exp = jnp.exp(s_exp - row_peak)
    e_virt = jnp.exp(s_virt - row_peak)
    norm_total = (e_loc.sum(-1) + e_exp.sum(-1) + e_virt.sum(-1))[..., None]
    p_loc = e_loc / norm_total
    p_exp = e_exp / norm_total
    p_virt = e_virt / norm_total
    pb_loc = p_loc.astype(jnp.bfloat16)
    pb_exp = p_exp.astype(jnp.bfloat16)
    pb_virt = p_virt.astype(jnp.bfloat16)
    pb_tiles = pb_loc.reshape(tile_count, tile_rows, head_count, 2 * tile_rows)
    summed = einsum_f32('tqhk,tkhd->tqhd', pb_tiles, win_vals).reshape(row_count, feat_width) + einsum_f32('rhk,rkhd->rhd', pb_exp, exp_vals).reshape(row_count, feat_width) + einsum_f32('rhk,khd->rhd', pb_virt, virt_vals).reshape(row_count, feat_width)
    attn_out = summed.astype(jnp.bfloat16)
    dp_loc = einsum_f32('tqhd,tkhd->tqhk', d_tiles, win_vals).reshape(row_count, head_count, 2 * tile_rows)
    dp_exp = einsum_f32('rhd,rkhd->rhk', d_heads, exp_vals)
    dp_virt = einsum_f32('rhd,khd->rhk', d_heads, virt_vals)
    delta = ((p_loc * dp_loc).sum(-1) + (p_exp * dp_exp).sum(-1) + (p_virt * dp_virt).sum(-1))[..., None]
    ds_loc = (p_loc * (dp_loc - delta) * score_scale).astype(jnp.bfloat16)
    ds_exp = (p_exp * (dp_exp - delta) * score_scale).astype(jnp.bfloat16)
    ds_virt = (p_virt * (dp_virt - delta) * score_scale).astype(jnp.bfloat16)
    ds_tiles = ds_loc.reshape(tile_count, tile_rows, head_count, 2 * tile_rows)
    grad_query = (einsum_f32('tqhk,tkhd->tqhd', ds_tiles, win_keys).reshape(row_count, feat_width) + einsum_f32('rhk,rkhd->rhd', ds_exp, exp_keys).reshape(row_count, feat_width) + einsum_f32('rhk,khd->rhd', ds_virt, virt_keys).reshape(row_count, feat_width)).astype(jnp.bfloat16)
    win_kgrad = einsum_f32('tqhk,tqhd->tkhd', ds_tiles, q_tiles).reshape(tile_count, 2 * tile_rows, feat_width)
    win_vgrad = einsum_f32('tqhk,tqhd->tkhd', pb_tiles, d_tiles).reshape(tile_count, 2 * tile_rows, feat_width)
    window_grad = jnp.concatenate([win_kgrad, win_vgrad], axis=-1)
    exp_grad = jnp.concatenate([einsum_f32('rhk,rhd->rkhd', ds_exp, q_heads).reshape(row_count, -1, feat_width), einsum_f32('rhk,rhd->rkhd', pb_exp, d_heads).reshape(row_count, -1, feat_width)], axis=-1)
    virt_grad = jnp.concatenate([einsum_f32('rhk,rhd->khd', ds_virt, q_heads).reshape(-1, feat_width), einsum_f32('rhk,rhd->khd', pb_virt, d_heads).reshape(-1, feat_width)], axis=-1)
    return (attn_out, grad_query, window_grad, exp_grad, virt_grad)

def rows_contracted(left, right):
    return lax.dot_general(left, right, (((0,), (0,)), ((), ())), preferred_element_type=jnp.float32)

def times_transposed(left, right):
    return lax.dot_general(left, right, (((1,), (1,)), ((), ())), preferred_element_type=jnp.float32)

def reference(features, out_grad, w_query, w_keyval, w_out, virtual, local_nbr, expander, send_rows):
    device_count = N_DOM * N_ROWS
    row_count = ROWS_DEV
    feat_width = D
    tile_rows = TILE
    queries = jnp.dot(features, w_query, preferred_element_type=jnp.float32).astype(jnp.bfloat16)
    key_value = jnp.dot(features, w_keyval, preferred_element_type=jnp.float32).astype(jnp.bfloat16)
    virtual_kv = jnp.dot(virtual, w_keyval, preferred_element_type=jnp.float32).astype(jnp.bfloat16)
    out_delta = times_transposed(out_grad, w_out).astype(jnp.bfloat16)
    device_ids = jnp.arange(device_count, dtype=jnp.int32)
    dom_of = device_ids // N_ROWS
    row_of = device_ids % N_ROWS
    previous = dom_of * N_ROWS + (row_of - 1) % N_ROWS
    following = dom_of * N_ROWS + (row_of + 1) % N_ROWS
    kv_dev = key_value.reshape(device_count, row_count, 2 * feat_width)
    halo_all = kv_dev[previous, row_count - tile_rows:]
    send_all = send_rows.reshape(device_count, N_DOM, SLOTS_PEER)
    sources = jnp.arange(N_DOM, dtype=jnp.int32)[None, :] * N_ROWS + row_of[:, None]
    picked = send_all[sources, dom_of[:, None], :]
    slot_nodes = (sources[:, :, None] * row_count + picked).reshape(device_count, N_DOM * SLOTS_PEER).astype(jnp.int32)

    def per_device(inputs):
        q_dev, kv_here, halo_kv, nodes_here, local_here, expand_here, delta_here = inputs
        slot_kv = key_value[nodes_here]
        expand_kv = slot_kv[expand_here]
        attn_out, grad_query, window_grad, exp_grad, virt_grad = attend(q_dev, kv_here, halo_kv, expand_kv, virtual_kv, local_here, delta_here)
        own_grad = window_grad[:, tile_rows:].reshape(row_count, 2 * feat_width)
        prev_grad = window_grad[:, :tile_rows].reshape(row_count, 2 * feat_width)
        partial_grad = own_grad + jnp.concatenate([prev_grad[tile_rows:], jnp.zeros((tile_rows, 2 * feat_width), jnp.float32)], axis=0)
        slot_grad = jax.ops.segment_sum(exp_grad.reshape(-1, 2 * feat_width), expand_here.reshape(-1), num_segments=nodes_here.shape[0]).astype(jnp.bfloat16)
        return (attn_out, grad_query, partial_grad, prev_grad[:tile_rows], slot_grad, virt_grad)
    attn_out, grad_query, partial_grad, halo_grad, slot_grad, virt_grad = lax.map(per_device, (queries.reshape(device_count, row_count, feat_width), kv_dev, halo_all, slot_nodes, local_nbr.reshape(device_count, row_count, LOCAL), expander.reshape(device_count, row_count, EXP_DEG), out_delta.reshape(device_count, row_count, feat_width)))
    returned = halo_grad[following]
    local_grad = partial_grad + jnp.concatenate([jnp.zeros((device_count, row_count - tile_rows, 2 * feat_width), jnp.float32), returned], axis=1)
    local_grad = local_grad.reshape(-1, 2 * feat_width).astype(jnp.bfloat16)
    grad_query = grad_query.reshape(-1, feat_width)
    attn_out = attn_out.reshape(-1, feat_width)
    slot_flat = slot_grad.reshape(-1, 2 * feat_width)
    nodes_flat = slot_nodes.reshape(-1)
    slot_feat = lax.optimization_barrier(times_transposed(slot_flat, w_keyval).astype(jnp.bfloat16))
    grad_features = times_transposed(grad_query, w_query) + times_transposed(local_grad, w_keyval)
    grad_features = grad_features.at[nodes_flat].add(slot_feat.astype(jnp.float32))
    virt_total = lax.optimization_barrier(jnp.sum(virt_grad, axis=0))
    factor = NODES ** (-0.5)
    grad_wq = rows_contracted(features, grad_query)
    grad_wkv = rows_contracted(features, local_grad) + rows_contracted(features[nodes_flat], slot_flat)
    grad_wkv = grad_wkv + jnp.dot(virtual.astype(jnp.float32).T, virt_total, precision=lax.Precision.HIGHEST)
    grad_wo = rows_contracted(attn_out, out_grad)
    grad_virtual = jnp.dot(virt_total, w_keyval.astype(jnp.float32).T, precision=lax.Precision.HIGHEST)
    return (grad_features, grad_wq * factor, grad_wkv * factor, grad_wo * factor, grad_virtual * factor)
```

```python
import math

import jax
import jax.numpy as jnp
from jax import lax
from jax.sharding import PartitionSpec as P

HEADS = 8
TILE = 128


NEGATIVE_FILL = -1e30


def shifted(block, axis, distance):
    devices = range(lax.axis_size(axis))
    route = [((i - distance) % len(devices), i) for i in devices]
    return lax.ppermute(block, axis, route)


def einsum_bf(spec, left, right):
    return jnp.einsum(spec, left, right, preferred_element_type=jnp.float32)


def rows_contracted(left, right):
    return lax.dot_general(
        left, right, (((0,), (0,)), ((), ())), preferred_element_type=jnp.float32
    )


def times_transposed(left, right):
    return lax.dot_general(
        left, right, (((1,), (1,)), ((), ())), preferred_element_type=jnp.float32
    )


def attend(queries, key_value, halo_kv, expand_kv, virtual_kv, local_nbr, out_delta):
    row_count, feat_width = queries.shape
    head_count = HEADS
    head_dim = feat_width // head_count
    tile_rows = TILE
    tile_count = row_count // tile_rows
    score_scale = 1.0 / math.sqrt(head_dim)
    extended = jnp.concatenate([halo_kv, key_value], axis=0)
    window = jnp.concatenate(
        [
            extended[:row_count].reshape(tile_count, tile_rows, 2 * feat_width),
            key_value.reshape(tile_count, tile_rows, 2 * feat_width),
        ],
        axis=1,
    )
    win_keys = window[:, :, :feat_width].reshape(tile_count, 2 * tile_rows, head_count, head_dim)
    win_vals = window[:, :, feat_width:].reshape(tile_count, 2 * tile_rows, head_count, head_dim)
    exp_keys = expand_kv[:, :, :feat_width].reshape(row_count, -1, head_count, head_dim)
    exp_vals = expand_kv[:, :, feat_width:].reshape(row_count, -1, head_count, head_dim)
    virt_keys = virtual_kv[:, :feat_width].reshape(-1, head_count, head_dim)
    virt_vals = virtual_kv[:, feat_width:].reshape(-1, head_count, head_dim)
    q_heads = queries.reshape(row_count, head_count, head_dim)
    q_tiles = queries.reshape(tile_count, tile_rows, head_count, head_dim)
    d_heads = out_delta.reshape(row_count, head_count, head_dim)
    d_tiles = out_delta.reshape(tile_count, tile_rows, head_count, head_dim)
    positions = jnp.arange(2 * tile_rows, dtype=jnp.int32)
    local_mask = jnp.any(local_nbr[:, :, None] == positions[None, None, :], axis=1)[:, None, :]
    s_loc = (
        einsum_bf("tqhd,tkhd->tqhk", q_tiles, win_keys).reshape(
            row_count, head_count, 2 * tile_rows
        )
        * score_scale
    )
    s_loc = jnp.where(local_mask, s_loc, NEGATIVE_FILL)
    s_exp = einsum_bf("rhd,rkhd->rhk", q_heads, exp_keys) * score_scale
    s_virt = einsum_bf("rhd,khd->rhk", q_heads, virt_keys) * score_scale
    row_peak = jnp.maximum(jnp.maximum(s_loc.max(-1), s_exp.max(-1)), s_virt.max(-1))[..., None]
    e_loc = jnp.where(local_mask, jnp.exp(s_loc - row_peak), 0.0)
    e_exp = jnp.exp(s_exp - row_peak)
    e_virt = jnp.exp(s_virt - row_peak)
    norm_total = (e_loc.sum(-1) + e_exp.sum(-1) + e_virt.sum(-1))[..., None]
    p_loc = e_loc / norm_total
    p_exp = e_exp / norm_total
    p_virt = e_virt / norm_total
    pb_loc = p_loc.astype(jnp.bfloat16)
    pb_exp = p_exp.astype(jnp.bfloat16)
    pb_virt = p_virt.astype(jnp.bfloat16)
    pb_tiles = pb_loc.reshape(tile_count, tile_rows, head_count, 2 * tile_rows)
    summed = (
        einsum_bf("tqhk,tkhd->tqhd", pb_tiles, win_vals).reshape(row_count, feat_width)
        + einsum_bf("rhk,rkhd->rhd", pb_exp, exp_vals).reshape(row_count, feat_width)
        + einsum_bf("rhk,khd->rhd", pb_virt, virt_vals).reshape(row_count, feat_width)
    )
    attn_out = summed.astype(jnp.bfloat16)
    dp_loc = einsum_bf("tqhd,tkhd->tqhk", d_tiles, win_vals).reshape(
        row_count, head_count, 2 * tile_rows
    )
    dp_exp = einsum_bf("rhd,rkhd->rhk", d_heads, exp_vals)
    dp_virt = einsum_bf("rhd,khd->rhk", d_heads, virt_vals)
    delta = ((p_loc * dp_loc).sum(-1) + (p_exp * dp_exp).sum(-1) + (p_virt * dp_virt).sum(-1))[
        ..., None
    ]
    ds_loc = (p_loc * (dp_loc - delta) * score_scale).astype(jnp.bfloat16)
    ds_exp = (p_exp * (dp_exp - delta) * score_scale).astype(jnp.bfloat16)
    ds_virt = (p_virt * (dp_virt - delta) * score_scale).astype(jnp.bfloat16)
    ds_tiles = ds_loc.reshape(tile_count, tile_rows, head_count, 2 * tile_rows)
    grad_query = (
        einsum_bf("tqhk,tkhd->tqhd", ds_tiles, win_keys).reshape(row_count, feat_width)
        + einsum_bf("rhk,rkhd->rhd", ds_exp, exp_keys).reshape(row_count, feat_width)
        + einsum_bf("rhk,khd->rhd", ds_virt, virt_keys).reshape(row_count, feat_width)
    ).astype(jnp.bfloat16)
    win_kgrad = einsum_bf("tqhk,tqhd->tkhd", ds_tiles, q_tiles).reshape(
        tile_count, 2 * tile_rows, feat_width
    )
    win_vgrad = einsum_bf("tqhk,tqhd->tkhd", pb_tiles, d_tiles).reshape(
        tile_count, 2 * tile_rows, feat_width
    )
    window_grad = jnp.concatenate([win_kgrad, win_vgrad], axis=-1)
    exp_grad = jnp.concatenate(
        [
            einsum_bf("rhk,rhd->rkhd", ds_exp, q_heads).reshape(row_count, -1, feat_width),
            einsum_bf("rhk,rhd->rkhd", pb_exp, d_heads).reshape(row_count, -1, feat_width),
        ],
        axis=-1,
    )
    virt_grad = jnp.concatenate(
        [
            einsum_bf("rhk,rhd->khd", ds_virt, q_heads).reshape(-1, feat_width),
            einsum_bf("rhk,rhd->khd", pb_virt, d_heads).reshape(-1, feat_width),
        ],
        axis=-1,
    )
    return (attn_out, grad_query, window_grad, exp_grad, virt_grad)


ROW_PACK = 16


def exchange_stages(dom_size, rows_size):
    dom_bits = [1 << i for i in range(dom_size.bit_length() - 1)]
    rows_bits = [1 << i for i in range(rows_size.bit_length() - 1)]
    stages = [[("rows", bit)] for bit in rows_bits[:1]]
    rest = [("rows", bit) for bit in rows_bits[1:2]] + [("dom", bit) for bit in dom_bits[:1]]
    rest += [("dom", bit) for bit in dom_bits[1:]] + [("rows", bit) for bit in rows_bits[2:]]
    for at in range(0, len(rest), 2):
        stages.append(rest[at : at + 2])
    return stages


def partner_masks(stage):
    masks = []
    for digit in range(1, 1 << len(stage)):
        dom_mask = sum(bit for i, (axis, bit) in enumerate(stage) if axis == "dom" and digit >> i & 1)
        rows_mask = sum(
            bit for i, (axis, bit) in enumerate(stage) if axis == "rows" and digit >> i & 1
        )
        masks.append((digit, dom_mask, rows_mask))
    return masks


def own_digit(stage):
    digit = jnp.int32(0)
    for i, (axis, bit) in enumerate(stage):
        digit += jnp.where(lax.axis_index(axis) & bit, 1 << i, 0)
    return digit


def swapped(block, dom_mask, rows_mask):
    dom_size, rows_size = lax.axis_size("dom"), lax.axis_size("rows")
    route = [
        (a * rows_size + b, (a ^ dom_mask) * rows_size + (b ^ rows_mask))
        for a in range(dom_size)
        for b in range(rows_size)
    ]
    return lax.ppermute(block, ("dom", "rows"), route)


def paired_sum(terms):
    while len(terms) > 1:
        terms = [left + right for left, right in zip(terms[::2], terms[1::2])]
    return terms[0]


def summed_everywhere(chunk, rider):
    stages = exchange_stages(lax.axis_size("dom"), lax.axis_size("rows"))
    scattered = []
    for stage in stages:
        group = 1 << len(stage)
        own = own_digit(stage)
        rows = chunk.shape[0]
        halved = rows % (group * ROW_PACK) == 0
        part = rows // group if halved else rows
        scattered.append((stage, own, part, halved))
        rider_bf = rider.astype(jnp.bfloat16)
        kept = lax.dynamic_slice_in_dim(chunk, own * part, part) if halved else chunk
        if not halved:
            kept = kept.astype(jnp.bfloat16).astype(jnp.float32)
        terms, rider_terms = [kept], [rider_bf.astype(jnp.float32)]
        for digit, dom_mask, rows_mask in partner_masks(stage):
            block = (
                lax.dynamic_slice_in_dim(chunk, (own ^ digit) * part, part) if halved else chunk
            )
            message = jnp.concatenate([block.astype(jnp.bfloat16), rider_bf], axis=0)
            arrived = swapped(message, dom_mask, rows_mask).astype(jnp.float32)
            terms.append(arrived[:part])
            rider_terms.append(arrived[part:])
        chunk, rider = paired_sum(terms), paired_sum(rider_terms)
    held = chunk.astype(jnp.bfloat16)
    for stage, own, part, halved in reversed(scattered):
        if not halved:
            continue
        whole = jnp.zeros((part << len(stage), held.shape[1]), jnp.bfloat16)
        whole = lax.dynamic_update_slice_in_dim(whole, held, own * part, 0)
        for digit, dom_mask, rows_mask in partner_masks(stage):
            arrived = swapped(held, dom_mask, rows_mask)
            whole = lax.dynamic_update_slice_in_dim(whole, arrived, (own ^ digit) * part, 0)
        held = whole
    return held.astype(jnp.float32), rider


def project_slots(slot_grad, w_keyval):
    return lax.optimization_barrier(times_transposed(slot_grad, w_keyval).astype(jnp.bfloat16))


def shards(features, out_grad, w_query, w_keyval, w_out, virtual, local_nbr, expander, send_rows):
    row_count, feat_width = features.shape
    tile_rows = TILE
    queries = jnp.dot(features, w_query, preferred_element_type=jnp.float32).astype(jnp.bfloat16)
    key_value = jnp.dot(features, w_keyval, preferred_element_type=jnp.float32).astype(jnp.bfloat16)
    virtual_kv = jnp.dot(virtual, w_keyval, preferred_element_type=jnp.float32).astype(jnp.bfloat16)
    send_flat = send_rows.reshape(-1)
    sent_features = features[send_flat]
    halo_kv = shifted(key_value[row_count - tile_rows :], "rows", 1)
    arrived = lax.all_to_all(sent_features, "dom", split_axis=0, concat_axis=0, tiled=True)
    slot_kv = jnp.dot(arrived, w_keyval, preferred_element_type=jnp.float32).astype(jnp.bfloat16)
    expand_kv = slot_kv[expander]
    out_delta = times_transposed(out_grad, w_out).astype(jnp.bfloat16)
    attn_out, grad_query, window_grad, exp_grad, virt_grad = attend(
        queries, key_value, halo_kv, expand_kv, virtual_kv, local_nbr, out_delta
    )
    own_grad = window_grad[:, tile_rows:].reshape(row_count, 2 * feat_width)
    prev_grad = window_grad[:, :tile_rows].reshape(row_count, 2 * feat_width)
    returned = shifted(prev_grad[:tile_rows].astype(jnp.bfloat16), "rows", -1).astype(jnp.float32)
    local_grad = (own_grad + jnp.concatenate([prev_grad[tile_rows:], returned], axis=0)).astype(
        jnp.bfloat16
    )
    slot_grad = jax.ops.segment_sum(
        exp_grad.reshape(-1, 2 * feat_width), expander.reshape(-1), num_segments=slot_kv.shape[0]
    ).astype(jnp.bfloat16)
    slot_weight = rows_contracted(arrived, slot_grad)
    returned_feat = lax.all_to_all(
        project_slots(slot_grad, w_keyval), "dom", split_axis=0, concat_axis=0, tiled=True
    )
    grad_features = times_transposed(grad_query, w_query) + times_transposed(local_grad, w_keyval)
    grad_features = grad_features.at[send_flat].add(returned_feat.astype(jnp.float32))
    factor = (row_count * lax.axis_size("dom") * lax.axis_size("rows")) ** (-0.5)
    virt_wkv = jnp.dot(virtual.astype(jnp.float32).T, virt_grad, precision=lax.Precision.HIGHEST)
    grad_wkv = rows_contracted(features, local_grad) + slot_weight + virt_wkv
    partial = jnp.concatenate(
        [
            rows_contracted(features, grad_query),
            grad_wkv[:, :feat_width],
            grad_wkv[:, feat_width:],
            rows_contracted(attn_out, out_grad),
        ],
        axis=0,
    )
    virt_part = jnp.dot(virt_grad, w_keyval.astype(jnp.float32).T, precision=lax.Precision.HIGHEST)
    virt_rows = virt_part.shape[0]
    virt_part = jnp.pad(virt_part, ((0, -virt_rows % ROW_PACK), (0, 0)))
    total, virt_total = summed_everywhere(partial * factor, virt_part * factor)
    grad_wq, grad_wk, grad_wv, grad_wo = jnp.split(total, 4, axis=0)
    return (
        grad_features,
        grad_wq,
        jnp.concatenate([grad_wk, grad_wv], axis=1),
        grad_wo,
        virt_total[:virt_rows],
    )


def solution(mesh):
    placed = (
        P(("dom", "rows"), None),
        P(("dom", "rows"), None),
        P(),
        P(),
        P(),
        P(),
        P(("dom", "rows"), None),
        P(("dom", "rows"), None),
        P(("dom", "rows"), None),
    )
    return jax.shard_map(
        shards,
        mesh=mesh,
        in_specs=placed,
        out_specs=(P(("dom", "rows"), None), P(), P(), P(), P()),
        check_vma=False,
    )
```

```python
import functools
import math

import jax
import jax.numpy as jnp
from jax import lax
from jax.experimental import pallas as pl
from jax.experimental.pallas import tpu as pltpu
from jax.sharding import PartitionSpec as P

HEADS = 8
TILE = 128
ROW_PACK = 16
NEGATIVE_FILL = -1e30
VMEM_BYTES = 48 * 1024 * 1024


def f32_dot(left, right):
    return jnp.dot(left, right, preferred_element_type=jnp.float32)


def rows_contracted(left, right):
    return lax.dot_general(
        left, right, (((0,), (0,)), ((), ())), preferred_element_type=jnp.float32
    )


def times_transposed(left, right):
    return lax.dot_general(
        left, right, (((1,), (1,)), ((), ())), preferred_element_type=jnp.float32
    )


def rounded(value):
    return value.astype(jnp.bfloat16)


def exchange_stages(dom_size, rows_size):
    dom_bits = [1 << i for i in range(dom_size.bit_length() - 1)]
    rows_bits = [1 << i for i in range(rows_size.bit_length() - 1)]
    stages = [[("rows", bit)] for bit in rows_bits[:1]]
    rest = [("rows", bit) for bit in rows_bits[1:2]] + [("dom", bit) for bit in dom_bits]
    rest += [("rows", bit) for bit in rows_bits[2:]]
    for at in range(0, len(rest), 2):
        stages.append(rest[at : at + 2])
    return stages


def scattered_stages(stages, rows):
    taken = []
    for stage in stages:
        if rows % (ROW_PACK << len(stage)):
            break
        rows >>= len(stage)
        taken.append(stage)
    return taken


def partner_masks(stage):
    masks = []
    for digit in range(1, 1 << len(stage)):
        by_axis = {"dom": 0, "rows": 0}
        for i, (axis, bit) in enumerate(stage):
            if digit >> i & 1:
                by_axis[axis] |= bit
        masks.append((by_axis["dom"], by_axis["rows"]))
    return masks


def own_piece(stages):
    index = jnp.int32(0)
    for stage in stages:
        index = index << len(stage)
        for i, (axis, bit) in enumerate(stage):
            index += jnp.where(lax.axis_index(axis) & bit, 1 << i, 0)
    return index


def swapped(block, dom_mask, rows_mask):
    dom_size, rows_size = lax.axis_size("dom"), lax.axis_size("rows")
    route = [
        (a * rows_size + b, (a ^ dom_mask) * rows_size + (b ^ rows_mask))
        for a in range(dom_size)
        for b in range(rows_size)
    ]
    return lax.ppermute(block, ("dom", "rows"), route)


def shifted(block, axis, distance):
    devices = range(lax.axis_size(axis))
    route = [((i - distance) % len(devices), i) for i in devices]
    return lax.ppermute(block, axis, route)


def paired_sum(terms):
    while len(terms) > 1:
        terms = [left + right for left, right in zip(terms[::2], terms[1::2])]
    return terms[0]


def summed_everywhere(keep, message, rider, stages, scattered):
    pieces = []
    first = True
    for stage in stages:
        halved = stage in scattered
        rider_bf = rounded(rider)
        masks = partner_masks(stage)
        if not halved:
            keep = rounded(keep).astype(jnp.float32)
        part = keep.shape[0]
        if halved and not first:
            part //= 1 << len(stage)
        terms, rider_terms = [keep[:part]], [rider_bf.astype(jnp.float32)]
        for at, (dom_mask, rows_mask) in enumerate(masks, 1):
            if not first:
                block = keep[at * part : (at + 1) * part] if halved else keep
                message = jnp.concatenate([rounded(block), rider_bf], axis=0)
            arrived = swapped(message, dom_mask, rows_mask).astype(jnp.float32)
            terms.append(arrived[:part])
            rider_terms.append(arrived[part:])
        keep, rider = paired_sum(terms), paired_sum(rider_terms)
        first = False
    held = rounded(keep)
    for stage in reversed(scattered[1:]):
        held = jnp.concatenate(
            [held] + [swapped(held, *masks) for masks in partner_masks(stage)], axis=0
        )
    return held, swapped(held, *partner_masks(scattered[0])[0]), rider


def listed_rows(dom, send_ref, row_count):
    dom_size, per_peer = send_ref.shape
    slots = dom_size * per_peer
    slot = lax.broadcasted_iota(jnp.int32, (slots, per_peer), 0)
    place = lax.broadcasted_iota(jnp.int32, (slots, per_peer), 1)
    peer = (slot // per_peer) ^ dom
    listed = jnp.zeros((slots, per_peer), jnp.int32)
    for at in range(dom_size):
        listed += jnp.where((peer == at) & (place == slot % per_peer), send_ref[at : at + 1, :], 0)
    column = jnp.sum(listed, axis=1, keepdims=True)
    rows = lax.broadcasted_iota(jnp.int32, (slots, row_count), 1)
    return jnp.where(column == rows, 1.0, 0.0).astype(jnp.bfloat16)


def pick_kernel(place_ref, feat_ref, send_ref, *out_refs):
    chosen = listed_rows(place_ref[0], send_ref, feat_ref.shape[0])
    picked = rounded(f32_dot(chosen, feat_ref[...]))
    per_peer = send_ref.shape[1]
    for at, out_ref in enumerate(out_refs):
        out_ref[...] = picked[at * per_peer : (at + 1) * per_peer]


def attend_kernel(
    dom_size,
    rows_per_piece,
    factor,
    place_ref,
    feat_ref,
    halo_ref,
    *refs,
):
    piece_refs, refs = refs[:dom_size], refs[dom_size:]
    og_ref, wq_ref, wkv_ref, wo_ref, virt_ref, nbr_ref, exp_ref = refs[:7]
    refs = refs[7:]
    gf_ref, halo_feat_ref = refs[:2]
    slot_feat_refs, refs = refs[2 : 2 + dom_size], refs[2 + dom_size :]
    keep_ref, send_ref, rider_ref = refs[:3]
    ext_ref, kv_ref, kvt_ref, extt_ref, qt_ref, odt_ref, gqt_ref, gkvt_ref, ot_ref = refs[3:12]

    row_count, width = feat_ref.shape
    tile = halo_ref.shape[0]
    tile_count = row_count // tile
    per_peer = piece_refs[0].shape[0]
    slots = dom_size * per_peer
    near = tile + row_count
    virt_at = near + slots
    ext_rows = ext_ref.shape[0]
    far = ext_rows - near
    virt_rows = virt_ref.shape[0]
    head_dim = width // HEADS
    scale = 1.0 / math.sqrt(head_dim)

    ext_ref[:tile] = halo_ref[...]
    ext_ref[tile:near] = feat_ref[...]
    for at, piece_ref in enumerate(piece_refs):
        ext_ref[near + at * per_peer : near + (at + 1) * per_peer] = piece_ref[...]
    ext_ref[virt_at:] = jnp.concatenate(
        [virt_ref[...], jnp.zeros((ext_rows - virt_at - virt_rows, width), jnp.bfloat16)], axis=0
    )
    kv_ref[...] = rounded(f32_dot(ext_ref[...], wkv_ref[...]))
    extt_ref[...] = ext_ref[...].T
    kvt_ref[...] = kv_ref[...].T
    qt_ref[...] = rounded(rows_contracted(wq_ref[...], extt_ref[:, tile:near]))
    odt_ref[...] = rounded(times_transposed(wo_ref[...], og_ref[...]))

    def multiplicity(key_rows, named, first, last):
        position = lax.broadcasted_iota(jnp.int32, (key_rows, row_count), 0)
        count = jnp.zeros((key_rows, row_count), jnp.float32)
        for at in range(first, last):
            count += jnp.where(named[at : at + 1, :] == position, 1.0, 0.0)
        return count

    local_bias = jnp.where(
        multiplicity(2 * tile, nbr_ref[...], 0, nbr_ref.shape[0]) > 0.0, 0.0, NEGATIVE_FILL
    )
    expander = exp_ref[...]
    expander = ((expander // per_peer) ^ place_ref[0]) * per_peer + expander % per_peer
    named_times = multiplicity(slots, expander, 0, expander.shape[0])
    slot_bias = jnp.full((slots, row_count), NEGATIVE_FILL, jnp.float32)
    for times in range(1, expander.shape[0] + 1):
        slot_bias = jnp.where(named_times == float(times), math.log(times) / scale, slot_bias)
    virt_row = lax.broadcasted_iota(jnp.int32, (ext_rows - virt_at, row_count), 0)
    virt_bias = jnp.where(virt_row < virt_rows, 0.0, NEGATIVE_FILL)
    far_bias = jnp.concatenate([slot_bias, virt_bias], axis=0)

    def tiles(of):
        return jnp.concatenate([of(t, slice(t * tile, (t + 1) * tile)) for t in range(tile_count)], 1)

    for head in range(HEADS):
        low, high = head * head_dim, (head + 1) * head_dim
        first = low // 128 * 128
        last = min(-(-high // 128) * 128, width)
        column = lax.broadcasted_iota(jnp.int32, (last - first, row_count), 0) + first
        of_head = (column >= low) & (column < high)
        q_rows = jnp.where(of_head, qt_ref[first:last, :], 0)
        d_rows = jnp.where(of_head, odt_ref[first:last, :], 0)

        def products(operand, start, stop):
            local = tiles(
                lambda t, lanes: f32_dot(
                    kv_ref[t * tile : (t + 2) * tile, start:stop], operand[:, lanes]
                )
            )
            return local, f32_dot(kv_ref[near:, start:stop], operand)

        s_local, s_far = products(q_rows, first, last)
        s_local += local_bias
        s_far += far_bias
        peak = jnp.maximum(
            jnp.max(s_local, axis=0, keepdims=True), jnp.max(s_far, axis=0, keepdims=True)
        )
        exponent_scale = scale * math.log2(math.e)
        e_local = jnp.exp2((s_local - peak) * exponent_scale)
        e_far = jnp.exp2((s_far - peak) * exponent_scale)
        total = jnp.sum(e_local, axis=0, keepdims=True) + jnp.sum(e_far, axis=0, keepdims=True)
        inverse = 1.0 / total
        p_local = e_local * inverse
        p_far = e_far * inverse
        dp_local, dp_far = products(d_rows, width + first, width + last)
        delta = jnp.sum(p_local * dp_local, axis=0, keepdims=True) + jnp.sum(
            p_far * dp_far, axis=0, keepdims=True
        )
        pb_local, pb_far = rounded(p_local), rounded(p_far)
        ds_local = rounded(p_local * (dp_local - delta))
        ds_far = rounded(p_far * (dp_far - delta))

        def to_queries(start, local, beyond):
            rows = slice(start + low, start + high)
            near_part = tiles(
                lambda t, lanes: f32_dot(kvt_ref[rows, t * tile : (t + 2) * tile], local[:, lanes])
            )
            return near_part + f32_dot(kvt_ref[rows, near:], beyond)

        ot_ref[low:high] = rounded(to_queries(width, pb_local, pb_far))
        gqt_ref[low:high] = rounded(to_queries(0, ds_local, ds_far) * scale)

        def to_keys(start, operand, local, beyond, factor):
            rows = slice(start + low, start + high)
            parts = []
            carried = None
            for t in range(tile_count):
                lanes = slice(t * tile, (t + 1) * tile)
                window = times_transposed(operand[:, lanes], local[:, lanes])
                previous = window[:, :tile]
                parts.append(previous if carried is None else previous + carried)
                carried = window[:, tile:]
            parts.append(carried)
            parts.append(times_transposed(operand, beyond))
            gathered = jnp.concatenate(parts, axis=1)
            gkvt_ref[rows] = rounded(gathered if factor is None else gathered * factor)

        to_keys(0, qt_ref[low:high], ds_local, ds_far, scale)
        to_keys(width, odt_ref[low:high], pb_local, pb_far, None)

    by_feature = f32_dot(wkv_ref[...], gkvt_ref[...])
    own = by_feature[:, tile:near] + f32_dot(wq_ref[...], gqt_ref[...])
    gf_ref[...] = own.T
    halo_feat_ref[...] = rounded(by_feature[:, :tile].T)
    slot_feat = rounded(by_feature[:, near:virt_at].T)
    for at, out_ref in enumerate(slot_feat_refs):
        out_ref[...] = slot_feat[at * per_peer : (at + 1) * per_peer]
    rider_ref[...] = by_feature[:, virt_at:].T * factor

    held = place_ref[1]
    blocks = keep_ref.shape[0] // rows_per_piece
    sums = (
        times_transposed(extt_ref[:, tile:near], gqt_ref[...]),
        times_transposed(extt_ref[...], gkvt_ref[:width]),
        times_transposed(extt_ref[...], gkvt_ref[width:]),
        f32_dot(ot_ref[...], og_ref[...]),
    )
    for at in range(2 * blocks):
        start = at * rows_per_piece
        value = sums[start // width][start % width : start % width + rows_per_piece] * factor
        distance = held ^ at
        kept = distance < blocks
        offset = pl.multiple_of((distance % blocks) * rows_per_piece, ROW_PACK)

        @pl.when(kept)
        def _():
            keep_ref[pl.ds(offset, rows_per_piece), :] = value

        @pl.when(jnp.logical_not(kept))
        def _():
            send_ref[pl.ds(offset, rows_per_piece), :] = rounded(value)

    send_ref[keep_ref.shape[0] :] = rounded(rider_ref[...])


def place_kernel(rows_per_piece, place_ref, near_ref, far_ref, gq_ref, gkv_ref, go_ref, all_ref):
    width = gq_ref.shape[0]
    half = near_ref.shape[0]
    all_ref[:half] = near_ref[...]
    all_ref[half:] = far_ref[...]
    for at in range(2 * half // rows_per_piece):
        offset = pl.multiple_of((place_ref[1] ^ at) * rows_per_piece, ROW_PACK)
        value = all_ref[pl.ds(offset, rows_per_piece), :].astype(jnp.float32)
        start = at * rows_per_piece
        rows = slice(start % width, start % width + rows_per_piece)
        which = start // width
        if which == 0:
            gq_ref[rows] = value
        elif which == 3:
            go_ref[rows] = value
        else:
            gkv_ref[rows, (which - 1) * width : which * width] = value


def return_kernel(place_ref, gf_ref, halo_ref, send_ref, *refs):
    piece_refs, out_ref = refs[:-1], refs[-1]
    row_count = gf_ref.shape[0]
    tile = halo_ref.shape[0]
    chosen = listed_rows(place_ref[0], send_ref, row_count)
    returned = jnp.concatenate([ref[...] for ref in piece_refs], axis=0)
    total = gf_ref[...] + rows_contracted(chosen, returned)
    out_ref[: row_count - tile] = total[: row_count - tile]
    out_ref[row_count - tile :] = total[row_count - tile :] + halo_ref[...].astype(jnp.float32)


def call(kernel, outs, args, name, scratch=(), flops=0):
    in_specs = [pl.BlockSpec(memory_space=pltpu.SMEM)]
    in_specs += [pl.BlockSpec(memory_space=pltpu.VMEM)] * (len(args) - 1)
    moved = sum(x.size * x.dtype.itemsize for x in list(args) + list(outs))
    return pl.pallas_call(
        kernel,
        out_shape=outs,
        in_specs=in_specs,
        out_specs=[pl.BlockSpec(memory_space=pltpu.VMEM)] * len(outs),
        scratch_shapes=scratch,
        compiler_params=pltpu.CompilerParams(vmem_limit_bytes=VMEM_BYTES),
        cost_estimate=pl.CostEstimate(flops=flops, bytes_accessed=moved, transcendentals=0),
        name=name,
    )(*args)


def shards(features, out_grad, w_query, w_keyval, w_out, virtual, local_nbr, expander, send_rows):
    row_count, width = features.shape
    dom_size, per_peer = send_rows.shape
    devices = lax.axis_size("dom") * lax.axis_size("rows")
    stages = exchange_stages(lax.axis_size("dom"), lax.axis_size("rows"))
    scattered = scattered_stages(stages, 4 * width)
    pieces = 1 << sum(len(stage) for stage in scattered)
    rows_per_piece = 4 * width // pieces
    place = jnp.stack([lax.axis_index("dom").astype(jnp.int32), own_piece(scattered)])
    bf16, f32 = jnp.bfloat16, jnp.float32
    shape = jax.ShapeDtypeStruct

    sent = call(
        pick_kernel,
        [shape((per_peer, width), bf16)] * dom_size,
        [place, features, send_rows],
        "pick_rows",
    )
    halo = shifted(features[row_count - TILE :], "rows", 1)
    arrived = [sent[0]] + [swapped(sent[at], at, 0) for at in range(1, dom_size)]

    ext_rows = TILE + row_count + dom_size * per_peer + ROW_PACK * -(-virtual.shape[0] // ROW_PACK)
    half = 2 * width
    rider_rows = ext_rows - TILE - row_count - dom_size * per_peer
    outs = [
        shape((row_count, width), f32),
        shape((TILE, width), bf16),
        *[shape((per_peer, width), bf16)] * dom_size,
        shape((half, width), f32),
        shape((half + rider_rows, width), bf16),
        shape((rider_rows, width), f32),
    ]
    scratch = [
        pltpu.VMEM((ext_rows, width), bf16),
        pltpu.VMEM((ext_rows, 2 * width), bf16),
        pltpu.VMEM((2 * width, ext_rows), bf16),
        pltpu.VMEM((width, ext_rows), bf16),
        pltpu.VMEM((width, row_count), bf16),
        pltpu.VMEM((width, row_count), bf16),
        pltpu.VMEM((width, row_count), bf16),
        pltpu.VMEM((2 * width, ext_rows), bf16),
        pltpu.VMEM((width, row_count), bf16),
    ]
    results = call(
        functools.partial(attend_kernel, dom_size, rows_per_piece, (row_count * devices) ** -0.5),
        outs,
        [place, features, halo, *arrived, out_grad, w_query, w_keyval, w_out, virtual]
        + [local_nbr.T, expander.T],
        "attend",
        scratch,
        flops=8 * ext_rows * width * width * 4,
    )
    own_feat, halo_feat = results[:2]
    slot_feat = results[2 : 2 + dom_size]
    keep, message, rider = results[2 + dom_size :]

    halo_back = shifted(halo_feat, "rows", -1)
    slots_back = [slot_feat[0]] + [swapped(slot_feat[at], at, 0) for at in range(1, dom_size)]
    near, far, rider = summed_everywhere(keep, message, rider, stages, scattered)
    (grad_features,) = call(
        return_kernel,
        [shape((row_count, width), f32)],
        [place, own_feat, halo_back, send_rows, *slots_back],
        "return_rows",
    )
    grad_wq, grad_wkv, grad_wo = call(
        functools.partial(place_kernel, rows_per_piece),
        [shape((width, width), f32), shape((width, 2 * width), f32), shape((width, width), f32)],
        [place, near, far],
        "place_sums",
        [pltpu.VMEM((4 * width, width), bf16)],
    )
    return grad_features, grad_wq, grad_wkv, grad_wo, rider[: virtual.shape[0]]


def solution(mesh):
    placed = (
        P(("dom", "rows"), None),
        P(("dom", "rows"), None),
        P(),
        P(),
        P(),
        P(),
        P(("dom", "rows"), None),
        P(("dom", "rows"), None),
        P(("dom", "rows"), None),
    )
    return jax.shard_map(
        shards,
        mesh=mesh,
        in_specs=placed,
        out_specs=(P(("dom", "rows"), None), P(), P(), P(), P()),
        check_vma=False,
    )
```

```python
import functools
import math

import jax
import jax.numpy as jnp
from jax import lax
from jax.experimental import pallas as pl
from jax.experimental.pallas import tpu as pltpu
from jax.sharding import PartitionSpec as P

HEADS = 8
TILE = 128
ROW_PACK = 16
NEGATIVE_FILL = -1e30
VMEM_BYTES = 24 * 1024 * 1024
LANES = 128
CORE = "core"
ROWS = ("row_chip", CORE)
DOM = ("dom",)
CHIPS = ("dom", "row_chip")


def f32_dot(left, right):
    return jnp.dot(left, right, preferred_element_type=jnp.float32)


def rows_contracted(left, right):
    return lax.dot_general(
        left, right, (((0,), (0,)), ((), ())), preferred_element_type=jnp.float32
    )


def times_transposed(left, right):
    return lax.dot_general(
        left, right, (((1,), (1,)), ((), ())), preferred_element_type=jnp.float32
    )


def rounded(value):
    return value.astype(jnp.bfloat16)


def swapped(block, axis):
    return lax.ppermute(block, axis, [(i, i ^ 1) for i in range(lax.axis_size(axis))])


def shifted(block, axes, distance):
    count = math.prod(lax.axis_size(axis) for axis in axes)
    return lax.ppermute(block, axes, [((i - distance) % count, i) for i in range(count)])


def exchanged(blocks, axes):
    return lax.all_to_all(blocks, axes, split_axis=0, concat_axis=0, tiled=True)


def listed_rows(send_ref, row_count):
    dom_size, per_peer = send_ref.shape
    slots = dom_size * per_peer
    slot = lax.broadcasted_iota(jnp.int32, (slots, per_peer), 0)
    place = lax.broadcasted_iota(jnp.int32, (slots, per_peer), 1)
    listed = jnp.zeros((slots, per_peer), jnp.int32)
    for at in range(dom_size):
        here = slot == place + at * per_peer
        listed += jnp.where(here, send_ref[at : at + 1, :], 0)
    column = jnp.sum(listed, axis=1, keepdims=True)
    rows = lax.broadcasted_iota(jnp.int32, (slots, row_count), 1)
    return jnp.where(column == rows, 1.0, 0.0).astype(jnp.bfloat16)


def fetch(pairs, sems):
    copies = [
        pltpu.make_async_copy(source, target, sems.at[at])
        for at, (source, target) in enumerate(pairs)
    ]
    for copy in copies:
        copy.start()
    return copies


def pick_kernel(feat_hbm, send_hbm, out_ref, halo_ref, feat_ref, send_ref, sems):
    copies = fetch([(send_hbm, send_ref), (feat_hbm, feat_ref)], sems)
    copies[0].wait()
    chosen = listed_rows(send_ref, feat_ref.shape[0])
    copies[1].wait()
    halo_ref[...] = feat_ref[feat_ref.shape[0] - halo_ref.shape[0] :]
    out_ref[...] = rounded(f32_dot(chosen, feat_ref[...]))


def prepare_kernel(
    feat_hbm,
    og_hbm,
    wq_hbm,
    wkv_hbm,
    wo_hbm,
    virt_hbm,
    nbr_hbm,
    exp_hbm,
    og_ref,
    wq_ref,
    wkv_ref,
    featt_ref,
    qt_ref,
    odt_ref,
    kv_ref,
    kvt_ref,
    local_bias_ref,
    far_bias_ref,
    feat_ref,
    wo_ref,
    virt_ref,
    nbr_ref,
    exp_ref,
    sems,
):
    nbr_copy, exp_copy, feat_copy, virt_copy, wq_copy, wkv_copy, og_copy, wo_copy = fetch(
        [
            (nbr_hbm, nbr_ref),
            (exp_hbm, exp_ref),
            (feat_hbm, feat_ref),
            (virt_hbm, virt_ref),
            (wq_hbm, wq_ref),
            (wkv_hbm, wkv_ref),
            (og_hbm, og_ref),
            (wo_hbm, wo_ref),
        ],
        sems,
    )
    row_count, width = feat_ref.shape
    window = local_bias_ref.shape[0]
    far = far_bias_ref.shape[0]
    virt_rows = virt_ref.shape[0]
    padded = kv_ref.shape[0] - row_count
    slots = far - padded
    scale = 1.0 / math.sqrt(width // HEADS)

    def multiplicity(key_rows, named):
        position = lax.broadcasted_iota(jnp.int32, (key_rows, row_count), 0)
        count = jnp.zeros((key_rows, row_count), jnp.float32)
        for at in range(named.shape[0]):
            count += jnp.where(named[at : at + 1, :] == position, 1.0, 0.0)
        return count

    nbr_copy.wait()
    local_bias_ref[...] = jnp.where(multiplicity(window, nbr_ref) > 0.0, 0.0, NEGATIVE_FILL)
    exp_copy.wait()
    named_times = multiplicity(slots, exp_ref)
    slot_bias = jnp.full((slots, row_count), NEGATIVE_FILL, jnp.float32)
    for times in range(1, exp_ref.shape[0] + 1):
        slot_bias = jnp.where(named_times == float(times), math.log(times) / scale, slot_bias)
    far_bias_ref[:slots] = slot_bias
    virt_row = lax.broadcasted_iota(jnp.int32, (padded, row_count), 0)
    far_bias_ref[slots:] = jnp.where(virt_row < virt_rows, 0.0, NEGATIVE_FILL)

    feat_copy.wait()
    featt_ref[:, :row_count] = feat_ref[...].T
    virt_copy.wait()
    virt = jnp.concatenate(
        [virt_ref[...], jnp.zeros((padded - virt_rows, width), jnp.bfloat16)], axis=0
    )
    featt_ref[:, row_count:] = virt.T
    wq_copy.wait()
    qt_ref[...] = rounded(rows_contracted(wq_ref[...], featt_ref[:, :row_count]))
    wkv_copy.wait()
    kv_ref[:row_count] = rounded(f32_dot(feat_ref[...], wkv_ref[...]))
    kv_ref[row_count:] = rounded(f32_dot(virt, wkv_ref[...]))
    kvt_ref[...] = kv_ref[...].T
    og_copy.wait()
    wo_copy.wait()
    odt_ref[...] = rounded(times_transposed(wo_ref[...], og_ref[...]))


def attend_kernel(
    rows_per_piece,
    factor,
    virt_rows,
    core_ref,
    halo_ref,
    arrived_ref,
    og_ref,
    wq_ref,
    wkv_ref,
    featt_ref,
    qt_ref,
    odt_ref,
    own_kv_ref,
    own_kvt_ref,
    local_bias_ref,
    far_bias_ref,
    gf_ref,
    halo_feat_ref,
    slot_feat_ref,
    keep_ref,
    send_ref,
    kv_ref,
    kvt_ref,
    extt_ref,
    gqt_ref,
    gkvt_ref,
    ot_ref,
):
    width, row_count = qt_ref.shape
    tile = halo_ref.shape[0]
    tile_count = row_count // tile
    slots = arrived_ref.shape[0]
    near = tile + row_count
    virt_at = near + slots
    head_dim = width // HEADS
    scale = 1.0 / math.sqrt(head_dim)

    kv_ref[tile:near] = own_kv_ref[:row_count]
    kv_ref[virt_at:] = own_kv_ref[row_count:]
    kvt_ref[:, tile:near] = own_kvt_ref[:, :row_count]
    kvt_ref[:, virt_at:] = own_kvt_ref[:, row_count:]
    extt_ref[:, tile:near] = featt_ref[:, :row_count]
    extt_ref[:, virt_at:] = featt_ref[:, row_count:]
    for rows, source_ref in ((slice(0, tile), halo_ref), (slice(near, virt_at), arrived_ref)):
        extt_ref[:, rows] = source_ref[...].T
        kv_ref[rows] = rounded(f32_dot(source_ref[...], wkv_ref[...]))
        kvt_ref[:, rows] = kv_ref[rows].T

    def tiles(of):
        return jnp.concatenate([of(t, slice(t * tile, (t + 1) * tile)) for t in range(tile_count)], 1)

    for head in range(HEADS):
        low, high = head * head_dim, (head + 1) * head_dim
        first = low // 128 * 128
        last = min(-(-high // 128) * 128, width)
        column = lax.broadcasted_iota(jnp.int32, (last - first, row_count), 0) + first
        of_head = (column >= low) & (column < high)
        q_rows = jnp.where(of_head, qt_ref[first:last, :], 0)
        d_rows = jnp.where(of_head, odt_ref[first:last, :], 0)

        def products(operand, start, stop):
            local = tiles(
                lambda t, lanes: f32_dot(
                    kv_ref[t * tile : (t + 2) * tile, start:stop], operand[:, lanes]
                )
            )
            return local, f32_dot(kv_ref[near:, start:stop], operand)

        s_local, s_far = products(q_rows, first, last)
        s_local += local_bias_ref[...]
        s_far += far_bias_ref[...]
        peak = jnp.maximum(
            jnp.max(s_local, axis=0, keepdims=True), jnp.max(s_far, axis=0, keepdims=True)
        )
        exponent_scale = scale * math.log2(math.e)
        e_local = jnp.exp2((s_local - peak) * exponent_scale)
        e_far = jnp.exp2((s_far - peak) * exponent_scale)
        total = jnp.sum(e_local, axis=0, keepdims=True) + jnp.sum(e_far, axis=0, keepdims=True)
        inverse = 1.0 / total
        p_local = e_local * inverse
        p_far = e_far * inverse
        dp_local, dp_far = products(d_rows, width + first, width + last)
        delta = jnp.sum(p_local * dp_local, axis=0, keepdims=True) + jnp.sum(
            p_far * dp_far, axis=0, keepdims=True
        )
        pb_local, pb_far = rounded(p_local), rounded(p_far)
        ds_local = rounded(p_local * (dp_local - delta))
        ds_far = rounded(p_far * (dp_far - delta))

        def to_queries(start, local, beyond):
            rows = slice(start + low, start + high)
            near_part = tiles(
                lambda t, lanes: f32_dot(kvt_ref[rows, t * tile : (t + 2) * tile], local[:, lanes])
            )
            return near_part + f32_dot(kvt_ref[rows, near:], beyond)

        ot_ref[low:high] = rounded(to_queries(width, pb_local, pb_far))
        gqt_ref[low:high] = rounded(to_queries(0, ds_local, ds_far) * scale)

        def to_keys(start, operand, local, beyond, factor):
            rows = slice(start + low, start + high)
            parts = []
            carried = None
            for t in range(tile_count):
                lanes = slice(t * tile, (t + 1) * tile)
                window = times_transposed(operand[:, lanes], local[:, lanes])
                previous = window[:, :tile]
                parts.append(previous if carried is None else previous + carried)
                carried = window[:, tile:]
            parts.append(carried)
            parts.append(times_transposed(operand, beyond))
            gathered = jnp.concatenate(parts, axis=1)
            gkvt_ref[rows] = rounded(gathered if factor is None else gathered * factor)

        to_keys(0, qt_ref[low:high], ds_local, ds_far, scale)
        to_keys(width, odt_ref[low:high], pb_local, pb_far, None)

    by_feature = f32_dot(wkv_ref[...], gkvt_ref[...])
    own = by_feature[:, tile:near] + f32_dot(wq_ref[...], gqt_ref[...])
    gf_ref[...] = own.T
    halo_feat_ref[...] = rounded(by_feature[:, :tile].T)
    slot_feat_ref[...] = rounded(by_feature[:, near:virt_at].T)
    virt_feat = by_feature[:, virt_at:].T * factor

    sums = (
        times_transposed(extt_ref[:, tile:near], gqt_ref[...]),
        times_transposed(extt_ref[...], gkvt_ref[:width]),
        times_transposed(extt_ref[...], gkvt_ref[width:]),
        f32_dot(ot_ref[...], og_ref[...]),
    )
    pieces = keep_ref.shape[0]
    columns = width // LANES

    def write(half, piece_ref, cast):
        rest = piece_ref.shape[1] - columns * rows_per_piece
        for piece in range(pieces):
            start = (half * pieces + piece) * rows_per_piece
            value = sums[start // width][start % width : start % width + rows_per_piece] * factor
            for at in range(columns):
                rows = slice(at * rows_per_piece, (at + 1) * rows_per_piece)
                piece_ref[piece, rows] = cast(value[:, at * LANES : (at + 1) * LANES])
            rider = half * pieces + piece
            padding = jnp.zeros((rest, LANES), jnp.float32)
            if rider < virt_rows * columns:
                row, at = rider // columns, rider % columns
                padding = jnp.broadcast_to(
                    virt_feat[row : row + 1, at * LANES : (at + 1) * LANES], (rest, LANES)
                )
            piece_ref[piece, columns * rows_per_piece :] = cast(padding)

    for core in range(2):

        @pl.when(core_ref[0] == core)
        def _():
            write(core, keep_ref, lambda value: value)
            write(1 - core, send_ref, rounded)


def place_kernel(rows_per_piece, core_ref, near_ref, far_ref, gq_ref, gkv_ref, go_ref, gvirt_ref):
    width = gq_ref.shape[0]
    pieces = near_ref.shape[0]
    columns = width // LANES

    def write(half, piece_ref):
        for piece in range(pieces):
            start = (half * pieces + piece) * rows_per_piece
            which, row = start // width, start % width
            rows = slice(row, row + rows_per_piece)
            for at in range(columns):
                lanes = slice(at * LANES, (at + 1) * LANES)
                value = piece_ref[piece, at * rows_per_piece : (at + 1) * rows_per_piece]
                value = value.astype(jnp.float32)
                if which == 0:
                    gq_ref[rows, lanes] = value
                elif which == 3:
                    go_ref[rows, lanes] = value
                else:
                    shift = (which - 1) * width
                    gkv_ref[rows, slice(lanes.start + shift, lanes.stop + shift)] = value
            rider = half * pieces + piece
            if rider < gvirt_ref.shape[0] * columns:
                row, at = rider // columns, rider % columns
                rest = piece_ref[piece, columns * rows_per_piece :].astype(jnp.float32)
                gvirt_ref[row : row + 1, at * LANES : (at + 1) * LANES] = rest[:1]

    for core in range(2):

        @pl.when(core_ref[0] == core)
        def _():
            write(core, near_ref)
            write(1 - core, far_ref)


def return_kernel(gf_ref, halo_ref, send_ref, returned_ref, out_ref):
    row_count = gf_ref.shape[0]
    tile = halo_ref.shape[0]
    chosen = listed_rows(send_ref, row_count)
    total = gf_ref[...] + rows_contracted(chosen, returned_ref[...])
    out_ref[: row_count - tile] = total[: row_count - tile]
    out_ref[row_count - tile :] = total[row_count - tile :] + halo_ref[...].astype(jnp.float32)


def call(kernel, name, outs, args, scratch=(), fetched=0, scalars=0, flops=0):
    spaces = [pltpu.SMEM] * scalars + [pl.ANY] * fetched
    spaces += [pltpu.VMEM] * (len(args) - len(spaces))
    moved = sum(x.size * x.dtype.itemsize for x in list(args) + list(outs))
    scratch = list(scratch)
    if fetched:
        scratch.append(pltpu.SemaphoreType.DMA((fetched,)))
    return pl.pallas_call(
        kernel,
        out_shape=outs,
        in_specs=[pl.BlockSpec(memory_space=space) for space in spaces],
        out_specs=[pl.BlockSpec(memory_space=pltpu.VMEM)] * len(outs),
        scratch_shapes=scratch,
        compiler_params=pltpu.CompilerParams(vmem_limit_bytes=VMEM_BYTES),
        cost_estimate=pl.CostEstimate(flops=flops, bytes_accessed=moved, transcendentals=0),
        name=name,
    )(*args)


def shards(features, out_grad, w_query, w_keyval, w_out, virtual, local_nbr, expander, send_rows):
    row_count, width = features.shape
    dom_size, per_peer = send_rows.shape
    slots = dom_size * per_peer
    virt_rows = virtual.shape[0]
    padded = ROW_PACK * -(-virt_rows // ROW_PACK)
    ext_rows = TILE + row_count + slots + padded
    chips = math.prod(lax.axis_size(axis) for axis in CHIPS)
    rows_per_piece = 2 * width // chips
    piece_rows = width // LANES * rows_per_piece + 1
    piece_rows = ROW_PACK * -(-piece_rows // ROW_PACK)
    bf16, f32 = jnp.bfloat16, jnp.float32
    shape = jax.ShapeDtypeStruct
    core = lax.axis_index(CORE).astype(jnp.int32).reshape(1)

    sent, halo = call(
        pick_kernel,
        "pick_rows",
        [shape((slots, width), bf16), shape((TILE, width), bf16)],
        [features, send_rows],
        [pltpu.VMEM(features.shape, bf16), pltpu.VMEM(send_rows.shape, jnp.int32)],
        fetched=2,
    )
    arrived = exchanged(sent, DOM)
    halo = shifted(halo, ROWS, 1)
    prepared = call(
        prepare_kernel,
        "prepare",
        [
            shape(out_grad.shape, bf16),
            shape(w_query.shape, bf16),
            shape(w_keyval.shape, bf16),
            shape((width, row_count + padded), bf16),
            shape((width, row_count), bf16),
            shape((width, row_count), bf16),
            shape((row_count + padded, 2 * width), bf16),
            shape((2 * width, row_count + padded), bf16),
            shape((2 * TILE, row_count), f32),
            shape((slots + padded, row_count), f32),
        ],
        [features, out_grad, w_query, w_keyval, w_out, virtual, local_nbr.T, expander.T],
        [
            pltpu.VMEM(features.shape, bf16),
            pltpu.VMEM(w_out.shape, bf16),
            pltpu.VMEM(virtual.shape, bf16),
            pltpu.VMEM(local_nbr.shape[::-1], jnp.int32),
            pltpu.VMEM(expander.shape[::-1], jnp.int32),
        ],
        fetched=8,
        flops=10 * row_count * width * width,
    )
    own_feat, halo_feat, slot_feat, keep, message = call(
        functools.partial(
            attend_kernel, rows_per_piece, (row_count * dom_size * lax.axis_size(CORE) * lax.axis_size(ROWS[0])) ** -0.5, virt_rows
        ),
        "attend",
        [
            shape((row_count, width), f32),
            shape((TILE, width), bf16),
            shape((slots, width), bf16),
            shape((chips, piece_rows, LANES), f32),
            shape((chips, piece_rows, LANES), bf16),
        ],
        [core, halo, arrived, *prepared],
        [
            pltpu.VMEM((ext_rows, 2 * width), bf16),
            pltpu.VMEM((2 * width, ext_rows), bf16),
            pltpu.VMEM((width, ext_rows), bf16),
            pltpu.VMEM((width, row_count), bf16),
            pltpu.VMEM((2 * width, ext_rows), bf16),
            pltpu.VMEM((width, row_count), bf16),
        ],
        scalars=1,
        flops=32 * ext_rows * width * width,
    )

    both = rounded(keep + swapped(message, CORE).astype(f32))
    parts = exchanged(both, CHIPS)
    slots_back = exchanged(slot_feat, DOM)
    halo_back = shifted(halo_feat, ROWS, -1)
    (grad_features,) = call(
        return_kernel,
        "return_rows",
        [shape((row_count, width), f32)],
        [own_feat, halo_back, send_rows, slots_back],
    )
    summed = rounded(jnp.sum(parts.astype(f32), axis=0))
    near = exchanged(jnp.broadcast_to(summed, parts.shape), CHIPS)
    grad_wq, grad_wkv, grad_wo, grad_virtual = call(
        functools.partial(place_kernel, rows_per_piece),
        "place_sums",
        [
            shape((width, width), f32),
            shape((width, 2 * width), f32),
            shape((width, width), f32),
            shape((virt_rows, width), f32),
        ],
        [core, near, swapped(near, CORE)],
        scalars=1,
    )
    return grad_features, grad_wq, grad_wkv, grad_wo, grad_virtual


def solution(mesh):
    dom_size, rows_size = mesh.shape["dom"], mesh.shape["rows"]
    split = jax.sharding.Mesh(
        mesh.devices.reshape(dom_size, rows_size // 2, 2), (*DOM, *ROWS)
    )
    nodes = P((*DOM, *ROWS), None)
    placed = (nodes, nodes, P(), P(), P(), P(), nodes, nodes, nodes)
    return jax.shard_map(
        shards,
        mesh=split,
        in_specs=placed,
        out_specs=(nodes, P(), P(), P(), P()),
        check_vma=False,
    )
```

```python
import functools
import math

import jax
import jax.numpy as jnp
from jax import lax
from jax.experimental import pallas as pl
from jax.experimental.pallas import tpu as pltpu
from jax.sharding import PartitionSpec as P

HEADS = 8
TILE = 128
ROW_PACK = 16
NEGATIVE_FILL = -1e30
VMEM_BYTES = 24 * 1024 * 1024
LANES = 128


def f32_dot(left, right):
    return jnp.dot(left, right, preferred_element_type=jnp.float32)


def rows_contracted(left, right):
    return lax.dot_general(
        left, right, (((0,), (0,)), ((), ())), preferred_element_type=jnp.float32
    )


def times_transposed(left, right):
    return lax.dot_general(
        left, right, (((1,), (1,)), ((), ())), preferred_element_type=jnp.float32
    )


def rounded(value):
    return value.astype(jnp.bfloat16)


def exchange_stages(dom_size, rows_size):
    dom_bits = [1 << i for i in range(dom_size.bit_length() - 1)]
    rows_bits = [1 << i for i in range(rows_size.bit_length() - 1)]
    stages = [[("rows", bit)] for bit in rows_bits[:1]]
    rest = [("rows", bit) for bit in rows_bits[1:2]] + [("dom", bit) for bit in dom_bits]
    rest += [("rows", bit) for bit in rows_bits[2:]]
    for at in range(0, len(rest), 2):
        stages.append(rest[at : at + 2])
    return stages


def scattered_stages(stages, rows):
    taken = []
    for stage in stages:
        if rows % (ROW_PACK << len(stage)):
            break
        rows >>= len(stage)
        taken.append(stage)
    return taken


def partner_masks(stage):
    masks = []
    for digit in range(1, 1 << len(stage)):
        by_axis = {"dom": 0, "rows": 0}
        for i, (axis, bit) in enumerate(stage):
            if digit >> i & 1:
                by_axis[axis] |= bit
        masks.append((by_axis["dom"], by_axis["rows"]))
    return masks


def own_piece(stages):
    index = jnp.int32(0)
    for stage in stages:
        index = index << len(stage)
        for i, (axis, bit) in enumerate(stage):
            index += jnp.where(lax.axis_index(axis) & bit, 1 << i, 0)
    return index


def swapped(block, dom_mask, rows_mask):
    dom_size, rows_size = lax.axis_size("dom"), lax.axis_size("rows")
    route = [
        (a * rows_size + b, (a ^ dom_mask) * rows_size + (b ^ rows_mask))
        for a in range(dom_size)
        for b in range(rows_size)
    ]
    return lax.ppermute(block, ("dom", "rows"), route)


def shifted(block, axis, distance):
    devices = range(lax.axis_size(axis))
    route = [((i - distance) % len(devices), i) for i in devices]
    return lax.ppermute(block, axis, route)


def paired_sum(terms):
    while len(terms) > 1:
        terms = [left + right for left, right in zip(terms[::2], terms[1::2])]
    return terms[0]


def summed_everywhere(keep, message, rider, stages, scattered, slots):
    per_peer = slots[0].shape[0]
    returned = [slots[0]]
    handed_on = {}
    dom_masks = set(range(2, len(slots), 2))

    def riding(dom_mask, rows_mask):
        if rows_mask or not dom_mask:
            return []
        if dom_mask == 1:
            return slots[1::2]
        dom_masks.discard(dom_mask)
        return [slots[dom_mask], handed_on[dom_mask]]

    def unloaded(dom_mask, rows_mask, load):
        if rows_mask or not dom_mask:
            return
        if dom_mask == 1:
            returned.append(load[:per_peer])
            for at in range(1, len(slots) // 2):
                handed_on[2 * at] = load[at * per_peer : (at + 1) * per_peer]
        else:
            returned.append((dom_mask, load))

    first = True
    for stage in stages:
        halved = stage in scattered
        rider_bf = rounded(rider)
        masks = partner_masks(stage)
        if not halved:
            keep = rounded(keep).astype(jnp.float32)
        part = keep.shape[0]
        if halved and not first:
            part //= 1 << len(stage)
        base = part + rider.shape[0]
        messages = {}
        for at, (dom_mask, rows_mask) in enumerate(masks, 1):
            if not first:
                block = keep[at * part : (at + 1) * part] if halved else keep
                message = jnp.concatenate(
                    [rounded(block), rider_bf, *riding(dom_mask, rows_mask)], axis=0
                )
            messages[at] = message
        order = reversed(messages) if ("rows", 2) in stage else messages
        sent = {at: swapped(messages[at], *masks[at - 1]) for at in order}
        terms, rider_terms = [keep[:part]], [rider_bf.astype(jnp.float32)]
        for at, (dom_mask, rows_mask) in enumerate(masks, 1):
            arrived = sent[at]
            terms.append(arrived[:part].astype(jnp.float32))
            rider_terms.append(arrived[part:base].astype(jnp.float32))
            if not first:
                unloaded(dom_mask, rows_mask, arrived[base:])
        keep, rider = paired_sum(terms), paired_sum(rider_terms)
        first = False
    for mask in sorted(dom_masks):
        load = jnp.concatenate([slots[mask], handed_on[mask]], axis=0)
        returned.append((mask, swapped(load, mask, 0)))
    loads = dict(returned[2:])
    returned = returned[:2] + [loads[mask] for mask in sorted(loads)]

    held = rounded(keep)
    for stage in reversed(scattered[2:]):
        held = jnp.concatenate(
            [held] + [swapped(held, *masks) for masks in partner_masks(stage)], axis=0
        )
    near = [held]
    if len(scattered) > 1:
        arrived = [swapped(held, *masks) for masks in reversed(partner_masks(scattered[1]))]
        near += arrived[::-1]
    far = [swapped(block, *partner_masks(scattered[0])[0]) for block in near]
    return near, far, rider, returned


def listed_rows(dom, send_ref, row_count):
    dom_size, per_peer = send_ref.shape
    slots = dom_size * per_peer
    slot = lax.broadcasted_iota(jnp.int32, (slots, per_peer), 0)
    place = lax.broadcasted_iota(jnp.int32, (slots, per_peer), 1)
    peer = (slot // per_peer) ^ dom
    listed = jnp.zeros((slots, per_peer), jnp.int32)
    for at in range(dom_size):
        listed += jnp.where((peer == at) & (place == slot % per_peer), send_ref[at : at + 1, :], 0)
    column = jnp.sum(listed, axis=1, keepdims=True)
    rows = lax.broadcasted_iota(jnp.int32, (slots, row_count), 1)
    return jnp.where(column == rows, 1.0, 0.0).astype(jnp.bfloat16)


def fetch(pairs, sems):
    copies = [
        pltpu.make_async_copy(source, target, sems.at[at])
        for at, (source, target) in enumerate(pairs)
    ]
    for copy in copies:
        copy.start()
    return copies


def pick_kernel(place_ref, feat_hbm, send_hbm, halo_ref, through_ref, *refs):
    direct_refs, (feat_ref, send_ref, sems) = refs[:-3], refs[-3:]
    copies = fetch([(send_hbm, send_ref), (feat_hbm, feat_ref)], sems)
    copies[0].wait()
    per_peer = send_ref.shape[1]
    chosen = listed_rows(place_ref[0], send_ref, feat_ref.shape[0])
    copies[1].wait()
    halo_ref[...] = feat_ref[feat_ref.shape[0] - halo_ref.shape[0] :]
    picked = rounded(f32_dot(chosen, feat_ref[...]))
    for at, out_ref in enumerate(direct_refs):
        out_ref[...] = picked[2 * at * per_peer : (2 * at + 1) * per_peer]
        through_ref[at * per_peer : (at + 1) * per_peer] = picked[
            (2 * at + 1) * per_peer : (2 * at + 2) * per_peer
        ]


def prepare_kernel(
    per_peer,
    place_ref,
    feat_hbm,
    og_hbm,
    wq_hbm,
    wkv_hbm,
    wo_hbm,
    virt_hbm,
    nbr_hbm,
    exp_hbm,
    og_ref,
    wq_ref,
    wkv_ref,
    featt_ref,
    qt_ref,
    odt_ref,
    kv_ref,
    kvt_ref,
    local_bias_ref,
    far_bias_ref,
    feat_ref,
    wo_ref,
    virt_ref,
    nbr_ref,
    exp_ref,
    sems,
):
    nbr_copy, exp_copy, feat_copy, virt_copy, wq_copy, wkv_copy, og_copy, wo_copy = fetch(
        [
            (nbr_hbm, nbr_ref),
            (exp_hbm, exp_ref),
            (feat_hbm, feat_ref),
            (virt_hbm, virt_ref),
            (wq_hbm, wq_ref),
            (wkv_hbm, wkv_ref),
            (og_hbm, og_ref),
            (wo_hbm, wo_ref),
        ],
        sems,
    )
    row_count, width = feat_ref.shape
    window = local_bias_ref.shape[0]
    far = far_bias_ref.shape[0]
    virt_rows = virt_ref.shape[0]
    padded = kv_ref.shape[0] - row_count
    slots = far - padded
    scale = 1.0 / math.sqrt(width // HEADS)

    def multiplicity(key_rows, named):
        position = lax.broadcasted_iota(jnp.int32, (key_rows, row_count), 0)
        count = jnp.zeros((key_rows, row_count), jnp.float32)
        for at in range(named.shape[0]):
            count += jnp.where(named[at : at + 1, :] == position, 1.0, 0.0)
        return count

    nbr_copy.wait()
    local_bias_ref[...] = jnp.where(multiplicity(window, nbr_ref) > 0.0, 0.0, NEGATIVE_FILL)
    exp_copy.wait()
    expander = exp_ref[...]
    expander = ((expander // per_peer) ^ place_ref[0]) * per_peer + expander % per_peer
    named_times = multiplicity(slots, expander)
    slot_bias = jnp.full((slots, row_count), NEGATIVE_FILL, jnp.float32)
    for times in range(1, exp_ref.shape[0] + 1):
        slot_bias = jnp.where(named_times == float(times), math.log(times) / scale, slot_bias)
    far_bias_ref[:slots] = slot_bias
    virt_row = lax.broadcasted_iota(jnp.int32, (padded, row_count), 0)
    far_bias_ref[slots:] = jnp.where(virt_row < virt_rows, 0.0, NEGATIVE_FILL)

    feat_copy.wait()
    featt_ref[:, :row_count] = feat_ref[...].T
    virt_copy.wait()
    virt = jnp.concatenate(
        [virt_ref[...], jnp.zeros((padded - virt_rows, width), jnp.bfloat16)], axis=0
    )
    featt_ref[:, row_count:] = virt.T
    wq_copy.wait()
    qt_ref[...] = rounded(rows_contracted(wq_ref[...], featt_ref[:, :row_count]))
    wkv_copy.wait()
    kv_ref[:row_count] = rounded(f32_dot(feat_ref[...], wkv_ref[...]))
    kv_ref[row_count:] = rounded(f32_dot(virt, wkv_ref[...]))
    kvt_ref[...] = kv_ref[...].T
    og_copy.wait()
    wo_copy.wait()
    odt_ref[...] = rounded(times_transposed(wo_ref[...], og_ref[...]))


def attend_kernel(
    rows_per_piece,
    factor,
    per_peer,
    dom_size,
    place_ref,
    halo_ref,
    *refs,
):
    piece_refs, refs = refs[: 1 + dom_size // 2], refs[1 + dom_size // 2 :]
    og_ref, wq_ref, wkv_ref, featt_ref, qt_ref, odt_ref, own_kv_ref, own_kvt_ref = refs[:8]
    local_bias_ref, far_bias_ref, gf_ref, halo_feat_ref = refs[8:12]
    slot_feat_refs, refs = refs[12 : 12 + dom_size], refs[12 + dom_size :]
    keep_ref, send_ref, rider_ref = refs[:3]
    slot_ref, kv_ref, kvt_ref, extt_ref, gqt_ref, gkvt_ref, ot_ref = refs[3:]
    width, row_count = qt_ref.shape
    tile = halo_ref.shape[0]
    tile_count = row_count // tile
    slots = dom_size * per_peer
    near = tile + row_count
    virt_at = near + slots
    head_dim = width // HEADS
    scale = 1.0 / math.sqrt(head_dim)

    kv_ref[tile:near] = own_kv_ref[:row_count]
    kv_ref[virt_at:] = own_kv_ref[row_count:]
    kvt_ref[:, tile:near] = own_kvt_ref[:, :row_count]
    kvt_ref[:, virt_at:] = own_kvt_ref[:, row_count:]
    extt_ref[:, tile:near] = featt_ref[:, :row_count]
    extt_ref[:, virt_at:] = featt_ref[:, row_count:]
    slot_ref[:per_peer] = piece_refs[0][...]
    slot_ref[per_peer : 2 * per_peer] = piece_refs[1][:per_peer]
    for at, piece_ref in enumerate(piece_refs[2:], 1):
        slot_ref[2 * at * per_peer : (2 * at + 2) * per_peer] = piece_ref[...]
    for rows, source_ref in ((slice(0, tile), halo_ref), (slice(near, virt_at), slot_ref)):
        extt_ref[:, rows] = source_ref[...].T
        kv_ref[rows] = rounded(f32_dot(source_ref[...], wkv_ref[...]))
        kvt_ref[:, rows] = kv_ref[rows].T

    def tiles(of):
        return jnp.concatenate([of(t, slice(t * tile, (t + 1) * tile)) for t in range(tile_count)], 1)

    for head in range(HEADS):
        low, high = head * head_dim, (head + 1) * head_dim
        first = low // 128 * 128
        last = min(-(-high // 128) * 128, width)
        column = lax.broadcasted_iota(jnp.int32, (last - first, row_count), 0) + first
        of_head = (column >= low) & (column < high)
        q_rows = jnp.where(of_head, qt_ref[first:last, :], 0)
        d_rows = jnp.where(of_head, odt_ref[first:last, :], 0)

        def products(operand, start, stop):
            local = tiles(
                lambda t, lanes: f32_dot(
                    kv_ref[t * tile : (t + 2) * tile, start:stop], operand[:, lanes]
                )
            )
            return local, f32_dot(kv_ref[near:, start:stop], operand)

        s_local, s_far = products(q_rows, first, last)
        s_local += local_bias_ref[...]
        s_far += far_bias_ref[...]
        peak = jnp.maximum(
            jnp.max(s_local, axis=0, keepdims=True), jnp.max(s_far, axis=0, keepdims=True)
        )
        exponent_scale = scale * math.log2(math.e)
        e_local = jnp.exp2((s_local - peak) * exponent_scale)
        e_far = jnp.exp2((s_far - peak) * exponent_scale)
        total = jnp.sum(e_local, axis=0, keepdims=True) + jnp.sum(e_far, axis=0, keepdims=True)
        inverse = 1.0 / total
        p_local = e_local * inverse
        p_far = e_far * inverse
        dp_local, dp_far = products(d_rows, width + first, width + last)
        delta = jnp.sum(p_local * dp_local, axis=0, keepdims=True) + jnp.sum(
            p_far * dp_far, axis=0, keepdims=True
        )
        pb_local, pb_far = rounded(p_local), rounded(p_far)
        ds_local = rounded(p_local * (dp_local - delta))
        ds_far = rounded(p_far * (dp_far - delta))

        def to_queries(start, local, beyond):
            rows = slice(start + low, start + high)
            near_part = tiles(
                lambda t, lanes: f32_dot(kvt_ref[rows, t * tile : (t + 2) * tile], local[:, lanes])
            )
            return near_part + f32_dot(kvt_ref[rows, near:], beyond)

        ot_ref[low:high] = rounded(to_queries(width, pb_local, pb_far))
        gqt_ref[low:high] = rounded(to_queries(0, ds_local, ds_far) * scale)

        def to_keys(start, operand, local, beyond, factor):
            rows = slice(start + low, start + high)
            parts = []
            carried = None
            for t in range(tile_count):
                lanes = slice(t * tile, (t + 1) * tile)
                window = times_transposed(operand[:, lanes], local[:, lanes])
                previous = window[:, :tile]
                parts.append(previous if carried is None else previous + carried)
                carried = window[:, tile:]
            parts.append(carried)
            parts.append(times_transposed(operand, beyond))
            gathered = jnp.concatenate(parts, axis=1)
            gkvt_ref[rows] = rounded(gathered if factor is None else gathered * factor)

        to_keys(0, qt_ref[low:high], ds_local, ds_far, scale)
        to_keys(width, odt_ref[low:high], pb_local, pb_far, None)

    by_feature = f32_dot(wkv_ref[...], gkvt_ref[...])
    own = by_feature[:, tile:near] + f32_dot(wq_ref[...], gqt_ref[...])
    gf_ref[...] = own.T
    halo_feat_ref[...] = rounded(by_feature[:, :tile].T)
    slot_feat = rounded(by_feature[:, near:virt_at].T)
    for at, out_ref in enumerate(slot_feat_refs):
        out_ref[...] = slot_feat[at * per_peer : (at + 1) * per_peer]
    rider_ref[...] = by_feature[:, virt_at:].T * factor

    sums = (
        times_transposed(extt_ref[:, tile:near], gqt_ref[...]),
        times_transposed(extt_ref[...], gkvt_ref[:width]),
        times_transposed(extt_ref[...], gkvt_ref[width:]),
        f32_dot(ot_ref[...], og_ref[...]),
    )
    pieces = keep_ref.shape[0] // rows_per_piece
    held = place_ref[1] % pieces

    def write(half, out_ref, cast):
        for piece in range(pieces):
            start = (half * pieces + piece) * rows_per_piece
            value = sums[start // width][start % width : start % width + rows_per_piece] * factor
            offset = pl.multiple_of((piece ^ held) * rows_per_piece, ROW_PACK)
            out_ref[pl.ds(offset, rows_per_piece), :] = cast(value)

    for half in range(2):

        @pl.when(place_ref[1] // pieces == half)
        def _():
            write(half, keep_ref, lambda value: value)
            write(1 - half, send_ref, rounded)

    send_ref[keep_ref.shape[0] :] = rounded(rider_ref[...])


def place_kernel(rows_per_piece, place_ref, *refs):
    part_refs, (gq_ref, gkv_ref, go_ref, all_ref) = refs[:-4], refs[-4:]
    width = gq_ref.shape[0]
    rows = part_refs[0].shape[0]
    for at, part_ref in enumerate(part_refs):
        all_ref[at * rows : (at + 1) * rows] = part_ref[...]
    for at in range(all_ref.shape[0] // rows_per_piece):
        offset = pl.multiple_of((place_ref[1] ^ at) * rows_per_piece, ROW_PACK)
        value = all_ref[pl.ds(offset, rows_per_piece), :].astype(jnp.float32)
        start = at * rows_per_piece
        rows = slice(start % width, start % width + rows_per_piece)
        which = start // width
        if which == 0:
            gq_ref[rows] = value
        elif which == 3:
            go_ref[rows] = value
        else:
            gkv_ref[rows, (which - 1) * width : which * width] = value


def return_kernel(place_ref, gf_ref, halo_ref, send_ref, *refs):
    piece_refs, out_ref = refs[:-1], refs[-1]
    row_count = gf_ref.shape[0]
    tile = halo_ref.shape[0]
    chosen = listed_rows(place_ref[0], send_ref, row_count)
    returned = jnp.concatenate([ref[...] for ref in piece_refs], axis=0)
    total = gf_ref[...] + rows_contracted(chosen, returned)
    out_ref[: row_count - tile] = total[: row_count - tile]
    out_ref[row_count - tile :] = total[row_count - tile :] + halo_ref[...].astype(jnp.float32)


def call(kernel, name, outs, args, scratch=(), fetched=0, flops=0):
    spaces = [pltpu.SMEM] + [pltpu.HBM] * fetched
    spaces += [pltpu.VMEM] * (len(args) - len(spaces))
    moved = sum(x.size * x.dtype.itemsize for x in list(args) + list(outs))
    scratch = list(scratch)
    if fetched:
        scratch.append(pltpu.SemaphoreType.DMA((fetched,)))
    return pl.pallas_call(
        kernel,
        out_shape=outs,
        in_specs=[pl.BlockSpec(memory_space=space) for space in spaces],
        out_specs=[pl.BlockSpec(memory_space=pltpu.VMEM)] * len(outs),
        scratch_shapes=scratch,
        compiler_params=pltpu.CompilerParams(vmem_limit_bytes=VMEM_BYTES),
        cost_estimate=pl.CostEstimate(flops=flops, bytes_accessed=moved, transcendentals=0),
        name=name,
    )(*args)


def shards(features, out_grad, w_query, w_keyval, w_out, virtual, local_nbr, expander, send_rows):
    row_count, width = features.shape
    dom_size, per_peer = send_rows.shape
    slots = dom_size * per_peer
    virt_rows = virtual.shape[0]
    padded = ROW_PACK * -(-virt_rows // ROW_PACK)
    ext_rows = TILE + row_count + slots + padded
    nodes = row_count * lax.axis_size("dom") * lax.axis_size("rows")
    stages = exchange_stages(lax.axis_size("dom"), lax.axis_size("rows"))
    scattered = scattered_stages(stages, 4 * width)
    rows_per_piece = 4 * width >> sum(len(stage) for stage in scattered)
    place = jnp.stack([lax.axis_index("dom").astype(jnp.int32), own_piece(scattered)])
    bf16, f32 = jnp.bfloat16, jnp.float32
    shape = jax.ShapeDtypeStruct

    halo, through, *direct = call(
        pick_kernel,
        "pick_rows",
        [shape((TILE, width), bf16), shape((slots // 2, width), bf16)]
        + [shape((per_peer, width), bf16)] * (dom_size // 2),
        [place, features, send_rows],
        [pltpu.VMEM(features.shape, bf16), pltpu.VMEM(send_rows.shape, jnp.int32)],
        fetched=2,
    )
    through = swapped(through, 1, 0)
    halo = shifted(halo, "rows", 1)
    arrived = [direct[0], through]
    for at in range(1, dom_size // 2):
        handed_on = through[at * per_peer : (at + 1) * per_peer]
        arrived.append(swapped(jnp.concatenate([direct[at], handed_on], axis=0), 2 * at, 0))
    prepared = call(
        functools.partial(prepare_kernel, per_peer),
        "prepare",
        [
            shape(out_grad.shape, bf16),
            shape(w_query.shape, bf16),
            shape(w_keyval.shape, bf16),
            shape((width, row_count + padded), bf16),
            shape((width, row_count), bf16),
            shape((width, row_count), bf16),
            shape((row_count + padded, 2 * width), bf16),
            shape((2 * width, row_count + padded), bf16),
            shape((2 * TILE, row_count), f32),
            shape((slots + padded, row_count), f32),
        ],
        [place, features, out_grad, w_query, w_keyval, w_out, virtual, local_nbr.T, expander.T],
        [
            pltpu.VMEM(features.shape, bf16),
            pltpu.VMEM(w_out.shape, bf16),
            pltpu.VMEM(virtual.shape, bf16),
            pltpu.VMEM(local_nbr.shape[::-1], jnp.int32),
            pltpu.VMEM(expander.shape[::-1], jnp.int32),
        ],
        fetched=8,
        flops=10 * row_count * width * width,
    )
    own_feat, halo_feat, *results = call(
        functools.partial(attend_kernel, rows_per_piece, nodes**-0.5, per_peer, dom_size),
        "attend",
        [
            shape((row_count, width), f32),
            shape((TILE, width), bf16),
            *[shape((per_peer, width), bf16)] * dom_size,
            shape((2 * width, width), f32),
            shape((2 * width + padded, width), bf16),
            shape((padded, width), f32),
        ],
        [place, halo, *arrived, *prepared],
        [
            pltpu.VMEM((slots, width), bf16),
            pltpu.VMEM((ext_rows, 2 * width), bf16),
            pltpu.VMEM((2 * width, ext_rows), bf16),
            pltpu.VMEM((width, ext_rows), bf16),
            pltpu.VMEM((width, row_count), bf16),
            pltpu.VMEM((2 * width, ext_rows), bf16),
            pltpu.VMEM((width, row_count), bf16),
        ],
        flops=32 * ext_rows * width * width,
    )
    slot_feat, (keep, message, rider) = results[:dom_size], results[dom_size:]

    near, far, rider, returned = summed_everywhere(
        keep, message, rider, stages, scattered, slot_feat
    )
    halo_back = shifted(halo_feat, "rows", -1)
    (grad_features,) = call(
        return_kernel,
        "return_rows",
        [shape((row_count, width), f32)],
        [place, own_feat, halo_back, send_rows, *returned],
    )
    grad_wq, grad_wkv, grad_wo = call(
        functools.partial(place_kernel, rows_per_piece),
        "place_sums",
        [shape((width, width), f32), shape((width, 2 * width), f32), shape((width, width), f32)],
        [place, *near, *far],
        [pltpu.VMEM((4 * width, width), bf16)],
    )
    return grad_features, grad_wq, grad_wkv, grad_wo, rider[:virt_rows]


def solution(mesh):
    placed = (
        P(("dom", "rows"), None),
        P(("dom", "rows"), None),
        P(),
        P(),
        P(),
        P(),
        P(("dom", "rows"), None),
        P(("dom", "rows"), None),
        P(("dom", "rows"), None),
    )
    return jax.shard_map(
        shards,
        mesh=mesh,
        in_specs=placed,
        out_specs=(P(("dom", "rows"), None), P(), P(), P(), P()),
        check_vma=False,
    )
```

```python
import functools
import math

import jax
import jax.numpy as jnp
from jax import lax
from jax.experimental import pallas as pl
from jax.experimental.pallas import tpu as pltpu
from jax.sharding import PartitionSpec as P

HEADS = 8
TILE = 128
ROW_PACK = 16
NEGATIVE_FILL = -1e30
VMEM_BYTES = 24 * 1024 * 1024
LANES = 128


def f32_dot(left, right):
    return jnp.dot(left, right, preferred_element_type=jnp.float32)


def rows_contracted(left, right):
    return lax.dot_general(
        left, right, (((0,), (0,)), ((), ())), preferred_element_type=jnp.float32
    )


def times_transposed(left, right):
    return lax.dot_general(
        left, right, (((1,), (1,)), ((), ())), preferred_element_type=jnp.float32
    )


def rounded(value):
    return value.astype(jnp.bfloat16)


def exchange_stages(dom_size, rows_size):
    dom_bits = [1 << i for i in range(dom_size.bit_length() - 1)]
    rows_bits = [1 << i for i in range(rows_size.bit_length() - 1)]
    stages = [[("rows", bit)] for bit in rows_bits[:1]]
    rest = [("rows", bit) for bit in rows_bits[1:2]] + [("dom", bit) for bit in dom_bits]
    rest += [("rows", bit) for bit in rows_bits[2:]]
    for at in range(0, len(rest), 2):
        stages.append(rest[at : at + 2])
    return stages


def scattered_stages(stages, rows):
    taken = []
    for stage in stages:
        if rows % (ROW_PACK << len(stage)):
            break
        rows >>= len(stage)
        taken.append(stage)
    return taken


def partner_masks(stage):
    masks = []
    for digit in range(1, 1 << len(stage)):
        by_axis = {"dom": 0, "rows": 0}
        for i, (axis, bit) in enumerate(stage):
            if digit >> i & 1:
                by_axis[axis] |= bit
        masks.append((by_axis["dom"], by_axis["rows"]))
    return masks


def own_piece(stages):
    index = jnp.int32(0)
    for stage in stages:
        index = index << len(stage)
        for i, (axis, bit) in enumerate(stage):
            index += jnp.where(lax.axis_index(axis) & bit, 1 << i, 0)
    return index


def swapped(block, dom_mask, rows_mask):
    dom_size, rows_size = lax.axis_size("dom"), lax.axis_size("rows")
    route = [
        (a * rows_size + b, (a ^ dom_mask) * rows_size + (b ^ rows_mask))
        for a in range(dom_size)
        for b in range(rows_size)
    ]
    return lax.ppermute(block, ("dom", "rows"), route)


def shifted(block, axis, distance):
    devices = range(lax.axis_size(axis))
    route = [((i - distance) % len(devices), i) for i in devices]
    return lax.ppermute(block, axis, route)


def paired_sum(terms):
    while len(terms) > 1:
        terms = [left + right for left, right in zip(terms[::2], terms[1::2])]
    return terms[0]


def routed(direct, through):
    return handed_on(direct, swapped(through, 1, 0))


def handed_on(direct, through):
    rows = direct[0].shape[0]
    arrived = [direct[0], through]
    for at in range(1, len(direct)):
        message = jnp.concatenate([direct[at], through[at * rows : (at + 1) * rows]], axis=0)
        arrived.append(swapped(message, 2 * at, 0))
    return arrived


def scatter_stage(keep, rider, stage, halved):
    part = keep.shape[0] >> len(stage) if halved else keep.shape[0]
    rider_bf = rounded(rider)
    if not halved:
        keep = rounded(keep).astype(jnp.float32)
    messages = []
    for at in range(1, 1 << len(stage)):
        block = keep[at * part : (at + 1) * part] if halved else keep
        messages.append(jnp.concatenate([rounded(block), rider_bf], axis=0))
    return keep[:part], rider_bf.astype(jnp.float32), messages


def exchange(messages, stage, last_first):
    routes = list(zip(messages, partner_masks(stage)))
    if last_first:
        return [swapped(message, *masks) for message, masks in routes[::-1]][::-1]
    return [swapped(message, *masks) for message, masks in routes]


def added(keep, rider, arrived):
    part = keep.shape[0]
    terms = [keep] + [block[:part].astype(jnp.float32) for block in arrived]
    riders = [rider] + [block[part:].astype(jnp.float32) for block in arrived]
    return paired_sum(terms), paired_sum(riders)


def gathered(held, stage):
    return jnp.concatenate([held] + exchange([held] * ((1 << len(stage)) - 1), stage, True), axis=0)


def listed_rows(dom, send_ref, row_count):
    dom_size, per_peer = send_ref.shape
    slots = dom_size * per_peer
    slot = lax.broadcasted_iota(jnp.int32, (slots, per_peer), 0)
    place = lax.broadcasted_iota(jnp.int32, (slots, per_peer), 1)
    peer = (slot // per_peer) ^ dom
    listed = jnp.zeros((slots, per_peer), jnp.int32)
    for at in range(dom_size):
        listed += jnp.where((peer == at) & (place == slot % per_peer), send_ref[at : at + 1, :], 0)
    column = jnp.sum(listed, axis=1, keepdims=True)
    rows = lax.broadcasted_iota(jnp.int32, (slots, row_count), 1)
    return jnp.where(column == rows, 1.0, 0.0).astype(jnp.bfloat16)


def fetch(pairs, sems):
    copies = [
        pltpu.make_async_copy(source, target, sems.at[at])
        for at, (source, target) in enumerate(pairs)
    ]
    for copy in copies:
        copy.start()
    return copies


def pick_kernel(place_ref, feat_hbm, send_hbm, halo_ref, through_ref, *refs):
    direct_refs, (feat_ref, send_ref, sems) = refs[:-3], refs[-3:]
    copies = fetch([(send_hbm, send_ref), (feat_hbm, feat_ref)], sems)
    copies[0].wait()
    per_peer = send_ref.shape[1]
    chosen = listed_rows(place_ref[0], send_ref, feat_ref.shape[0])
    copies[1].wait()
    halo_ref[...] = feat_ref[feat_ref.shape[0] - halo_ref.shape[0] :]
    picked = rounded(f32_dot(chosen, feat_ref[...]))
    for at, out_ref in enumerate(direct_refs):
        out_ref[...] = picked[2 * at * per_peer : (2 * at + 1) * per_peer]
        through_ref[at * per_peer : (at + 1) * per_peer] = picked[
            (2 * at + 1) * per_peer : (2 * at + 2) * per_peer
        ]


def prepare_kernel(
    per_peer,
    place_ref,
    feat_hbm,
    og_hbm,
    wq_hbm,
    wkv_hbm,
    wo_hbm,
    virt_hbm,
    nbr_hbm,
    exp_hbm,
    og_ref,
    wq_ref,
    wkv_ref,
    featt_ref,
    qt_ref,
    odt_ref,
    kv_ref,
    kvt_ref,
    local_bias_ref,
    far_bias_ref,
    feat_ref,
    wo_ref,
    virt_ref,
    nbr_ref,
    exp_ref,
    sems,
):
    nbr_copy, exp_copy, feat_copy, virt_copy, wq_copy, wkv_copy, og_copy, wo_copy = fetch(
        [
            (nbr_hbm, nbr_ref),
            (exp_hbm, exp_ref),
            (feat_hbm, feat_ref),
            (virt_hbm, virt_ref),
            (wq_hbm, wq_ref),
            (wkv_hbm, wkv_ref),
            (og_hbm, og_ref),
            (wo_hbm, wo_ref),
        ],
        sems,
    )
    row_count, width = feat_ref.shape
    window = local_bias_ref.shape[0]
    far = far_bias_ref.shape[0]
    virt_rows = virt_ref.shape[0]
    padded = kv_ref.shape[0] - row_count
    slots = far - padded
    scale = 1.0 / math.sqrt(width // HEADS)

    def multiplicity(key_rows, named):
        position = lax.broadcasted_iota(jnp.int32, (key_rows, row_count), 0)
        count = jnp.zeros((key_rows, row_count), jnp.float32)
        for at in range(named.shape[0]):
            count += jnp.where(named[at : at + 1, :] == position, 1.0, 0.0)
        return count

    nbr_copy.wait()
    local_bias_ref[...] = jnp.where(multiplicity(window, nbr_ref) > 0.0, 0.0, NEGATIVE_FILL)
    exp_copy.wait()
    expander = exp_ref[...]
    expander = ((expander // per_peer) ^ place_ref[0]) * per_peer + expander % per_peer
    named_times = multiplicity(slots, expander)
    slot_bias = jnp.full((slots, row_count), NEGATIVE_FILL, jnp.float32)
    for times in range(1, exp_ref.shape[0] + 1):
        slot_bias = jnp.where(named_times == float(times), math.log(times) / scale, slot_bias)
    far_bias_ref[:slots] = slot_bias
    virt_row = lax.broadcasted_iota(jnp.int32, (padded, row_count), 0)
    far_bias_ref[slots:] = jnp.where(virt_row < virt_rows, 0.0, NEGATIVE_FILL)

    feat_copy.wait()
    featt_ref[:, :row_count] = feat_ref[...].T
    virt_copy.wait()
    virt = jnp.concatenate(
        [virt_ref[...], jnp.zeros((padded - virt_rows, width), jnp.bfloat16)], axis=0
    )
    featt_ref[:, row_count:] = virt.T
    wq_copy.wait()
    qt_ref[...] = rounded(rows_contracted(wq_ref[...], featt_ref[:, :row_count]))
    wkv_copy.wait()
    kv_ref[:row_count] = rounded(f32_dot(feat_ref[...], wkv_ref[...]))
    kv_ref[row_count:] = rounded(f32_dot(virt, wkv_ref[...]))
    kvt_ref[...] = kv_ref[...].T
    og_copy.wait()
    wo_copy.wait()
    odt_ref[...] = rounded(times_transposed(wo_ref[...], og_ref[...]))


def attend_kernel(
    rows_per_piece,
    factor,
    per_peer,
    dom_size,
    place_ref,
    halo_ref,
    *refs,
):
    piece_refs, refs = refs[: 1 + dom_size // 2], refs[1 + dom_size // 2 :]
    og_ref, wq_ref, wkv_ref, featt_ref, qt_ref, odt_ref, own_kv_ref, own_kvt_ref = refs[:8]
    local_bias_ref, far_bias_ref, gf_ref, halo_feat_ref = refs[8:12]
    direct_refs, refs = refs[12 : 12 + dom_size // 2], refs[12 + dom_size // 2 :]
    through_ref, refs = refs[0], refs[1:]
    keep_ref, send_ref, rider_ref = refs[:3]
    slot_ref, kv_ref, kvt_ref, extt_ref, gqt_ref, gkvt_ref, ot_ref = refs[3:]
    width, row_count = qt_ref.shape
    tile = halo_ref.shape[0]
    tile_count = row_count // tile
    slots = dom_size * per_peer
    near = tile + row_count
    virt_at = near + slots
    head_dim = width // HEADS
    scale = 1.0 / math.sqrt(head_dim)

    kv_ref[tile:near] = own_kv_ref[:row_count]
    kv_ref[virt_at:] = own_kv_ref[row_count:]
    kvt_ref[:, tile:near] = own_kvt_ref[:, :row_count]
    kvt_ref[:, virt_at:] = own_kvt_ref[:, row_count:]
    extt_ref[:, tile:near] = featt_ref[:, :row_count]
    extt_ref[:, virt_at:] = featt_ref[:, row_count:]
    slot_ref[:per_peer] = piece_refs[0][...]
    slot_ref[per_peer : 2 * per_peer] = piece_refs[1][:per_peer]
    for at, piece_ref in enumerate(piece_refs[2:], 1):
        slot_ref[2 * at * per_peer : (2 * at + 2) * per_peer] = piece_ref[...]
    for rows, source_ref in ((slice(0, tile), halo_ref), (slice(near, virt_at), slot_ref)):
        extt_ref[:, rows] = source_ref[...].T
        kv_ref[rows] = rounded(f32_dot(source_ref[...], wkv_ref[...]))
        kvt_ref[:, rows] = kv_ref[rows].T

    def tiles(of):
        return jnp.concatenate([of(t, slice(t * tile, (t + 1) * tile)) for t in range(tile_count)], 1)

    for head in range(HEADS):
        low, high = head * head_dim, (head + 1) * head_dim
        first = low // 128 * 128
        last = min(-(-high // 128) * 128, width)
        column = lax.broadcasted_iota(jnp.int32, (last - first, row_count), 0) + first
        of_head = (column >= low) & (column < high)
        q_rows = jnp.where(of_head, qt_ref[first:last, :], 0)
        d_rows = jnp.where(of_head, odt_ref[first:last, :], 0)

        def products(operand, start, stop):
            local = tiles(
                lambda t, lanes: f32_dot(
                    kv_ref[t * tile : (t + 2) * tile, start:stop], operand[:, lanes]
                )
            )
            return local, f32_dot(kv_ref[near:, start:stop], operand)

        s_local, s_far = products(q_rows, first, last)
        s_local += local_bias_ref[...]
        s_far += far_bias_ref[...]
        peak = jnp.maximum(
            jnp.max(s_local, axis=0, keepdims=True), jnp.max(s_far, axis=0, keepdims=True)
        )
        exponent_scale = scale * math.log2(math.e)
        e_local = jnp.exp2((s_local - peak) * exponent_scale)
        e_far = jnp.exp2((s_far - peak) * exponent_scale)
        total = jnp.sum(e_local, axis=0, keepdims=True) + jnp.sum(e_far, axis=0, keepdims=True)
        inverse = 1.0 / total
        p_local = e_local * inverse
        p_far = e_far * inverse
        dp_local, dp_far = products(d_rows, width + first, width + last)
        delta = jnp.sum(p_local * dp_local, axis=0, keepdims=True) + jnp.sum(
            p_far * dp_far, axis=0, keepdims=True
        )
        pb_local, pb_far = rounded(p_local), rounded(p_far)
        ds_local = rounded(p_local * (dp_local - delta))
        ds_far = rounded(p_far * (dp_far - delta))

        def to_queries(start, local, beyond):
            rows = slice(start + low, start + high)
            near_part = tiles(
                lambda t, lanes: f32_dot(kvt_ref[rows, t * tile : (t + 2) * tile], local[:, lanes])
            )
            return near_part + f32_dot(kvt_ref[rows, near:], beyond)

        ot_ref[low:high] = rounded(to_queries(width, pb_local, pb_far))
        gqt_ref[low:high] = rounded(to_queries(0, ds_local, ds_far) * scale)

        def to_keys(start, operand, local, beyond, factor):
            rows = slice(start + low, start + high)
            parts = []
            carried = None
            for t in range(tile_count):
                lanes = slice(t * tile, (t + 1) * tile)
                window = times_transposed(operand[:, lanes], local[:, lanes])
                previous = window[:, :tile]
                parts.append(previous if carried is None else previous + carried)
                carried = window[:, tile:]
            parts.append(carried)
            parts.append(times_transposed(operand, beyond))
            gathered = jnp.concatenate(parts, axis=1)
            gkvt_ref[rows] = rounded(gathered if factor is None else gathered * factor)

        to_keys(0, qt_ref[low:high], ds_local, ds_far, scale)
        to_keys(width, odt_ref[low:high], pb_local, pb_far, None)

    by_feature = f32_dot(wkv_ref[...], gkvt_ref[...])
    own = by_feature[:, tile:near] + f32_dot(wq_ref[...], gqt_ref[...])
    gf_ref[...] = own.T
    halo_feat_ref[...] = rounded(by_feature[:, :tile].T)
    slot_feat = rounded(by_feature[:, near:virt_at].T)
    for at, out_ref in enumerate(direct_refs):
        out_ref[...] = slot_feat[2 * at * per_peer : (2 * at + 1) * per_peer]
        through_ref[at * per_peer : (at + 1) * per_peer] = slot_feat[
            (2 * at + 1) * per_peer : (2 * at + 2) * per_peer
        ]
    rider_ref[...] = by_feature[:, virt_at:].T * factor

    sums = (
        times_transposed(extt_ref[:, tile:near], gqt_ref[...]),
        times_transposed(extt_ref[...], gkvt_ref[:width]),
        times_transposed(extt_ref[...], gkvt_ref[width:]),
        f32_dot(ot_ref[...], og_ref[...]),
    )
    pieces = keep_ref.shape[0] // rows_per_piece
    held = place_ref[1] % pieces

    def write(half, out_ref, cast):
        for piece in range(pieces):
            start = (half * pieces + piece) * rows_per_piece
            value = sums[start // width][start % width : start % width + rows_per_piece] * factor
            offset = pl.multiple_of((piece ^ held) * rows_per_piece, ROW_PACK)
            out_ref[pl.ds(offset, rows_per_piece), :] = cast(value)

    for half in range(2):

        @pl.when(place_ref[1] // pieces == half)
        def _():
            write(half, keep_ref, lambda value: value)
            write(1 - half, send_ref, rounded)

    send_ref[keep_ref.shape[0] :] = rounded(rider_ref[...])


def place_kernel(rows_per_piece, place_ref, *refs):
    part_refs, (gq_ref, gkv_ref, go_ref, all_ref) = refs[:-4], refs[-4:]
    width = gq_ref.shape[0]
    rows = part_refs[0].shape[0]
    for at, part_ref in enumerate(part_refs):
        all_ref[at * rows : (at + 1) * rows] = part_ref[...]
    for at in range(all_ref.shape[0] // rows_per_piece):
        offset = pl.multiple_of((place_ref[1] ^ at) * rows_per_piece, ROW_PACK)
        value = all_ref[pl.ds(offset, rows_per_piece), :].astype(jnp.float32)
        start = at * rows_per_piece
        rows = slice(start % width, start % width + rows_per_piece)
        which = start // width
        if which == 0:
            gq_ref[rows] = value
        elif which == 3:
            go_ref[rows] = value
        else:
            gkv_ref[rows, (which - 1) * width : which * width] = value


def return_kernel(place_ref, send_hbm, gf_ref, halo_ref, *refs):
    piece_refs, (out_ref, send_ref, sems) = refs[:-3], refs[-3:]
    fetch([(send_hbm, send_ref)], sems)[0].wait()
    row_count = gf_ref.shape[0]
    tile = halo_ref.shape[0]
    per_peer = send_ref.shape[1]
    chosen = listed_rows(place_ref[0], send_ref, row_count)
    returned = jnp.concatenate(
        [piece_refs[0][...], piece_refs[1][:per_peer]] + [ref[...] for ref in piece_refs[2:]],
        axis=0,
    )
    total = gf_ref[...] + rows_contracted(chosen, returned)
    out_ref[: row_count - tile] = total[: row_count - tile]
    out_ref[row_count - tile :] = total[row_count - tile :] + halo_ref[...].astype(jnp.float32)


def call(kernel, name, outs, args, scratch=(), fetched=0, flops=0):
    spaces = [pltpu.SMEM] + [pltpu.HBM] * fetched
    spaces += [pltpu.VMEM] * (len(args) - len(spaces))
    moved = sum(x.size * x.dtype.itemsize for x in list(args) + list(outs))
    scratch = list(scratch)
    if fetched:
        scratch.append(pltpu.SemaphoreType.DMA((fetched,)))
    constrained = [
        pltpu.with_memory_space_constraint(x, pltpu.HBM) if space is pltpu.HBM else x
        for x, space in zip(args, spaces)
    ]
    return pl.pallas_call(
        kernel,
        out_shape=outs,
        in_specs=[pl.BlockSpec(memory_space=space) for space in spaces],
        out_specs=[pl.BlockSpec(memory_space=pltpu.VMEM)] * len(outs),
        scratch_shapes=scratch,
        compiler_params=pltpu.CompilerParams(vmem_limit_bytes=VMEM_BYTES),
        cost_estimate=pl.CostEstimate(flops=flops, bytes_accessed=moved, transcendentals=0),
        name=name,
    )(*constrained)


def shards(features, out_grad, w_query, w_keyval, w_out, virtual, local_nbr, expander, send_rows):
    row_count, width = features.shape
    dom_size, per_peer = send_rows.shape
    slots = dom_size * per_peer
    virt_rows = virtual.shape[0]
    padded = ROW_PACK * -(-virt_rows // ROW_PACK)
    ext_rows = TILE + row_count + slots + padded
    nodes = row_count * lax.axis_size("dom") * lax.axis_size("rows")
    stages = exchange_stages(lax.axis_size("dom"), lax.axis_size("rows"))
    scattered = scattered_stages(stages, 4 * width)
    rows_per_piece = 4 * width >> sum(len(stage) for stage in scattered)
    place = jnp.stack([lax.axis_index("dom").astype(jnp.int32), own_piece(scattered)])
    bf16, f32 = jnp.bfloat16, jnp.float32
    shape = jax.ShapeDtypeStruct

    halo, through, *direct = call(
        pick_kernel,
        "pick_rows",
        [shape((TILE, width), bf16), shape((slots // 2, width), bf16)]
        + [shape((per_peer, width), bf16)] * (dom_size // 2),
        [place, features, send_rows],
        [pltpu.VMEM(features.shape, bf16), pltpu.VMEM(send_rows.shape, jnp.int32)],
        fetched=2,
    )
    arrived = routed(direct, through)
    halo = shifted(halo, "rows", 1)
    prepared = call(
        functools.partial(prepare_kernel, per_peer),
        "prepare",
        [
            shape(out_grad.shape, bf16),
            shape(w_query.shape, bf16),
            shape(w_keyval.shape, bf16),
            shape((width, row_count + padded), bf16),
            shape((width, row_count), bf16),
            shape((width, row_count), bf16),
            shape((row_count + padded, 2 * width), bf16),
            shape((2 * width, row_count + padded), bf16),
            shape((2 * TILE, row_count), f32),
            shape((slots + padded, row_count), f32),
        ],
        [place, features, out_grad, w_query, w_keyval, w_out, virtual, local_nbr.T, expander.T],
        [
            pltpu.VMEM(features.shape, bf16),
            pltpu.VMEM(w_out.shape, bf16),
            pltpu.VMEM(virtual.shape, bf16),
            pltpu.VMEM(local_nbr.shape[::-1], jnp.int32),
            pltpu.VMEM(expander.shape[::-1], jnp.int32),
        ],
        fetched=8,
        flops=10 * row_count * width * width,
    )
    own_feat, halo_feat, *results = call(
        functools.partial(attend_kernel, rows_per_piece, nodes**-0.5, per_peer, dom_size),
        "attend",
        [
            shape((row_count, width), f32),
            shape((TILE, width), bf16),
            *[shape((per_peer, width), bf16)] * (dom_size // 2),
            shape((slots // 2, width), bf16),
            shape((2 * width, width), f32),
            shape((2 * width + padded, width), bf16),
            shape((padded, width), f32),
        ],
        [place, halo, *arrived, *prepared],
        [
            pltpu.VMEM((slots, width), bf16),
            pltpu.VMEM((ext_rows, 2 * width), bf16),
            pltpu.VMEM((2 * width, ext_rows), bf16),
            pltpu.VMEM((width, ext_rows), bf16),
            pltpu.VMEM((width, row_count), bf16),
            pltpu.VMEM((2 * width, ext_rows), bf16),
            pltpu.VMEM((width, row_count), bf16),
        ],
        flops=32 * ext_rows * width * width,
    )
    *direct, through, keep, message, rider = results

    rider = rounded(rider).astype(f32)
    keep, rider = added(keep, rider, exchange([message], stages[0], False))
    through = swapped(through, 1, 0)
    halo_back = shifted(halo_feat, "rows", -1)
    for at, stage in enumerate(stages[1:], 1):
        keep, rider, messages = scatter_stage(keep, rider, stage, stage in scattered)
        if at == 1:
            through, _ = lax.optimization_barrier((through, messages))
            returned = handed_on(direct, through)
        if at == 2:
            messages, returned = lax.optimization_barrier((messages, returned))
        keep, rider = added(keep, rider, exchange(messages, stage, False))
    (grad_features,) = call(
        return_kernel,
        "return_rows",
        [shape((row_count, width), f32)],
        [place, send_rows, own_feat, halo_back, *returned],
        [pltpu.VMEM(send_rows.shape, jnp.int32)],
        fetched=1,
    )
    held = rounded(keep)
    for stage in reversed(scattered[2:]):
        held = gathered(held, stage)
    held, grad_features = lax.optimization_barrier((held, grad_features))
    near = [held] + exchange([held] * ((1 << len(scattered[1])) - 1), scattered[1], True)
    far = [swapped(block, *partner_masks(scattered[0])[0]) for block in near]
    grad_wq, grad_wkv, grad_wo = call(
        functools.partial(place_kernel, rows_per_piece),
        "place_sums",
        [shape((width, width), f32), shape((width, 2 * width), f32), shape((width, width), f32)],
        [place, *near, *far],
        [pltpu.VMEM((4 * width, width), bf16)],
    )
    return grad_features, grad_wq, grad_wkv, grad_wo, rider[:virt_rows]


def solution(mesh):
    placed = (
        P(("dom", "rows"), None),
        P(("dom", "rows"), None),
        P(),
        P(),
        P(),
        P(),
        P(("dom", "rows"), None),
        P(("dom", "rows"), None),
        P(("dom", "rows"), None),
    )
    return jax.shard_map(
        shards,
        mesh=mesh,
        in_specs=placed,
        out_specs=(P(("dom", "rows"), None), P(), P(), P(), P()),
        check_vma=False,
    )
```

```python
import functools
import math

import jax
import jax.numpy as jnp
from jax import lax
from jax.experimental import pallas as pl
from jax.experimental.pallas import tpu as pltpu
from jax.sharding import PartitionSpec as P

HEADS = 8
TILE = 128
ROW_PACK = 16
NEGATIVE_FILL = -1e30
VMEM_BYTES = 24 * 1024 * 1024
LANES = 128


def f32_dot(left, right):
    return jnp.dot(left, right, preferred_element_type=jnp.float32)


def rows_contracted(left, right):
    return lax.dot_general(
        left, right, (((0,), (0,)), ((), ())), preferred_element_type=jnp.float32
    )


def times_transposed(left, right):
    return lax.dot_general(
        left, right, (((1,), (1,)), ((), ())), preferred_element_type=jnp.float32
    )


def rounded(value):
    return value.astype(jnp.bfloat16)


def exchange_stages(dom_size, rows_size):
    stages = [[((0, 1), (0, 1))], [((1, 2), (0, 2)), ((1, 0), (1, 2))]]
    stages += [[((bit, 0), (bit, 0))] for bit in powers_of_two(2, dom_size)]
    stages += [[((0, bit), (0, bit))] for bit in powers_of_two(4, rows_size)]
    return stages


def powers_of_two(first, size):
    return [1 << i for i in range(size.bit_length() - 1) if 1 << i >= first]


def partner_masks(stage):
    masks = []
    for digit in range(1, 1 << len(stage)):
        dom_mask = rows_mask = 0
        for i, (mask, _) in enumerate(stage):
            if digit >> i & 1:
                dom_mask ^= mask[0]
                rows_mask ^= mask[1]
        masks.append((dom_mask, rows_mask))
    return masks


def own_piece(stages):
    index = jnp.int32(0)
    for stage in stages:
        index = index << len(stage)
        for i, (_, parity) in enumerate(stage):
            odd = jnp.int32(0)
            for axis, mask in zip(("dom", "rows"), parity):
                for bit in powers_of_two(1, 2 * mask) if mask else []:
                    odd ^= jnp.where(lax.axis_index(axis) & bit & mask, 1, 0)
            index += odd << i
    return index


def swapped(block, dom_mask, rows_mask):
    dom_size, rows_size = lax.axis_size("dom"), lax.axis_size("rows")
    route = [
        (a * rows_size + b, (a ^ dom_mask) * rows_size + (b ^ rows_mask))
        for a in range(dom_size)
        for b in range(rows_size)
    ]
    return lax.ppermute(block, ("dom", "rows"), route)


def shifted(block, axis, distance):
    devices = range(lax.axis_size(axis))
    route = [((i - distance) % len(devices), i) for i in devices]
    return lax.ppermute(block, axis, route)


def paired_sum(terms):
    while len(terms) > 1:
        terms = [left + right for left, right in zip(terms[::2], terms[1::2])]
    return terms[0]


def routed(direct, through):
    return handed_on(direct, swapped(through, 1, 0))


def handed_on(direct, through):
    rows = direct[0].shape[0]
    arrived = [direct[0], through]
    for at in range(1, len(direct)):
        message = jnp.concatenate([direct[at], through[at * rows : (at + 1) * rows]], axis=0)
        arrived.append(swapped(message, 2 * at, 0))
    return arrived


def scatter_stage(keep, rider, stage, halved):
    part = keep.shape[0] >> len(stage) if halved else keep.shape[0]
    rider_bf = rounded(rider)
    if not halved:
        keep = rounded(keep).astype(jnp.float32)
    messages = []
    for at in range(1, 1 << len(stage)):
        block = keep[at * part : (at + 1) * part] if halved else keep
        messages.append(jnp.concatenate([rounded(block), rider_bf], axis=0))
    return keep[:part], rider_bf.astype(jnp.float32), messages


def exchange(messages, stage):
    return [swapped(message, *masks) for message, masks in zip(messages, partner_masks(stage))]


def added(keep, rider, arrived):
    part = keep.shape[0]
    terms = [keep] + [block[:part].astype(jnp.float32) for block in arrived]
    riders = [rider] + [block[part:].astype(jnp.float32) for block in arrived]
    return paired_sum(terms), paired_sum(riders)


def gathered(held, stage):
    return jnp.concatenate([held] + exchange([held] * ((1 << len(stage)) - 1), stage), axis=0)


def listed_rows(dom, send_ref, row_count):
    dom_size, per_peer = send_ref.shape
    slots = dom_size * per_peer
    slot = lax.broadcasted_iota(jnp.int32, (slots, per_peer), 0)
    place = lax.broadcasted_iota(jnp.int32, (slots, per_peer), 1)
    peer = (slot // per_peer) ^ dom
    listed = jnp.zeros((slots, per_peer), jnp.int32)
    for at in range(dom_size):
        listed += jnp.where((peer == at) & (place == slot % per_peer), send_ref[at : at + 1, :], 0)
    column = jnp.sum(listed, axis=1, keepdims=True)
    rows = lax.broadcasted_iota(jnp.int32, (slots, row_count), 1)
    return jnp.where(column == rows, 1.0, 0.0).astype(jnp.bfloat16)


def fetch(pairs, sems):
    copies = [
        pltpu.make_async_copy(source, target, sems.at[at])
        for at, (source, target) in enumerate(pairs)
    ]
    for copy in copies:
        copy.start()
    return copies


def pick_kernel(place_ref, feat_hbm, send_hbm, halo_ref, through_ref, *refs):
    direct_refs, (feat_ref, send_ref, sems) = refs[:-3], refs[-3:]
    copies = fetch([(send_hbm, send_ref), (feat_hbm, feat_ref)], sems)
    copies[0].wait()
    per_peer = send_ref.shape[1]
    chosen = listed_rows(place_ref[0], send_ref, feat_ref.shape[0])
    copies[1].wait()
    halo_ref[...] = feat_ref[feat_ref.shape[0] - halo_ref.shape[0] :]
    picked = rounded(f32_dot(chosen, feat_ref[...]))
    for at, out_ref in enumerate(direct_refs):
        out_ref[...] = picked[2 * at * per_peer : (2 * at + 1) * per_peer]
        through_ref[at * per_peer : (at + 1) * per_peer] = picked[
            (2 * at + 1) * per_peer : (2 * at + 2) * per_peer
        ]


def prepare_kernel(
    per_peer,
    place_ref,
    feat_hbm,
    og_hbm,
    wq_hbm,
    wkv_hbm,
    wo_hbm,
    virt_hbm,
    nbr_hbm,
    exp_hbm,
    og_ref,
    wq_ref,
    wkv_ref,
    featt_ref,
    qt_ref,
    odt_ref,
    kv_ref,
    kvt_ref,
    local_bias_ref,
    far_bias_ref,
    feat_ref,
    wo_ref,
    virt_ref,
    nbr_ref,
    exp_ref,
    sems,
):
    nbr_copy, exp_copy, feat_copy, virt_copy, wq_copy, wkv_copy, og_copy, wo_copy = fetch(
        [
            (nbr_hbm, nbr_ref),
            (exp_hbm, exp_ref),
            (feat_hbm, feat_ref),
            (virt_hbm, virt_ref),
            (wq_hbm, wq_ref),
            (wkv_hbm, wkv_ref),
            (og_hbm, og_ref),
            (wo_hbm, wo_ref),
        ],
        sems,
    )
    row_count, width = feat_ref.shape
    window = local_bias_ref.shape[0]
    far = far_bias_ref.shape[0]
    virt_rows = virt_ref.shape[0]
    padded = kv_ref.shape[0] - row_count
    slots = far - padded
    scale = 1.0 / math.sqrt(width // HEADS)

    def multiplicity(key_rows, named):
        position = lax.broadcasted_iota(jnp.int32, (key_rows, row_count), 0)
        count = jnp.zeros((key_rows, row_count), jnp.float32)
        for at in range(named.shape[0]):
            count += jnp.where(named[at : at + 1, :] == position, 1.0, 0.0)
        return count

    nbr_copy.wait()
    local_bias_ref[...] = jnp.where(multiplicity(window, nbr_ref) > 0.0, 0.0, NEGATIVE_FILL)
    exp_copy.wait()
    expander = exp_ref[...]
    expander = ((expander // per_peer) ^ place_ref[0]) * per_peer + expander % per_peer
    named_times = multiplicity(slots, expander)
    slot_bias = jnp.full((slots, row_count), NEGATIVE_FILL, jnp.float32)
    for times in range(1, exp_ref.shape[0] + 1):
        slot_bias = jnp.where(named_times == float(times), math.log(times) / scale, slot_bias)
    far_bias_ref[:slots] = slot_bias
    virt_row = lax.broadcasted_iota(jnp.int32, (padded, row_count), 0)
    far_bias_ref[slots:] = jnp.where(virt_row < virt_rows, 0.0, NEGATIVE_FILL)

    feat_copy.wait()
    featt_ref[:, :row_count] = feat_ref[...].T
    virt_copy.wait()
    virt = jnp.concatenate(
        [virt_ref[...], jnp.zeros((padded - virt_rows, width), jnp.bfloat16)], axis=0
    )
    featt_ref[:, row_count:] = virt.T
    wq_copy.wait()
    qt_ref[...] = rounded(rows_contracted(wq_ref[...], featt_ref[:, :row_count]))
    wkv_copy.wait()
    kv_ref[:row_count] = rounded(f32_dot(feat_ref[...], wkv_ref[...]))
    kv_ref[row_count:] = rounded(f32_dot(virt, wkv_ref[...]))
    kvt_ref[...] = kv_ref[...].T
    og_copy.wait()
    wo_copy.wait()
    odt_ref[...] = rounded(times_transposed(wo_ref[...], og_ref[...]))


def attend_kernel(
    rows_per_piece,
    factor,
    per_peer,
    dom_size,
    place_ref,
    halo_ref,
    *refs,
):
    piece_refs, refs = refs[: 1 + dom_size // 2], refs[1 + dom_size // 2 :]
    og_ref, wq_ref, wkv_ref, featt_ref, qt_ref, odt_ref, own_kv_ref, own_kvt_ref = refs[:8]
    local_bias_ref, far_bias_ref, gf_ref, halo_feat_ref = refs[8:12]
    direct_refs, refs = refs[12 : 12 + dom_size // 2], refs[12 + dom_size // 2 :]
    through_ref, refs = refs[0], refs[1:]
    keep_ref, send_ref, rider_ref = refs[:3]
    slot_ref, kv_ref, kvt_ref, extt_ref, gqt_ref, gkvt_ref, ot_ref = refs[3:]
    width, row_count = qt_ref.shape
    tile = halo_ref.shape[0]
    tile_count = row_count // tile
    slots = dom_size * per_peer
    near = tile + row_count
    virt_at = near + slots
    head_dim = width // HEADS
    scale = 1.0 / math.sqrt(head_dim)

    kv_ref[tile:near] = own_kv_ref[:row_count]
    kv_ref[virt_at:] = own_kv_ref[row_count:]
    kvt_ref[:, tile:near] = own_kvt_ref[:, :row_count]
    kvt_ref[:, virt_at:] = own_kvt_ref[:, row_count:]
    extt_ref[:, tile:near] = featt_ref[:, :row_count]
    extt_ref[:, virt_at:] = featt_ref[:, row_count:]
    slot_ref[:per_peer] = piece_refs[0][...]
    slot_ref[per_peer : 2 * per_peer] = piece_refs[1][:per_peer]
    for at, piece_ref in enumerate(piece_refs[2:], 1):
        slot_ref[2 * at * per_peer : (2 * at + 2) * per_peer] = piece_ref[...]
    for rows, source_ref in ((slice(0, tile), halo_ref), (slice(near, virt_at), slot_ref)):
        extt_ref[:, rows] = source_ref[...].T
        kv_ref[rows] = rounded(f32_dot(source_ref[...], wkv_ref[...]))
        kvt_ref[:, rows] = kv_ref[rows].T

    def tiles(of):
        return jnp.concatenate([of(t, slice(t * tile, (t + 1) * tile)) for t in range(tile_count)], 1)

    for head in range(HEADS):
        low, high = head * head_dim, (head + 1) * head_dim
        first = low // 128 * 128
        last = min(-(-high // 128) * 128, width)
        column = lax.broadcasted_iota(jnp.int32, (last - first, row_count), 0) + first
        of_head = (column >= low) & (column < high)
        q_rows = jnp.where(of_head, qt_ref[first:last, :], 0)
        d_rows = jnp.where(of_head, odt_ref[first:last, :], 0)

        def products(operand, start, stop):
            local = tiles(
                lambda t, lanes: f32_dot(
                    kv_ref[t * tile : (t + 2) * tile, start:stop], operand[:, lanes]
                )
            )
            return local, f32_dot(kv_ref[near:, start:stop], operand)

        s_local, s_far = products(q_rows, first, last)
        s_local += local_bias_ref[...]
        s_far += far_bias_ref[...]
        peak = jnp.maximum(
            jnp.max(s_local, axis=0, keepdims=True), jnp.max(s_far, axis=0, keepdims=True)
        )
        exponent_scale = scale * math.log2(math.e)
        e_local = jnp.exp2((s_local - peak) * exponent_scale)
        e_far = jnp.exp2((s_far - peak) * exponent_scale)
        total = jnp.sum(e_local, axis=0, keepdims=True) + jnp.sum(e_far, axis=0, keepdims=True)
        inverse = 1.0 / total
        p_local = e_local * inverse
        p_far = e_far * inverse
        dp_local, dp_far = products(d_rows, width + first, width + last)
        delta = jnp.sum(p_local * dp_local, axis=0, keepdims=True) + jnp.sum(
            p_far * dp_far, axis=0, keepdims=True
        )
        pb_local, pb_far = rounded(p_local), rounded(p_far)
        ds_local = rounded(p_local * (dp_local - delta))
        ds_far = rounded(p_far * (dp_far - delta))

        def to_queries(start, local, beyond):
            rows = slice(start + low, start + high)
            near_part = tiles(
                lambda t, lanes: f32_dot(kvt_ref[rows, t * tile : (t + 2) * tile], local[:, lanes])
            )
            return near_part + f32_dot(kvt_ref[rows, near:], beyond)

        ot_ref[low:high] = rounded(to_queries(width, pb_local, pb_far))
        gqt_ref[low:high] = rounded(to_queries(0, ds_local, ds_far) * scale)

        def to_keys(start, operand, local, beyond, factor):
            rows = slice(start + low, start + high)
            parts = []
            carried = None
            for t in range(tile_count):
                lanes = slice(t * tile, (t + 1) * tile)
                window = times_transposed(operand[:, lanes], local[:, lanes])
                previous = window[:, :tile]
                parts.append(previous if carried is None else previous + carried)
                carried = window[:, tile:]
            parts.append(carried)
            parts.append(times_transposed(operand, beyond))
            gathered = jnp.concatenate(parts, axis=1)
            gkvt_ref[rows] = rounded(gathered if factor is None else gathered * factor)

        to_keys(0, qt_ref[low:high], ds_local, ds_far, scale)
        to_keys(width, odt_ref[low:high], pb_local, pb_far, None)

    by_feature = f32_dot(wkv_ref[...], gkvt_ref[...])
    own = by_feature[:, tile:near] + f32_dot(wq_ref[...], gqt_ref[...])
    gf_ref[...] = own.T
    halo_feat_ref[...] = rounded(by_feature[:, :tile].T)
    slot_feat = rounded(by_feature[:, near:virt_at].T)
    for at, out_ref in enumerate(direct_refs):
        out_ref[...] = slot_feat[2 * at * per_peer : (2 * at + 1) * per_peer]
        through_ref[at * per_peer : (at + 1) * per_peer] = slot_feat[
            (2 * at + 1) * per_peer : (2 * at + 2) * per_peer
        ]
    rider_ref[...] = by_feature[:, virt_at:].T * factor

    sums = (
        times_transposed(extt_ref[:, tile:near], gqt_ref[...]),
        times_transposed(extt_ref[...], gkvt_ref[:width]),
        times_transposed(extt_ref[...], gkvt_ref[width:]),
        f32_dot(ot_ref[...], og_ref[...]),
    )
    pieces = keep_ref.shape[0] // rows_per_piece
    held = place_ref[1] % pieces

    def write(half, out_ref, cast):
        for piece in range(pieces):
            start = (half * pieces + piece) * rows_per_piece
            value = sums[start // width][start % width : start % width + rows_per_piece] * factor
            offset = pl.multiple_of((piece ^ held) * rows_per_piece, ROW_PACK)
            out_ref[pl.ds(offset, rows_per_piece), :] = cast(value)

    for half in range(2):

        @pl.when(place_ref[1] // pieces == half)
        def _():
            write(half, keep_ref, lambda value: value)
            write(1 - half, send_ref, rounded)

    send_ref[keep_ref.shape[0] :] = rounded(rider_ref[...])


def place_kernel(rows_per_piece, place_ref, *refs):
    part_refs, (gq_ref, gkv_ref, go_ref, all_ref) = refs[:-4], refs[-4:]
    width = gq_ref.shape[0]
    rows = part_refs[0].shape[0]
    for at, part_ref in enumerate(part_refs):
        all_ref[at * rows : (at + 1) * rows] = part_ref[...]
    for at in range(all_ref.shape[0] // rows_per_piece):
        offset = pl.multiple_of((place_ref[1] ^ at) * rows_per_piece, ROW_PACK)
        value = all_ref[pl.ds(offset, rows_per_piece), :].astype(jnp.float32)
        start = at * rows_per_piece
        rows = slice(start % width, start % width + rows_per_piece)
        which = start // width
        if which == 0:
            gq_ref[rows] = value
        elif which == 3:
            go_ref[rows] = value
        else:
            gkv_ref[rows, (which - 1) * width : which * width] = value


def return_kernel(place_ref, send_hbm, gf_ref, halo_ref, *refs):
    piece_refs, (out_ref, send_ref, sems) = refs[:-3], refs[-3:]
    fetch([(send_hbm, send_ref)], sems)[0].wait()
    row_count = gf_ref.shape[0]
    tile = halo_ref.shape[0]
    per_peer = send_ref.shape[1]
    chosen = listed_rows(place_ref[0], send_ref, row_count)
    returned = jnp.concatenate(
        [piece_refs[0][...], piece_refs[1][:per_peer]] + [ref[...] for ref in piece_refs[2:]],
        axis=0,
    )
    total = gf_ref[...] + rows_contracted(chosen, returned)
    out_ref[: row_count - tile] = total[: row_count - tile]
    out_ref[row_count - tile :] = total[row_count - tile :] + halo_ref[...].astype(jnp.float32)


def call(kernel, name, outs, args, scratch=(), fetched=0, flops=0):
    spaces = [pltpu.SMEM] + [pltpu.HBM] * fetched
    spaces += [pltpu.VMEM] * (len(args) - len(spaces))
    moved = sum(x.size * x.dtype.itemsize for x in list(args) + list(outs))
    scratch = list(scratch)
    if fetched:
        scratch.append(pltpu.SemaphoreType.DMA((fetched,)))
    constrained = [
        pltpu.with_memory_space_constraint(x, pltpu.HBM) if space is pltpu.HBM else x
        for x, space in zip(args, spaces)
    ]
    return pl.pallas_call(
        kernel,
        out_shape=outs,
        in_specs=[pl.BlockSpec(memory_space=space) for space in spaces],
        out_specs=[pl.BlockSpec(memory_space=pltpu.VMEM)] * len(outs),
        scratch_shapes=scratch,
        compiler_params=pltpu.CompilerParams(vmem_limit_bytes=VMEM_BYTES),
        cost_estimate=pl.CostEstimate(flops=flops, bytes_accessed=moved, transcendentals=0),
        name=name,
    )(*constrained)


def shards(features, out_grad, w_query, w_keyval, w_out, virtual, local_nbr, expander, send_rows):
    row_count, width = features.shape
    dom_size, per_peer = send_rows.shape
    slots = dom_size * per_peer
    virt_rows = virtual.shape[0]
    padded = ROW_PACK * -(-virt_rows // ROW_PACK)
    ext_rows = TILE + row_count + slots + padded
    nodes = row_count * lax.axis_size("dom") * lax.axis_size("rows")
    stages = exchange_stages(lax.axis_size("dom"), lax.axis_size("rows"))
    scattered = stages[:3]
    rows_per_piece = 4 * width >> sum(len(stage) for stage in scattered)
    place = jnp.stack([lax.axis_index("dom").astype(jnp.int32), own_piece(scattered)])
    bf16, f32 = jnp.bfloat16, jnp.float32
    shape = jax.ShapeDtypeStruct

    halo, through, *direct = call(
        pick_kernel,
        "pick_rows",
        [shape((TILE, width), bf16), shape((slots // 2, width), bf16)]
        + [shape((per_peer, width), bf16)] * (dom_size // 2),
        [place, features, send_rows],
        [pltpu.VMEM(features.shape, bf16), pltpu.VMEM(send_rows.shape, jnp.int32)],
        fetched=2,
    )
    arrived = routed(direct, through)
    halo = shifted(halo, "rows", 1)
    prepared = call(
        functools.partial(prepare_kernel, per_peer),
        "prepare",
        [
            shape(out_grad.shape, bf16),
            shape(w_query.shape, bf16),
            shape(w_keyval.shape, bf16),
            shape((width, row_count + padded), bf16),
            shape((width, row_count), bf16),
            shape((width, row_count), bf16),
            shape((row_count + padded, 2 * width), bf16),
            shape((2 * width, row_count + padded), bf16),
            shape((2 * TILE, row_count), f32),
            shape((slots + padded, row_count), f32),
        ],
        [place, features, out_grad, w_query, w_keyval, w_out, virtual, local_nbr.T, expander.T],
        [
            pltpu.VMEM(features.shape, bf16),
            pltpu.VMEM(w_out.shape, bf16),
            pltpu.VMEM(virtual.shape, bf16),
            pltpu.VMEM(local_nbr.shape[::-1], jnp.int32),
            pltpu.VMEM(expander.shape[::-1], jnp.int32),
        ],
        fetched=8,
        flops=10 * row_count * width * width,
    )
    own_feat, halo_feat, *results = call(
        functools.partial(attend_kernel, rows_per_piece, nodes**-0.5, per_peer, dom_size),
        "attend",
        [
            shape((row_count, width), f32),
            shape((TILE, width), bf16),
            *[shape((per_peer, width), bf16)] * (dom_size // 2),
            shape((slots // 2, width), bf16),
            shape((2 * width, width), f32),
            shape((2 * width + padded, width), bf16),
            shape((padded, width), f32),
        ],
        [place, halo, *arrived, *prepared],
        [
            pltpu.VMEM((slots, width), bf16),
            pltpu.VMEM((ext_rows, 2 * width), bf16),
            pltpu.VMEM((2 * width, ext_rows), bf16),
            pltpu.VMEM((width, ext_rows), bf16),
            pltpu.VMEM((width, row_count), bf16),
            pltpu.VMEM((2 * width, ext_rows), bf16),
            pltpu.VMEM((width, row_count), bf16),
        ],
        flops=32 * ext_rows * width * width,
    )
    *direct, through, keep, message, rider = results

    rider = rounded(rider).astype(f32)
    keep, rider = added(keep, rider, exchange([message], stages[0]))
    through = swapped(through, 1, 0)
    halo_back = shifted(halo_feat, "rows", -1)
    for at, stage in enumerate(stages[1:], 1):
        keep, rider, messages = scatter_stage(keep, rider, stage, stage in scattered)
        if at == 1:
            through, _ = lax.optimization_barrier((through, messages))
            returned = handed_on(direct, through)
        if at == 3:
            messages, returned = lax.optimization_barrier((messages, returned))
        keep, rider = added(keep, rider, exchange(messages, stage))
    (grad_features,) = call(
        return_kernel,
        "return_rows",
        [shape((row_count, width), f32)],
        [place, send_rows, own_feat, halo_back, *returned],
        [pltpu.VMEM(send_rows.shape, jnp.int32)],
        fetched=1,
    )
    held, grad_features = lax.optimization_barrier((rounded(keep), grad_features))
    held = gathered(held, scattered[2])
    square = partner_masks(scattered[1])
    near = [held] + [swapped(held, *masks) for masks in square[::-1]][::-1]
    far = [swapped(block, *partner_masks(scattered[0])[0]) for block in near]
    grad_wq, grad_wkv, grad_wo = call(
        functools.partial(place_kernel, rows_per_piece),
        "place_sums",
        [shape((width, width), f32), shape((width, 2 * width), f32), shape((width, width), f32)],
        [place, *near, *far],
        [pltpu.VMEM((4 * width, width), bf16)],
    )
    return grad_features, grad_wq, grad_wkv, grad_wo, rider[:virt_rows]


def solution(mesh):
    placed = (
        P(("dom", "rows"), None),
        P(("dom", "rows"), None),
        P(),
        P(),
        P(),
        P(),
        P(("dom", "rows"), None),
        P(("dom", "rows"), None),
        P(("dom", "rows"), None),
    )
    return jax.shard_map(
        shards,
        mesh=mesh,
        in_specs=placed,
        out_specs=(P(("dom", "rows"), None), P(), P(), P(), P()),
        check_vma=False,
    )
```

```python
import functools
import math

import jax
import jax.numpy as jnp
from jax import lax
from jax.experimental import pallas as pl
from jax.experimental.pallas import tpu as pltpu
from jax.sharding import PartitionSpec as P

HEADS = 8
TILE = 128
ROW_PACK = 16
NEGATIVE_FILL = -1e30
VMEM_BYTES = 24 * 1024 * 1024
LANES = 128


def f32_dot(left, right):
    return jnp.dot(left, right, preferred_element_type=jnp.float32)


def rows_contracted(left, right):
    return lax.dot_general(
        left, right, (((0,), (0,)), ((), ())), preferred_element_type=jnp.float32
    )


def times_transposed(left, right):
    return lax.dot_general(
        left, right, (((1,), (1,)), ((), ())), preferred_element_type=jnp.float32
    )


def rounded(value):
    return value.astype(jnp.bfloat16)


def exchange_stages(dom_size, rows_size):
    stages = [[((0, 1), (0, 1))], [((1, 2), (0, 2)), ((1, 0), (1, 2))]]
    stages += [[((bit, 0), (bit, 0))] for bit in powers_of_two(2, dom_size)]
    stages += [[((0, bit), (0, bit))] for bit in powers_of_two(4, rows_size)]
    return stages


def powers_of_two(first, size):
    return [1 << i for i in range(size.bit_length() - 1) if 1 << i >= first]


def partner_masks(stage):
    masks = []
    for digit in range(1, 1 << len(stage)):
        dom_mask = rows_mask = 0
        for i, (mask, _) in enumerate(stage):
            if digit >> i & 1:
                dom_mask ^= mask[0]
                rows_mask ^= mask[1]
        masks.append((dom_mask, rows_mask))
    return masks


def own_piece(stages):
    index = jnp.int32(0)
    for stage in stages:
        index = index << len(stage)
        for i, (_, parity) in enumerate(stage):
            odd = jnp.int32(0)
            for axis, mask in zip(("dom", "rows"), parity):
                for bit in powers_of_two(1, 2 * mask) if mask else []:
                    odd ^= jnp.where(lax.axis_index(axis) & bit & mask, 1, 0)
            index += odd << i
    return index


def swapped(block, dom_mask, rows_mask):
    dom_size, rows_size = lax.axis_size("dom"), lax.axis_size("rows")
    route = [
        (a * rows_size + b, (a ^ dom_mask) * rows_size + (b ^ rows_mask))
        for a in range(dom_size)
        for b in range(rows_size)
    ]
    return lax.ppermute(block, ("dom", "rows"), route)


def shifted(block, axis, distance):
    devices = range(lax.axis_size(axis))
    route = [((i - distance) % len(devices), i) for i in devices]
    return lax.ppermute(block, axis, route)


def paired_sum(terms):
    while len(terms) > 1:
        terms = [left + right for left, right in zip(terms[::2], terms[1::2])]
    return terms[0]


def routed(direct, through):
    return handed_on(direct, swapped(through, 1, 0))


def handed_on(direct, through):
    rows = direct[0].shape[0]
    arrived = []
    for at in reversed(range(1, len(direct))):
        message = jnp.concatenate([direct[at], through[at * rows : (at + 1) * rows]], axis=0)
        arrived.append(swapped(message, 2 * at, 0))
    return [direct[0], through] + arrived


def scatter_stage(keep, rider, stage, halved):
    part = keep.shape[0] >> len(stage) if halved else keep.shape[0]
    rider_bf = rounded(rider)
    if not halved:
        keep = rounded(keep).astype(jnp.float32)
    messages = []
    for at in range(1, 1 << len(stage)):
        block = keep[at * part : (at + 1) * part] if halved else keep
        messages.append(jnp.concatenate([rounded(block), rider_bf], axis=0))
    return keep[:part], rider_bf.astype(jnp.float32), messages


def exchange(messages, stage):
    return [swapped(message, *masks) for message, masks in zip(messages, partner_masks(stage))]


def added(keep, rider, arrived):
    part = keep.shape[0]
    terms = [keep] + [block[:part].astype(jnp.float32) for block in arrived]
    riders = [rider] + [block[part:].astype(jnp.float32) for block in arrived]
    return paired_sum(terms), paired_sum(riders)


def gathered(held, stage):
    return jnp.concatenate([held] + exchange([held] * ((1 << len(stage)) - 1), stage), axis=0)


def listed_rows(dom, send_ref, row_count):
    dom_size, per_peer = send_ref.shape
    slots = dom_size * per_peer
    slot = lax.broadcasted_iota(jnp.int32, (slots, per_peer), 0)
    place = lax.broadcasted_iota(jnp.int32, (slots, per_peer), 1)
    peer = (slot // per_peer) ^ dom
    listed = jnp.zeros((slots, per_peer), jnp.int32)
    for at in range(dom_size):
        listed += jnp.where((peer == at) & (place == slot % per_peer), send_ref[at : at + 1, :], 0)
    column = jnp.sum(listed, axis=1, keepdims=True)
    rows = lax.broadcasted_iota(jnp.int32, (slots, row_count), 1)
    return jnp.where(column == rows, 1.0, 0.0).astype(jnp.bfloat16)


def fetch(pairs, sems):
    copies = [
        pltpu.make_async_copy(source, target, sems.at[at])
        for at, (source, target) in enumerate(pairs)
    ]
    for copy in copies:
        copy.start()
    return copies


def pick_kernel(place_ref, feat_hbm, send_hbm, halo_ref, through_ref, *refs):
    direct_refs, (feat_ref, send_ref, sems) = refs[:-3], refs[-3:]
    copies = fetch([(send_hbm, send_ref), (feat_hbm, feat_ref)], sems)
    copies[0].wait()
    per_peer = send_ref.shape[1]
    chosen = listed_rows(place_ref[0], send_ref, feat_ref.shape[0])
    copies[1].wait()
    halo_ref[...] = feat_ref[feat_ref.shape[0] - halo_ref.shape[0] :]
    picked = rounded(f32_dot(chosen, feat_ref[...]))
    for at, out_ref in enumerate(direct_refs):
        out_ref[...] = picked[2 * at * per_peer : (2 * at + 1) * per_peer]
        through_ref[at * per_peer : (at + 1) * per_peer] = picked[
            (2 * at + 1) * per_peer : (2 * at + 2) * per_peer
        ]


def prepare_kernel(
    per_peer,
    place_ref,
    feat_hbm,
    og_hbm,
    wq_hbm,
    wkv_hbm,
    wo_hbm,
    virt_hbm,
    nbr_hbm,
    exp_hbm,
    og_ref,
    wq_ref,
    wkv_ref,
    featt_ref,
    qt_ref,
    odt_ref,
    kv_ref,
    kvt_ref,
    local_bias_ref,
    far_bias_ref,
    feat_ref,
    wo_ref,
    virt_ref,
    nbr_ref,
    exp_ref,
    sems,
):
    nbr_copy, exp_copy, feat_copy, virt_copy, wq_copy, wkv_copy, og_copy, wo_copy = fetch(
        [
            (nbr_hbm, nbr_ref),
            (exp_hbm, exp_ref),
            (feat_hbm, feat_ref),
            (virt_hbm, virt_ref),
            (wq_hbm, wq_ref),
            (wkv_hbm, wkv_ref),
            (og_hbm, og_ref),
            (wo_hbm, wo_ref),
        ],
        sems,
    )
    row_count, width = feat_ref.shape
    window = local_bias_ref.shape[0]
    far = far_bias_ref.shape[0]
    virt_rows = virt_ref.shape[0]
    padded = kv_ref.shape[0] - row_count
    slots = far - padded
    scale = 1.0 / math.sqrt(width // HEADS)

    def multiplicity(key_rows, named):
        position = lax.broadcasted_iota(jnp.int32, (key_rows, row_count), 0)
        count = jnp.zeros((key_rows, row_count), jnp.float32)
        for at in range(named.shape[0]):
            count += jnp.where(named[at : at + 1, :] == position, 1.0, 0.0)
        return count

    nbr_copy.wait()
    local_bias_ref[...] = jnp.where(multiplicity(window, nbr_ref) > 0.0, 0.0, NEGATIVE_FILL)
    exp_copy.wait()
    expander = exp_ref[...]
    expander = ((expander // per_peer) ^ place_ref[0]) * per_peer + expander % per_peer
    named_times = multiplicity(slots, expander)
    slot_bias = jnp.full((slots, row_count), NEGATIVE_FILL, jnp.float32)
    for times in range(1, exp_ref.shape[0] + 1):
        slot_bias = jnp.where(named_times == float(times), math.log(times) / scale, slot_bias)
    far_bias_ref[:slots] = slot_bias
    virt_row = lax.broadcasted_iota(jnp.int32, (padded, row_count), 0)
    far_bias_ref[slots:] = jnp.where(virt_row < virt_rows, 0.0, NEGATIVE_FILL)

    feat_copy.wait()
    featt_ref[:, :row_count] = feat_ref[...].T
    virt_copy.wait()
    virt = jnp.concatenate(
        [virt_ref[...], jnp.zeros((padded - virt_rows, width), jnp.bfloat16)], axis=0
    )
    featt_ref[:, row_count:] = virt.T
    wq_copy.wait()
    qt_ref[...] = rounded(rows_contracted(wq_ref[...], featt_ref[:, :row_count]))
    wkv_copy.wait()
    kv_ref[:row_count] = rounded(f32_dot(feat_ref[...], wkv_ref[...]))
    kv_ref[row_count:] = rounded(f32_dot(virt, wkv_ref[...]))
    kvt_ref[...] = kv_ref[...].T
    og_copy.wait()
    wo_copy.wait()
    odt_ref[...] = rounded(times_transposed(wo_ref[...], og_ref[...]))


def attend_kernel(
    rows_per_piece,
    factor,
    per_peer,
    dom_size,
    place_ref,
    halo_ref,
    *refs,
):
    piece_refs, refs = refs[: 1 + dom_size // 2], refs[1 + dom_size // 2 :]
    og_ref, wq_ref, wkv_ref, featt_ref, qt_ref, odt_ref, own_kv_ref, own_kvt_ref = refs[:8]
    local_bias_ref, far_bias_ref, gf_ref, halo_feat_ref = refs[8:12]
    direct_refs, refs = refs[12 : 12 + dom_size // 2], refs[12 + dom_size // 2 :]
    through_ref, refs = refs[0], refs[1:]
    keep_ref, send_ref, rider_ref = refs[:3]
    slot_ref, kv_ref, kvt_ref, extt_ref, gqt_ref, gkvt_ref, ot_ref = refs[3:]
    width, row_count = qt_ref.shape
    tile = halo_ref.shape[0]
    tile_count = row_count // tile
    slots = dom_size * per_peer
    near = tile + row_count
    virt_at = near + slots
    head_dim = width // HEADS
    scale = 1.0 / math.sqrt(head_dim)

    kv_ref[tile:near] = own_kv_ref[:row_count]
    kv_ref[virt_at:] = own_kv_ref[row_count:]
    kvt_ref[:, tile:near] = own_kvt_ref[:, :row_count]
    kvt_ref[:, virt_at:] = own_kvt_ref[:, row_count:]
    extt_ref[:, tile:near] = featt_ref[:, :row_count]
    extt_ref[:, virt_at:] = featt_ref[:, row_count:]
    slot_ref[:per_peer] = piece_refs[0][...]
    slot_ref[per_peer : 2 * per_peer] = piece_refs[1][:per_peer]
    for at, piece_ref in enumerate(piece_refs[:1:-1], 1):
        slot_ref[2 * at * per_peer : (2 * at + 2) * per_peer] = piece_ref[...]
    for rows, source_ref in ((slice(0, tile), halo_ref), (slice(near, virt_at), slot_ref)):
        extt_ref[:, rows] = source_ref[...].T
        kv_ref[rows] = rounded(f32_dot(source_ref[...], wkv_ref[...]))
        kvt_ref[:, rows] = kv_ref[rows].T

    def tiles(of):
        return jnp.concatenate([of(t, slice(t * tile, (t + 1) * tile)) for t in range(tile_count)], 1)

    for head in range(HEADS):
        low, high = head * head_dim, (head + 1) * head_dim
        first = low // 128 * 128
        last = min(-(-high // 128) * 128, width)
        column = lax.broadcasted_iota(jnp.int32, (last - first, row_count), 0) + first
        of_head = (column >= low) & (column < high)
        q_rows = jnp.where(of_head, qt_ref[first:last, :], 0)
        d_rows = jnp.where(of_head, odt_ref[first:last, :], 0)

        def products(operand, start, stop):
            local = tiles(
                lambda t, lanes: f32_dot(
                    kv_ref[t * tile : (t + 2) * tile, start:stop], operand[:, lanes]
                )
            )
            return local, f32_dot(kv_ref[near:, start:stop], operand)

        s_local, s_far = products(q_rows, first, last)
        s_local += local_bias_ref[...]
        s_far += far_bias_ref[...]
        peak = jnp.maximum(
            jnp.max(s_local, axis=0, keepdims=True), jnp.max(s_far, axis=0, keepdims=True)
        )
        exponent_scale = scale * math.log2(math.e)
        e_local = jnp.exp2((s_local - peak) * exponent_scale)
        e_far = jnp.exp2((s_far - peak) * exponent_scale)
        total = jnp.sum(e_local, axis=0, keepdims=True) + jnp.sum(e_far, axis=0, keepdims=True)
        inverse = 1.0 / total
        p_local = e_local * inverse
        p_far = e_far * inverse
        dp_local, dp_far = products(d_rows, width + first, width + last)
        delta = jnp.sum(p_local * dp_local, axis=0, keepdims=True) + jnp.sum(
            p_far * dp_far, axis=0, keepdims=True
        )
        pb_local, pb_far = rounded(p_local), rounded(p_far)
        ds_local = rounded(p_local * (dp_local - delta))
        ds_far = rounded(p_far * (dp_far - delta))

        def to_queries(start, local, beyond):
            rows = slice(start + low, start + high)
            near_part = tiles(
                lambda t, lanes: f32_dot(kvt_ref[rows, t * tile : (t + 2) * tile], local[:, lanes])
            )
            return near_part + f32_dot(kvt_ref[rows, near:], beyond)

        ot_ref[low:high] = rounded(to_queries(width, pb_local, pb_far))
        gqt_ref[low:high] = rounded(to_queries(0, ds_local, ds_far) * scale)

        def to_keys(start, operand, local, beyond, factor):
            rows = slice(start + low, start + high)
            parts = []
            carried = None
            for t in range(tile_count):
                lanes = slice(t * tile, (t + 1) * tile)
                window = times_transposed(operand[:, lanes], local[:, lanes])
                previous = window[:, :tile]
                parts.append(previous if carried is None else previous + carried)
                carried = window[:, tile:]
            parts.append(carried)
            parts.append(times_transposed(operand, beyond))
            gathered = jnp.concatenate(parts, axis=1)
            gkvt_ref[rows] = rounded(gathered if factor is None else gathered * factor)

        to_keys(0, qt_ref[low:high], ds_local, ds_far, scale)
        to_keys(width, odt_ref[low:high], pb_local, pb_far, None)

    by_feature = f32_dot(wkv_ref[...], gkvt_ref[...])
    own = by_feature[:, tile:near] + f32_dot(wq_ref[...], gqt_ref[...])
    gf_ref[...] = own.T
    halo_feat_ref[...] = rounded(by_feature[:, :tile].T)
    slot_feat = rounded(by_feature[:, near:virt_at].T)
    for at, out_ref in enumerate(direct_refs):
        out_ref[...] = slot_feat[2 * at * per_peer : (2 * at + 1) * per_peer]
        through_ref[at * per_peer : (at + 1) * per_peer] = slot_feat[
            (2 * at + 1) * per_peer : (2 * at + 2) * per_peer
        ]
    rider_ref[...] = by_feature[:, virt_at:].T * factor

    sums = (
        times_transposed(extt_ref[:, tile:near], gqt_ref[...]),
        times_transposed(extt_ref[...], gkvt_ref[:width]),
        times_transposed(extt_ref[...], gkvt_ref[width:]),
        f32_dot(ot_ref[...], og_ref[...]),
    )
    pieces = keep_ref.shape[0] // rows_per_piece
    held = place_ref[1] % pieces

    def write(half, out_ref, cast):
        for piece in range(pieces):
            start = (half * pieces + piece) * rows_per_piece
            value = sums[start // width][start % width : start % width + rows_per_piece] * factor
            offset = pl.multiple_of((piece ^ held) * rows_per_piece, ROW_PACK)
            out_ref[pl.ds(offset, rows_per_piece), :] = cast(value)

    for half in range(2):

        @pl.when(place_ref[1] // pieces == half)
        def _():
            write(half, keep_ref, lambda value: value)
            write(1 - half, send_ref, rounded)

    send_ref[keep_ref.shape[0] :] = rounded(rider_ref[...])


def place_kernel(rows_per_piece, place_ref, *refs):
    part_refs, (gq_hbm, gkv_hbm, go_hbm, all_ref, out_ref, sems) = refs[:-6], refs[-6:]
    width = gq_hbm.shape[0]
    rows = part_refs[0].shape[0]
    half = len(part_refs) // 2
    for at, part_ref in enumerate(part_refs):
        digit = at // half * half + -at % half
        all_ref[digit * rows : (digit + 1) * rows] = part_ref[...]
    copies = []
    for at in range(all_ref.shape[0] // rows_per_piece):
        offset = pl.multiple_of((place_ref[1] ^ at) * rows_per_piece, ROW_PACK)
        start = at * rows_per_piece
        piece = slice(start, start + rows_per_piece)
        out_ref[piece] = all_ref[pl.ds(offset, rows_per_piece), :].astype(jnp.float32)
        rows_out = pl.ds(start % width, rows_per_piece)
        which = start // width
        if which == 0:
            target = gq_hbm.at[rows_out]
        elif which == 3:
            target = go_hbm.at[rows_out]
        else:
            target = gkv_hbm.at[rows_out, pl.ds((which - 1) * width, width)]
        copies.append(pltpu.make_async_copy(out_ref.at[piece], target, sems.at[at]))
        copies[-1].start()
    for copy in copies:
        copy.wait()


def return_kernel(place_ref, send_hbm, gf_ref, halo_ref, *refs):
    piece_refs, (out_ref, send_ref, sems) = refs[:-3], refs[-3:]
    fetch([(send_hbm, send_ref)], sems)[0].wait()
    row_count = gf_ref.shape[0]
    tile = halo_ref.shape[0]
    per_peer = send_ref.shape[1]
    chosen = listed_rows(place_ref[0], send_ref, row_count)
    returned = jnp.concatenate(
        [piece_refs[0][...], piece_refs[1][:per_peer]] + [ref[...] for ref in piece_refs[:1:-1]],
        axis=0,
    )
    total = gf_ref[...] + rows_contracted(chosen, returned)
    out_ref[: row_count - tile] = total[: row_count - tile]
    out_ref[row_count - tile :] = total[row_count - tile :] + halo_ref[...].astype(jnp.float32)


def call(kernel, name, outs, args, scratch=(), fetched=0, flops=0, stored=False):
    spaces = [pltpu.SMEM] + [pltpu.HBM] * fetched
    spaces += [pltpu.VMEM] * (len(args) - len(spaces))
    moved = sum(x.size * x.dtype.itemsize for x in list(args) + list(outs))
    scratch = list(scratch)
    if fetched:
        scratch.append(pltpu.SemaphoreType.DMA((fetched,)))
    constrained = [
        pltpu.with_memory_space_constraint(x, pltpu.HBM) if space is pltpu.HBM else x
        for x, space in zip(args, spaces)
    ]
    return pl.pallas_call(
        kernel,
        out_shape=outs,
        in_specs=[pl.BlockSpec(memory_space=space) for space in spaces],
        out_specs=[pl.BlockSpec(memory_space=pl.ANY if stored else pltpu.VMEM)] * len(outs),
        scratch_shapes=scratch,
        compiler_params=pltpu.CompilerParams(vmem_limit_bytes=VMEM_BYTES),
        cost_estimate=pl.CostEstimate(flops=flops, bytes_accessed=moved, transcendentals=0),
        name=name,
    )(*constrained)


def shards(features, out_grad, w_query, w_keyval, w_out, virtual, local_nbr, expander, send_rows):
    row_count, width = features.shape
    dom_size, per_peer = send_rows.shape
    slots = dom_size * per_peer
    virt_rows = virtual.shape[0]
    padded = ROW_PACK * -(-virt_rows // ROW_PACK)
    ext_rows = TILE + row_count + slots + padded
    nodes = row_count * lax.axis_size("dom") * lax.axis_size("rows")
    stages = exchange_stages(lax.axis_size("dom"), lax.axis_size("rows"))
    scattered = stages[:3]
    rows_per_piece = 4 * width >> sum(len(stage) for stage in scattered)
    place = jnp.stack([lax.axis_index("dom").astype(jnp.int32), own_piece(scattered)])
    bf16, f32 = jnp.bfloat16, jnp.float32
    shape = jax.ShapeDtypeStruct

    halo, through, *direct = call(
        pick_kernel,
        "pick_rows",
        [shape((TILE, width), bf16), shape((slots // 2, width), bf16)]
        + [shape((per_peer, width), bf16)] * (dom_size // 2),
        [place, features, send_rows],
        [pltpu.VMEM(features.shape, bf16), pltpu.VMEM(send_rows.shape, jnp.int32)],
        fetched=2,
    )
    arrived = routed(direct, through)
    halo = shifted(halo, "rows", 1)
    prepared = call(
        functools.partial(prepare_kernel, per_peer),
        "prepare",
        [
            shape(out_grad.shape, bf16),
            shape(w_query.shape, bf16),
            shape(w_keyval.shape, bf16),
            shape((width, row_count + padded), bf16),
            shape((width, row_count), bf16),
            shape((width, row_count), bf16),
            shape((row_count + padded, 2 * width), bf16),
            shape((2 * width, row_count + padded), bf16),
            shape((2 * TILE, row_count), f32),
            shape((slots + padded, row_count), f32),
        ],
        [place, features, out_grad, w_query, w_keyval, w_out, virtual, local_nbr.T, expander.T],
        [
            pltpu.VMEM(features.shape, bf16),
            pltpu.VMEM(w_out.shape, bf16),
            pltpu.VMEM(virtual.shape, bf16),
            pltpu.VMEM(local_nbr.shape[::-1], jnp.int32),
            pltpu.VMEM(expander.shape[::-1], jnp.int32),
        ],
        fetched=8,
        flops=10 * row_count * width * width,
    )
    own_feat, halo_feat, *results = call(
        functools.partial(attend_kernel, rows_per_piece, nodes**-0.5, per_peer, dom_size),
        "attend",
        [
            shape((row_count, width), f32),
            shape((TILE, width), bf16),
            *[shape((per_peer, width), bf16)] * (dom_size // 2),
            shape((slots // 2, width), bf16),
            shape((2 * width, width), f32),
            shape((2 * width + padded, width), bf16),
            shape((padded, width), f32),
        ],
        [place, halo, *arrived, *prepared],
        [
            pltpu.VMEM((slots, width), bf16),
            pltpu.VMEM((ext_rows, 2 * width), bf16),
            pltpu.VMEM((2 * width, ext_rows), bf16),
            pltpu.VMEM((width, ext_rows), bf16),
            pltpu.VMEM((width, row_count), bf16),
            pltpu.VMEM((2 * width, ext_rows), bf16),
            pltpu.VMEM((width, row_count), bf16),
        ],
        flops=32 * ext_rows * width * width,
    )
    *direct, through, keep, message, rider = results

    rider = rounded(rider).astype(f32)
    keep, rider = added(keep, rider, exchange([message], stages[0]))
    through = swapped(through, 1, 0)
    for at, stage in enumerate(stages[1:], 1):
        keep, rider, messages = scatter_stage(keep, rider, stage, stage in scattered)
        if at == 1:
            through, _ = lax.optimization_barrier((through, messages))
            returned = handed_on(direct, through)
        if at == 2:
            messages, returned, halo_feat = lax.optimization_barrier(
                (messages, returned, halo_feat)
            )
            halo_back = shifted(halo_feat, "rows", -1)
        keep, rider = added(keep, rider, exchange(messages, stage))
    (grad_features,) = call(
        return_kernel,
        "return_rows",
        [shape((row_count, width), f32)],
        [place, send_rows, own_feat, halo_back, *returned],
        [pltpu.VMEM(send_rows.shape, jnp.int32)],
        fetched=1,
    )
    held, grad_features = lax.optimization_barrier((rounded(keep), grad_features))
    held = gathered(held, scattered[2])
    square = partner_masks(scattered[1])
    near = [held] + [swapped(held, *masks) for masks in square[::-1]]
    far = [swapped(block, *partner_masks(scattered[0])[0]) for block in near]
    grad_wq, grad_wkv, grad_wo = call(
        functools.partial(place_kernel, rows_per_piece),
        "place_sums",
        [shape((width, width), f32), shape((width, 2 * width), f32), shape((width, width), f32)],
        [place, *near, *far],
        [
            pltpu.VMEM((4 * width, width), bf16),
            pltpu.VMEM((4 * width, width), f32),
            pltpu.SemaphoreType.DMA((4 * width // rows_per_piece,)),
        ],
        stored=True,
    )
    return grad_features, grad_wq, grad_wkv, grad_wo, rider[:virt_rows]


def solution(mesh):
    placed = (
        P(("dom", "rows"), None),
        P(("dom", "rows"), None),
        P(),
        P(),
        P(),
        P(),
        P(("dom", "rows"), None),
        P(("dom", "rows"), None),
        P(("dom", "rows"), None),
    )
    return jax.shard_map(
        shards,
        mesh=mesh,
        in_specs=placed,
        out_specs=(P(("dom", "rows"), None), P(), P(), P(), P()),
        check_vma=False,
    )
```

```python
import functools
import math

import jax
import jax.numpy as jnp
from jax import lax
from jax.experimental import pallas as pl
from jax.experimental.pallas import tpu as pltpu
from jax.sharding import PartitionSpec as P

HEADS = 8
TILE = 128
ROW_PACK = 16
NEGATIVE_FILL = -1e30
VMEM_BYTES = 24 * 1024 * 1024
LANES = 128


def f32_dot(left, right):
    return jnp.dot(left, right, preferred_element_type=jnp.float32)


def rows_contracted(left, right):
    return lax.dot_general(
        left, right, (((0,), (0,)), ((), ())), preferred_element_type=jnp.float32
    )


def times_transposed(left, right):
    return lax.dot_general(
        left, right, (((1,), (1,)), ((), ())), preferred_element_type=jnp.float32
    )


def rounded(value):
    return value.astype(jnp.bfloat16)


HALVINGS = 3


def exchange_steps(dom_size, rows_size):
    near = [(0, 2), (1, 0)]
    rest = [(bit, 0) for bit in powers_of_two(2, dom_size)]
    rest += [(0, bit) for bit in powers_of_two(4, rows_size)]
    return near + rest, near[::-1] + rest


def powers_of_two(first, size):
    return [1 << i for i in range(size.bit_length() - 1) if 1 << i >= first]


def own_piece(steps):
    index = jnp.int32(0)
    for dom_mask, rows_mask in steps[:HALVINGS]:
        own = (lax.axis_index("dom") & dom_mask) | (lax.axis_index("rows") & rows_mask)
        index = index * 2 + jnp.where(own != 0, 1, 0)
    return index


def swapped(block, dom_mask, rows_mask):
    dom_size, rows_size = lax.axis_size("dom"), lax.axis_size("rows")
    route = [
        (a * rows_size + b, (a ^ dom_mask) * rows_size + (b ^ rows_mask))
        for a in range(dom_size)
        for b in range(rows_size)
    ]
    return lax.ppermute(block, ("dom", "rows"), route)


def shifted(block, axis, distance):
    devices = range(lax.axis_size(axis))
    route = [((i - distance) % len(devices), i) for i in devices]
    return lax.ppermute(block, axis, route)


def handed_on(direct, through):
    rows = direct[0].shape[0]
    arrived = []
    for at in reversed(range(1, len(direct))):
        message = jnp.concatenate([direct[at], through[at * rows : (at + 1) * rows]], axis=0)
        arrived.append(swapped(message, 2 * at, 0))
    return [direct[0], through] + arrived


class Chain:
    def __init__(self, keep, message, rider):
        self.keep, self.message = keep, message
        self.rider = None if rider is None else rounded(rider).astype(jnp.float32)

    def form(self, halved):
        rows = self.keep.shape[0]
        if halved:
            block = rounded(self.keep[rows // 2 :])
            self.keep = self.keep[: rows // 2]
        else:
            block = rounded(self.keep)
            self.keep = block.astype(jnp.float32)
        if self.rider is not None:
            rider = rounded(self.rider)
            self.rider = rider.astype(jnp.float32)
            block = jnp.concatenate([block, rider], axis=0)
        self.message = block

    def send(self, masks):
        self.message = swapped(self.message, *masks)

    def add(self):
        rows = self.keep.shape[0]
        self.keep += self.message[:rows].astype(jnp.float32)
        if self.rider is not None:
            self.rider += self.message[rows:].astype(jnp.float32)


def listed_rows(dom, send_ref, row_count):
    dom_size, per_peer = send_ref.shape
    slots = dom_size * per_peer
    slot = lax.broadcasted_iota(jnp.int32, (slots, per_peer), 0)
    place = lax.broadcasted_iota(jnp.int32, (slots, per_peer), 1)
    peer = (slot // per_peer) ^ dom
    listed = jnp.zeros((slots, per_peer), jnp.int32)
    for at in range(dom_size):
        listed += jnp.where((peer == at) & (place == slot % per_peer), send_ref[at : at + 1, :], 0)
    column = jnp.sum(listed, axis=1, keepdims=True)
    rows = lax.broadcasted_iota(jnp.int32, (slots, row_count), 1)
    return jnp.where(column == rows, 1.0, 0.0).astype(jnp.bfloat16)


def fetch(pairs, sems):
    copies = [
        pltpu.make_async_copy(source, target, sems.at[at])
        for at, (source, target) in enumerate(pairs)
    ]
    for copy in copies:
        copy.start()
    return copies


def pick_kernel(place_ref, feat_hbm, send_hbm, halo_ref, through_ref, *refs):
    direct_refs, (feat_ref, send_ref, sems) = refs[:-3], refs[-3:]
    copies = fetch([(send_hbm, send_ref), (feat_hbm, feat_ref)], sems)
    copies[0].wait()
    per_peer = send_ref.shape[1]
    chosen = listed_rows(place_ref[0], send_ref, feat_ref.shape[0])
    copies[1].wait()
    halo_ref[...] = feat_ref[feat_ref.shape[0] - halo_ref.shape[0] :]
    picked = rounded(f32_dot(chosen, feat_ref[...]))
    for at, out_ref in enumerate(direct_refs):
        out_ref[...] = picked[2 * at * per_peer : (2 * at + 1) * per_peer]
        through_ref[at * per_peer : (at + 1) * per_peer] = picked[
            (2 * at + 1) * per_peer : (2 * at + 2) * per_peer
        ]


def prepare_kernel(
    per_peer,
    place_ref,
    feat_hbm,
    og_hbm,
    wq_hbm,
    wkv_hbm,
    wo_hbm,
    virt_hbm,
    nbr_hbm,
    exp_hbm,
    og_ref,
    wq_ref,
    wkv_ref,
    featt_ref,
    qt_ref,
    odt_ref,
    kv_ref,
    kvt_ref,
    local_bias_ref,
    far_bias_ref,
    feat_ref,
    wo_ref,
    virt_ref,
    nbr_ref,
    exp_ref,
    sems,
):
    nbr_copy, exp_copy, feat_copy, virt_copy, wq_copy, wkv_copy, og_copy, wo_copy = fetch(
        [
            (nbr_hbm, nbr_ref),
            (exp_hbm, exp_ref),
            (feat_hbm, feat_ref),
            (virt_hbm, virt_ref),
            (wq_hbm, wq_ref),
            (wkv_hbm, wkv_ref),
            (og_hbm, og_ref),
            (wo_hbm, wo_ref),
        ],
        sems,
    )
    row_count, width = feat_ref.shape
    window = local_bias_ref.shape[0]
    far = far_bias_ref.shape[0]
    virt_rows = virt_ref.shape[0]
    padded = kv_ref.shape[0] - row_count
    slots = far - padded
    scale = 1.0 / math.sqrt(width // HEADS)

    def multiplicity(key_rows, named):
        position = lax.broadcasted_iota(jnp.int32, (key_rows, row_count), 0)
        count = jnp.zeros((key_rows, row_count), jnp.float32)
        for at in range(named.shape[0]):
            count += jnp.where(named[at : at + 1, :] == position, 1.0, 0.0)
        return count

    nbr_copy.wait()
    local_bias_ref[...] = jnp.where(multiplicity(window, nbr_ref) > 0.0, 0.0, NEGATIVE_FILL)
    exp_copy.wait()
    expander = exp_ref[...]
    expander = ((expander // per_peer) ^ place_ref[0]) * per_peer + expander % per_peer
    named_times = multiplicity(slots, expander)
    slot_bias = jnp.full((slots, row_count), NEGATIVE_FILL, jnp.float32)
    for times in range(1, exp_ref.shape[0] + 1):
        slot_bias = jnp.where(named_times == float(times), math.log(times) / scale, slot_bias)
    far_bias_ref[:slots] = slot_bias
    virt_row = lax.broadcasted_iota(jnp.int32, (padded, row_count), 0)
    far_bias_ref[slots:] = jnp.where(virt_row < virt_rows, 0.0, NEGATIVE_FILL)

    feat_copy.wait()
    featt_ref[:, :row_count] = feat_ref[...].T
    virt_copy.wait()
    virt = jnp.concatenate(
        [virt_ref[...], jnp.zeros((padded - virt_rows, width), jnp.bfloat16)], axis=0
    )
    featt_ref[:, row_count:] = virt.T
    wq_copy.wait()
    qt_ref[...] = rounded(rows_contracted(wq_ref[...], featt_ref[:, :row_count]))
    wkv_copy.wait()
    kv_ref[:row_count] = rounded(f32_dot(feat_ref[...], wkv_ref[...]))
    kv_ref[row_count:] = rounded(f32_dot(virt, wkv_ref[...]))
    kvt_ref[...] = kv_ref[...].T
    og_copy.wait()
    wo_copy.wait()
    odt_ref[...] = rounded(times_transposed(wo_ref[...], og_ref[...]))


def attend_kernel(
    rows_per_piece,
    factor,
    per_peer,
    dom_size,
    place_ref,
    halo_ref,
    *refs,
):
    piece_refs, refs = refs[: 1 + dom_size // 2], refs[1 + dom_size // 2 :]
    og_ref, wq_ref, wkv_ref, featt_ref, qt_ref, odt_ref, own_kv_ref, own_kvt_ref = refs[:8]
    local_bias_ref, far_bias_ref, gf_ref, halo_feat_ref = refs[8:12]
    direct_refs, refs = refs[12 : 12 + dom_size // 2], refs[12 + dom_size // 2 :]
    through_ref, refs = refs[0], refs[1:]
    keep_refs, send_refs, rider_ref = refs[:2], refs[2:4], refs[4]
    slot_ref, kv_ref, kvt_ref, extt_ref, gqt_ref, gkvt_ref, ot_ref = refs[5:]
    width, row_count = qt_ref.shape
    tile = halo_ref.shape[0]
    tile_count = row_count // tile
    slots = dom_size * per_peer
    near = tile + row_count
    virt_at = near + slots
    head_dim = width // HEADS
    scale = 1.0 / math.sqrt(head_dim)

    kv_ref[tile:near] = own_kv_ref[:row_count]
    kv_ref[virt_at:] = own_kv_ref[row_count:]
    kvt_ref[:, tile:near] = own_kvt_ref[:, :row_count]
    kvt_ref[:, virt_at:] = own_kvt_ref[:, row_count:]
    extt_ref[:, tile:near] = featt_ref[:, :row_count]
    extt_ref[:, virt_at:] = featt_ref[:, row_count:]
    slot_ref[:per_peer] = piece_refs[0][...]
    slot_ref[per_peer : 2 * per_peer] = piece_refs[1][:per_peer]
    for at, piece_ref in enumerate(piece_refs[:1:-1], 1):
        slot_ref[2 * at * per_peer : (2 * at + 2) * per_peer] = piece_ref[...]
    for rows, source_ref in ((slice(0, tile), halo_ref), (slice(near, virt_at), slot_ref)):
        extt_ref[:, rows] = source_ref[...].T
        kv_ref[rows] = rounded(f32_dot(source_ref[...], wkv_ref[...]))
        kvt_ref[:, rows] = kv_ref[rows].T

    def tiles(of):
        return jnp.concatenate([of(t, slice(t * tile, (t + 1) * tile)) for t in range(tile_count)], 1)

    for head in range(HEADS):
        low, high = head * head_dim, (head + 1) * head_dim
        first = low // 128 * 128
        last = min(-(-high // 128) * 128, width)
        column = lax.broadcasted_iota(jnp.int32, (last - first, row_count), 0) + first
        of_head = (column >= low) & (column < high)
        q_rows = jnp.where(of_head, qt_ref[first:last, :], 0)
        d_rows = jnp.where(of_head, odt_ref[first:last, :], 0)

        def products(operand, start, stop):
            local = tiles(
                lambda t, lanes: f32_dot(
                    kv_ref[t * tile : (t + 2) * tile, start:stop], operand[:, lanes]
                )
            )
            return local, f32_dot(kv_ref[near:, start:stop], operand)

        s_local, s_far = products(q_rows, first, last)
        s_local += local_bias_ref[...]
        s_far += far_bias_ref[...]
        peak = jnp.maximum(
            jnp.max(s_local, axis=0, keepdims=True), jnp.max(s_far, axis=0, keepdims=True)
        )
        exponent_scale = scale * math.log2(math.e)
        e_local = jnp.exp2((s_local - peak) * exponent_scale)
        e_far = jnp.exp2((s_far - peak) * exponent_scale)
        total = jnp.sum(e_local, axis=0, keepdims=True) + jnp.sum(e_far, axis=0, keepdims=True)
        inverse = 1.0 / total
        p_local = e_local * inverse
        p_far = e_far * inverse
        dp_local, dp_far = products(d_rows, width + first, width + last)
        delta = jnp.sum(p_local * dp_local, axis=0, keepdims=True) + jnp.sum(
            p_far * dp_far, axis=0, keepdims=True
        )
        pb_local, pb_far = rounded(p_local), rounded(p_far)
        ds_local = rounded(p_local * (dp_local - delta))
        ds_far = rounded(p_far * (dp_far - delta))

        def to_queries(start, local, beyond):
            rows = slice(start + low, start + high)
            near_part = tiles(
                lambda t, lanes: f32_dot(kvt_ref[rows, t * tile : (t + 2) * tile], local[:, lanes])
            )
            return near_part + f32_dot(kvt_ref[rows, near:], beyond)

        ot_ref[low:high] = rounded(to_queries(width, pb_local, pb_far))
        gqt_ref[low:high] = rounded(to_queries(0, ds_local, ds_far) * scale)

        def to_keys(start, operand, local, beyond, factor):
            rows = slice(start + low, start + high)
            parts = []
            carried = None
            for t in range(tile_count):
                lanes = slice(t * tile, (t + 1) * tile)
                window = times_transposed(operand[:, lanes], local[:, lanes])
                previous = window[:, :tile]
                parts.append(previous if carried is None else previous + carried)
                carried = window[:, tile:]
            parts.append(carried)
            parts.append(times_transposed(operand, beyond))
            gathered = jnp.concatenate(parts, axis=1)
            gkvt_ref[rows] = rounded(gathered if factor is None else gathered * factor)

        to_keys(0, qt_ref[low:high], ds_local, ds_far, scale)
        to_keys(width, odt_ref[low:high], pb_local, pb_far, None)

    by_feature = f32_dot(wkv_ref[...], gkvt_ref[...])
    own = by_feature[:, tile:near] + f32_dot(wq_ref[...], gqt_ref[...])
    gf_ref[...] = own.T
    halo_feat_ref[...] = rounded(by_feature[:, :tile].T)
    slot_feat = rounded(by_feature[:, near:virt_at].T)
    for at, out_ref in enumerate(direct_refs):
        out_ref[...] = slot_feat[2 * at * per_peer : (2 * at + 1) * per_peer]
        through_ref[at * per_peer : (at + 1) * per_peer] = slot_feat[
            (2 * at + 1) * per_peer : (2 * at + 2) * per_peer
        ]
    rider_ref[...] = by_feature[:, virt_at:].T * factor

    features, queries = extt_ref[:, tile:near], gqt_ref[...]
    sums = (
        (
            lambda: times_transposed(features, queries),
            lambda: times_transposed(extt_ref[...], gkvt_ref[:width]),
        ),
        (
            lambda: f32_dot(ot_ref[...], og_ref[...]),
            lambda: times_transposed(extt_ref[...], gkvt_ref[width:]),
        ),
    )
    sums = [[make() * factor for make in of_core] for of_core in sums]

    def write(total, chain, out_ref, cast):
        for piece in range(width // rows_per_piece):
            value = total[piece * rows_per_piece : (piece + 1) * rows_per_piece]
            offset = pl.multiple_of((piece ^ place_ref[2 + chain]) * rows_per_piece, ROW_PACK)
            out_ref[pl.ds(offset, rows_per_piece), :] = cast(value)

    for core in range(2):

        @pl.when(place_ref[1] == core)
        def _():
            for chain in range(2):
                write(sums[1 - core][chain], chain, send_refs[chain], rounded)
                write(sums[core][chain], chain, keep_refs[chain], lambda value: value)

    send_refs[0][width:] = rounded(rider_ref[...])


def place_kernel(rows_per_piece, chain, place_ref, *refs):
    outs = 2 if chain == 0 else 1
    part_refs, out_hbms = refs[: -3 - outs], refs[-3 - outs : -3]
    all_ref, out_ref, sems = refs[-3:]
    rows = part_refs[0].shape[0]
    width = all_ref.shape[1]
    for at, part_ref in enumerate(part_refs):
        all_ref[at * rows : (at + 1) * rows] = part_ref[...]
    copies = []
    for at in range(2 * width // rows_per_piece):
        core, start = at * rows_per_piece // width, at * rows_per_piece % width
        distance = (start // rows_per_piece) ^ place_ref[2 + chain]
        offset = (core ^ place_ref[1]) * width + distance * rows_per_piece
        offset = pl.multiple_of(offset, ROW_PACK)
        piece = slice(at * rows_per_piece, (at + 1) * rows_per_piece)
        out_ref[piece] = all_ref[pl.ds(offset, rows_per_piece), :].astype(jnp.float32)
        target = pl.ds(start, rows_per_piece)
        if chain == 0:
            target = out_hbms[core].at[target]
        else:
            target = out_hbms[0].at[target, pl.ds(core * width, width)]
        copies.append(pltpu.make_async_copy(out_ref.at[piece], target, sems.at[at]))
        copies[-1].start()
    for copy in copies:
        copy.wait()


def return_kernel(place_ref, send_hbm, gf_ref, halo_ref, *refs):
    piece_refs, (out_ref, send_ref, sems) = refs[:-3], refs[-3:]
    fetch([(send_hbm, send_ref)], sems)[0].wait()
    row_count = gf_ref.shape[0]
    tile = halo_ref.shape[0]
    per_peer = send_ref.shape[1]
    chosen = listed_rows(place_ref[0], send_ref, row_count)
    returned = jnp.concatenate(
        [piece_refs[0][...], piece_refs[1][:per_peer]] + [ref[...] for ref in piece_refs[:1:-1]],
        axis=0,
    )
    total = gf_ref[...] + rows_contracted(chosen, returned)
    out_ref[: row_count - tile] = total[: row_count - tile]
    out_ref[row_count - tile :] = total[row_count - tile :] + halo_ref[...].astype(jnp.float32)


def call(kernel, name, outs, args, scratch=(), fetched=0, flops=0, stored=False):
    spaces = [pltpu.SMEM] + [pltpu.HBM] * fetched
    spaces += [pltpu.VMEM] * (len(args) - len(spaces))
    moved = sum(x.size * x.dtype.itemsize for x in list(args) + list(outs))
    scratch = list(scratch)
    if fetched:
        scratch.append(pltpu.SemaphoreType.DMA((fetched,)))
    constrained = [
        pltpu.with_memory_space_constraint(x, pltpu.HBM) if space is pltpu.HBM else x
        for x, space in zip(args, spaces)
    ]
    return pl.pallas_call(
        kernel,
        out_shape=outs,
        in_specs=[pl.BlockSpec(memory_space=space) for space in spaces],
        out_specs=[pl.BlockSpec(memory_space=pl.ANY if stored else pltpu.VMEM)] * len(outs),
        scratch_shapes=scratch,
        compiler_params=pltpu.CompilerParams(vmem_limit_bytes=VMEM_BYTES),
        cost_estimate=pl.CostEstimate(flops=flops, bytes_accessed=moved, transcendentals=0),
        name=name,
    )(*constrained)


def shards(features, out_grad, w_query, w_keyval, w_out, virtual, local_nbr, expander, send_rows):
    row_count, width = features.shape
    dom_size, per_peer = send_rows.shape
    slots = dom_size * per_peer
    virt_rows = virtual.shape[0]
    padded = ROW_PACK * -(-virt_rows // ROW_PACK)
    ext_rows = TILE + row_count + slots + padded
    nodes = row_count * lax.axis_size("dom") * lax.axis_size("rows")
    chain_steps = exchange_steps(lax.axis_size("dom"), lax.axis_size("rows"))
    rows_per_piece = width >> HALVINGS
    place = jnp.stack(
        [lax.axis_index("dom").astype(jnp.int32), lax.axis_index("rows").astype(jnp.int32) & 1]
        + [own_piece(steps) for steps in chain_steps]
    )
    bf16, f32 = jnp.bfloat16, jnp.float32
    shape = jax.ShapeDtypeStruct

    halo, through, *direct = call(
        pick_kernel,
        "pick_rows",
        [shape((TILE, width), bf16), shape((slots // 2, width), bf16)]
        + [shape((per_peer, width), bf16)] * (dom_size // 2),
        [place, features, send_rows],
        [pltpu.VMEM(features.shape, bf16), pltpu.VMEM(send_rows.shape, jnp.int32)],
        fetched=2,
    )
    through = swapped(through, 1, 0)
    arrived = handed_on(direct, through)
    halo, _ = lax.optimization_barrier((halo, through))
    halo = shifted(halo, "rows", 1)
    prepared = call(
        functools.partial(prepare_kernel, per_peer),
        "prepare",
        [
            shape(out_grad.shape, bf16),
            shape(w_query.shape, bf16),
            shape(w_keyval.shape, bf16),
            shape((width, row_count + padded), bf16),
            shape((width, row_count), bf16),
            shape((width, row_count), bf16),
            shape((row_count + padded, 2 * width), bf16),
            shape((2 * width, row_count + padded), bf16),
            shape((2 * TILE, row_count), f32),
            shape((slots + padded, row_count), f32),
        ],
        [place, features, out_grad, w_query, w_keyval, w_out, virtual, local_nbr.T, expander.T],
        [
            pltpu.VMEM(features.shape, bf16),
            pltpu.VMEM(w_out.shape, bf16),
            pltpu.VMEM(virtual.shape, bf16),
            pltpu.VMEM(local_nbr.shape[::-1], jnp.int32),
            pltpu.VMEM(expander.shape[::-1], jnp.int32),
        ],
        fetched=8,
        flops=10 * row_count * width * width,
    )
    own_feat, halo_feat, *results = call(
        functools.partial(attend_kernel, rows_per_piece, nodes**-0.5, per_peer, dom_size),
        "attend",
        [
            shape((row_count, width), f32),
            shape((TILE, width), bf16),
            *[shape((per_peer, width), bf16)] * (dom_size // 2),
            shape((slots // 2, width), bf16),
            *[shape((width, width), f32)] * 2,
            shape((width + padded, width), bf16),
            shape((width, width), bf16),
            shape((padded, width), f32),
        ],
        [place, halo, *arrived, *prepared],
        [
            pltpu.VMEM((slots, width), bf16),
            pltpu.VMEM((ext_rows, 2 * width), bf16),
            pltpu.VMEM((2 * width, ext_rows), bf16),
            pltpu.VMEM((width, ext_rows), bf16),
            pltpu.VMEM((width, row_count), bf16),
            pltpu.VMEM((2 * width, ext_rows), bf16),
            pltpu.VMEM((width, row_count), bf16),
        ],
        flops=32 * ext_rows * width * width,
    )
    *direct, through, keep, other_keep, message, other_message, rider = results

    chains = [Chain(keep, message, rider), Chain(other_keep, other_message, None)]
    through = swapped(through, 1, 0)
    for chain in chains:
        chain.send((0, 1))
    for chain in chains:
        chain.add()
    for at, masks in enumerate(zip(*chain_steps)):
        for chain in chains:
            chain.form(at < HALVINGS)
        if at == 0:
            through, _ = lax.optimization_barrier((through, [chain.message for chain in chains]))
            returned = handed_on(direct, through)
        if at == 2:
            messages, returned, halo_feat = lax.optimization_barrier(
                ([chain.message for chain in chains], returned, halo_feat)
            )
            chains[0].message, chains[1].message = messages
            halo_back = shifted(halo_feat, "rows", -1)
        for chain, mask in zip(chains, masks):
            chain.send(mask)
            chain.add()
    (grad_features,) = call(
        return_kernel,
        "return_rows",
        [shape((row_count, width), f32)],
        [place, send_rows, own_feat, halo_back, *returned],
        [pltpu.VMEM(send_rows.shape, jnp.int32)],
        fetched=1,
    )
    placed = []
    for at, (chain, steps) in enumerate(zip(chains, chain_steps)):
        held = rounded(chain.keep)
        for masks in steps[HALVINGS - 1 : 0 : -1]:
            held = jnp.concatenate([held, swapped(held, *masks)], axis=0)
        near = [held, swapped(held, *steps[0])]
        far = [swapped(block, 0, 1) for block in near]
        placed += call(
            functools.partial(place_kernel, rows_per_piece, at),
            ("place_wq_wo", "place_wkv")[at],
            [shape((width, width), f32)] * 2 if at == 0 else [shape((width, 2 * width), f32)],
            [place, *near, *far],
            [
                pltpu.VMEM((2 * width, width), bf16),
                pltpu.VMEM((2 * width, width), f32),
                pltpu.SemaphoreType.DMA((2 * width // rows_per_piece,)),
            ],
            stored=True,
        )
    grad_wq, grad_wo, grad_wkv = placed
    rider = chains[0].rider
    return grad_features, grad_wq, grad_wkv, grad_wo, rider[:virt_rows]


def solution(mesh):
    placed = (
        P(("dom", "rows"), None),
        P(("dom", "rows"), None),
        P(),
        P(),
        P(),
        P(),
        P(("dom", "rows"), None),
        P(("dom", "rows"), None),
        P(("dom", "rows"), None),
    )
    return jax.shard_map(
        shards,
        mesh=mesh,
        in_specs=placed,
        out_specs=(P(("dom", "rows"), None), P(), P(), P(), P()),
        check_vma=False,
    )
```

```python
import functools
import math

import jax
import jax.numpy as jnp
from jax import lax
from jax.experimental import pallas as pl
from jax.experimental.pallas import tpu as pltpu
from jax.sharding import PartitionSpec as P

HEADS = 8
TILE = 128
ROW_PACK = 16
NEGATIVE_FILL = -1e30
VMEM_BYTES = 24 * 1024 * 1024
LANES = 128


def f32_dot(left, right):
    return jnp.dot(left, right, preferred_element_type=jnp.float32)


def rows_contracted(left, right):
    return lax.dot_general(
        left, right, (((0,), (0,)), ((), ())), preferred_element_type=jnp.float32
    )


def times_transposed(left, right):
    return lax.dot_general(
        left, right, (((1,), (1,)), ((), ())), preferred_element_type=jnp.float32
    )


def rounded(value):
    return value.astype(jnp.bfloat16)


CORES = (0, 1)


def bits_of(size, first=1):
    return [1 << i for i in range(size.bit_length() - 1) if 1 << i >= first]


def exchange_plan():
    dom_size, rows_size = lax.axis_size("dom"), lax.axis_size("rows")
    block = [(1, 0), (0, 2), (2, 0)]
    rest = [(bit, 0) for bit in bits_of(dom_size, 4)] + [(0, bit) for bit in bits_of(rows_size, 4)]
    return block, rest


def partner_masks(block):
    masks = []
    for digit in range(1 << len(block)):
        chosen = [mask for i, mask in enumerate(block) if digit >> i & 1]
        masks.append((sum(mask[0] for mask in chosen), sum(mask[1] for mask in chosen)))
    return masks


def farthest_first(count):
    return sorted(range(1, count), key=lambda digit: (-digit.bit_count(), -digit))


def own_digit(block):
    digit = 0
    for i, (dom_mask, rows_mask) in enumerate(block):
        own = (lax.axis_index("dom") & dom_mask) | (lax.axis_index("rows") & rows_mask)
        digit += jnp.where(own != 0, 1 << i, 0)
    return digit


def swapped(block, dom_mask, rows_mask):
    dom_size, rows_size = lax.axis_size("dom"), lax.axis_size("rows")
    route = [
        (a * rows_size + b, (a ^ dom_mask) * rows_size + (b ^ rows_mask))
        for a in range(dom_size)
        for b in range(rows_size)
    ]
    return lax.ppermute(block, ("dom", "rows"), route)


def shifted(block, axis, distance):
    devices = range(lax.axis_size(axis))
    route = [((i - distance) % len(devices), i) for i in devices]
    return lax.ppermute(block, axis, route)


def paired_sum(terms):
    while len(terms) > 1:
        terms = [left + right for left, right in zip(terms[::2], terms[1::2])]
    return terms[0]


def with_rider(block, rider):
    return jnp.concatenate([rounded(block), rounded(rider)], axis=0)


def added(keep, rider, arrived):
    rows = keep.shape[0]
    riders = [rider] + [arrived[at][rows:].astype(jnp.float32) for at in sorted(arrived)]
    for block in arrived.values():
        keep = keep + block[:rows].astype(jnp.float32)
    return keep, paired_sum(riders)


def hop(blocks, bit):
    moving = [at for at in range(len(blocks)) if at & bit]
    rows = blocks[0].shape[0]
    arrived = swapped(jnp.concatenate([blocks[at] for at in moving], axis=0), bit, 0)
    return {at: arrived[i * rows : (i + 1) * rows] for i, at in enumerate(moving)}


def listed_rows(send_ref, row_count):
    dom_size, per_peer = send_ref.shape
    slots = dom_size * per_peer
    slot = lax.broadcasted_iota(jnp.int32, (slots, per_peer), 0)
    place = lax.broadcasted_iota(jnp.int32, (slots, per_peer), 1)
    peer = (slot // per_peer) ^ lax.axis_index("dom")
    listed = jnp.zeros((slots, per_peer), jnp.int32)
    for at in range(dom_size):
        listed += jnp.where((peer == at) & (place == slot % per_peer), send_ref[at : at + 1, :], 0)
    column = jnp.sum(listed, axis=1, keepdims=True)
    rows = lax.broadcasted_iota(jnp.int32, (slots, row_count), 1)
    return jnp.where(column == rows, 1.0, 0.0).astype(jnp.bfloat16)


def fetch(pairs, sems):
    copies = [
        pltpu.make_async_copy(source, target, sems.at[at])
        for at, (source, target) in enumerate(pairs)
    ]
    for copy in copies:
        copy.start()
    return copies


def pick_kernel(feat_hbm, send_hbm, halo_ref, chosen_ref, *refs):
    out_refs, (feat_ref, send_ref, sems) = refs[:-3], refs[-3:]
    copies = fetch([(send_hbm, send_ref), (feat_hbm, feat_ref)], sems)
    copies[0].wait()
    per_peer = send_ref.shape[1]
    chosen_ref[...] = listed_rows(send_ref, feat_ref.shape[0])
    copies[1].wait()
    halo_ref[...] = feat_ref[feat_ref.shape[0] - halo_ref.shape[0] :]
    picked = rounded(f32_dot(chosen_ref[...], feat_ref[...]))
    for at, out_ref in enumerate(out_refs):
        out_ref[...] = picked[at * per_peer : (at + 1) * per_peer]


def prepare_kernel(
    per_peer,
    feat_hbm,
    og_hbm,
    wq_hbm,
    wkv_hbm,
    wo_hbm,
    virt_hbm,
    nbr_hbm,
    exp_hbm,
    og_ref,
    wq_ref,
    wkv_ref,
    featt_ref,
    qt_ref,
    odt_ref,
    kv_ref,
    kvt_ref,
    local_bias_ref,
    far_bias_ref,
    feat_ref,
    wo_ref,
    virt_ref,
    nbr_ref,
    exp_ref,
    sems,
):
    nbr_copy, exp_copy, feat_copy, virt_copy, wq_copy, wkv_copy, og_copy, wo_copy = fetch(
        [
            (nbr_hbm, nbr_ref),
            (exp_hbm, exp_ref),
            (feat_hbm, feat_ref),
            (virt_hbm, virt_ref),
            (wq_hbm, wq_ref),
            (wkv_hbm, wkv_ref),
            (og_hbm, og_ref),
            (wo_hbm, wo_ref),
        ],
        sems,
    )
    row_count, width = feat_ref.shape
    window = local_bias_ref.shape[0]
    far = far_bias_ref.shape[0]
    virt_rows = virt_ref.shape[0]
    padded = kv_ref.shape[0] - row_count
    slots = far - padded
    scale = 1.0 / math.sqrt(width // HEADS)

    def multiplicity(key_rows, named):
        position = lax.broadcasted_iota(jnp.int32, (key_rows, row_count), 0)
        count = jnp.zeros((key_rows, row_count), jnp.float32)
        for at in range(named.shape[0]):
            count += jnp.where(named[at : at + 1, :] == position, 1.0, 0.0)
        return count

    nbr_copy.wait()
    local_bias_ref[...] = jnp.where(multiplicity(window, nbr_ref) > 0.0, 0.0, NEGATIVE_FILL)
    exp_copy.wait()
    expander = exp_ref[...]
    expander = ((expander // per_peer) ^ lax.axis_index("dom")) * per_peer + expander % per_peer
    named_times = multiplicity(slots, expander)
    slot_bias = jnp.full((slots, row_count), NEGATIVE_FILL, jnp.float32)
    for times in range(1, exp_ref.shape[0] + 1):
        slot_bias = jnp.where(named_times == float(times), math.log(times) / scale, slot_bias)
    far_bias_ref[:slots] = slot_bias
    virt_row = lax.broadcasted_iota(jnp.int32, (padded, row_count), 0)
    far_bias_ref[slots:] = jnp.where(virt_row < virt_rows, 0.0, NEGATIVE_FILL)

    feat_copy.wait()
    featt_ref[:, :row_count] = feat_ref[...].T
    virt_copy.wait()
    virt = jnp.concatenate(
        [virt_ref[...], jnp.zeros((padded - virt_rows, width), jnp.bfloat16)], axis=0
    )
    featt_ref[:, row_count:] = virt.T
    wq_copy.wait()
    qt_ref[...] = rounded(rows_contracted(wq_ref[...], featt_ref[:, :row_count]))
    wkv_copy.wait()
    kv_ref[:row_count] = rounded(f32_dot(feat_ref[...], wkv_ref[...]))
    kv_ref[row_count:] = rounded(f32_dot(virt, wkv_ref[...]))
    kvt_ref[...] = kv_ref[...].T
    og_copy.wait()
    wo_copy.wait()
    odt_ref[...] = rounded(times_transposed(wo_ref[...], og_ref[...]))


def attend_kernel(
    rows_per_piece,
    factor,
    per_peer,
    dom_size,
    *refs,
):
    piece_refs, halo_ref, refs = refs[:dom_size], refs[dom_size], refs[dom_size + 1 :]
    og_ref, wq_ref, wkv_ref, featt_ref, qt_ref, odt_ref, own_kv_ref, own_kvt_ref = refs[:8]
    local_bias_ref, far_bias_ref, gf_ref, halo_feat_ref = refs[8:12]
    slot_feat_refs, refs = refs[12 : 12 + dom_size], refs[12 + dom_size :]
    keep_ref, send_ref, rider_ref = refs[:3]
    slot_ref, kv_ref, kvt_ref, extt_ref, gqt_ref, gkvt_ref, ot_ref = refs[3:]
    width, row_count = qt_ref.shape
    tile = halo_ref.shape[0]
    tile_count = row_count // tile
    slots = dom_size * per_peer
    near = tile + row_count
    virt_at = near + slots
    head_dim = width // HEADS
    scale = 1.0 / math.sqrt(head_dim)

    kv_ref[tile:near] = own_kv_ref[:row_count]
    kv_ref[virt_at:] = own_kv_ref[row_count:]
    kvt_ref[:, tile:near] = own_kvt_ref[:, :row_count]
    kvt_ref[:, virt_at:] = own_kvt_ref[:, row_count:]
    extt_ref[:, tile:near] = featt_ref[:, :row_count]
    extt_ref[:, virt_at:] = featt_ref[:, row_count:]
    for at, piece_ref in zip([0] + farthest_first(dom_size), piece_refs):
        slot_ref[at * per_peer : (at + 1) * per_peer] = piece_ref[...]
    for rows, source_ref in ((slice(0, tile), halo_ref), (slice(near, virt_at), slot_ref)):
        extt_ref[:, rows] = source_ref[...].T
        kv_ref[rows] = rounded(f32_dot(source_ref[...], wkv_ref[...]))
        kvt_ref[:, rows] = kv_ref[rows].T

    def tiles(of):
        return jnp.concatenate([of(t, slice(t * tile, (t + 1) * tile)) for t in range(tile_count)], 1)

    for head in range(HEADS):
        low, high = head * head_dim, (head + 1) * head_dim
        first = low // 128 * 128
        last = min(-(-high // 128) * 128, width)
        column = lax.broadcasted_iota(jnp.int32, (last - first, row_count), 0) + first
        of_head = (column >= low) & (column < high)
        q_rows = jnp.where(of_head, qt_ref[first:last, :], 0)
        d_rows = jnp.where(of_head, odt_ref[first:last, :], 0)

        def products(operand, start, stop):
            local = tiles(
                lambda t, lanes: f32_dot(
                    kv_ref[t * tile : (t + 2) * tile, start:stop], operand[:, lanes]
                )
            )
            return local, f32_dot(kv_ref[near:, start:stop], operand)

        s_local, s_far = products(q_rows, first, last)
        s_local += local_bias_ref[...]
        s_far += far_bias_ref[...]
        peak = jnp.maximum(
            jnp.max(s_local, axis=0, keepdims=True), jnp.max(s_far, axis=0, keepdims=True)
        )
        exponent_scale = scale * math.log2(math.e)
        e_local = jnp.exp2((s_local - peak) * exponent_scale)
        e_far = jnp.exp2((s_far - peak) * exponent_scale)
        total = jnp.sum(e_local, axis=0, keepdims=True) + jnp.sum(e_far, axis=0, keepdims=True)
        inverse = 1.0 / total
        p_local = e_local * inverse
        p_far = e_far * inverse
        dp_local, dp_far = products(d_rows, width + first, width + last)
        delta = jnp.sum(p_local * dp_local, axis=0, keepdims=True) + jnp.sum(
            p_far * dp_far, axis=0, keepdims=True
        )
        pb_local, pb_far = rounded(p_local), rounded(p_far)
        ds_local = rounded(p_local * (dp_local - delta))
        ds_far = rounded(p_far * (dp_far - delta))

        def to_queries(start, local, beyond):
            rows = slice(start + low, start + high)
            near_part = tiles(
                lambda t, lanes: f32_dot(kvt_ref[rows, t * tile : (t + 2) * tile], local[:, lanes])
            )
            return near_part + f32_dot(kvt_ref[rows, near:], beyond)

        ot_ref[low:high] = rounded(to_queries(width, pb_local, pb_far))
        gqt_ref[low:high] = rounded(to_queries(0, ds_local, ds_far) * scale)

        def to_keys(start, operand, local, beyond, factor):
            rows = slice(start + low, start + high)
            parts = []
            carried = None
            for t in range(tile_count):
                lanes = slice(t * tile, (t + 1) * tile)
                window = times_transposed(operand[:, lanes], local[:, lanes])
                previous = window[:, :tile]
                parts.append(previous if carried is None else previous + carried)
                carried = window[:, tile:]
            parts.append(carried)
            parts.append(times_transposed(operand, beyond))
            gathered = jnp.concatenate(parts, axis=1)
            gkvt_ref[rows] = rounded(gathered if factor is None else gathered * factor)

        to_keys(0, qt_ref[low:high], ds_local, ds_far, scale)
        to_keys(width, odt_ref[low:high], pb_local, pb_far, None)

    by_feature = f32_dot(wkv_ref[...], gkvt_ref[...])
    own = by_feature[:, tile:near] + f32_dot(wq_ref[...], gqt_ref[...])
    gf_ref[...] = own.T
    halo_feat_ref[...] = rounded(by_feature[:, :tile].T)
    slot_feat = rounded(by_feature[:, near:virt_at].T)
    for at, out_ref in enumerate(slot_feat_refs):
        out_ref[...] = slot_feat[at * per_peer : (at + 1) * per_peer]
    rider_ref[...] = by_feature[:, virt_at:].T * factor

    sums = (
        times_transposed(extt_ref[:, tile:near], gqt_ref[...]),
        times_transposed(extt_ref[...], gkvt_ref[:width]),
        times_transposed(extt_ref[...], gkvt_ref[width:]),
        f32_dot(ot_ref[...], og_ref[...]),
    )
    pieces = keep_ref.shape[0] // rows_per_piece
    held = own_digit(exchange_plan()[0])

    def write(half, out_ref, cast):
        for piece in range(pieces):
            start = (half * pieces + piece) * rows_per_piece
            value = sums[start // width][start % width : start % width + rows_per_piece] * factor
            offset = pl.multiple_of((piece ^ held) * rows_per_piece, ROW_PACK)
            out_ref[pl.ds(offset, rows_per_piece), :] = cast(value)

    for half in range(2):

        @pl.when(lax.axis_index("rows") % 2 == half)
        def _():
            write(half, keep_ref, lambda value: value)
            write(1 - half, send_ref, rounded)

    send_ref[keep_ref.shape[0] :] = rounded(rider_ref[...])


def place_kernel(*refs):
    part_refs, (gq_hbm, gkv_hbm, go_hbm, all_ref, out_ref, sems) = refs[:-6], refs[-6:]
    width = gq_hbm.shape[0]
    rows = part_refs[0].shape[0]
    half = len(part_refs) // 2
    for at, digit in enumerate([0] + farthest_first(half)[::-1]):
        for core in range(2):
            place = (core * half + digit) * rows
            all_ref[place : place + rows] = part_refs[core * half + at][...]
    held = own_digit(exchange_plan()[0]) + (lax.axis_index("rows") % 2) * half
    copies = []
    for at in range(2 * half):
        start = at * rows
        piece = slice(start, start + rows)
        offset = pl.multiple_of((held ^ at) * rows, ROW_PACK)
        out_ref[piece] = all_ref[pl.ds(offset, rows), :].astype(jnp.float32)
        rows_out = pl.ds(start % width, rows)
        which = start // width
        if which == 0:
            target = gq_hbm.at[rows_out]
        elif which == 3:
            target = go_hbm.at[rows_out]
        else:
            target = gkv_hbm.at[rows_out, pl.ds((which - 1) * width, width)]
        copies.append(pltpu.make_async_copy(out_ref.at[piece], target, sems.at[at]))
        copies[-1].start()
    for copy in copies:
        copy.wait()


def return_kernel(gf_ref, chosen_ref, halo_ref, *refs):
    piece_refs, out_ref = refs[:-1], refs[-1]
    row_count = gf_ref.shape[0]
    tile = halo_ref.shape[0]
    returned = jnp.concatenate([ref[...] for ref in piece_refs], axis=0)
    total = gf_ref[...] + rows_contracted(chosen_ref[...], returned)
    out_ref[: row_count - tile] = total[: row_count - tile]
    out_ref[row_count - tile :] = total[row_count - tile :] + halo_ref[...].astype(jnp.float32)


def call(kernel, name, outs, args, scratch=(), fetched=0, flops=0, stored=False):
    spaces = [pltpu.HBM] * fetched
    spaces += [pltpu.VMEM] * (len(args) - len(spaces))
    moved = sum(x.size * x.dtype.itemsize for x in list(args) + list(outs))
    scratch = list(scratch)
    if fetched:
        scratch.append(pltpu.SemaphoreType.DMA((fetched,)))
    constrained = [
        pltpu.with_memory_space_constraint(x, pltpu.HBM) if space is pltpu.HBM else x
        for x, space in zip(args, spaces)
    ]
    return pl.pallas_call(
        kernel,
        out_shape=outs,
        in_specs=[pl.BlockSpec(memory_space=space) for space in spaces],
        out_specs=[pl.BlockSpec(memory_space=pl.ANY if stored else pltpu.VMEM)] * len(outs),
        scratch_shapes=scratch,
        compiler_params=pltpu.CompilerParams(vmem_limit_bytes=VMEM_BYTES),
        cost_estimate=pl.CostEstimate(flops=flops, bytes_accessed=moved, transcendentals=0),
        name=name,
    )(*constrained)


def shards(features, out_grad, w_query, w_keyval, w_out, virtual, local_nbr, expander, send_rows):
    row_count, width = features.shape
    dom_size, per_peer = send_rows.shape
    slots = dom_size * per_peer
    virt_rows = virtual.shape[0]
    padded = ROW_PACK * -(-virt_rows // ROW_PACK)
    ext_rows = TILE + row_count + slots + padded
    nodes = row_count * lax.axis_size("dom") * lax.axis_size("rows")
    block, rest = exchange_plan()
    masks = partner_masks(block)
    order = farthest_first(len(masks))
    rows_per_piece = 2 * width // len(masks)
    bf16, f32 = jnp.bfloat16, jnp.float32
    shape = jax.ShapeDtypeStruct

    halo, chosen, *sent = call(
        pick_kernel,
        "pick_rows",
        [shape((TILE, width), bf16), shape((slots, row_count), bf16)]
        + [shape((per_peer, width), bf16)] * dom_size,
        [features, send_rows],
        [pltpu.VMEM(features.shape, bf16), pltpu.VMEM(send_rows.shape, jnp.int32)],
        fetched=2,
    )
    arrived = [sent[0]] + [swapped(sent[at], at, 0) for at in farthest_first(dom_size)]
    halo, _ = lax.optimization_barrier((halo, arrived[1]))
    halo = shifted(halo, "rows", 1)
    prepared = call(
        functools.partial(prepare_kernel, per_peer),
        "prepare",
        [
            shape(out_grad.shape, bf16),
            shape(w_query.shape, bf16),
            shape(w_keyval.shape, bf16),
            shape((width, row_count + padded), bf16),
            shape((width, row_count), bf16),
            shape((width, row_count), bf16),
            shape((row_count + padded, 2 * width), bf16),
            shape((2 * width, row_count + padded), bf16),
            shape((2 * TILE, row_count), f32),
            shape((slots + padded, row_count), f32),
        ],
        [features, out_grad, w_query, w_keyval, w_out, virtual, local_nbr.T, expander.T],
        [
            pltpu.VMEM(features.shape, bf16),
            pltpu.VMEM(w_out.shape, bf16),
            pltpu.VMEM(virtual.shape, bf16),
            pltpu.VMEM(local_nbr.shape[::-1], jnp.int32),
            pltpu.VMEM(expander.shape[::-1], jnp.int32),
        ],
        fetched=8,
        flops=10 * row_count * width * width,
    )
    own_feat, halo_feat, *results = call(
        functools.partial(attend_kernel, rows_per_piece, nodes**-0.5, per_peer, dom_size),
        "attend",
        [
            shape((row_count, width), f32),
            shape((TILE, width), bf16),
            *[shape((per_peer, width), bf16)] * dom_size,
            shape((2 * width, width), f32),
            shape((2 * width + padded, width), bf16),
            shape((padded, width), f32),
        ],
        [*arrived, halo, *prepared],
        [
            pltpu.VMEM((slots, width), bf16),
            pltpu.VMEM((ext_rows, 2 * width), bf16),
            pltpu.VMEM((2 * width, ext_rows), bf16),
            pltpu.VMEM((width, ext_rows), bf16),
            pltpu.VMEM((width, row_count), bf16),
            pltpu.VMEM((2 * width, ext_rows), bf16),
            pltpu.VMEM((width, row_count), bf16),
        ],
        flops=32 * ext_rows * width * width,
    )
    *slot_feat, keep, message, rider = results

    rider = rounded(rider).astype(f32)
    keep, rider = added(keep, rider, {1: swapped(message, *CORES)})
    rider = rider[: -(-virt_rows // 8) * 8]
    dom_bits = bits_of(dom_size)
    slot_feat = [hop(slot_feat, dom_bits[0]).get(at, own) for at, own in enumerate(slot_feat)]

    parts = [keep[at * rows_per_piece : (at + 1) * rows_per_piece] for at in range(len(masks))]
    messages = {at: swapped(with_rider(parts[at], rider), *masks[at]) for at in order}
    rider = rounded(rider).astype(f32)
    keep, rider = added(parts[0], rider, messages)

    for at, mask in enumerate(rest):
        message = with_rider(keep, rider)
        if at == 0:
            (slot_feat, halo_feat), _ = lax.optimization_barrier(
                ((slot_feat, halo_feat), message)
            )
            for bit in dom_bits[1:-1]:
                slot_feat = [hop(slot_feat, bit).get(i, own) for i, own in enumerate(slot_feat)]
            halo_back = shifted(halo_feat, "rows", -1)
        keep, rider = rounded(keep).astype(f32), rounded(rider).astype(f32)
        keep, rider = added(keep, rider, {1: swapped(message, *mask)})

    held = rounded(keep)
    held, slot_feat, halo_back = lax.optimization_barrier((held, slot_feat, halo_back))
    slot_feat = [hop(slot_feat, dom_bits[-1]).get(at, own) for at, own in enumerate(slot_feat)]
    near = [held] + [swapped(held, *masks[at]) for at in order[::-1]]
    far = [swapped(part, *CORES) for part in near]
    (grad_features,) = call(
        return_kernel,
        "return_rows",
        [shape((row_count, width), f32)],
        [own_feat, chosen, halo_back, *slot_feat],
    )
    grad_wq, grad_wkv, grad_wo = call(
        place_kernel,
        "place_sums",
        [shape((width, width), f32), shape((width, 2 * width), f32), shape((width, width), f32)],
        [*near, *far],
        [
            pltpu.VMEM((4 * width, width), bf16),
            pltpu.VMEM((4 * width, width), f32),
            pltpu.SemaphoreType.DMA((2 * len(masks),)),
        ],
        stored=True,
    )
    return grad_features, grad_wq, grad_wkv, grad_wo, rider[:virt_rows]


def solution(mesh):
    placed = (
        P(("dom", "rows"), None),
        P(("dom", "rows"), None),
        P(),
        P(),
        P(),
        P(),
        P(("dom", "rows"), None),
        P(("dom", "rows"), None),
        P(("dom", "rows"), None),
    )
    return jax.shard_map(
        shards,
        mesh=mesh,
        in_specs=placed,
        out_specs=(P(("dom", "rows"), None), P(), P(), P(), P()),
        check_vma=False,
    )
```

```python
import functools
import math

import jax
import jax.numpy as jnp
from jax import lax
from jax.experimental import pallas as pl
from jax.experimental.pallas import tpu as pltpu
from jax.sharding import PartitionSpec as P

HEADS = 8
TILE = 128
ROW_PACK = 16
NEGATIVE_FILL = -1e30
VMEM_BYTES = 24 * 1024 * 1024
LANES = 128


def f32_dot(left, right):
    return jnp.dot(left, right, preferred_element_type=jnp.float32)


def rows_contracted(left, right):
    return lax.dot_general(
        left, right, (((0,), (0,)), ((), ())), preferred_element_type=jnp.float32
    )


def times_transposed(left, right):
    return lax.dot_general(
        left, right, (((1,), (1,)), ((), ())), preferred_element_type=jnp.float32
    )


def rounded(value):
    return value.astype(jnp.bfloat16)


CORES = (0, 1)


def bits_of(size, first=1):
    return [1 << i for i in range(size.bit_length() - 1) if 1 << i >= first]


def exchange_plan():
    dom_size, rows_size = lax.axis_size("dom"), lax.axis_size("rows")
    block = [(1, 0), (0, 2), (2, 0)]
    rest = [(bit, 0) for bit in bits_of(dom_size, 4)] + [(0, bit) for bit in bits_of(rows_size, 4)]
    return block, rest


def partner_masks(block):
    masks = []
    for digit in range(1 << len(block)):
        chosen = [mask for i, mask in enumerate(block) if digit >> i & 1]
        masks.append((sum(mask[0] for mask in chosen), sum(mask[1] for mask in chosen)))
    return masks


def farthest_first(count):
    return sorted(range(1, count), key=lambda digit: (-digit.bit_count(), -digit))


def own_digit(block):
    digit = 0
    for i, (dom_mask, rows_mask) in enumerate(block):
        own = (lax.axis_index("dom") & dom_mask) | (lax.axis_index("rows") & rows_mask)
        digit += jnp.where(own != 0, 1 << i, 0)
    return digit


def swapped(block, dom_mask, rows_mask):
    dom_size, rows_size = lax.axis_size("dom"), lax.axis_size("rows")
    route = [
        (a * rows_size + b, (a ^ dom_mask) * rows_size + (b ^ rows_mask))
        for a in range(dom_size)
        for b in range(rows_size)
    ]
    return lax.ppermute(block, ("dom", "rows"), route)


def shifted(block, axis, distance):
    devices = range(lax.axis_size(axis))
    route = [((i - distance) % len(devices), i) for i in devices]
    return lax.ppermute(block, axis, route)


def paired_sum(terms):
    while len(terms) > 1:
        terms = [left + right for left, right in zip(terms[::2], terms[1::2])]
    return terms[0]


def with_rider(block, rider):
    return jnp.concatenate([rounded(block), rounded(rider)], axis=0)


def added(keep, rider, arrived):
    rows = keep.shape[0]
    riders = [rider] + [arrived[at][rows:].astype(jnp.float32) for at in sorted(arrived)]
    for block in arrived.values():
        keep = keep + block[:rows].astype(jnp.float32)
    return keep, paired_sum(riders)


def hop(blocks, bit):
    moving = [at for at in range(len(blocks)) if at & bit]
    rows = blocks[0].shape[0]
    arrived = swapped(jnp.concatenate([blocks[at] for at in moving], axis=0), bit, 0)
    return {at: arrived[i * rows : (i + 1) * rows] for i, at in enumerate(moving)}


def listed_rows(send_ref, row_count):
    dom_size, per_peer = send_ref.shape
    slots = dom_size * per_peer
    slot = lax.broadcasted_iota(jnp.int32, (slots, per_peer), 0)
    place = lax.broadcasted_iota(jnp.int32, (slots, per_peer), 1)
    peer = (slot // per_peer) ^ lax.axis_index("dom")
    listed = jnp.zeros((slots, per_peer), jnp.int32)
    for at in range(dom_size):
        listed += jnp.where((peer == at) & (place == slot % per_peer), send_ref[at : at + 1, :], 0)
    column = jnp.sum(listed, axis=1, keepdims=True)
    rows = lax.broadcasted_iota(jnp.int32, (slots, row_count), 1)
    return jnp.where(column == rows, 1.0, 0.0).astype(jnp.bfloat16)


def fetch(pairs, sems):
    copies = [
        pltpu.make_async_copy(source, target, sems.at[at])
        for at, (source, target) in enumerate(pairs)
    ]
    for copy in copies:
        copy.start()
    return copies


def store_blocks(rows, through_ref, direct_refs):
    size = direct_refs[0].shape[0]
    for at, out_ref in enumerate(direct_refs):
        out_ref[...] = rows[2 * at * size : (2 * at + 1) * size]
        through_ref[at * size : (at + 1) * size] = rows[(2 * at + 1) * size : (2 * at + 2) * size]


def pick_kernel(feat_hbm, send_hbm, halo_ref, chosen_ref, through_ref, *refs):
    direct_refs, (feat_ref, send_ref, sems) = refs[:-3], refs[-3:]
    copies = fetch([(send_hbm, send_ref), (feat_hbm, feat_ref)], sems)
    copies[0].wait()
    chosen_ref[...] = listed_rows(send_ref, feat_ref.shape[0])
    copies[1].wait()
    halo_ref[...] = feat_ref[feat_ref.shape[0] - halo_ref.shape[0] :]
    store_blocks(rounded(f32_dot(chosen_ref[...], feat_ref[...])), through_ref, direct_refs)


def prepare_kernel(
    per_peer,
    feat_hbm,
    og_hbm,
    wq_hbm,
    wkv_hbm,
    wo_hbm,
    virt_hbm,
    nbr_hbm,
    exp_hbm,
    og_ref,
    wq_ref,
    wkv_ref,
    featt_ref,
    qt_ref,
    odt_ref,
    kv_ref,
    kvt_ref,
    local_bias_ref,
    far_bias_ref,
    feat_ref,
    wo_ref,
    virt_ref,
    nbr_ref,
    exp_ref,
    sems,
):
    nbr_copy, exp_copy, feat_copy, virt_copy, wq_copy, wkv_copy, og_copy, wo_copy = fetch(
        [
            (nbr_hbm, nbr_ref),
            (exp_hbm, exp_ref),
            (feat_hbm, feat_ref),
            (virt_hbm, virt_ref),
            (wq_hbm, wq_ref),
            (wkv_hbm, wkv_ref),
            (og_hbm, og_ref),
            (wo_hbm, wo_ref),
        ],
        sems,
    )
    row_count, width = feat_ref.shape
    window = local_bias_ref.shape[0]
    far = far_bias_ref.shape[0]
    virt_rows = virt_ref.shape[0]
    padded = kv_ref.shape[0] - row_count
    slots = far - padded
    scale = 1.0 / math.sqrt(width // HEADS)

    def multiplicity(key_rows, named):
        position = lax.broadcasted_iota(jnp.int32, (key_rows, row_count), 0)
        count = jnp.zeros((key_rows, row_count), jnp.float32)
        for at in range(named.shape[0]):
            count += jnp.where(named[at : at + 1, :] == position, 1.0, 0.0)
        return count

    nbr_copy.wait()
    local_bias_ref[...] = jnp.where(multiplicity(window, nbr_ref) > 0.0, 0.0, NEGATIVE_FILL)
    exp_copy.wait()
    expander = exp_ref[...]
    expander = ((expander // per_peer) ^ lax.axis_index("dom")) * per_peer + expander % per_peer
    named_times = multiplicity(slots, expander)
    slot_bias = jnp.full((slots, row_count), NEGATIVE_FILL, jnp.float32)
    for times in range(1, exp_ref.shape[0] + 1):
        slot_bias = jnp.where(named_times == float(times), math.log(times) / scale, slot_bias)
    far_bias_ref[:slots] = slot_bias
    virt_row = lax.broadcasted_iota(jnp.int32, (padded, row_count), 0)
    far_bias_ref[slots:] = jnp.where(virt_row < virt_rows, 0.0, NEGATIVE_FILL)

    feat_copy.wait()
    featt_ref[:, :row_count] = feat_ref[...].T
    virt_copy.wait()
    virt = jnp.concatenate(
        [virt_ref[...], jnp.zeros((padded - virt_rows, width), jnp.bfloat16)], axis=0
    )
    featt_ref[:, row_count:] = virt.T
    wq_copy.wait()
    qt_ref[...] = rounded(rows_contracted(wq_ref[...], featt_ref[:, :row_count]))
    wkv_copy.wait()
    kv_ref[:row_count] = rounded(f32_dot(feat_ref[...], wkv_ref[...]))
    kv_ref[row_count:] = rounded(f32_dot(virt, wkv_ref[...]))
    kvt_ref[...] = kv_ref[...].T
    og_copy.wait()
    wo_copy.wait()
    odt_ref[...] = rounded(times_transposed(wo_ref[...], og_ref[...]))


def attend_kernel(
    rows_per_piece,
    factor,
    per_peer,
    dom_size,
    *refs,
):
    count = dom_size // 2 + 1
    piece_refs, halo_ref, refs = refs[:count], refs[count], refs[count + 1 :]
    og_ref, wq_ref, wkv_ref, featt_ref, qt_ref, odt_ref, own_kv_ref, own_kvt_ref = refs[:8]
    local_bias_ref, far_bias_ref, gf_ref, halo_feat_ref = refs[8:12]
    through_ref, direct_refs, refs = refs[12], refs[13 : 12 + count], refs[12 + count :]
    keep_ref, send_ref, rider_ref = refs[:3]
    slot_ref, kv_ref, kvt_ref, extt_ref, gqt_ref, gkvt_ref, ot_ref = refs[3:]
    width, row_count = qt_ref.shape
    tile = halo_ref.shape[0]
    tile_count = row_count // tile
    slots = dom_size * per_peer
    near = tile + row_count
    virt_at = near + slots
    head_dim = width // HEADS
    scale = 1.0 / math.sqrt(head_dim)

    kv_ref[tile:near] = own_kv_ref[:row_count]
    kv_ref[virt_at:] = own_kv_ref[row_count:]
    kvt_ref[:, tile:near] = own_kvt_ref[:, :row_count]
    kvt_ref[:, virt_at:] = own_kvt_ref[:, row_count:]
    extt_ref[:, tile:near] = featt_ref[:, :row_count]
    extt_ref[:, virt_at:] = featt_ref[:, row_count:]
    slot_ref[:per_peer] = piece_refs[0][...]
    slot_ref[per_peer : 2 * per_peer] = piece_refs[1][:per_peer]
    for at, piece_ref in enumerate(piece_refs[:1:-1], 1):
        slot_ref[2 * at * per_peer : (2 * at + 2) * per_peer] = piece_ref[...]
    for rows, source_ref in ((slice(0, tile), halo_ref), (slice(near, virt_at), slot_ref)):
        extt_ref[:, rows] = source_ref[...].T
        kv_ref[rows] = rounded(f32_dot(source_ref[...], wkv_ref[...]))
        kvt_ref[:, rows] = kv_ref[rows].T

    def tiles(of):
        return jnp.concatenate([of(t, slice(t * tile, (t + 1) * tile)) for t in range(tile_count)], 1)

    for head in range(HEADS):
        low, high = head * head_dim, (head + 1) * head_dim
        first = low // 128 * 128
        last = min(-(-high // 128) * 128, width)
        column = lax.broadcasted_iota(jnp.int32, (last - first, row_count), 0) + first
        of_head = (column >= low) & (column < high)
        q_rows = jnp.where(of_head, qt_ref[first:last, :], 0)
        d_rows = jnp.where(of_head, odt_ref[first:last, :], 0)

        def products(operand, start, stop):
            local = tiles(
                lambda t, lanes: f32_dot(
                    kv_ref[t * tile : (t + 2) * tile, start:stop], operand[:, lanes]
                )
            )
            return local, f32_dot(kv_ref[near:, start:stop], operand)

        s_local, s_far = products(q_rows, first, last)
        s_local += local_bias_ref[...]
        s_far += far_bias_ref[...]
        peak = jnp.maximum(
            jnp.max(s_local, axis=0, keepdims=True), jnp.max(s_far, axis=0, keepdims=True)
        )
        exponent_scale = scale * math.log2(math.e)
        e_local = jnp.exp2((s_local - peak) * exponent_scale)
        e_far = jnp.exp2((s_far - peak) * exponent_scale)
        total = jnp.sum(e_local, axis=0, keepdims=True) + jnp.sum(e_far, axis=0, keepdims=True)
        inverse = 1.0 / total
        p_local = e_local * inverse
        p_far = e_far * inverse
        dp_local, dp_far = products(d_rows, width + first, width + last)
        delta = jnp.sum(p_local * dp_local, axis=0, keepdims=True) + jnp.sum(
            p_far * dp_far, axis=0, keepdims=True
        )
        pb_local, pb_far = rounded(p_local), rounded(p_far)
        ds_local = rounded(p_local * (dp_local - delta))
        ds_far = rounded(p_far * (dp_far - delta))

        def to_queries(start, local, beyond):
            rows = slice(start + low, start + high)
            near_part = tiles(
                lambda t, lanes: f32_dot(kvt_ref[rows, t * tile : (t + 2) * tile], local[:, lanes])
            )
            return near_part + f32_dot(kvt_ref[rows, near:], beyond)

        ot_ref[low:high] = rounded(to_queries(width, pb_local, pb_far))
        gqt_ref[low:high] = rounded(to_queries(0, ds_local, ds_far) * scale)

        def to_keys(start, operand, local, beyond, factor):
            rows = slice(start + low, start + high)
            parts = []
            carried = None
            for t in range(tile_count):
                lanes = slice(t * tile, (t + 1) * tile)
                window = times_transposed(operand[:, lanes], local[:, lanes])
                previous = window[:, :tile]
                parts.append(previous if carried is None else previous + carried)
                carried = window[:, tile:]
            parts.append(carried)
            parts.append(times_transposed(operand, beyond))
            gathered = jnp.concatenate(parts, axis=1)
            gkvt_ref[rows] = rounded(gathered if factor is None else gathered * factor)

        to_keys(0, qt_ref[low:high], ds_local, ds_far, scale)
        to_keys(width, odt_ref[low:high], pb_local, pb_far, None)

    by_feature = f32_dot(wkv_ref[...], gkvt_ref[...])
    own = by_feature[:, tile:near] + f32_dot(wq_ref[...], gqt_ref[...])
    gf_ref[...] = own.T
    halo_feat_ref[...] = rounded(by_feature[:, :tile].T)
    store_blocks(rounded(by_feature[:, near:virt_at].T), through_ref, direct_refs)
    rider_ref[...] = by_feature[:, virt_at:].T * factor

    sums = (
        times_transposed(extt_ref[:, tile:near], gqt_ref[...]),
        times_transposed(extt_ref[...], gkvt_ref[:width]),
        times_transposed(extt_ref[...], gkvt_ref[width:]),
        f32_dot(ot_ref[...], og_ref[...]),
    )
    pieces = keep_ref.shape[0] // rows_per_piece
    held = own_digit(exchange_plan()[0])

    def write(half, out_ref, cast):
        for piece in range(pieces):
            start = (half * pieces + piece) * rows_per_piece
            value = sums[start // width][start % width : start % width + rows_per_piece] * factor
            offset = pl.multiple_of((piece ^ held) * rows_per_piece, ROW_PACK)
            out_ref[pl.ds(offset, rows_per_piece), :] = cast(value)

    for half in range(2):

        @pl.when(lax.axis_index("rows") % 2 == half)
        def _():
            write(half, keep_ref, lambda value: value)
            write(1 - half, send_ref, rounded)

    send_ref[keep_ref.shape[0] :] = rounded(rider_ref[...])


def place_kernel(*refs):
    part_refs, (gq_hbm, gkv_hbm, go_hbm, all_ref, out_ref, sems) = refs[:-6], refs[-6:]
    width = gq_hbm.shape[0]
    square = len(part_refs) // 2
    rows = part_refs[0].shape[0] // 2
    half = 2 * square
    for at, digit in enumerate(range(square)):
        for core in range(2):
            for near_z in range(2):
                place = (core * half + near_z * square + digit) * rows
                part = part_refs[core * square + at][near_z * rows : (near_z + 1) * rows]
                all_ref[place : place + rows] = part
    held = own_digit(exchange_plan()[0]) + (lax.axis_index("rows") % 2) * half
    copies = []
    for at in range(2 * half):
        start = at * rows
        piece = slice(start, start + rows)
        offset = pl.multiple_of((held ^ at) * rows, ROW_PACK)
        out_ref[piece] = all_ref[pl.ds(offset, rows), :].astype(jnp.float32)
        rows_out = pl.ds(start % width, rows)
        which = start // width
        if which == 0:
            target = gq_hbm.at[rows_out]
        elif which == 3:
            target = go_hbm.at[rows_out]
        else:
            target = gkv_hbm.at[rows_out, pl.ds((which - 1) * width, width)]
        copies.append(pltpu.make_async_copy(out_ref.at[piece], target, sems.at[at]))
        copies[-1].start()
    for copy in copies:
        copy.wait()


def return_kernel(gf_ref, chosen_ref, halo_ref, *refs):
    piece_refs, out_ref = refs[:-1], refs[-1]
    row_count = gf_ref.shape[0]
    tile = halo_ref.shape[0]
    returned = jnp.concatenate([ref[...] for ref in piece_refs], axis=0)
    total = gf_ref[...] + rows_contracted(chosen_ref[...], returned)
    out_ref[: row_count - tile] = total[: row_count - tile]
    out_ref[row_count - tile :] = total[row_count - tile :] + halo_ref[...].astype(jnp.float32)


def call(kernel, name, outs, args, scratch=(), fetched=0, flops=0, stored=False):
    spaces = [pltpu.HBM] * fetched
    spaces += [pltpu.VMEM] * (len(args) - len(spaces))
    moved = sum(x.size * x.dtype.itemsize for x in list(args) + list(outs))
    scratch = list(scratch)
    if fetched:
        scratch.append(pltpu.SemaphoreType.DMA((fetched,)))
    constrained = [
        pltpu.with_memory_space_constraint(x, pltpu.HBM) if space is pltpu.HBM else x
        for x, space in zip(args, spaces)
    ]
    return pl.pallas_call(
        kernel,
        out_shape=outs,
        in_specs=[pl.BlockSpec(memory_space=space) for space in spaces],
        out_specs=[pl.BlockSpec(memory_space=pl.ANY if stored else pltpu.VMEM)] * len(outs),
        scratch_shapes=scratch,
        compiler_params=pltpu.CompilerParams(vmem_limit_bytes=VMEM_BYTES),
        cost_estimate=pl.CostEstimate(flops=flops, bytes_accessed=moved, transcendentals=0),
        name=name,
    )(*constrained)


def shards(features, out_grad, w_query, w_keyval, w_out, virtual, local_nbr, expander, send_rows):
    row_count, width = features.shape
    dom_size, per_peer = send_rows.shape
    slots = dom_size * per_peer
    virt_rows = virtual.shape[0]
    padded = ROW_PACK * -(-virt_rows // ROW_PACK)
    ext_rows = TILE + row_count + slots + padded
    nodes = row_count * lax.axis_size("dom") * lax.axis_size("rows")
    block, rest = exchange_plan()
    square = block[:2]
    masks = partner_masks(block)
    order = farthest_first(len(masks))
    rows_per_piece = 2 * width // len(masks)
    bf16, f32 = jnp.bfloat16, jnp.float32
    shape = jax.ShapeDtypeStruct

    halo, chosen, through, *direct = call(
        pick_kernel,
        "pick_rows",
        [shape((TILE, width), bf16), shape((slots, row_count), bf16)]
        + [shape((slots // 2, width), bf16)]
        + [shape((per_peer, width), bf16)] * (dom_size // 2),
        [features, send_rows],
        [pltpu.VMEM(features.shape, bf16), pltpu.VMEM(send_rows.shape, jnp.int32)],
        fetched=2,
    )
    through = swapped(through, 1, 0)
    prepared = call(
        functools.partial(prepare_kernel, per_peer),
        "prepare",
        [
            shape(out_grad.shape, bf16),
            shape(w_query.shape, bf16),
            shape(w_keyval.shape, bf16),
            shape((width, row_count + padded), bf16),
            shape((width, row_count), bf16),
            shape((width, row_count), bf16),
            shape((row_count + padded, 2 * width), bf16),
            shape((2 * width, row_count + padded), bf16),
            shape((2 * TILE, row_count), f32),
            shape((slots + padded, row_count), f32),
        ],
        [features, out_grad, w_query, w_keyval, w_out, virtual, local_nbr.T, expander.T],
        [
            pltpu.VMEM(features.shape, bf16),
            pltpu.VMEM(w_out.shape, bf16),
            pltpu.VMEM(virtual.shape, bf16),
            pltpu.VMEM(local_nbr.shape[::-1], jnp.int32),
            pltpu.VMEM(expander.shape[::-1], jnp.int32),
        ],
        fetched=8,
        flops=10 * row_count * width * width,
    )
    (through, halo), _ = lax.optimization_barrier(((through, halo), prepared[0]))
    arrived = [direct[0], through]
    for at in reversed(range(1, dom_size // 2)):
        handed_on = through[at * per_peer : (at + 1) * per_peer]
        arrived.append(swapped(jnp.concatenate([direct[at], handed_on], axis=0), 2 * at, 0))
    halo = shifted(halo, "rows", 1)
    own_feat, halo_feat, *results = call(
        functools.partial(attend_kernel, rows_per_piece, nodes**-0.5, per_peer, dom_size),
        "attend",
        [
            shape((row_count, width), f32),
            shape((TILE, width), bf16),
            shape((slots // 2, width), bf16),
            *[shape((per_peer, width), bf16)] * (dom_size // 2),
            shape((2 * width, width), f32),
            shape((2 * width + padded, width), bf16),
            shape((padded, width), f32),
        ],
        [*arrived, halo, *prepared],
        [
            pltpu.VMEM((slots, width), bf16),
            pltpu.VMEM((ext_rows, 2 * width), bf16),
            pltpu.VMEM((2 * width, ext_rows), bf16),
            pltpu.VMEM((width, ext_rows), bf16),
            pltpu.VMEM((width, row_count), bf16),
            pltpu.VMEM((2 * width, ext_rows), bf16),
            pltpu.VMEM((width, row_count), bf16),
        ],
        flops=32 * ext_rows * width * width,
    )
    through, *direct, keep, message, rider = results

    rider = rounded(rider).astype(f32)
    keep, rider = added(keep, rider, {1: swapped(message, *CORES)})
    rider = rider[: -(-virt_rows // 8) * 8]
    dom_bits = bits_of(dom_size)
    through = swapped(through, 1, 0)
    slot_feat = []
    for at, block_rows in enumerate(direct):
        slot_feat += [block_rows, through[at * per_peer : (at + 1) * per_peer]]

    parts = [keep[at * rows_per_piece : (at + 1) * rows_per_piece] for at in range(len(masks))]
    messages = {at: swapped(with_rider(parts[at], rider), *masks[at]) for at in order}
    rider = rounded(rider).astype(f32)
    keep, rider = added(parts[0], rider, messages)

    for at, mask in enumerate(rest):
        message = with_rider(keep, rider)
        if at == 0:
            (slot_feat, halo_feat), _ = lax.optimization_barrier(
                ((slot_feat, halo_feat), message)
            )
            for bit in dom_bits[1:-1]:
                slot_feat = [hop(slot_feat, bit).get(i, own) for i, own in enumerate(slot_feat)]
            halo_back = shifted(halo_feat, "rows", -1)
        keep, rider = rounded(keep).astype(f32), rounded(rider).astype(f32)
        keep, rider = added(keep, rider, {1: swapped(message, *mask)})

    held = rounded(keep)
    held, slot_feat, halo_back = lax.optimization_barrier((held, slot_feat, halo_back))
    slot_feat = [hop(slot_feat, dom_bits[-1]).get(at, own) for at, own in enumerate(slot_feat)]
    held = jnp.concatenate([held, swapped(held, *block[2])], axis=0)
    arrived = [swapped(held, *masks[at]) for at in (1, 2, 3)]
    (grad_features,) = call(
        return_kernel,
        "return_rows",
        [shape((row_count, width), f32)],
        [own_feat, chosen, halo_back, *slot_feat],
    )
    arrived, _ = lax.optimization_barrier((arrived, grad_features))
    near = [held, *arrived]
    far = [swapped(part, *CORES) for part in near]
    grad_wq, grad_wkv, grad_wo = call(
        place_kernel,
        "place_sums",
        [shape((width, width), f32), shape((width, 2 * width), f32), shape((width, width), f32)],
        [*near, *far],
        [
            pltpu.VMEM((4 * width, width), bf16),
            pltpu.VMEM((4 * width, width), f32),
            pltpu.SemaphoreType.DMA((2 * len(masks),)),
        ],
        stored=True,
    )
    return grad_features, grad_wq, grad_wkv, grad_wo, rider[:virt_rows]


def solution(mesh):
    placed = (
        P(("dom", "rows"), None),
        P(("dom", "rows"), None),
        P(),
        P(),
        P(),
        P(),
        P(("dom", "rows"), None),
        P(("dom", "rows"), None),
        P(("dom", "rows"), None),
    )
    return jax.shard_map(
        shards,
        mesh=mesh,
        in_specs=placed,
        out_specs=(P(("dom", "rows"), None), P(), P(), P(), P()),
        check_vma=False,
    )
```

```python
import functools
import math

import jax
import jax.numpy as jnp
from jax import lax
from jax.experimental import pallas as pl
from jax.experimental.pallas import tpu as pltpu
from jax.sharding import PartitionSpec as P

HEADS = 8
TILE = 128
ROW_PACK = 16
NEGATIVE_FILL = -1e30
VMEM_BYTES = 24 * 1024 * 1024
LANES = 128


def f32_dot(left, right):
    return jnp.dot(left, right, preferred_element_type=jnp.float32)


def rows_contracted(left, right):
    return lax.dot_general(
        left, right, (((0,), (0,)), ((), ())), preferred_element_type=jnp.float32
    )


def times_transposed(left, right):
    return lax.dot_general(
        left, right, (((1,), (1,)), ((), ())), preferred_element_type=jnp.float32
    )


def rounded(value):
    return value.astype(jnp.bfloat16)


CORES = (0, 1)


def bits_of(size, first=1):
    return [1 << i for i in range(size.bit_length() - 1) if 1 << i >= first]


def exchange_plan():
    dom_size, rows_size = lax.axis_size("dom"), lax.axis_size("rows")
    line, square = [(2, 0), (4, 0)], [(1, 0), (0, 2)]
    rest = [(bit, 0) for bit in bits_of(dom_size, 8)] + [(0, bit) for bit in bits_of(rows_size, 4)]
    return line, square, rest


def partner_masks(block):
    masks = []
    for digit in range(1 << len(block)):
        chosen = [mask for i, mask in enumerate(block) if digit >> i & 1]
        masks.append((sum(mask[0] for mask in chosen), sum(mask[1] for mask in chosen)))
    return masks


def farthest_first(count):
    return sorted(range(1, count), key=lambda digit: (-digit.bit_count(), -digit))


def own_digit():
    line, square, _ = exchange_plan()
    digit = 0
    for i, (dom_mask, rows_mask) in enumerate(line + square):
        own = (lax.axis_index("dom") & dom_mask) | (lax.axis_index("rows") & rows_mask)
        digit += jnp.where(own != 0, 1 << i, 0)
    return digit


def swapped(block, dom_mask, rows_mask):
    dom_size, rows_size = lax.axis_size("dom"), lax.axis_size("rows")
    route = [
        (a * rows_size + b, (a ^ dom_mask) * rows_size + (b ^ rows_mask))
        for a in range(dom_size)
        for b in range(rows_size)
    ]
    return lax.ppermute(block, ("dom", "rows"), route)


def shifted(block, axis, distance):
    devices = range(lax.axis_size(axis))
    route = [((i - distance) % len(devices), i) for i in devices]
    return lax.ppermute(block, axis, route)


def paired_sum(terms):
    while len(terms) > 1:
        terms = [left + right for left, right in zip(terms[::2], terms[1::2])]
    return terms[0]


def with_rider(block, rider):
    return jnp.concatenate([rounded(block), rounded(rider)], axis=0)


def added(keep, rider, arrived):
    rows = keep.shape[0]
    riders = [rider] + [arrived[at][rows:].astype(jnp.float32) for at in sorted(arrived)]
    for block in arrived.values():
        keep = keep + block[:rows].astype(jnp.float32)
    return keep, paired_sum(riders)


def scattered(keep, rider, bits):
    masks = partner_masks(bits)
    rows = keep.shape[0] // len(masks)
    parts = [keep[at * rows : (at + 1) * rows] for at in range(len(masks))]
    messages = {at: with_rider(parts[at], rider) for at in farthest_first(len(masks))}
    arrived = {at: swapped(message, *masks[at]) for at, message in messages.items()}
    return added(parts[0], rounded(rider).astype(jnp.float32), arrived)


def handed_on(direct, through):
    rows = direct[0].shape[0]
    arrived = [direct[0], through]
    for at in reversed(range(1, len(direct))):
        message = jnp.concatenate([direct[at], through[at * rows : (at + 1) * rows]], axis=0)
        arrived.append(swapped(message, 2 * at, 0))
    return arrived


def listed_rows(send_ref, row_count):
    dom_size, per_peer = send_ref.shape
    slots = dom_size * per_peer
    slot = lax.broadcasted_iota(jnp.int32, (slots, per_peer), 0)
    place = lax.broadcasted_iota(jnp.int32, (slots, per_peer), 1)
    peer = (slot // per_peer) ^ lax.axis_index("dom")
    listed = jnp.zeros((slots, per_peer), jnp.int32)
    for at in range(dom_size):
        listed += jnp.where((peer == at) & (place == slot % per_peer), send_ref[at : at + 1, :], 0)
    column = jnp.sum(listed, axis=1, keepdims=True)
    rows = lax.broadcasted_iota(jnp.int32, (slots, row_count), 1)
    return jnp.where(column == rows, 1.0, 0.0).astype(jnp.bfloat16)


def fetch(pairs, sems):
    copies = [
        pltpu.make_async_copy(source, target, sems.at[at])
        for at, (source, target) in enumerate(pairs)
    ]
    for copy in copies:
        copy.start()
    return copies


def store_blocks(rows, through_ref, direct_refs):
    size = direct_refs[0].shape[0]
    for at, out_ref in enumerate(direct_refs):
        out_ref[...] = rows[2 * at * size : (2 * at + 1) * size]
        through_ref[at * size : (at + 1) * size] = rows[(2 * at + 1) * size : (2 * at + 2) * size]


def pick_kernel(feat_hbm, send_hbm, halo_ref, chosen_ref, through_ref, *refs):
    direct_refs, (feat_ref, send_ref, sems) = refs[:-3], refs[-3:]
    copies = fetch([(send_hbm, send_ref), (feat_hbm, feat_ref)], sems)
    copies[0].wait()
    chosen_ref[...] = listed_rows(send_ref, feat_ref.shape[0])
    copies[1].wait()
    halo_ref[...] = feat_ref[feat_ref.shape[0] - halo_ref.shape[0] :]
    store_blocks(rounded(f32_dot(chosen_ref[...], feat_ref[...])), through_ref, direct_refs)


def prepare_kernel(
    per_peer,
    feat_hbm,
    og_hbm,
    wq_hbm,
    wkv_hbm,
    wo_hbm,
    virt_hbm,
    nbr_hbm,
    exp_hbm,
    og_ref,
    wq_ref,
    wkv_ref,
    featt_ref,
    qt_ref,
    odt_ref,
    kv_ref,
    kvt_ref,
    local_bias_ref,
    far_bias_ref,
    feat_ref,
    wo_ref,
    virt_ref,
    nbr_ref,
    exp_ref,
    sems,
):
    nbr_copy, exp_copy, feat_copy, virt_copy, wq_copy, wkv_copy, og_copy, wo_copy = fetch(
        [
            (nbr_hbm, nbr_ref),
            (exp_hbm, exp_ref),
            (feat_hbm, feat_ref),
            (virt_hbm, virt_ref),
            (wq_hbm, wq_ref),
            (wkv_hbm, wkv_ref),
            (og_hbm, og_ref),
            (wo_hbm, wo_ref),
        ],
        sems,
    )
    row_count, width = feat_ref.shape
    window = local_bias_ref.shape[0]
    far = far_bias_ref.shape[0]
    virt_rows = virt_ref.shape[0]
    padded = kv_ref.shape[0] - row_count
    slots = far - padded
    scale = 1.0 / math.sqrt(width // HEADS)

    def multiplicity(key_rows, named):
        position = lax.broadcasted_iota(jnp.int32, (key_rows, row_count), 0)
        count = jnp.zeros((key_rows, row_count), jnp.float32)
        for at in range(named.shape[0]):
            count += jnp.where(named[at : at + 1, :] == position, 1.0, 0.0)
        return count

    nbr_copy.wait()
    local_bias_ref[...] = jnp.where(multiplicity(window, nbr_ref) > 0.0, 0.0, NEGATIVE_FILL)
    exp_copy.wait()
    expander = exp_ref[...]
    expander = ((expander // per_peer) ^ lax.axis_index("dom")) * per_peer + expander % per_peer
    named_times = multiplicity(slots, expander)
    slot_bias = jnp.full((slots, row_count), NEGATIVE_FILL, jnp.float32)
    for times in range(1, exp_ref.shape[0] + 1):
        slot_bias = jnp.where(named_times == float(times), math.log(times) / scale, slot_bias)
    far_bias_ref[:slots] = slot_bias
    virt_row = lax.broadcasted_iota(jnp.int32, (padded, row_count), 0)
    far_bias_ref[slots:] = jnp.where(virt_row < virt_rows, 0.0, NEGATIVE_FILL)

    feat_copy.wait()
    featt_ref[:, :row_count] = feat_ref[...].T
    virt_copy.wait()
    virt = jnp.concatenate(
        [virt_ref[...], jnp.zeros((padded - virt_rows, width), jnp.bfloat16)], axis=0
    )
    featt_ref[:, row_count:] = virt.T
    wq_copy.wait()
    qt_ref[...] = rounded(rows_contracted(wq_ref[...], featt_ref[:, :row_count]))
    wkv_copy.wait()
    kv_ref[:row_count] = rounded(f32_dot(feat_ref[...], wkv_ref[...]))
    kv_ref[row_count:] = rounded(f32_dot(virt, wkv_ref[...]))
    kvt_ref[...] = kv_ref[...].T
    og_copy.wait()
    wo_copy.wait()
    odt_ref[...] = rounded(times_transposed(wo_ref[...], og_ref[...]))


def attend_kernel(
    factor,
    per_peer,
    dom_size,
    *refs,
):
    count = dom_size // 2 + 1
    piece_refs, halo_ref, refs = refs[:count], refs[count], refs[count + 1 :]
    og_ref, wq_ref, wkv_ref, featt_ref, qt_ref, odt_ref, own_kv_ref, own_kvt_ref = refs[:8]
    local_bias_ref, far_bias_ref, send_ref, rider_ref = refs[8:12]
    extt_ref, gqt_ref, gkvt_ref, ot_ref, slot_ref, kv_ref, kvt_ref = refs[12:]
    width, row_count = qt_ref.shape
    tile = halo_ref.shape[0]
    tile_count = row_count // tile
    slots = dom_size * per_peer
    near = tile + row_count
    virt_at = near + slots
    head_dim = width // HEADS
    scale = 1.0 / math.sqrt(head_dim)

    kv_ref[tile:near] = own_kv_ref[:row_count]
    kv_ref[virt_at:] = own_kv_ref[row_count:]
    kvt_ref[:, tile:near] = own_kvt_ref[:, :row_count]
    kvt_ref[:, virt_at:] = own_kvt_ref[:, row_count:]
    extt_ref[:, tile:near] = featt_ref[:, :row_count]
    extt_ref[:, virt_at:] = featt_ref[:, row_count:]
    slot_ref[:per_peer] = piece_refs[0][...]
    slot_ref[per_peer : 2 * per_peer] = piece_refs[1][:per_peer]
    for at, piece_ref in enumerate(piece_refs[:1:-1], 1):
        slot_ref[2 * at * per_peer : (2 * at + 2) * per_peer] = piece_ref[...]
    for rows, source_ref in ((slice(0, tile), halo_ref), (slice(near, virt_at), slot_ref)):
        extt_ref[:, rows] = source_ref[...].T
        kv_ref[rows] = rounded(f32_dot(source_ref[...], wkv_ref[...]))
        kvt_ref[:, rows] = kv_ref[rows].T

    def tiles(of):
        return jnp.concatenate([of(t, slice(t * tile, (t + 1) * tile)) for t in range(tile_count)], 1)

    for head in range(HEADS):
        low, high = head * head_dim, (head + 1) * head_dim
        first = low // 128 * 128
        last = min(-(-high // 128) * 128, width)
        column = lax.broadcasted_iota(jnp.int32, (last - first, row_count), 0) + first
        of_head = (column >= low) & (column < high)
        q_rows = jnp.where(of_head, qt_ref[first:last, :], 0)
        d_rows = jnp.where(of_head, odt_ref[first:last, :], 0)

        def products(operand, start, stop):
            local = tiles(
                lambda t, lanes: f32_dot(
                    kv_ref[t * tile : (t + 2) * tile, start:stop], operand[:, lanes]
                )
            )
            return local, f32_dot(kv_ref[near:, start:stop], operand)

        s_local, s_far = products(q_rows, first, last)
        s_local += local_bias_ref[...]
        s_far += far_bias_ref[...]
        peak = jnp.maximum(
            jnp.max(s_local, axis=0, keepdims=True), jnp.max(s_far, axis=0, keepdims=True)
        )
        exponent_scale = scale * math.log2(math.e)
        e_local = jnp.exp2((s_local - peak) * exponent_scale)
        e_far = jnp.exp2((s_far - peak) * exponent_scale)
        total = jnp.sum(e_local, axis=0, keepdims=True) + jnp.sum(e_far, axis=0, keepdims=True)
        inverse = 1.0 / total
        p_local = e_local * inverse
        p_far = e_far * inverse
        dp_local, dp_far = products(d_rows, width + first, width + last)
        delta = jnp.sum(p_local * dp_local, axis=0, keepdims=True) + jnp.sum(
            p_far * dp_far, axis=0, keepdims=True
        )
        pb_local, pb_far = rounded(p_local), rounded(p_far)
        ds_local = rounded(p_local * (dp_local - delta))
        ds_far = rounded(p_far * (dp_far - delta))

        def to_queries(start, local, beyond):
            rows = slice(start + low, start + high)
            near_part = tiles(
                lambda t, lanes: f32_dot(kvt_ref[rows, t * tile : (t + 2) * tile], local[:, lanes])
            )
            return near_part + f32_dot(kvt_ref[rows, near:], beyond)

        ot_ref[low:high] = rounded(to_queries(width, pb_local, pb_far))
        gqt_ref[low:high] = rounded(to_queries(0, ds_local, ds_far) * scale)

        def to_keys(start, operand, local, beyond, factor):
            rows = slice(start + low, start + high)
            parts = []
            carried = None
            for t in range(tile_count):
                lanes = slice(t * tile, (t + 1) * tile)
                window = times_transposed(operand[:, lanes], local[:, lanes])
                previous = window[:, :tile]
                parts.append(previous if carried is None else previous + carried)
                carried = window[:, tile:]
            parts.append(carried)
            parts.append(times_transposed(operand, beyond))
            gathered = jnp.concatenate(parts, axis=1)
            gkvt_ref[rows] = rounded(gathered if factor is None else gathered * factor)

        to_keys(0, qt_ref[low:high], ds_local, ds_far, scale)
        to_keys(width, odt_ref[low:high], pb_local, pb_far, None)

    rider_ref[...] = f32_dot(wkv_ref[...], gkvt_ref[:, virt_at:]).T * factor
    weight_sums(
        1 - lax.axis_index("rows") % 2, send_ref, extt_ref, gqt_ref, gkvt_ref, ot_ref, og_ref, factor
    )
    send_ref[2 * width :] = rounded(rider_ref[...])


def weight_sums(core, out_ref, extt_ref, gqt_ref, gkvt_ref, ot_ref, og_ref, factor):
    width, row_count = gqt_ref.shape
    held = own_digit()
    line, square, _ = exchange_plan()
    rows = 2 * width >> len(line + square)

    def write(at, total):
        total = (total * factor).astype(out_ref.dtype)
        for start in range(0, width, rows):
            piece = (at * width + start) // rows
            offset = pl.multiple_of((piece ^ held) * rows, ROW_PACK)
            out_ref[pl.ds(offset, rows), :] = total[start : start + rows]

    @pl.when(core == 0)
    def _():
        own = slice(TILE, TILE + row_count)
        write(0, times_transposed(extt_ref[:, own], gqt_ref[...]))
        write(1, times_transposed(extt_ref[...], gkvt_ref[:width]))

    @pl.when(core == 1)
    def _():
        write(0, times_transposed(extt_ref[...], gkvt_ref[width:]))
        write(1, f32_dot(ot_ref[...], og_ref[...]))


def finish_kernel(factor, og_ref, wq_ref, wkv_ref, extt_ref, gqt_ref, gkvt_ref, ot_ref, *refs):
    gf_ref, halo_feat_ref, keep_ref, through_ref = refs[:4]
    direct_refs = refs[4:]
    width, row_count = gqt_ref.shape
    near = TILE + row_count
    slots = 2 * through_ref.shape[0]
    weight_sums(
        lax.axis_index("rows") % 2, keep_ref, extt_ref, gqt_ref, gkvt_ref, ot_ref, og_ref, factor
    )
    by_feature = f32_dot(wkv_ref[...], gkvt_ref[:, : near + slots])
    own = by_feature[:, TILE:near] + f32_dot(wq_ref[...], gqt_ref[...])
    gf_ref[...] = own.T
    halo_feat_ref[...] = rounded(by_feature[:, :TILE].T)
    store_blocks(rounded(by_feature[:, near:].T), through_ref, direct_refs)


def place_kernel(*refs):
    part_refs, (gq_hbm, gkv_hbm, go_hbm, all_ref, out_ref, sems) = refs[:-6], refs[-6:]
    width = gq_hbm.shape[0]
    line, square, _ = exchange_plan()
    half = 1 << len(line + square)
    rows = 2 * width // half
    step = part_refs[0].shape[0]
    for at, part_ref in enumerate(part_refs):
        all_ref[at * step : (at + 1) * step] = part_ref[...]
    held = own_digit() + (lax.axis_index("rows") % 2) * half
    copies = []
    for at in range(2 * half):
        start = at * rows
        piece = slice(start, start + rows)
        offset = pl.multiple_of((held ^ at) * rows, ROW_PACK)
        out_ref[piece] = all_ref[pl.ds(offset, rows), :].astype(jnp.float32)
        rows_out = pl.ds(start % width, rows)
        which = start // width
        if which == 0:
            target = gq_hbm.at[rows_out]
        elif which == 3:
            target = go_hbm.at[rows_out]
        else:
            target = gkv_hbm.at[rows_out, pl.ds((which - 1) * width, width)]
        copies.append(pltpu.make_async_copy(out_ref.at[piece], target, sems.at[at]))
        copies[-1].start()
    for copy in copies:
        copy.wait()


def return_kernel(gf_ref, chosen_ref, halo_ref, *refs):
    piece_refs, out_ref = refs[:-1], refs[-1]
    row_count = gf_ref.shape[0]
    tile = halo_ref.shape[0]
    per_peer = piece_refs[0].shape[0]
    returned = jnp.concatenate(
        [piece_refs[0][...], piece_refs[1][:per_peer]] + [ref[...] for ref in piece_refs[:1:-1]],
        axis=0,
    )
    total = gf_ref[...] + rows_contracted(chosen_ref[...], returned)
    out_ref[: row_count - tile] = total[: row_count - tile]
    out_ref[row_count - tile :] = total[row_count - tile :] + halo_ref[...].astype(jnp.float32)


def call(kernel, name, outs, args, scratch=(), fetched=0, flops=0, stored=False):
    spaces = [pltpu.HBM] * fetched
    spaces += [pltpu.VMEM] * (len(args) - len(spaces))
    moved = sum(x.size * x.dtype.itemsize for x in list(args) + list(outs))
    scratch = list(scratch)
    if fetched:
        scratch.append(pltpu.SemaphoreType.DMA((fetched,)))
    constrained = [
        pltpu.with_memory_space_constraint(x, pltpu.HBM) if space is pltpu.HBM else x
        for x, space in zip(args, spaces)
    ]
    return pl.pallas_call(
        kernel,
        out_shape=outs,
        in_specs=[pl.BlockSpec(memory_space=space) for space in spaces],
        out_specs=[pl.BlockSpec(memory_space=pl.ANY if stored else pltpu.VMEM)] * len(outs),
        scratch_shapes=scratch,
        compiler_params=pltpu.CompilerParams(vmem_limit_bytes=VMEM_BYTES),
        cost_estimate=pl.CostEstimate(flops=flops, bytes_accessed=moved, transcendentals=0),
        name=name,
    )(*constrained)


def shards(features, out_grad, w_query, w_keyval, w_out, virtual, local_nbr, expander, send_rows):
    row_count, width = features.shape
    dom_size, per_peer = send_rows.shape
    slots = dom_size * per_peer
    virt_rows = virtual.shape[0]
    padded = ROW_PACK * -(-virt_rows // ROW_PACK)
    ext_rows = TILE + row_count + slots + padded
    nodes = row_count * lax.axis_size("dom") * lax.axis_size("rows")
    line, square, rest = exchange_plan()
    bf16, f32 = jnp.bfloat16, jnp.float32
    shape = jax.ShapeDtypeStruct

    halo, chosen, through, *direct = call(
        pick_kernel,
        "pick_rows",
        [shape((TILE, width), bf16), shape((slots, row_count), bf16)]
        + [shape((slots // 2, width), bf16)]
        + [shape((per_peer, width), bf16)] * (dom_size // 2),
        [features, send_rows],
        [pltpu.VMEM(features.shape, bf16), pltpu.VMEM(send_rows.shape, jnp.int32)],
        fetched=2,
    )
    through = swapped(through, 1, 0)
    prepared = call(
        functools.partial(prepare_kernel, per_peer),
        "prepare",
        [
            shape(out_grad.shape, bf16),
            shape(w_query.shape, bf16),
            shape(w_keyval.shape, bf16),
            shape((width, row_count + padded), bf16),
            shape((width, row_count), bf16),
            shape((width, row_count), bf16),
            shape((row_count + padded, 2 * width), bf16),
            shape((2 * width, row_count + padded), bf16),
            shape((2 * TILE, row_count), f32),
            shape((slots + padded, row_count), f32),
        ],
        [features, out_grad, w_query, w_keyval, w_out, virtual, local_nbr.T, expander.T],
        [
            pltpu.VMEM(features.shape, bf16),
            pltpu.VMEM(w_out.shape, bf16),
            pltpu.VMEM(virtual.shape, bf16),
            pltpu.VMEM(local_nbr.shape[::-1], jnp.int32),
            pltpu.VMEM(expander.shape[::-1], jnp.int32),
        ],
        fetched=8,
        flops=10 * row_count * width * width,
    )
    (through, halo), _ = lax.optimization_barrier(((through, halo), prepared[0]))
    arrived = handed_on(direct, through)
    halo = shifted(halo, "rows", 1)
    message, rider, *gradients = call(
        functools.partial(attend_kernel, nodes**-0.5, per_peer, dom_size),
        "attend",
        [
            shape((2 * width + padded, width), bf16),
            shape((padded, width), f32),
            shape((width, ext_rows), bf16),
            shape((width, row_count), bf16),
            shape((2 * width, ext_rows), bf16),
            shape((width, row_count), bf16),
        ],
        [*arrived, halo, *prepared],
        [
            pltpu.VMEM((slots, width), bf16),
            pltpu.VMEM((ext_rows, 2 * width), bf16),
            pltpu.VMEM((2 * width, ext_rows), bf16),
        ],
        flops=28 * ext_rows * width * width,
    )
    message = swapped(message, *CORES)
    own_feat, halo_feat, keep, through, *direct = call(
        functools.partial(finish_kernel, nodes**-0.5),
        "finish",
        [
            shape((row_count, width), f32),
            shape((TILE, width), bf16),
            shape((2 * width, width), f32),
            shape((slots // 2, width), bf16),
        ]
        + [shape((per_peer, width), bf16)] * (dom_size // 2),
        [*prepared[:3], *gradients],
        flops=6 * ext_rows * width * width,
    )

    keep, rider = added(keep, rounded(rider).astype(f32), {1: message})
    rider = rider[: -(-virt_rows // 8) * 8]
    through, halo_feat, _ = lax.optimization_barrier((through, halo_feat, keep))
    through = swapped(through, 1, 0)
    halo_back = shifted(halo_feat, "rows", -1)
    keep, rider = scattered(keep, rider, square)
    keep, through, halo_back = lax.optimization_barrier((keep, through, halo_back))
    keep, rider = scattered(keep, rider, line)
    for mask in rest:
        message = swapped(with_rider(keep, rider), *mask)
        keep, rider = rounded(keep).astype(f32), rounded(rider).astype(f32)
        keep, rider = added(keep, rider, {1: message})

    held = rounded(keep)
    back = {at: swapped(held, *partner_masks(line)[at]) for at in (3, 2, 1)}
    held = jnp.concatenate([held] + [back[at] for at in sorted(back)], axis=0)
    through, _ = lax.optimization_barrier((through, held))
    returned = handed_on(direct, through)
    arrived = [swapped(held, *masks) for masks in partner_masks(square)[1:]]
    (grad_features,) = call(
        return_kernel,
        "return_rows",
        [shape((row_count, width), f32)],
        [own_feat, chosen, halo_back, *returned],
    )
    near = [held, *arrived]
    far = [swapped(part, *CORES) for part in near]
    grad_wq, grad_wkv, grad_wo = call(
        place_kernel,
        "place_sums",
        [shape((width, width), f32), shape((width, 2 * width), f32), shape((width, width), f32)],
        [*near, *far],
        [
            pltpu.VMEM((4 * width, width), bf16),
            pltpu.VMEM((4 * width, width), f32),
            pltpu.SemaphoreType.DMA((2 << len(line + square),)),
        ],
        stored=True,
    )
    return grad_features, grad_wq, grad_wkv, grad_wo, rider[:virt_rows]


def solution(mesh):
    placed = (
        P(("dom", "rows"), None),
        P(("dom", "rows"), None),
        P(),
        P(),
        P(),
        P(),
        P(("dom", "rows"), None),
        P(("dom", "rows"), None),
        P(("dom", "rows"), None),
    )
    return jax.shard_map(
        shards,
        mesh=mesh,
        in_specs=placed,
        out_specs=(P(("dom", "rows"), None), P(), P(), P(), P()),
        check_vma=False,
    )
```

```python
import functools
import math

import jax
import jax.numpy as jnp
from jax import lax
from jax.experimental import pallas as pl
from jax.experimental.pallas import tpu as pltpu
from jax.sharding import PartitionSpec as P

HEADS = 8
TILE = 128
ROW_PACK = 16
NEGATIVE_FILL = -1e30
VMEM_BYTES = 24 * 1024 * 1024
LANES = 128


def f32_dot(left, right):
    return jnp.dot(left, right, preferred_element_type=jnp.float32)


def rows_contracted(left, right):
    return lax.dot_general(
        left, right, (((0,), (0,)), ((), ())), preferred_element_type=jnp.float32
    )


def times_transposed(left, right):
    return lax.dot_general(
        left, right, (((1,), (1,)), ((), ())), preferred_element_type=jnp.float32
    )


def rounded(value):
    return value.astype(jnp.bfloat16)


CORES = (0, 1)


def bits_of(size, first=1):
    return [1 << i for i in range(size.bit_length() - 1) if 1 << i >= first]


def exchange_plan():
    dom_size, rows_size = lax.axis_size("dom"), lax.axis_size("rows")
    pair, square = [(2, 0)], [(1, 0), (0, 2)]
    rest = [(bit, 0) for bit in bits_of(dom_size, 4)] + [(0, bit) for bit in bits_of(rows_size, 4)]
    return pair, square, rest


def partner_masks(block):
    masks = []
    for digit in range(1 << len(block)):
        chosen = [mask for i, mask in enumerate(block) if digit >> i & 1]
        masks.append((sum(mask[0] for mask in chosen), sum(mask[1] for mask in chosen)))
    return masks


def farthest_first(count):
    return sorted(range(1, count), key=lambda digit: (-digit.bit_count(), -digit))


def own_digit():
    pair, square, _ = exchange_plan()
    digit = 0
    for i, (dom_mask, rows_mask) in enumerate(pair + square):
        own = (lax.axis_index("dom") & dom_mask) | (lax.axis_index("rows") & rows_mask)
        digit += jnp.where(own != 0, 1 << i, 0)
    return digit


def swapped(block, dom_mask, rows_mask):
    dom_size, rows_size = lax.axis_size("dom"), lax.axis_size("rows")
    route = [
        (a * rows_size + b, (a ^ dom_mask) * rows_size + (b ^ rows_mask))
        for a in range(dom_size)
        for b in range(rows_size)
    ]
    return lax.ppermute(block, ("dom", "rows"), route)


def shifted(block, axis, distance):
    devices = range(lax.axis_size(axis))
    route = [((i - distance) % len(devices), i) for i in devices]
    return lax.ppermute(block, axis, route)


def paired_sum(terms):
    while len(terms) > 1:
        terms = [left + right for left, right in zip(terms[::2], terms[1::2])]
    return terms[0]


def with_rider(block, rider):
    return jnp.concatenate([rounded(block), rounded(rider)], axis=0)


def added(keep, rider, arrived):
    rows = keep.shape[0]
    riders = [rider] + [arrived[at][rows:].astype(jnp.float32) for at in sorted(arrived)]
    for block in arrived.values():
        keep = keep + block[:rows].astype(jnp.float32)
    return keep, paired_sum(riders)


def scattered(keep, rider, bits):
    masks = partner_masks(bits)
    rows = keep.shape[0] // len(masks)
    parts = [keep[at * rows : (at + 1) * rows] for at in range(len(masks))]
    messages = {at: with_rider(parts[at], rider) for at in farthest_first(len(masks))}
    arrived = {at: swapped(message, *masks[at]) for at, message in messages.items()}
    return added(parts[0], rounded(rider).astype(jnp.float32), arrived)


def handed_on(direct, through):
    rows = direct[0].shape[0]
    arrived = [direct[0], through]
    for at in reversed(range(1, len(direct))):
        message = jnp.concatenate([direct[at], through[at * rows : (at + 1) * rows]], axis=0)
        arrived.append(swapped(message, 2 * at, 0))
    return arrived


def listed_rows(send_ref, row_count):
    dom_size, per_peer = send_ref.shape
    slots = dom_size * per_peer
    slot = lax.broadcasted_iota(jnp.int32, (slots, per_peer), 0)
    place = lax.broadcasted_iota(jnp.int32, (slots, per_peer), 1)
    peer = (slot // per_peer) ^ lax.axis_index("dom")
    listed = jnp.zeros((slots, per_peer), jnp.int32)
    for at in range(dom_size):
        listed += jnp.where((peer == at) & (place == slot % per_peer), send_ref[at : at + 1, :], 0)
    column = jnp.sum(listed, axis=1, keepdims=True)
    rows = lax.broadcasted_iota(jnp.int32, (slots, row_count), 1)
    return jnp.where(column == rows, 1.0, 0.0).astype(jnp.bfloat16)


def fetch(pairs, sems):
    copies = [
        pltpu.make_async_copy(source, target, sems.at[at])
        for at, (source, target) in enumerate(pairs)
    ]
    for copy in copies:
        copy.start()
    return copies


def store_blocks(rows, through_ref, direct_refs):
    size = direct_refs[0].shape[0]
    for at, out_ref in enumerate(direct_refs):
        out_ref[...] = rows[2 * at * size : (2 * at + 1) * size]
        through_ref[at * size : (at + 1) * size] = rows[(2 * at + 1) * size : (2 * at + 2) * size]


def pick_kernel(feat_hbm, send_hbm, halo_ref, chosen_ref, through_ref, *refs):
    direct_refs, (feat_ref, send_ref, sems) = refs[:-3], refs[-3:]
    copies = fetch([(send_hbm, send_ref), (feat_hbm, feat_ref)], sems)
    copies[0].wait()
    chosen_ref[...] = listed_rows(send_ref, feat_ref.shape[0])
    copies[1].wait()
    halo_ref[...] = feat_ref[feat_ref.shape[0] - halo_ref.shape[0] :]
    store_blocks(rounded(f32_dot(chosen_ref[...], feat_ref[...])), through_ref, direct_refs)


def prepare_kernel(
    per_peer,
    feat_hbm,
    og_hbm,
    wq_hbm,
    wkv_hbm,
    wo_hbm,
    virt_hbm,
    nbr_hbm,
    exp_hbm,
    og_ref,
    wq_ref,
    wkv_ref,
    featt_ref,
    qt_ref,
    odt_ref,
    kv_ref,
    kvt_ref,
    local_bias_ref,
    far_bias_ref,
    feat_ref,
    wo_ref,
    virt_ref,
    nbr_ref,
    exp_ref,
    sems,
):
    nbr_copy, exp_copy, feat_copy, virt_copy, wq_copy, wkv_copy, og_copy, wo_copy = fetch(
        [
            (nbr_hbm, nbr_ref),
            (exp_hbm, exp_ref),
            (feat_hbm, feat_ref),
            (virt_hbm, virt_ref),
            (wq_hbm, wq_ref),
            (wkv_hbm, wkv_ref),
            (og_hbm, og_ref),
            (wo_hbm, wo_ref),
        ],
        sems,
    )
    row_count, width = feat_ref.shape
    window = local_bias_ref.shape[0]
    far = far_bias_ref.shape[0]
    virt_rows = virt_ref.shape[0]
    padded = kv_ref.shape[0] - row_count
    slots = far - padded
    scale = 1.0 / math.sqrt(width // HEADS)

    def multiplicity(key_rows, named):
        position = lax.broadcasted_iota(jnp.int32, (key_rows, row_count), 0)
        count = jnp.zeros((key_rows, row_count), jnp.float32)
        for at in range(named.shape[0]):
            count += jnp.where(named[at : at + 1, :] == position, 1.0, 0.0)
        return count

    nbr_copy.wait()
    local_bias_ref[...] = jnp.where(multiplicity(window, nbr_ref) > 0.0, 0.0, NEGATIVE_FILL)
    exp_copy.wait()
    expander = exp_ref[...]
    expander = ((expander // per_peer) ^ lax.axis_index("dom")) * per_peer + expander % per_peer
    named_times = multiplicity(slots, expander)
    slot_bias = jnp.full((slots, row_count), NEGATIVE_FILL, jnp.float32)
    for times in range(1, exp_ref.shape[0] + 1):
        slot_bias = jnp.where(named_times == float(times), math.log(times) / scale, slot_bias)
    far_bias_ref[:slots] = slot_bias
    virt_row = lax.broadcasted_iota(jnp.int32, (padded, row_count), 0)
    far_bias_ref[slots:] = jnp.where(virt_row < virt_rows, 0.0, NEGATIVE_FILL)

    feat_copy.wait()
    featt_ref[:, :row_count] = feat_ref[...].T
    virt_copy.wait()
    virt = jnp.concatenate(
        [virt_ref[...], jnp.zeros((padded - virt_rows, width), jnp.bfloat16)], axis=0
    )
    featt_ref[:, row_count:] = virt.T
    wq_copy.wait()
    qt_ref[...] = rounded(rows_contracted(wq_ref[...], featt_ref[:, :row_count]))
    wkv_copy.wait()
    kv_ref[:row_count] = rounded(f32_dot(feat_ref[...], wkv_ref[...]))
    kv_ref[row_count:] = rounded(f32_dot(virt, wkv_ref[...]))
    kvt_ref[...] = kv_ref[...].T
    og_copy.wait()
    wo_copy.wait()
    odt_ref[...] = rounded(times_transposed(wo_ref[...], og_ref[...]))


def attend_kernel(
    factor,
    per_peer,
    dom_size,
    *refs,
):
    count = dom_size // 2 + 1
    piece_refs, halo_ref, refs = refs[:count], refs[count], refs[count + 1 :]
    og_ref, wq_ref, wkv_ref, featt_ref, qt_ref, odt_ref, own_kv_ref, own_kvt_ref = refs[:8]
    local_bias_ref, far_bias_ref, send_ref, rider_ref = refs[8:12]
    extt_ref, gqt_ref, gkvt_ref, ot_ref, slot_ref, kv_ref, kvt_ref = refs[12:]
    width, row_count = qt_ref.shape
    tile = halo_ref.shape[0]
    tile_count = row_count // tile
    slots = dom_size * per_peer
    near = tile + row_count
    virt_at = near + slots
    head_dim = width // HEADS
    scale = 1.0 / math.sqrt(head_dim)

    kv_ref[tile:near] = own_kv_ref[:row_count]
    kv_ref[virt_at:] = own_kv_ref[row_count:]
    kvt_ref[:, tile:near] = own_kvt_ref[:, :row_count]
    kvt_ref[:, virt_at:] = own_kvt_ref[:, row_count:]
    extt_ref[:, tile:near] = featt_ref[:, :row_count]
    extt_ref[:, virt_at:] = featt_ref[:, row_count:]
    slot_ref[:per_peer] = piece_refs[0][...]
    slot_ref[per_peer : 2 * per_peer] = piece_refs[1][:per_peer]
    for at, piece_ref in enumerate(piece_refs[:1:-1], 1):
        slot_ref[2 * at * per_peer : (2 * at + 2) * per_peer] = piece_ref[...]
    for rows, source_ref in ((slice(0, tile), halo_ref), (slice(near, virt_at), slot_ref)):
        extt_ref[:, rows] = source_ref[...].T
        kv_ref[rows] = rounded(f32_dot(source_ref[...], wkv_ref[...]))
        kvt_ref[:, rows] = kv_ref[rows].T

    def tiles(of):
        return jnp.concatenate([of(t, slice(t * tile, (t + 1) * tile)) for t in range(tile_count)], 1)

    for head in range(HEADS):
        low, high = head * head_dim, (head + 1) * head_dim
        first = low // 128 * 128
        last = min(-(-high // 128) * 128, width)
        column = lax.broadcasted_iota(jnp.int32, (last - first, row_count), 0) + first
        of_head = (column >= low) & (column < high)
        q_rows = jnp.where(of_head, qt_ref[first:last, :], 0)
        d_rows = jnp.where(of_head, odt_ref[first:last, :], 0)

        def products(operand, start, stop):
            local = tiles(
                lambda t, lanes: f32_dot(
                    kv_ref[t * tile : (t + 2) * tile, start:stop], operand[:, lanes]
                )
            )
            return local, f32_dot(kv_ref[near:, start:stop], operand)

        s_local, s_far = products(q_rows, first, last)
        s_local += local_bias_ref[...]
        s_far += far_bias_ref[...]
        peak = jnp.maximum(
            jnp.max(s_local, axis=0, keepdims=True), jnp.max(s_far, axis=0, keepdims=True)
        )
        exponent_scale = scale * math.log2(math.e)
        e_local = jnp.exp2((s_local - peak) * exponent_scale)
        e_far = jnp.exp2((s_far - peak) * exponent_scale)
        total = jnp.sum(e_local, axis=0, keepdims=True) + jnp.sum(e_far, axis=0, keepdims=True)
        inverse = 1.0 / total
        p_local = e_local * inverse
        p_far = e_far * inverse
        dp_local, dp_far = products(d_rows, width + first, width + last)
        delta = jnp.sum(p_local * dp_local, axis=0, keepdims=True) + jnp.sum(
            p_far * dp_far, axis=0, keepdims=True
        )
        pb_local, pb_far = rounded(p_local), rounded(p_far)
        ds_local = rounded(p_local * (dp_local - delta))
        ds_far = rounded(p_far * (dp_far - delta))

        def to_queries(start, local, beyond):
            rows = slice(start + low, start + high)
            near_part = tiles(
                lambda t, lanes: f32_dot(kvt_ref[rows, t * tile : (t + 2) * tile], local[:, lanes])
            )
            return near_part + f32_dot(kvt_ref[rows, near:], beyond)

        ot_ref[low:high] = rounded(to_queries(width, pb_local, pb_far))
        gqt_ref[low:high] = rounded(to_queries(0, ds_local, ds_far) * scale)

        def to_keys(start, operand, local, beyond, factor):
            rows = slice(start + low, start + high)
            parts = []
            carried = None
            for t in range(tile_count):
                lanes = slice(t * tile, (t + 1) * tile)
                window = times_transposed(operand[:, lanes], local[:, lanes])
                previous = window[:, :tile]
                parts.append(previous if carried is None else previous + carried)
                carried = window[:, tile:]
            parts.append(carried)
            parts.append(times_transposed(operand, beyond))
            gathered = jnp.concatenate(parts, axis=1)
            gkvt_ref[rows] = rounded(gathered if factor is None else gathered * factor)

        to_keys(0, qt_ref[low:high], ds_local, ds_far, scale)
        to_keys(width, odt_ref[low:high], pb_local, pb_far, None)

    rider_ref[...] = f32_dot(wkv_ref[...], gkvt_ref[:, virt_at:]).T * factor
    weight_sums(
        1 - lax.axis_index("rows") % 2, send_ref, extt_ref, gqt_ref, gkvt_ref, ot_ref, og_ref, factor
    )
    send_ref[2 * width :] = rounded(rider_ref[...])


def weight_sums(core, out_ref, extt_ref, gqt_ref, gkvt_ref, ot_ref, og_ref, factor):
    width, row_count = gqt_ref.shape
    held = own_digit()
    pair, square, _ = exchange_plan()
    rows = 2 * width >> len(pair + square)

    def write(at, total):
        total = (total * factor).astype(out_ref.dtype)
        for start in range(0, width, rows):
            piece = (at * width + start) // rows
            offset = pl.multiple_of((piece ^ held) * rows, ROW_PACK)
            out_ref[pl.ds(offset, rows), :] = total[start : start + rows]

    @pl.when(core == 0)
    def _():
        own = slice(TILE, TILE + row_count)
        write(0, times_transposed(extt_ref[:, own], gqt_ref[...]))
        write(1, times_transposed(extt_ref[...], gkvt_ref[:width]))

    @pl.when(core == 1)
    def _():
        write(0, times_transposed(extt_ref[...], gkvt_ref[width:]))
        write(1, f32_dot(ot_ref[...], og_ref[...]))


def finish_kernel(factor, og_ref, wq_ref, wkv_ref, extt_ref, gqt_ref, gkvt_ref, ot_ref, *refs):
    gf_ref, halo_feat_ref, keep_ref = refs[:3]
    pair_refs = refs[3:]
    width, row_count = gqt_ref.shape
    near = TILE + row_count
    step = pair_refs[0].shape[0]
    slots = step * len(pair_refs)
    weight_sums(
        lax.axis_index("rows") % 2, keep_ref, extt_ref, gqt_ref, gkvt_ref, ot_ref, og_ref, factor
    )
    by_feature = f32_dot(wkv_ref[...], gkvt_ref[:, : near + slots])
    own = by_feature[:, TILE:near] + f32_dot(wq_ref[...], gqt_ref[...])
    gf_ref[...] = own.T
    halo_feat_ref[...] = rounded(by_feature[:, :TILE].T)
    slot_feat = rounded(by_feature[:, near:].T)
    for at, out_ref in enumerate(pair_refs):
        out_ref[...] = slot_feat[at * step : (at + 1) * step]


def place_kernel(*refs):
    part_refs, (gq_hbm, gkv_hbm, go_hbm, all_ref, out_ref, sems) = refs[:-6], refs[-6:]
    width = gq_hbm.shape[0]
    pair, square, _ = exchange_plan()
    half = 1 << len(pair + square)
    rows = 2 * width // half
    step = part_refs[0].shape[0]
    for at, part_ref in enumerate(part_refs):
        all_ref[at * step : (at + 1) * step] = part_ref[...]
    held = own_digit() + (lax.axis_index("rows") % 2) * half
    copies = []
    for at in range(2 * half):
        start = at * rows
        piece = slice(start, start + rows)
        offset = pl.multiple_of((held ^ at) * rows, ROW_PACK)
        out_ref[piece] = all_ref[pl.ds(offset, rows), :].astype(jnp.float32)
        rows_out = pl.ds(start % width, rows)
        which = start // width
        if which == 0:
            target = gq_hbm.at[rows_out]
        elif which == 3:
            target = go_hbm.at[rows_out]
        else:
            target = gkv_hbm.at[rows_out, pl.ds((which - 1) * width, width)]
        copies.append(pltpu.make_async_copy(out_ref.at[piece], target, sems.at[at]))
        copies[-1].start()
    for copy in copies:
        copy.wait()


def return_kernel(gf_ref, chosen_ref, halo_ref, own_ref, through_ref, *refs):
    far_refs, out_ref = refs[:-1], refs[-1]
    row_count = gf_ref.shape[0]
    tile = halo_ref.shape[0]
    per_peer = own_ref.shape[0] // 2
    returned = []
    for at, even_ref in enumerate([own_ref, *far_refs[::-1]]):
        returned += [even_ref[:per_peer], through_ref[at * per_peer : (at + 1) * per_peer]]
    total = gf_ref[...] + rows_contracted(chosen_ref[...], jnp.concatenate(returned, axis=0))
    out_ref[: row_count - tile] = total[: row_count - tile]
    out_ref[row_count - tile :] = total[row_count - tile :] + halo_ref[...].astype(jnp.float32)


def call(kernel, name, outs, args, scratch=(), fetched=0, flops=0, stored=False):
    spaces = [pltpu.HBM] * fetched
    spaces += [pltpu.VMEM] * (len(args) - len(spaces))
    moved = sum(x.size * x.dtype.itemsize for x in list(args) + list(outs))
    scratch = list(scratch)
    if fetched:
        scratch.append(pltpu.SemaphoreType.DMA((fetched,)))
    constrained = [
        pltpu.with_memory_space_constraint(x, pltpu.HBM) if space is pltpu.HBM else x
        for x, space in zip(args, spaces)
    ]
    return pl.pallas_call(
        kernel,
        out_shape=outs,
        in_specs=[pl.BlockSpec(memory_space=space) for space in spaces],
        out_specs=[pl.BlockSpec(memory_space=pl.ANY if stored else pltpu.VMEM)] * len(outs),
        scratch_shapes=scratch,
        compiler_params=pltpu.CompilerParams(vmem_limit_bytes=VMEM_BYTES),
        cost_estimate=pl.CostEstimate(flops=flops, bytes_accessed=moved, transcendentals=0),
        name=name,
    )(*constrained)


def shards(features, out_grad, w_query, w_keyval, w_out, virtual, local_nbr, expander, send_rows):
    row_count, width = features.shape
    dom_size, per_peer = send_rows.shape
    slots = dom_size * per_peer
    virt_rows = virtual.shape[0]
    padded = ROW_PACK * -(-virt_rows // ROW_PACK)
    ext_rows = TILE + row_count + slots + padded
    nodes = row_count * lax.axis_size("dom") * lax.axis_size("rows")
    pair, square, rest = exchange_plan()
    bf16, f32 = jnp.bfloat16, jnp.float32
    shape = jax.ShapeDtypeStruct

    halo, chosen, through, *direct = call(
        pick_kernel,
        "pick_rows",
        [shape((TILE, width), bf16), shape((slots, row_count), bf16)]
        + [shape((slots // 2, width), bf16)]
        + [shape((per_peer, width), bf16)] * (dom_size // 2),
        [features, send_rows],
        [pltpu.VMEM(features.shape, bf16), pltpu.VMEM(send_rows.shape, jnp.int32)],
        fetched=2,
    )
    through = swapped(through, 1, 0)
    prepared = call(
        functools.partial(prepare_kernel, per_peer),
        "prepare",
        [
            shape(out_grad.shape, bf16),
            shape(w_query.shape, bf16),
            shape(w_keyval.shape, bf16),
            shape((width, row_count + padded), bf16),
            shape((width, row_count), bf16),
            shape((width, row_count), bf16),
            shape((row_count + padded, 2 * width), bf16),
            shape((2 * width, row_count + padded), bf16),
            shape((2 * TILE, row_count), f32),
            shape((slots + padded, row_count), f32),
        ],
        [features, out_grad, w_query, w_keyval, w_out, virtual, local_nbr.T, expander.T],
        [
            pltpu.VMEM(features.shape, bf16),
            pltpu.VMEM(w_out.shape, bf16),
            pltpu.VMEM(virtual.shape, bf16),
            pltpu.VMEM(local_nbr.shape[::-1], jnp.int32),
            pltpu.VMEM(expander.shape[::-1], jnp.int32),
        ],
        fetched=8,
        flops=10 * row_count * width * width,
    )
    (through, halo), _ = lax.optimization_barrier(((through, halo), prepared[0]))
    arrived = handed_on(direct, through)
    halo = shifted(halo, "rows", 1)
    message, rider, *gradients = call(
        functools.partial(attend_kernel, nodes**-0.5, per_peer, dom_size),
        "attend",
        [
            shape((2 * width + padded, width), bf16),
            shape((padded, width), f32),
            shape((width, ext_rows), bf16),
            shape((width, row_count), bf16),
            shape((2 * width, ext_rows), bf16),
            shape((width, row_count), bf16),
        ],
        [*arrived, halo, *prepared],
        [
            pltpu.VMEM((slots, width), bf16),
            pltpu.VMEM((ext_rows, 2 * width), bf16),
            pltpu.VMEM((2 * width, ext_rows), bf16),
        ],
        flops=28 * ext_rows * width * width,
    )
    message = swapped(message, *CORES)
    own_feat, halo_feat, keep, *pairs = call(
        functools.partial(finish_kernel, nodes**-0.5),
        "finish",
        [shape((row_count, width), f32), shape((TILE, width), bf16), shape((2 * width, width), f32)]
        + [shape((2 * per_peer, width), bf16)] * (dom_size // 2),
        [*prepared[:3], *gradients],
        flops=6 * ext_rows * width * width,
    )

    keep, rider = added(keep, rounded(rider).astype(f32), {1: message})
    rider = rider[: -(-virt_rows // 8) * 8]
    pairs, _ = lax.optimization_barrier((pairs, keep))
    returned = [swapped(pairs[at], 2 * at, 0) for at in reversed(range(1, dom_size // 2))]
    keep, rider = scattered(keep, rider, square)
    (returned, halo_feat), _ = lax.optimization_barrier(((returned, halo_feat), keep))
    through = swapped(jnp.concatenate([x[per_peer:] for x in [pairs[0]] + returned[::-1]]), 1, 0)
    halo_back = shifted(halo_feat, "rows", -1)
    keep, rider = scattered(keep, rider, pair)
    for mask in rest:
        message = swapped(with_rider(keep, rider), *mask)
        keep, rider = rounded(keep).astype(f32), rounded(rider).astype(f32)
        keep, rider = added(keep, rider, {1: message})
    (grad_features,) = call(
        return_kernel,
        "return_rows",
        [shape((row_count, width), f32)],
        [own_feat, chosen, halo_back, pairs[0], through, *returned],
    )

    held, grad_features = lax.optimization_barrier((rounded(keep), grad_features))
    held = jnp.concatenate([held, swapped(held, *pair[0])], axis=0)
    arrived = [swapped(held, *masks) for masks in partner_masks(square)[1:]]
    near = [held, *arrived]
    far = [swapped(part, *CORES) for part in near]
    grad_wq, grad_wkv, grad_wo = call(
        place_kernel,
        "place_sums",
        [shape((width, width), f32), shape((width, 2 * width), f32), shape((width, width), f32)],
        [*near, *far],
        [
            pltpu.VMEM((4 * width, width), bf16),
            pltpu.VMEM((4 * width, width), f32),
            pltpu.SemaphoreType.DMA((2 << len(pair + square),)),
        ],
        stored=True,
    )
    return grad_features, grad_wq, grad_wkv, grad_wo, rider[:virt_rows]


def solution(mesh):
    placed = (
        P(("dom", "rows"), None),
        P(("dom", "rows"), None),
        P(),
        P(),
        P(),
        P(),
        P(("dom", "rows"), None),
        P(("dom", "rows"), None),
        P(("dom", "rows"), None),
    )
    return jax.shard_map(
        shards,
        mesh=mesh,
        in_specs=placed,
        out_specs=(P(("dom", "rows"), None), P(), P(), P(), P()),
        check_vma=False,
    )
```

```python
import functools
import math

import jax
import jax.numpy as jnp
from jax import lax
from jax.experimental import pallas as pl
from jax.experimental.pallas import tpu as pltpu
from jax.sharding import PartitionSpec as P

HEADS = 8
TILE = 128
ROW_PACK = 16
NEGATIVE_FILL = -1e30
VMEM_BYTES = 24 * 1024 * 1024
LANES = 128


def f32_dot(left, right):
    return jnp.dot(left, right, preferred_element_type=jnp.float32)


def rows_contracted(left, right):
    return lax.dot_general(
        left, right, (((0,), (0,)), ((), ())), preferred_element_type=jnp.float32
    )


def times_transposed(left, right):
    return lax.dot_general(
        left, right, (((1,), (1,)), ((), ())), preferred_element_type=jnp.float32
    )


def rounded(value):
    return value.astype(jnp.bfloat16)


CORES = (0, 1)


def bits_of(size, first=1):
    return [1 << i for i in range(size.bit_length() - 1) if 1 << i >= first]


def exchange_plan():
    dom_size, rows_size = lax.axis_size("dom"), lax.axis_size("rows")
    pair, square = [(2, 0)], [(1, 0), (0, 2)]
    rest = [(bit, 0) for bit in bits_of(dom_size, 4)] + [(0, bit) for bit in bits_of(rows_size, 4)]
    return pair, square, rest


def partner_masks(block):
    masks = []
    for digit in range(1 << len(block)):
        chosen = [mask for i, mask in enumerate(block) if digit >> i & 1]
        masks.append((sum(mask[0] for mask in chosen), sum(mask[1] for mask in chosen)))
    return masks


def farthest_first(count):
    return sorted(range(1, count), key=lambda digit: (-digit.bit_count(), -digit))


def own_digit():
    pair, square, _ = exchange_plan()
    digit = 0
    for i, (dom_mask, rows_mask) in enumerate(pair + square):
        own = (lax.axis_index("dom") & dom_mask) | (lax.axis_index("rows") & rows_mask)
        digit += jnp.where(own != 0, 1 << i, 0)
    return digit


def swapped(block, dom_mask, rows_mask):
    dom_size, rows_size = lax.axis_size("dom"), lax.axis_size("rows")
    route = [
        (a * rows_size + b, (a ^ dom_mask) * rows_size + (b ^ rows_mask))
        for a in range(dom_size)
        for b in range(rows_size)
    ]
    return lax.ppermute(block, ("dom", "rows"), route)


def shifted(block, axis, distance):
    devices = range(lax.axis_size(axis))
    route = [((i - distance) % len(devices), i) for i in devices]
    return lax.ppermute(block, axis, route)


def paired_sum(terms):
    while len(terms) > 1:
        terms = [left + right for left, right in zip(terms[::2], terms[1::2])]
    return terms[0]


def with_rider(block, rider):
    return jnp.concatenate([rounded(block), rounded(rider)], axis=0)


def added(keep, rider, arrived):
    rows = keep.shape[0]
    riders = [rider] + [arrived[at][rows:].astype(jnp.float32) for at in sorted(arrived)]
    for block in arrived.values():
        keep = keep + block[:rows].astype(jnp.float32)
    return keep, paired_sum(riders)


def scattered(keep, rider, bits):
    masks = partner_masks(bits)
    rows = keep.shape[0] // len(masks)
    parts = [keep[at * rows : (at + 1) * rows] for at in range(len(masks))]
    messages = {at: with_rider(parts[at], rider) for at in farthest_first(len(masks))}
    arrived = {at: swapped(message, *masks[at]) for at, message in messages.items()}
    return added(parts[0], rounded(rider).astype(jnp.float32), arrived)


def handed_on(direct, through):
    rows = direct[0].shape[0]
    arrived = [direct[0], through]
    for at in reversed(range(1, len(direct))):
        message = jnp.concatenate([direct[at], through[at * rows : (at + 1) * rows]], axis=0)
        arrived.append(swapped(message, 2 * at, 0))
    return arrived


def listed_rows(send_ref, row_count):
    dom_size, per_peer = send_ref.shape
    slots = dom_size * per_peer
    slot = lax.broadcasted_iota(jnp.int32, (slots, per_peer), 0)
    place = lax.broadcasted_iota(jnp.int32, (slots, per_peer), 1)
    peer = (slot // per_peer) ^ lax.axis_index("dom")
    listed = jnp.zeros((slots, per_peer), jnp.int32)
    for at in range(dom_size):
        listed += jnp.where((peer == at) & (place == slot % per_peer), send_ref[at : at + 1, :], 0)
    column = jnp.sum(listed, axis=1, keepdims=True)
    rows = lax.broadcasted_iota(jnp.int32, (slots, row_count), 1)
    return jnp.where(column == rows, 1.0, 0.0).astype(jnp.bfloat16)


def fetch(pairs, sems):
    copies = [
        pltpu.make_async_copy(source, target, sems.at[at])
        for at, (source, target) in enumerate(pairs)
    ]
    for copy in copies:
        copy.start()
    return copies


def store_blocks(rows, through_ref, direct_refs):
    size = direct_refs[0].shape[0]
    for at, out_ref in enumerate(direct_refs):
        out_ref[...] = rows[2 * at * size : (2 * at + 1) * size]
        through_ref[at * size : (at + 1) * size] = rows[(2 * at + 1) * size : (2 * at + 2) * size]


def pick_kernel(feat_hbm, send_hbm, halo_ref, chosen_ref, through_ref, *refs):
    direct_refs, (feat_ref, send_ref, sems) = refs[:-3], refs[-3:]
    copies = fetch([(send_hbm, send_ref), (feat_hbm, feat_ref)], sems)
    copies[0].wait()
    chosen_ref[...] = listed_rows(send_ref, feat_ref.shape[0])
    copies[1].wait()
    halo_ref[...] = feat_ref[feat_ref.shape[0] - halo_ref.shape[0] :]
    store_blocks(rounded(f32_dot(chosen_ref[...], feat_ref[...])), through_ref, direct_refs)


def prepare_kernel(
    per_peer,
    feat_hbm,
    og_hbm,
    wq_hbm,
    wkv_hbm,
    wo_hbm,
    virt_hbm,
    nbr_hbm,
    exp_hbm,
    og_ref,
    wq_ref,
    wkv_ref,
    featt_ref,
    qt_ref,
    odt_ref,
    kv_ref,
    kvt_ref,
    local_bias_ref,
    far_bias_ref,
    feat_ref,
    wo_ref,
    virt_ref,
    nbr_ref,
    exp_ref,
    sems,
):
    nbr_copy, exp_copy, feat_copy, virt_copy, wq_copy, wkv_copy, og_copy, wo_copy = fetch(
        [
            (nbr_hbm, nbr_ref),
            (exp_hbm, exp_ref),
            (feat_hbm, feat_ref),
            (virt_hbm, virt_ref),
            (wq_hbm, wq_ref),
            (wkv_hbm, wkv_ref),
            (og_hbm, og_ref),
            (wo_hbm, wo_ref),
        ],
        sems,
    )
    row_count, width = feat_ref.shape
    window = local_bias_ref.shape[0]
    far = far_bias_ref.shape[0]
    virt_rows = virt_ref.shape[0]
    padded = kv_ref.shape[0] - row_count
    slots = far - padded
    scale = 1.0 / math.sqrt(width // HEADS)

    def multiplicity(key_rows, named):
        position = lax.broadcasted_iota(jnp.int32, (key_rows, row_count), 0)
        count = jnp.zeros((key_rows, row_count), jnp.float32)
        for at in range(named.shape[0]):
            count += jnp.where(named[at : at + 1, :] == position, 1.0, 0.0)
        return count

    nbr_copy.wait()
    local_bias_ref[...] = jnp.where(multiplicity(window, nbr_ref) > 0.0, 0.0, NEGATIVE_FILL)
    exp_copy.wait()
    expander = exp_ref[...]
    expander = ((expander // per_peer) ^ lax.axis_index("dom")) * per_peer + expander % per_peer
    named_times = multiplicity(slots, expander)
    slot_bias = jnp.full((slots, row_count), NEGATIVE_FILL, jnp.float32)
    for times in range(1, exp_ref.shape[0] + 1):
        slot_bias = jnp.where(named_times == float(times), math.log(times) / scale, slot_bias)
    far_bias_ref[:slots] = slot_bias
    virt_row = lax.broadcasted_iota(jnp.int32, (padded, row_count), 0)
    far_bias_ref[slots:] = jnp.where(virt_row < virt_rows, 0.0, NEGATIVE_FILL)

    feat_copy.wait()
    featt_ref[:, :row_count] = feat_ref[...].T
    virt_copy.wait()
    virt = jnp.concatenate(
        [virt_ref[...], jnp.zeros((padded - virt_rows, width), jnp.bfloat16)], axis=0
    )
    featt_ref[:, row_count:] = virt.T
    wq_copy.wait()
    qt_ref[...] = rounded(rows_contracted(wq_ref[...], featt_ref[:, :row_count]))
    wkv_copy.wait()
    kv_ref[:row_count] = rounded(f32_dot(feat_ref[...], wkv_ref[...]))
    kv_ref[row_count:] = rounded(f32_dot(virt, wkv_ref[...]))
    kvt_ref[...] = kv_ref[...].T
    og_copy.wait()
    wo_copy.wait()
    odt_ref[...] = rounded(times_transposed(wo_ref[...], og_ref[...]))


def head_rows(rows_ref, head):
    width, row_count = rows_ref.shape
    head_dim = width // HEADS
    low, high = head * head_dim, (head + 1) * head_dim
    first = low // LANES * LANES
    last = min(-(-high // LANES) * LANES, width)
    row = lax.broadcasted_iota(jnp.int32, (last - first, row_count), 0) + first
    return first, last, jnp.where((row >= low) & (row < high), rows_ref[first:last, :], 0)


def window_kernel(
    halo_ref, wkv_ref, qt_ref, odt_ref, own_kv_ref, bias_ref, halo_kv_ref, scores_ref, dprobs_ref, kv_ref
):
    width, row_count = qt_ref.shape
    tile = halo_ref.shape[0]
    halo_kv_ref[...] = rounded(f32_dot(halo_ref[...], wkv_ref[...]))
    kv_ref[:tile] = halo_kv_ref[...]
    kv_ref[tile:] = own_kv_ref[:row_count]
    for head in range(HEADS):
        for rows_ref, start, out_ref in ((qt_ref, 0, scores_ref), (odt_ref, width, dprobs_ref)):
            first, last, rows = head_rows(rows_ref, head)
            every = f32_dot(kv_ref[:, start + first : start + last], rows)
            for at in range(0, row_count, tile):
                lanes = slice(at, at + tile)
                value = every[at : at + 2 * tile, lanes]
                if start == 0:
                    value = value + bias_ref[:, lanes]
                out_ref[head, :, lanes] = value


def attend_kernel(
    factor,
    per_peer,
    dom_size,
    *refs,
):
    count = dom_size // 2 + 1
    piece_refs, halo_ref, refs = refs[:count], refs[count], refs[count + 1 :]
    og_ref, wq_ref, wkv_ref, featt_ref, qt_ref, odt_ref, own_kv_ref, own_kvt_ref = refs[:8]
    far_bias_ref, halo_kv_ref, scores_ref, dprobs_ref, send_ref, rider_ref = refs[8:14]
    extt_ref, gqt_ref, gkvt_ref, ot_ref, slot_ref, kv_ref, kvt_ref = refs[14:]
    width, row_count = qt_ref.shape
    tile = halo_ref.shape[0]
    tile_count = row_count // tile
    slots = dom_size * per_peer
    near = tile + row_count
    virt_at = near + slots
    head_dim = width // HEADS
    scale = 1.0 / math.sqrt(head_dim)

    kv_ref[virt_at - near :] = own_kv_ref[row_count:]
    kvt_ref[:, tile:near] = own_kvt_ref[:, :row_count]
    kvt_ref[:, virt_at:] = own_kvt_ref[:, row_count:]
    extt_ref[:, tile:near] = featt_ref[:, :row_count]
    extt_ref[:, virt_at:] = featt_ref[:, row_count:]
    extt_ref[:, :tile] = halo_ref[...].T
    kvt_ref[:, :tile] = halo_kv_ref[...].T
    slot_ref[:per_peer] = piece_refs[0][...]
    slot_ref[per_peer : 2 * per_peer] = piece_refs[1][:per_peer]
    for at, piece_ref in enumerate(piece_refs[:1:-1], 1):
        slot_ref[2 * at * per_peer : (2 * at + 2) * per_peer] = piece_ref[...]
    extt_ref[:, near:virt_at] = slot_ref[...].T
    kv_ref[:slots] = rounded(f32_dot(slot_ref[...], wkv_ref[...]))
    kvt_ref[:, near:virt_at] = kv_ref[:slots].T

    def tiles(of):
        return jnp.concatenate([of(t, slice(t * tile, (t + 1) * tile)) for t in range(tile_count)], 1)

    for head in range(HEADS):
        low, high = head * head_dim, (head + 1) * head_dim
        first, last, q_rows = head_rows(qt_ref, head)
        d_rows = head_rows(odt_ref, head)[2]
        s_local = scores_ref[head]
        s_far = f32_dot(kv_ref[:, first:last], q_rows) + far_bias_ref[...]
        peak = jnp.maximum(
            jnp.max(s_local, axis=0, keepdims=True), jnp.max(s_far, axis=0, keepdims=True)
        )
        exponent_scale = scale * math.log2(math.e)
        e_local = jnp.exp2((s_local - peak) * exponent_scale)
        e_far = jnp.exp2((s_far - peak) * exponent_scale)
        total = jnp.sum(e_local, axis=0, keepdims=True) + jnp.sum(e_far, axis=0, keepdims=True)
        inverse = 1.0 / total
        p_local = e_local * inverse
        p_far = e_far * inverse
        dp_local = dprobs_ref[head]
        dp_far = f32_dot(kv_ref[:, width + first : width + last], d_rows)
        delta = jnp.sum(p_local * dp_local, axis=0, keepdims=True) + jnp.sum(
            p_far * dp_far, axis=0, keepdims=True
        )
        pb_local, pb_far = rounded(p_local), rounded(p_far)
        ds_local = rounded(p_local * (dp_local - delta))
        ds_far = rounded(p_far * (dp_far - delta))

        def to_queries(start, local, beyond):
            rows = slice(start + low, start + high)
            near_part = tiles(
                lambda t, lanes: f32_dot(kvt_ref[rows, t * tile : (t + 2) * tile], local[:, lanes])
            )
            return near_part + f32_dot(kvt_ref[rows, near:], beyond)

        ot_ref[low:high] = rounded(to_queries(width, pb_local, pb_far))
        gqt_ref[low:high] = rounded(to_queries(0, ds_local, ds_far) * scale)

        def to_keys(start, operand, local, beyond, factor):
            rows = slice(start + low, start + high)
            parts = []
            carried = None
            for t in range(tile_count):
                lanes = slice(t * tile, (t + 1) * tile)
                window = times_transposed(operand[:, lanes], local[:, lanes])
                previous = window[:, :tile]
                parts.append(previous if carried is None else previous + carried)
                carried = window[:, tile:]
            parts.append(carried)
            parts.append(times_transposed(operand, beyond))
            gathered = jnp.concatenate(parts, axis=1)
            gkvt_ref[rows] = rounded(gathered if factor is None else gathered * factor)

        to_keys(0, qt_ref[low:high], ds_local, ds_far, scale)
        to_keys(width, odt_ref[low:high], pb_local, pb_far, None)

    rider_ref[...] = f32_dot(wkv_ref[...], gkvt_ref[:, virt_at:]).T * factor
    weight_sums(
        1 - lax.axis_index("rows") % 2, send_ref, extt_ref, gqt_ref, gkvt_ref, ot_ref, og_ref, factor
    )
    send_ref[2 * width :] = rounded(rider_ref[...])


def weight_sums(core, out_ref, extt_ref, gqt_ref, gkvt_ref, ot_ref, og_ref, factor):
    width, row_count = gqt_ref.shape
    held = own_digit()
    pair, square, _ = exchange_plan()
    rows = 2 * width >> len(pair + square)

    def write(at, total):
        total = (total * factor).astype(out_ref.dtype)
        for start in range(0, width, rows):
            piece = (at * width + start) // rows
            offset = pl.multiple_of((piece ^ held) * rows, ROW_PACK)
            out_ref[pl.ds(offset, rows), :] = total[start : start + rows]

    @pl.when(core == 0)
    def _():
        own = slice(TILE, TILE + row_count)
        write(0, times_transposed(extt_ref[:, own], gqt_ref[...]))
        write(1, times_transposed(extt_ref[...], gkvt_ref[:width]))

    @pl.when(core == 1)
    def _():
        write(0, times_transposed(extt_ref[...], gkvt_ref[width:]))
        write(1, f32_dot(ot_ref[...], og_ref[...]))


def finish_kernel(factor, og_ref, wq_ref, wkv_ref, extt_ref, gqt_ref, gkvt_ref, ot_ref, *refs):
    gf_ref, halo_feat_ref, keep_ref = refs[:3]
    pair_refs = refs[3:]
    width, row_count = gqt_ref.shape
    near = TILE + row_count
    step = pair_refs[0].shape[0]
    slots = step * len(pair_refs)
    weight_sums(
        lax.axis_index("rows") % 2, keep_ref, extt_ref, gqt_ref, gkvt_ref, ot_ref, og_ref, factor
    )
    by_feature = f32_dot(wkv_ref[...], gkvt_ref[:, : near + slots])
    own = by_feature[:, TILE:near] + f32_dot(wq_ref[...], gqt_ref[...])
    gf_ref[...] = own.T
    halo_feat_ref[...] = rounded(by_feature[:, :TILE].T)
    slot_feat = rounded(by_feature[:, near:].T)
    for at, out_ref in enumerate(pair_refs):
        out_ref[...] = slot_feat[at * step : (at + 1) * step]


def place_kernel(*refs):
    part_refs, (gq_hbm, gkv_hbm, go_hbm, all_ref, out_ref, sems) = refs[:-6], refs[-6:]
    width = gq_hbm.shape[0]
    pair, square, _ = exchange_plan()
    half = 1 << len(pair + square)
    rows = 2 * width // half
    step = part_refs[0].shape[0]
    for at, part_ref in enumerate(part_refs):
        all_ref[at * step : (at + 1) * step] = part_ref[...]
    held = own_digit() + (lax.axis_index("rows") % 2) * half
    copies = []
    for at in range(2 * half):
        start = at * rows
        piece = slice(start, start + rows)
        offset = pl.multiple_of((held ^ at) * rows, ROW_PACK)
        out_ref[piece] = all_ref[pl.ds(offset, rows), :].astype(jnp.float32)
        rows_out = pl.ds(start % width, rows)
        which = start // width
        if which == 0:
            target = gq_hbm.at[rows_out]
        elif which == 3:
            target = go_hbm.at[rows_out]
        else:
            target = gkv_hbm.at[rows_out, pl.ds((which - 1) * width, width)]
        copies.append(pltpu.make_async_copy(out_ref.at[piece], target, sems.at[at]))
        copies[-1].start()
    for copy in copies:
        copy.wait()


def return_kernel(gf_ref, chosen_ref, halo_ref, own_ref, through_ref, *refs):
    far_refs, out_ref = refs[:-1], refs[-1]
    row_count = gf_ref.shape[0]
    tile = halo_ref.shape[0]
    per_peer = own_ref.shape[0] // 2
    returned = []
    for at, even_ref in enumerate([own_ref, *far_refs[::-1]]):
        returned += [even_ref[:per_peer], through_ref[at * per_peer : (at + 1) * per_peer]]
    total = gf_ref[...] + rows_contracted(chosen_ref[...], jnp.concatenate(returned, axis=0))
    out_ref[: row_count - tile] = total[: row_count - tile]
    out_ref[row_count - tile :] = total[row_count - tile :] + halo_ref[...].astype(jnp.float32)


def call(kernel, name, outs, args, scratch=(), fetched=0, flops=0, stored=False):
    spaces = [pltpu.HBM] * fetched
    spaces += [pltpu.VMEM] * (len(args) - len(spaces))
    moved = sum(x.size * x.dtype.itemsize for x in list(args) + list(outs))
    scratch = list(scratch)
    if fetched:
        scratch.append(pltpu.SemaphoreType.DMA((fetched,)))
    constrained = [
        pltpu.with_memory_space_constraint(x, pltpu.HBM) if space is pltpu.HBM else x
        for x, space in zip(args, spaces)
    ]
    return pl.pallas_call(
        kernel,
        out_shape=outs,
        in_specs=[pl.BlockSpec(memory_space=space) for space in spaces],
        out_specs=[pl.BlockSpec(memory_space=pl.ANY if stored else pltpu.VMEM)] * len(outs),
        scratch_shapes=scratch,
        compiler_params=pltpu.CompilerParams(vmem_limit_bytes=VMEM_BYTES),
        cost_estimate=pl.CostEstimate(flops=flops, bytes_accessed=moved, transcendentals=0),
        name=name,
    )(*constrained)


def shards(features, out_grad, w_query, w_keyval, w_out, virtual, local_nbr, expander, send_rows):
    row_count, width = features.shape
    dom_size, per_peer = send_rows.shape
    slots = dom_size * per_peer
    virt_rows = virtual.shape[0]
    padded = ROW_PACK * -(-virt_rows // ROW_PACK)
    ext_rows = TILE + row_count + slots + padded
    nodes = row_count * lax.axis_size("dom") * lax.axis_size("rows")
    pair, square, rest = exchange_plan()
    bf16, f32 = jnp.bfloat16, jnp.float32
    shape = jax.ShapeDtypeStruct

    halo, chosen, through, *direct = call(
        pick_kernel,
        "pick_rows",
        [shape((TILE, width), bf16), shape((slots, row_count), bf16)]
        + [shape((slots // 2, width), bf16)]
        + [shape((per_peer, width), bf16)] * (dom_size // 2),
        [features, send_rows],
        [pltpu.VMEM(features.shape, bf16), pltpu.VMEM(send_rows.shape, jnp.int32)],
        fetched=2,
    )
    through = swapped(through, 1, 0)
    prepared = call(
        functools.partial(prepare_kernel, per_peer),
        "prepare",
        [
            shape(out_grad.shape, bf16),
            shape(w_query.shape, bf16),
            shape(w_keyval.shape, bf16),
            shape((width, row_count + padded), bf16),
            shape((width, row_count), bf16),
            shape((width, row_count), bf16),
            shape((row_count + padded, 2 * width), bf16),
            shape((2 * width, row_count + padded), bf16),
            shape((2 * TILE, row_count), f32),
            shape((slots + padded, row_count), f32),
        ],
        [features, out_grad, w_query, w_keyval, w_out, virtual, local_nbr.T, expander.T],
        [
            pltpu.VMEM(features.shape, bf16),
            pltpu.VMEM(w_out.shape, bf16),
            pltpu.VMEM(virtual.shape, bf16),
            pltpu.VMEM(local_nbr.shape[::-1], jnp.int32),
            pltpu.VMEM(expander.shape[::-1], jnp.int32),
        ],
        fetched=8,
        flops=10 * row_count * width * width,
    )
    halo = shifted(halo, "rows", 1)
    through, _ = lax.optimization_barrier((through, prepared[0]))
    arrived = handed_on(direct, through)
    *prepared, local_bias, far_bias = prepared
    window = call(
        window_kernel,
        "window",
        [
            shape((TILE, 2 * width), bf16),
            shape((HEADS, 2 * TILE, row_count), f32),
            shape((HEADS, 2 * TILE, row_count), f32),
        ],
        [halo, prepared[2], *prepared[4:7], local_bias],
        [pltpu.VMEM((TILE + row_count, 2 * width), bf16)],
        flops=8 * HEADS * TILE * row_count * LANES,
    )
    message, rider, *gradients = call(
        functools.partial(attend_kernel, nodes**-0.5, per_peer, dom_size),
        "attend",
        [
            shape((2 * width + padded, width), bf16),
            shape((padded, width), f32),
            shape((width, ext_rows), bf16),
            shape((width, row_count), bf16),
            shape((2 * width, ext_rows), bf16),
            shape((width, row_count), bf16),
        ],
        [*arrived, halo, *prepared, far_bias, *window],
        [
            pltpu.VMEM((slots, width), bf16),
            pltpu.VMEM((slots + padded, 2 * width), bf16),
            pltpu.VMEM((2 * width, ext_rows), bf16),
        ],
        flops=28 * ext_rows * width * width,
    )
    message = swapped(message, *CORES)
    own_feat, halo_feat, keep, *pairs = call(
        functools.partial(finish_kernel, nodes**-0.5),
        "finish",
        [shape((row_count, width), f32), shape((TILE, width), bf16), shape((2 * width, width), f32)]
        + [shape((2 * per_peer, width), bf16)] * (dom_size // 2),
        [*prepared[:3], *gradients],
        flops=6 * ext_rows * width * width,
    )

    keep, rider = added(keep, rounded(rider).astype(f32), {1: message})
    rider = rider[: -(-virt_rows // 8) * 8]
    pairs, _ = lax.optimization_barrier((pairs, keep))
    returned = [swapped(pairs[at], 2 * at, 0) for at in reversed(range(1, dom_size // 2))]
    keep, rider = scattered(keep, rider, square)
    (returned, halo_feat), _ = lax.optimization_barrier(((returned, halo_feat), keep))
    through = swapped(jnp.concatenate([x[per_peer:] for x in [pairs[0]] + returned[::-1]]), 1, 0)
    halo_back = shifted(halo_feat, "rows", -1)
    keep, rider = scattered(keep, rider, pair)
    for mask in rest:
        message = swapped(with_rider(keep, rider), *mask)
        keep, rider = rounded(keep).astype(f32), rounded(rider).astype(f32)
        keep, rider = added(keep, rider, {1: message})
    (grad_features,) = call(
        return_kernel,
        "return_rows",
        [shape((row_count, width), f32)],
        [own_feat, chosen, halo_back, pairs[0], through, *returned],
    )

    held, grad_features = lax.optimization_barrier((rounded(keep), grad_features))
    held = jnp.concatenate([held, swapped(held, *pair[0])], axis=0)
    arrived = [swapped(held, *masks) for masks in partner_masks(square)[1:]]
    near = [held, *arrived]
    far = [swapped(part, *CORES) for part in near]
    grad_wq, grad_wkv, grad_wo = call(
        place_kernel,
        "place_sums",
        [shape((width, width), f32), shape((width, 2 * width), f32), shape((width, width), f32)],
        [*near, *far],
        [
            pltpu.VMEM((4 * width, width), bf16),
            pltpu.VMEM((4 * width, width), f32),
            pltpu.SemaphoreType.DMA((2 << len(pair + square),)),
        ],
        stored=True,
    )
    return grad_features, grad_wq, grad_wkv, grad_wo, rider[:virt_rows]


def solution(mesh):
    placed = (
        P(("dom", "rows"), None),
        P(("dom", "rows"), None),
        P(),
        P(),
        P(),
        P(),
        P(("dom", "rows"), None),
        P(("dom", "rows"), None),
        P(("dom", "rows"), None),
    )
    return jax.shard_map(
        shards,
        mesh=mesh,
        in_specs=placed,
        out_specs=(P(("dom", "rows"), None), P(), P(), P(), P()),
        check_vma=False,
    )
```

```python
import functools
import math

import jax
import jax.numpy as jnp
from jax import lax
from jax.experimental import pallas as pl
from jax.experimental.pallas import tpu as pltpu
from jax.sharding import PartitionSpec as P

HEADS = 8
TILE = 128
ROW_PACK = 16
NEGATIVE_FILL = -1e30
VMEM_BYTES = 24 * 1024 * 1024
LANES = 128


def f32_dot(left, right):
    return jnp.dot(left, right, preferred_element_type=jnp.float32)


def rows_contracted(left, right):
    return lax.dot_general(
        left, right, (((0,), (0,)), ((), ())), preferred_element_type=jnp.float32
    )


def times_transposed(left, right):
    return lax.dot_general(
        left, right, (((1,), (1,)), ((), ())), preferred_element_type=jnp.float32
    )


def rounded(value):
    return value.astype(jnp.bfloat16)


CORES = (0, 1)


def bits_of(size, first=1):
    return [1 << i for i in range(size.bit_length() - 1) if 1 << i >= first]


def exchange_plan():
    dom_size, rows_size = lax.axis_size("dom"), lax.axis_size("rows")
    pair, square = [(2, 0)], [(1, 0), (0, 2)]
    rest = [(bit, 0) for bit in bits_of(dom_size, 4)] + [(0, bit) for bit in bits_of(rows_size, 4)]
    return pair, square, rest


def partner_masks(block):
    masks = []
    for digit in range(1 << len(block)):
        chosen = [mask for i, mask in enumerate(block) if digit >> i & 1]
        masks.append((sum(mask[0] for mask in chosen), sum(mask[1] for mask in chosen)))
    return masks


def farthest_first(count):
    return sorted(range(1, count), key=lambda digit: (-digit.bit_count(), -digit))


def own_digit():
    pair, square, _ = exchange_plan()
    digit = 0
    for i, (dom_mask, rows_mask) in enumerate(pair + square):
        own = (lax.axis_index("dom") & dom_mask) | (lax.axis_index("rows") & rows_mask)
        digit += jnp.where(own != 0, 1 << i, 0)
    return digit


def swapped(block, dom_mask, rows_mask):
    dom_size, rows_size = lax.axis_size("dom"), lax.axis_size("rows")
    route = [
        (a * rows_size + b, (a ^ dom_mask) * rows_size + (b ^ rows_mask))
        for a in range(dom_size)
        for b in range(rows_size)
    ]
    return lax.ppermute(block, ("dom", "rows"), route)


def shifted(block, axis, distance):
    devices = range(lax.axis_size(axis))
    route = [((i - distance) % len(devices), i) for i in devices]
    return lax.ppermute(block, axis, route)


def paired_sum(terms):
    while len(terms) > 1:
        terms = [left + right for left, right in zip(terms[::2], terms[1::2])]
    return terms[0]


def with_rider(block, rider):
    return jnp.concatenate([rounded(block), rounded(rider)], axis=0)


def added(keep, rider, arrived):
    rows = keep.shape[0]
    riders = [rider] + [arrived[at][rows:].astype(jnp.float32) for at in sorted(arrived)]
    for block in arrived.values():
        keep = keep + block[:rows].astype(jnp.float32)
    return keep, paired_sum(riders)


def scattered(keep, rider, bits):
    masks = partner_masks(bits)
    rows = keep.shape[0] // len(masks)
    parts = [keep[at * rows : (at + 1) * rows] for at in range(len(masks))]
    messages = {at: with_rider(parts[at], rider) for at in farthest_first(len(masks))}
    arrived = {at: swapped(message, *masks[at]) for at, message in messages.items()}
    return added(parts[0], rounded(rider).astype(jnp.float32), arrived)


def handed_on(direct, through):
    rows = direct[0].shape[0]
    arrived = [direct[0], through]
    for at in reversed(range(1, len(direct))):
        message = jnp.concatenate([direct[at], through[at * rows : (at + 1) * rows]], axis=0)
        arrived.append(swapped(message, 2 * at, 0))
    return arrived


def listed_rows(send_ref, row_count):
    dom_size, per_peer = send_ref.shape
    slots = dom_size * per_peer
    slot = lax.broadcasted_iota(jnp.int32, (slots, per_peer), 0)
    place = lax.broadcasted_iota(jnp.int32, (slots, per_peer), 1)
    peer = (slot // per_peer) ^ lax.axis_index("dom")
    listed = jnp.zeros((slots, per_peer), jnp.int32)
    for at in range(dom_size):
        listed += jnp.where((peer == at) & (place == slot % per_peer), send_ref[at : at + 1, :], 0)
    column = jnp.sum(listed, axis=1, keepdims=True)
    rows = lax.broadcasted_iota(jnp.int32, (slots, row_count), 1)
    return jnp.where(column == rows, 1.0, 0.0).astype(jnp.bfloat16)


def fetch(pairs, sems):
    copies = [
        pltpu.make_async_copy(source, target, sems.at[at])
        for at, (source, target) in enumerate(pairs)
    ]
    for copy in copies:
        copy.start()
    return copies


def store_blocks(rows, through_ref, direct_refs):
    size = direct_refs[0].shape[0]
    for at, out_ref in enumerate(direct_refs):
        out_ref[...] = rows[2 * at * size : (2 * at + 1) * size]
        through_ref[at * size : (at + 1) * size] = rows[(2 * at + 1) * size : (2 * at + 2) * size]


def pick_kernel(feat_hbm, send_hbm, halo_ref, chosen_ref, through_ref, *refs):
    direct_refs, (feat_ref, send_ref, sems) = refs[:-3], refs[-3:]
    copies = fetch([(send_hbm, send_ref), (feat_hbm, feat_ref)], sems)
    copies[0].wait()
    chosen_ref[...] = listed_rows(send_ref, feat_ref.shape[0])
    copies[1].wait()
    halo_ref[...] = feat_ref[feat_ref.shape[0] - halo_ref.shape[0] :]
    store_blocks(rounded(f32_dot(chosen_ref[...], feat_ref[...])), through_ref, direct_refs)


def prepare_kernel(
    per_peer,
    feat_hbm,
    og_hbm,
    wq_hbm,
    wkv_hbm,
    wo_hbm,
    virt_hbm,
    nbr_hbm,
    exp_hbm,
    og_ref,
    wq_ref,
    wkv_ref,
    featt_ref,
    qt_ref,
    odt_ref,
    kv_ref,
    kvt_ref,
    local_bias_ref,
    far_bias_ref,
    feat_ref,
    wo_ref,
    virt_ref,
    nbr_ref,
    exp_ref,
    sems,
):
    nbr_copy, exp_copy, feat_copy, virt_copy, wq_copy, wkv_copy, og_copy, wo_copy = fetch(
        [
            (nbr_hbm, nbr_ref),
            (exp_hbm, exp_ref),
            (feat_hbm, feat_ref),
            (virt_hbm, virt_ref),
            (wq_hbm, wq_ref),
            (wkv_hbm, wkv_ref),
            (og_hbm, og_ref),
            (wo_hbm, wo_ref),
        ],
        sems,
    )
    row_count, width = feat_ref.shape
    window = local_bias_ref.shape[0]
    far = far_bias_ref.shape[0]
    virt_rows = virt_ref.shape[0]
    padded = kv_ref.shape[0] - row_count
    slots = far - padded
    scale = 1.0 / math.sqrt(width // HEADS)

    def multiplicity(key_rows, named):
        position = lax.broadcasted_iota(jnp.int32, (key_rows, row_count), 0)
        count = jnp.zeros((key_rows, row_count), jnp.float32)
        for at in range(named.shape[0]):
            count += jnp.where(named[at : at + 1, :] == position, 1.0, 0.0)
        return count

    nbr_copy.wait()
    local_bias_ref[...] = jnp.where(multiplicity(window, nbr_ref) > 0.0, 0.0, NEGATIVE_FILL)
    exp_copy.wait()
    expander = exp_ref[...]
    expander = ((expander // per_peer) ^ lax.axis_index("dom")) * per_peer + expander % per_peer
    named_times = multiplicity(slots, expander)
    slot_bias = jnp.full((slots, row_count), NEGATIVE_FILL, jnp.float32)
    for times in range(1, exp_ref.shape[0] + 1):
        slot_bias = jnp.where(named_times == float(times), math.log(times) / scale, slot_bias)
    far_bias_ref[:slots] = slot_bias
    virt_row = lax.broadcasted_iota(jnp.int32, (padded, row_count), 0)
    far_bias_ref[slots:] = jnp.where(virt_row < virt_rows, 0.0, NEGATIVE_FILL)

    feat_copy.wait()
    featt_ref[:, :row_count] = feat_ref[...].T
    virt_copy.wait()
    virt = jnp.concatenate(
        [virt_ref[...], jnp.zeros((padded - virt_rows, width), jnp.bfloat16)], axis=0
    )
    featt_ref[:, row_count:] = virt.T
    wq_copy.wait()
    qt_ref[...] = rounded(rows_contracted(wq_ref[...], featt_ref[:, :row_count]))
    wkv_copy.wait()
    kv_ref[:row_count] = rounded(f32_dot(feat_ref[...], wkv_ref[...]))
    kv_ref[row_count:] = rounded(f32_dot(virt, wkv_ref[...]))
    kvt_ref[...] = kv_ref[...].T
    og_copy.wait()
    wo_copy.wait()
    odt_ref[...] = rounded(times_transposed(wo_ref[...], og_ref[...]))


def attend_kernel(
    factor,
    per_peer,
    dom_size,
    *refs,
):
    count = dom_size // 2 + 1
    piece_refs, halo_ref, refs = refs[:count], refs[count], refs[count + 1 :]
    og_ref, wq_ref, wkv_ref, featt_ref, qt_ref, odt_ref, own_kv_ref, own_kvt_ref = refs[:8]
    local_bias_ref, far_bias_ref, send_ref, rider_ref = refs[8:12]
    extt_ref, gqt_ref, gkvt_ref, ot_ref, slot_ref, kv_ref, kvt_ref = refs[12:]
    width, row_count = qt_ref.shape
    tile = halo_ref.shape[0]
    tile_count = row_count // tile
    slots = dom_size * per_peer
    near = tile + row_count
    virt_at = near + slots
    head_dim = width // HEADS
    scale = 1.0 / math.sqrt(head_dim)

    kv_ref[tile:near] = own_kv_ref[:row_count]
    kv_ref[virt_at:] = own_kv_ref[row_count:]
    kvt_ref[:, tile:near] = own_kvt_ref[:, :row_count]
    kvt_ref[:, virt_at:] = own_kvt_ref[:, row_count:]
    extt_ref[:, tile:near] = featt_ref[:, :row_count]
    extt_ref[:, virt_at:] = featt_ref[:, row_count:]
    slot_ref[:per_peer] = piece_refs[0][...]
    slot_ref[per_peer : 2 * per_peer] = piece_refs[1][:per_peer]
    for at, piece_ref in enumerate(piece_refs[:1:-1], 1):
        slot_ref[2 * at * per_peer : (2 * at + 2) * per_peer] = piece_ref[...]
    for rows, source_ref in ((slice(0, tile), halo_ref), (slice(near, virt_at), slot_ref)):
        extt_ref[:, rows] = source_ref[...].T
        kv_ref[rows] = rounded(f32_dot(source_ref[...], wkv_ref[...]))
        kvt_ref[:, rows] = kv_ref[rows].T

    def tiles(of):
        return jnp.concatenate([of(t, slice(t * tile, (t + 1) * tile)) for t in range(tile_count)], 1)

    def bounds(head):
        low, high = head * head_dim, (head + 1) * head_dim
        return low, high, low // LANES * LANES, min(-(-high // LANES) * LANES, width)

    def products(head):
        low, high, first, last = bounds(head)
        column = lax.broadcasted_iota(jnp.int32, (last - first, row_count), 0) + first
        of_head = (column >= low) & (column < high)
        out = []
        for rows_ref, start in ((qt_ref, 0), (odt_ref, width)):
            operand = jnp.where(of_head, rows_ref[first:last, :], 0)
            every = f32_dot(kv_ref[:, start + first : start + last], operand)
            out.append(tiles(lambda t, lanes: every[t * tile : (t + 2) * tile, lanes]))
            out.append(every[near:])
        return out

    def weights(s_local, s_far, dp_local, dp_far):
        s_local += local_bias_ref[...]
        s_far += far_bias_ref[...]
        peak = jnp.maximum(
            jnp.max(s_local, axis=0, keepdims=True), jnp.max(s_far, axis=0, keepdims=True)
        )
        exponent_scale = scale * math.log2(math.e)
        e_local = jnp.exp2((s_local - peak) * exponent_scale)
        e_far = jnp.exp2((s_far - peak) * exponent_scale)
        total = jnp.sum(e_local, axis=0, keepdims=True) + jnp.sum(e_far, axis=0, keepdims=True)
        inverse = 1.0 / total
        p_local = e_local * inverse
        p_far = e_far * inverse
        delta = jnp.sum(p_local * dp_local, axis=0, keepdims=True) + jnp.sum(
            p_far * dp_far, axis=0, keepdims=True
        )
        ds_local = rounded(p_local * (dp_local - delta))
        ds_far = rounded(p_far * (dp_far - delta))
        return rounded(p_local), rounded(p_far), ds_local, ds_far

    def outputs(head, pb_local, pb_far, ds_local, ds_far):
        low, high, _, _ = bounds(head)

        def to_queries(start, local, beyond):
            rows = slice(start + low, start + high)
            near_part = tiles(
                lambda t, lanes: f32_dot(kvt_ref[rows, t * tile : (t + 2) * tile], local[:, lanes])
            )
            return near_part + f32_dot(kvt_ref[rows, near:], beyond)

        def to_keys(start, operand, local, beyond, factor):
            rows = slice(start + low, start + high)
            parts = []
            carried = None
            for t in range(tile_count):
                lanes = slice(t * tile, (t + 1) * tile)
                window = times_transposed(operand[:, lanes], local[:, lanes])
                previous = window[:, :tile]
                parts.append(previous if carried is None else previous + carried)
                carried = window[:, tile:]
            parts.append(carried)
            parts.append(times_transposed(operand, beyond))
            gathered = jnp.concatenate(parts, axis=1)
            gkvt_ref[rows] = rounded(gathered if factor is None else gathered * factor)

        ot_ref[low:high] = rounded(to_queries(width, pb_local, pb_far))
        gqt_ref[low:high] = rounded(to_queries(0, ds_local, ds_far) * scale)
        to_keys(0, qt_ref[low:high], ds_local, ds_far, scale)
        to_keys(width, odt_ref[low:high], pb_local, pb_far, None)

    coming = products(0)
    done = None
    for head in range(HEADS):
        now = coming
        if head + 1 < HEADS:
            coming = products(head + 1)
        if done is not None:
            outputs(head - 1, *done)
        done = weights(*now)
    outputs(HEADS - 1, *done)

    rider_ref[...] = f32_dot(wkv_ref[...], gkvt_ref[:, virt_at:]).T * factor
    weight_sums(
        1 - lax.axis_index("rows") % 2, send_ref, extt_ref, gqt_ref, gkvt_ref, ot_ref, og_ref, factor
    )
    send_ref[2 * width :] = rounded(rider_ref[...])


def weight_sums(core, out_ref, extt_ref, gqt_ref, gkvt_ref, ot_ref, og_ref, factor):
    width, row_count = gqt_ref.shape
    held = own_digit()
    pair, square, _ = exchange_plan()
    rows = 2 * width >> len(pair + square)

    def write(at, total):
        total = (total * factor).astype(out_ref.dtype)
        for start in range(0, width, rows):
            piece = (at * width + start) // rows
            offset = pl.multiple_of((piece ^ held) * rows, ROW_PACK)
            out_ref[pl.ds(offset, rows), :] = total[start : start + rows]

    @pl.when(core == 0)
    def _():
        own = slice(TILE, TILE + row_count)
        write(0, times_transposed(extt_ref[:, own], gqt_ref[...]))
        write(1, times_transposed(extt_ref[...], gkvt_ref[:width]))

    @pl.when(core == 1)
    def _():
        write(0, times_transposed(extt_ref[...], gkvt_ref[width:]))
        write(1, f32_dot(ot_ref[...], og_ref[...]))


def finish_kernel(factor, og_ref, wq_ref, wkv_ref, extt_ref, gqt_ref, gkvt_ref, ot_ref, *refs):
    gf_ref, halo_feat_ref, keep_ref = refs[:3]
    pair_refs = refs[3:]
    width, row_count = gqt_ref.shape
    near = TILE + row_count
    step = pair_refs[0].shape[0]
    slots = step * len(pair_refs)
    weight_sums(
        lax.axis_index("rows") % 2, keep_ref, extt_ref, gqt_ref, gkvt_ref, ot_ref, og_ref, factor
    )
    by_feature = f32_dot(wkv_ref[...], gkvt_ref[:, : near + slots])
    own = by_feature[:, TILE:near] + f32_dot(wq_ref[...], gqt_ref[...])
    gf_ref[...] = own.T
    halo_feat_ref[...] = rounded(by_feature[:, :TILE].T)
    slot_feat = rounded(by_feature[:, near:].T)
    for at, out_ref in enumerate(pair_refs):
        out_ref[...] = slot_feat[at * step : (at + 1) * step]


def place_kernel(*refs):
    part_refs, (gq_hbm, gkv_hbm, go_hbm, all_ref, out_ref, sems) = refs[:-6], refs[-6:]
    width = gq_hbm.shape[0]
    pair, square, _ = exchange_plan()
    half = 1 << len(pair + square)
    rows = 2 * width // half
    step = part_refs[0].shape[0]
    for at, part_ref in enumerate(part_refs):
        all_ref[at * step : (at + 1) * step] = part_ref[...]
    held = own_digit() + (lax.axis_index("rows") % 2) * half
    copies = []
    for at in range(2 * half):
        start = at * rows
        piece = slice(start, start + rows)
        offset = pl.multiple_of((held ^ at) * rows, ROW_PACK)
        out_ref[piece] = all_ref[pl.ds(offset, rows), :].astype(jnp.float32)
        rows_out = pl.ds(start % width, rows)
        which = start // width
        if which == 0:
            target = gq_hbm.at[rows_out]
        elif which == 3:
            target = go_hbm.at[rows_out]
        else:
            target = gkv_hbm.at[rows_out, pl.ds((which - 1) * width, width)]
        copies.append(pltpu.make_async_copy(out_ref.at[piece], target, sems.at[at]))
        copies[-1].start()
    for copy in copies:
        copy.wait()


def return_kernel(gf_ref, chosen_ref, halo_ref, own_ref, through_ref, *refs):
    far_refs, out_ref = refs[:-1], refs[-1]
    row_count = gf_ref.shape[0]
    tile = halo_ref.shape[0]
    per_peer = own_ref.shape[0] // 2
    returned = []
    for at, even_ref in enumerate([own_ref, *far_refs[::-1]]):
        returned += [even_ref[:per_peer], through_ref[at * per_peer : (at + 1) * per_peer]]
    total = gf_ref[...] + rows_contracted(chosen_ref[...], jnp.concatenate(returned, axis=0))
    out_ref[: row_count - tile] = total[: row_count - tile]
    out_ref[row_count - tile :] = total[row_count - tile :] + halo_ref[...].astype(jnp.float32)


def call(kernel, name, outs, args, scratch=(), fetched=0, flops=0, stored=False):
    spaces = [pltpu.HBM] * fetched
    spaces += [pltpu.VMEM] * (len(args) - len(spaces))
    moved = sum(x.size * x.dtype.itemsize for x in list(args) + list(outs))
    scratch = list(scratch)
    if fetched:
        scratch.append(pltpu.SemaphoreType.DMA((fetched,)))
    constrained = [
        pltpu.with_memory_space_constraint(x, pltpu.HBM) if space is pltpu.HBM else x
        for x, space in zip(args, spaces)
    ]
    return pl.pallas_call(
        kernel,
        out_shape=outs,
        in_specs=[pl.BlockSpec(memory_space=space) for space in spaces],
        out_specs=[pl.BlockSpec(memory_space=pl.ANY if stored else pltpu.VMEM)] * len(outs),
        scratch_shapes=scratch,
        compiler_params=pltpu.CompilerParams(vmem_limit_bytes=VMEM_BYTES),
        cost_estimate=pl.CostEstimate(flops=flops, bytes_accessed=moved, transcendentals=0),
        name=name,
    )(*constrained)


def shards(features, out_grad, w_query, w_keyval, w_out, virtual, local_nbr, expander, send_rows):
    row_count, width = features.shape
    dom_size, per_peer = send_rows.shape
    slots = dom_size * per_peer
    virt_rows = virtual.shape[0]
    padded = ROW_PACK * -(-virt_rows // ROW_PACK)
    ext_rows = TILE + row_count + slots + padded
    nodes = row_count * lax.axis_size("dom") * lax.axis_size("rows")
    pair, square, rest = exchange_plan()
    bf16, f32 = jnp.bfloat16, jnp.float32
    shape = jax.ShapeDtypeStruct

    halo, chosen, through, *direct = call(
        pick_kernel,
        "pick_rows",
        [shape((TILE, width), bf16), shape((slots, row_count), bf16)]
        + [shape((slots // 2, width), bf16)]
        + [shape((per_peer, width), bf16)] * (dom_size // 2),
        [features, send_rows],
        [pltpu.VMEM(features.shape, bf16), pltpu.VMEM(send_rows.shape, jnp.int32)],
        fetched=2,
    )
    through = swapped(through, 1, 0)
    prepared = call(
        functools.partial(prepare_kernel, per_peer),
        "prepare",
        [
            shape(out_grad.shape, bf16),
            shape(w_query.shape, bf16),
            shape(w_keyval.shape, bf16),
            shape((width, row_count + padded), bf16),
            shape((width, row_count), bf16),
            shape((width, row_count), bf16),
            shape((row_count + padded, 2 * width), bf16),
            shape((2 * width, row_count + padded), bf16),
            shape((2 * TILE, row_count), f32),
            shape((slots + padded, row_count), f32),
        ],
        [features, out_grad, w_query, w_keyval, w_out, virtual, local_nbr.T, expander.T],
        [
            pltpu.VMEM(features.shape, bf16),
            pltpu.VMEM(w_out.shape, bf16),
            pltpu.VMEM(virtual.shape, bf16),
            pltpu.VMEM(local_nbr.shape[::-1], jnp.int32),
            pltpu.VMEM(expander.shape[::-1], jnp.int32),
        ],
        fetched=8,
        flops=10 * row_count * width * width,
    )
    (through, halo), _ = lax.optimization_barrier(((through, halo), prepared[0]))
    arrived = handed_on(direct, through)
    halo = shifted(halo, "rows", 1)
    message, rider, *gradients = call(
        functools.partial(attend_kernel, nodes**-0.5, per_peer, dom_size),
        "attend",
        [
            shape((2 * width + padded, width), bf16),
            shape((padded, width), f32),
            shape((width, ext_rows), bf16),
            shape((width, row_count), bf16),
            shape((2 * width, ext_rows), bf16),
            shape((width, row_count), bf16),
        ],
        [*arrived, halo, *prepared],
        [
            pltpu.VMEM((slots, width), bf16),
            pltpu.VMEM((ext_rows, 2 * width), bf16),
            pltpu.VMEM((2 * width, ext_rows), bf16),
        ],
        flops=28 * ext_rows * width * width,
    )
    message = swapped(message, *CORES)
    own_feat, halo_feat, keep, *pairs = call(
        functools.partial(finish_kernel, nodes**-0.5),
        "finish",
        [shape((row_count, width), f32), shape((TILE, width), bf16), shape((2 * width, width), f32)]
        + [shape((2 * per_peer, width), bf16)] * (dom_size // 2),
        [*prepared[:3], *gradients],
        flops=6 * ext_rows * width * width,
    )

    keep, rider = added(keep, rounded(rider).astype(f32), {1: message})
    rider = rider[: -(-virt_rows // 8) * 8]
    pairs, _ = lax.optimization_barrier((pairs, keep))
    returned = [swapped(pairs[at], 2 * at, 0) for at in reversed(range(1, dom_size // 2))]
    keep, rider = scattered(keep, rider, square)
    (returned, halo_feat), _ = lax.optimization_barrier(((returned, halo_feat), keep))
    through = swapped(jnp.concatenate([x[per_peer:] for x in [pairs[0]] + returned[::-1]]), 1, 0)
    halo_back = shifted(halo_feat, "rows", -1)
    keep, rider = scattered(keep, rider, pair)
    for mask in rest:
        message = swapped(with_rider(keep, rider), *mask)
        keep, rider = rounded(keep).astype(f32), rounded(rider).astype(f32)
        keep, rider = added(keep, rider, {1: message})
    (grad_features,) = call(
        return_kernel,
        "return_rows",
        [shape((row_count, width), f32)],
        [own_feat, chosen, halo_back, pairs[0], through, *returned],
    )

    held, grad_features = lax.optimization_barrier((rounded(keep), grad_features))
    held = jnp.concatenate([held, swapped(held, *pair[0])], axis=0)
    arrived = [swapped(held, *masks) for masks in partner_masks(square)[1:]]
    near = [held, *arrived]
    far = [swapped(part, *CORES) for part in near]
    grad_wq, grad_wkv, grad_wo = call(
        place_kernel,
        "place_sums",
        [shape((width, width), f32), shape((width, 2 * width), f32), shape((width, width), f32)],
        [*near, *far],
        [
            pltpu.VMEM((4 * width, width), bf16),
            pltpu.VMEM((4 * width, width), f32),
            pltpu.SemaphoreType.DMA((2 << len(pair + square),)),
        ],
        stored=True,
    )
    return grad_features, grad_wq, grad_wkv, grad_wo, rider[:virt_rows]


def solution(mesh):
    placed = (
        P(("dom", "rows"), None),
        P(("dom", "rows"), None),
        P(),
        P(),
        P(),
        P(),
        P(("dom", "rows"), None),
        P(("dom", "rows"), None),
        P(("dom", "rows"), None),
    )
    return jax.shard_map(
        shards,
        mesh=mesh,
        in_specs=placed,
        out_specs=(P(("dom", "rows"), None), P(), P(), P(), P()),
        check_vma=False,
    )
```

```python
import functools
import math

import jax
import jax.numpy as jnp
from jax import lax
from jax.experimental import pallas as pl
from jax.experimental.pallas import tpu as pltpu
from jax.sharding import PartitionSpec as P

HEADS = 8
TILE = 128
ROW_PACK = 16
NEGATIVE_FILL = -1e30
VMEM_BYTES = 24 * 1024 * 1024
LANES = 128


def f32_dot(left, right):
    return jnp.dot(left, right, preferred_element_type=jnp.float32)


def rows_contracted(left, right):
    return lax.dot_general(
        left, right, (((0,), (0,)), ((), ())), preferred_element_type=jnp.float32
    )


def times_transposed(left, right):
    return lax.dot_general(
        left, right, (((1,), (1,)), ((), ())), preferred_element_type=jnp.float32
    )


def rounded(value):
    return value.astype(jnp.bfloat16)


CORES = (0, 1)


def bits_of(size, first=1):
    return [1 << i for i in range(size.bit_length() - 1) if 1 << i >= first]


def exchange_plan():
    dom_size, rows_size = lax.axis_size("dom"), lax.axis_size("rows")
    pair, square = [(2, 0)], [(1, 0), (0, 2)]
    rest = [(bit, 0) for bit in bits_of(dom_size, 4)] + [(0, bit) for bit in bits_of(rows_size, 4)]
    return pair, square, rest


def partner_masks(block):
    masks = []
    for digit in range(1 << len(block)):
        chosen = [mask for i, mask in enumerate(block) if digit >> i & 1]
        masks.append((sum(mask[0] for mask in chosen), sum(mask[1] for mask in chosen)))
    return masks


def farthest_first(count):
    return sorted(range(1, count), key=lambda digit: (-digit.bit_count(), -digit))


def own_digit():
    pair, square, _ = exchange_plan()
    digit = 0
    for i, (dom_mask, rows_mask) in enumerate(pair + square):
        own = (lax.axis_index("dom") & dom_mask) | (lax.axis_index("rows") & rows_mask)
        digit += jnp.where(own != 0, 1 << i, 0)
    return digit


def swapped(block, dom_mask, rows_mask):
    dom_size, rows_size = lax.axis_size("dom"), lax.axis_size("rows")
    route = [
        (a * rows_size + b, (a ^ dom_mask) * rows_size + (b ^ rows_mask))
        for a in range(dom_size)
        for b in range(rows_size)
    ]
    return lax.ppermute(block, ("dom", "rows"), route)


def shifted(block, axis, distance):
    devices = range(lax.axis_size(axis))
    route = [((i - distance) % len(devices), i) for i in devices]
    return lax.ppermute(block, axis, route)


def paired_sum(terms):
    while len(terms) > 1:
        terms = [left + right for left, right in zip(terms[::2], terms[1::2])]
    return terms[0]


def with_rider(block, rider):
    return jnp.concatenate([rounded(block), rounded(rider)], axis=0)


def added(keep, rider, arrived):
    rows = keep.shape[0]
    riders = [rider] + [arrived[at][rows:].astype(jnp.float32) for at in sorted(arrived)]
    for block in arrived.values():
        keep = keep + block[:rows].astype(jnp.float32)
    return keep, paired_sum(riders)


def scattered(keep, rider, bits):
    masks = partner_masks(bits)
    rows = keep.shape[0] // len(masks)
    parts = [keep[at * rows : (at + 1) * rows] for at in range(len(masks))]
    messages = {at: with_rider(parts[at], rider) for at in farthest_first(len(masks))}
    arrived = {at: swapped(message, *masks[at]) for at, message in messages.items()}
    return added(parts[0], rounded(rider).astype(jnp.float32), arrived)


def handed_on(direct, through):
    rows = direct[0].shape[0]
    arrived = [direct[0], through]
    for at in reversed(range(1, len(direct))):
        message = jnp.concatenate([direct[at], through[at * rows : (at + 1) * rows]], axis=0)
        arrived.append(swapped(message, 2 * at, 0))
    return arrived


def listed_rows(send_ref, row_count):
    dom_size, per_peer = send_ref.shape
    slots = dom_size * per_peer
    slot = lax.broadcasted_iota(jnp.int32, (slots, per_peer), 0)
    place = lax.broadcasted_iota(jnp.int32, (slots, per_peer), 1)
    peer = (slot // per_peer) ^ lax.axis_index("dom")
    listed = jnp.zeros((slots, per_peer), jnp.int32)
    for at in range(dom_size):
        listed += jnp.where((peer == at) & (place == slot % per_peer), send_ref[at : at + 1, :], 0)
    column = jnp.sum(listed, axis=1, keepdims=True)
    rows = lax.broadcasted_iota(jnp.int32, (slots, row_count), 1)
    return jnp.where(column == rows, 1.0, 0.0).astype(jnp.bfloat16)


def fetch(pairs, sems):
    copies = [
        pltpu.make_async_copy(source, target, sems.at[at])
        for at, (source, target) in enumerate(pairs)
    ]
    for copy in copies:
        copy.start()
    return copies


def store_blocks(rows, through_ref, direct_refs):
    size = direct_refs[0].shape[0]
    for at, out_ref in enumerate(direct_refs):
        out_ref[...] = rows[2 * at * size : (2 * at + 1) * size]
        through_ref[at * size : (at + 1) * size] = rows[(2 * at + 1) * size : (2 * at + 2) * size]


def pick_kernel(feat_hbm, send_hbm, halo_ref, chosen_ref, through_ref, *refs):
    direct_refs, (feat_ref, send_ref, sems) = refs[:-3], refs[-3:]
    copies = fetch([(send_hbm, send_ref), (feat_hbm, feat_ref)], sems)
    copies[0].wait()
    chosen_ref[...] = listed_rows(send_ref, feat_ref.shape[0])
    copies[1].wait()
    halo_ref[...] = feat_ref[feat_ref.shape[0] - halo_ref.shape[0] :]
    store_blocks(rounded(f32_dot(chosen_ref[...], feat_ref[...])), through_ref, direct_refs)


def prepare_kernel(
    per_peer,
    feat_hbm,
    og_hbm,
    wq_hbm,
    wkv_hbm,
    wo_hbm,
    virt_hbm,
    nbr_hbm,
    exp_hbm,
    og_ref,
    wq_ref,
    wkv_ref,
    featt_ref,
    qt_ref,
    odt_ref,
    kv_ref,
    kvt_ref,
    local_bias_ref,
    far_bias_ref,
    feat_ref,
    wo_ref,
    virt_ref,
    nbr_ref,
    exp_ref,
    sems,
):
    nbr_copy, exp_copy, feat_copy, virt_copy, wq_copy, wkv_copy, og_copy, wo_copy = fetch(
        [
            (nbr_hbm, nbr_ref),
            (exp_hbm, exp_ref),
            (feat_hbm, feat_ref),
            (virt_hbm, virt_ref),
            (wq_hbm, wq_ref),
            (wkv_hbm, wkv_ref),
            (og_hbm, og_ref),
            (wo_hbm, wo_ref),
        ],
        sems,
    )
    row_count, width = feat_ref.shape
    window = local_bias_ref.shape[0]
    far = far_bias_ref.shape[0]
    virt_rows = virt_ref.shape[0]
    padded = kv_ref.shape[0] - row_count
    slots = far - padded
    scale = 1.0 / math.sqrt(width // HEADS)

    def multiplicity(key_rows, named):
        position = lax.broadcasted_iota(jnp.int32, (key_rows, row_count), 0)
        count = jnp.zeros((key_rows, row_count), jnp.float32)
        for at in range(named.shape[0]):
            count += jnp.where(named[at : at + 1, :] == position, 1.0, 0.0)
        return count

    nbr_copy.wait()
    local_bias_ref[...] = jnp.where(multiplicity(window, nbr_ref) > 0.0, 0.0, NEGATIVE_FILL)
    exp_copy.wait()
    expander = exp_ref[...]
    expander = ((expander // per_peer) ^ lax.axis_index("dom")) * per_peer + expander % per_peer
    named_times = multiplicity(slots, expander)
    slot_bias = jnp.full((slots, row_count), NEGATIVE_FILL, jnp.float32)
    for times in range(1, exp_ref.shape[0] + 1):
        slot_bias = jnp.where(named_times == float(times), math.log(times) / scale, slot_bias)
    far_bias_ref[:slots] = slot_bias
    virt_row = lax.broadcasted_iota(jnp.int32, (padded, row_count), 0)
    far_bias_ref[slots:] = jnp.where(virt_row < virt_rows, 0.0, NEGATIVE_FILL)

    feat_copy.wait()
    featt_ref[:, :row_count] = feat_ref[...].T
    virt_copy.wait()
    virt = jnp.concatenate(
        [virt_ref[...], jnp.zeros((padded - virt_rows, width), jnp.bfloat16)], axis=0
    )
    featt_ref[:, row_count:] = virt.T
    wq_copy.wait()
    qt_ref[...] = rounded(rows_contracted(wq_ref[...], featt_ref[:, :row_count]))
    wkv_copy.wait()
    kv_ref[:row_count] = rounded(f32_dot(feat_ref[...], wkv_ref[...]))
    kv_ref[row_count:] = rounded(f32_dot(virt, wkv_ref[...]))
    kvt_ref[...] = kv_ref[...].T
    og_copy.wait()
    wo_copy.wait()
    odt_ref[...] = rounded(times_transposed(wo_ref[...], og_ref[...]))


def attend_kernel(
    factor,
    per_peer,
    dom_size,
    *refs,
):
    count = dom_size // 2 + 1
    piece_refs, halo_ref, refs = refs[:count], refs[count], refs[count + 1 :]
    og_ref, wq_ref, wkv_ref, featt_ref, qt_ref, odt_ref, own_kv_ref, own_kvt_ref = refs[:8]
    local_bias_ref, far_bias_ref, send_ref, rider_ref = refs[8:12]
    extt_ref, gqt_ref, gkvt_ref, ot_ref, slot_ref, kv_ref, kvt_ref = refs[12:]
    width, row_count = qt_ref.shape
    tile = halo_ref.shape[0]
    tile_count = row_count // tile
    slots = dom_size * per_peer
    near = tile + row_count
    virt_at = near + slots
    head_dim = width // HEADS
    scale = 1.0 / math.sqrt(head_dim)

    kv_ref[tile:near] = own_kv_ref[:row_count]
    kv_ref[virt_at:] = own_kv_ref[row_count:]
    kvt_ref[:, tile:near] = own_kvt_ref[:, :row_count]
    kvt_ref[:, virt_at:] = own_kvt_ref[:, row_count:]
    extt_ref[:, tile:near] = featt_ref[:, :row_count]
    extt_ref[:, virt_at:] = featt_ref[:, row_count:]
    slot_ref[:per_peer] = piece_refs[0][...]
    slot_ref[per_peer : 2 * per_peer] = piece_refs[1][:per_peer]
    for at, piece_ref in enumerate(piece_refs[:1:-1], 1):
        slot_ref[2 * at * per_peer : (2 * at + 2) * per_peer] = piece_ref[...]
    for rows, source_ref in ((slice(0, tile), halo_ref), (slice(near, virt_at), slot_ref)):
        extt_ref[:, rows] = source_ref[...].T
        kv_ref[rows] = rounded(f32_dot(source_ref[...], wkv_ref[...]))
        kvt_ref[:, rows] = kv_ref[rows].T

    def tiles(of):
        return jnp.concatenate([of(t, slice(t * tile, (t + 1) * tile)) for t in range(tile_count)], 1)

    def bounds(head):
        low, high = head * head_dim, (head + 1) * head_dim
        return low, high, low // LANES * LANES, min(-(-high // LANES) * LANES, width)

    def products(head):
        low, high, first, last = bounds(head)
        column = lax.broadcasted_iota(jnp.int32, (last - first, row_count), 0) + first
        of_head = (column >= low) & (column < high)
        out = []
        for rows_ref, start in ((qt_ref, 0), (odt_ref, width)):
            operand = jnp.where(of_head, rows_ref[first:last, :], 0)
            every = f32_dot(kv_ref[:, start + first : start + last], operand)
            out.append(tiles(lambda t, lanes: every[t * tile : (t + 2) * tile, lanes]))
            out.append(every[near:])
        return out

    def weights(s_local, s_far, dp_local, dp_far):
        s_local += local_bias_ref[...]
        s_far += far_bias_ref[...]
        peak = jnp.maximum(
            jnp.max(s_local, axis=0, keepdims=True), jnp.max(s_far, axis=0, keepdims=True)
        )
        exponent_scale = scale * math.log2(math.e)
        e_local = jnp.exp2((s_local - peak) * exponent_scale)
        e_far = jnp.exp2((s_far - peak) * exponent_scale)
        total = jnp.sum(e_local, axis=0, keepdims=True) + jnp.sum(e_far, axis=0, keepdims=True)
        inverse = 1.0 / total
        p_local = e_local * inverse
        p_far = e_far * inverse
        delta = jnp.sum(p_local * dp_local, axis=0, keepdims=True) + jnp.sum(
            p_far * dp_far, axis=0, keepdims=True
        )
        ds_local = rounded(p_local * (dp_local - delta))
        ds_far = rounded(p_far * (dp_far - delta))
        return rounded(p_local), rounded(p_far), ds_local, ds_far

    def outputs(head, pb_local, pb_far, ds_local, ds_far):
        low, high, _, _ = bounds(head)

        def to_queries(start, local, beyond):
            rows = slice(start + low, start + high)
            near_part = tiles(
                lambda t, lanes: f32_dot(kvt_ref[rows, t * tile : (t + 2) * tile], local[:, lanes])
            )
            return near_part + f32_dot(kvt_ref[rows, near:], beyond)

        def to_keys(start, operand, local, beyond, factor):
            rows = slice(start + low, start + high)
            parts = []
            carried = None
            for t in range(tile_count):
                lanes = slice(t * tile, (t + 1) * tile)
                window = times_transposed(operand[:, lanes], local[:, lanes])
                previous = window[:, :tile]
                parts.append(previous if carried is None else previous + carried)
                carried = window[:, tile:]
            parts.append(carried)
            parts.append(times_transposed(operand, beyond))
            gathered = jnp.concatenate(parts, axis=1)
            gkvt_ref[rows] = rounded(gathered if factor is None else gathered * factor)

        ot_ref[low:high] = rounded(to_queries(width, pb_local, pb_far))
        gqt_ref[low:high] = rounded(to_queries(0, ds_local, ds_far) * scale)
        to_keys(0, qt_ref[low:high], ds_local, ds_far, scale)
        to_keys(width, odt_ref[low:high], pb_local, pb_far, None)

    coming = products(0)
    done = None
    for head in range(HEADS):
        now = coming
        if head + 1 < HEADS:
            coming = products(head + 1)
        if done is not None:
            outputs(head - 1, *done)
        done = weights(*now)
    outputs(HEADS - 1, *done)

    rider_ref[...] = f32_dot(wkv_ref[...], gkvt_ref[:, virt_at:]).T * factor
    weight_sums(
        1 - lax.axis_index("rows") % 2, send_ref, extt_ref, gqt_ref, gkvt_ref, ot_ref, og_ref, factor
    )
    send_ref[2 * width :] = rounded(rider_ref[...])


def weight_sums(core, out_ref, extt_ref, gqt_ref, gkvt_ref, ot_ref, og_ref, factor):
    width, row_count = gqt_ref.shape
    held = own_digit()
    pair, square, _ = exchange_plan()
    rows = 2 * width >> len(pair + square)

    def write(at, total):
        total = (total * factor).astype(out_ref.dtype)
        for start in range(0, width, rows):
            piece = (at * width + start) // rows
            offset = pl.multiple_of((piece ^ held) * rows, ROW_PACK)
            out_ref[pl.ds(offset, rows), :] = total[start : start + rows]

    @pl.when(core == 0)
    def _():
        own = slice(TILE, TILE + row_count)
        write(0, times_transposed(extt_ref[:, own], gqt_ref[...]))
        write(1, times_transposed(extt_ref[...], gkvt_ref[:width]))

    @pl.when(core == 1)
    def _():
        write(0, times_transposed(extt_ref[...], gkvt_ref[width:]))
        write(1, f32_dot(ot_ref[...], og_ref[...]))


def finish_kernel(factor, og_ref, wq_ref, wkv_ref, extt_ref, gqt_ref, gkvt_ref, ot_ref, *refs):
    gf_ref, halo_feat_ref, keep_ref = refs[:3]
    pair_refs = refs[3:]
    width, row_count = gqt_ref.shape
    near = TILE + row_count
    step = pair_refs[0].shape[0]
    slots = step * len(pair_refs)
    weight_sums(
        lax.axis_index("rows") % 2, keep_ref, extt_ref, gqt_ref, gkvt_ref, ot_ref, og_ref, factor
    )
    by_feature = f32_dot(wkv_ref[...], gkvt_ref[:, : near + slots])
    own = by_feature[:, TILE:near] + f32_dot(wq_ref[...], gqt_ref[...])
    gf_ref[...] = own.T
    halo_feat_ref[...] = rounded(by_feature[:, :TILE].T)
    slot_feat = rounded(by_feature[:, near:].T)
    for at, out_ref in enumerate(pair_refs):
        out_ref[...] = slot_feat[at * step : (at + 1) * step]


def place_kernel(*refs):
    part_refs, (gq_hbm, gkv_hbm, go_hbm, all_ref, out_ref, sems) = refs[:-6], refs[-6:]
    width = gq_hbm.shape[0]
    pair, square, _ = exchange_plan()
    half = 1 << len(pair + square)
    rows = 2 * width // half
    step = part_refs[0].shape[0]
    for at, part_ref in enumerate(part_refs):
        all_ref[at * step : (at + 1) * step] = part_ref[...]
    held = own_digit() + (lax.axis_index("rows") % 2) * half
    copies = []
    for at in range(2 * half):
        start = at * rows
        piece = slice(start, start + rows)
        offset = pl.multiple_of((held ^ at) * rows, ROW_PACK)
        out_ref[piece] = all_ref[pl.ds(offset, rows), :].astype(jnp.float32)
        rows_out = pl.ds(start % width, rows)
        which = start // width
        if which == 0:
            target = gq_hbm.at[rows_out]
        elif which == 3:
            target = go_hbm.at[rows_out]
        else:
            target = gkv_hbm.at[rows_out, pl.ds((which - 1) * width, width)]
        copies.append(pltpu.make_async_copy(out_ref.at[piece], target, sems.at[at]))
        copies[-1].start()
    for copy in copies:
        copy.wait()


def return_kernel(gf_ref, chosen_ref, halo_ref, own_ref, through_ref, *refs):
    far_refs, out_ref = refs[:-1], refs[-1]
    row_count = gf_ref.shape[0]
    tile = halo_ref.shape[0]
    per_peer = own_ref.shape[0] // 2
    returned = []
    for at, even_ref in enumerate([own_ref, *far_refs[::-1]]):
        returned += [even_ref[:per_peer], through_ref[at * per_peer : (at + 1) * per_peer]]
    total = gf_ref[...] + rows_contracted(chosen_ref[...], jnp.concatenate(returned, axis=0))
    out_ref[: row_count - tile] = total[: row_count - tile]
    out_ref[row_count - tile :] = total[row_count - tile :] + halo_ref[...].astype(jnp.float32)


def call(kernel, name, outs, args, scratch=(), fetched=0, flops=0, stored=False):
    spaces = [pltpu.HBM] * fetched
    spaces += [pltpu.VMEM] * (len(args) - len(spaces))
    moved = sum(x.size * x.dtype.itemsize for x in list(args) + list(outs))
    scratch = list(scratch)
    if fetched:
        scratch.append(pltpu.SemaphoreType.DMA((fetched,)))
    constrained = [
        pltpu.with_memory_space_constraint(x, pltpu.HBM) if space is pltpu.HBM else x
        for x, space in zip(args, spaces)
    ]
    return pl.pallas_call(
        kernel,
        out_shape=outs,
        in_specs=[pl.BlockSpec(memory_space=space) for space in spaces],
        out_specs=[pl.BlockSpec(memory_space=pl.ANY if stored else pltpu.VMEM)] * len(outs),
        scratch_shapes=scratch,
        compiler_params=pltpu.CompilerParams(vmem_limit_bytes=VMEM_BYTES),
        cost_estimate=pl.CostEstimate(flops=flops, bytes_accessed=moved, transcendentals=0),
        name=name,
    )(*constrained)


def shards(features, out_grad, w_query, w_keyval, w_out, virtual, local_nbr, expander, send_rows):
    row_count, width = features.shape
    dom_size, per_peer = send_rows.shape
    slots = dom_size * per_peer
    virt_rows = virtual.shape[0]
    padded = ROW_PACK * -(-virt_rows // ROW_PACK)
    ext_rows = TILE + row_count + slots + padded
    nodes = row_count * lax.axis_size("dom") * lax.axis_size("rows")
    pair, square, rest = exchange_plan()
    bf16, f32 = jnp.bfloat16, jnp.float32
    shape = jax.ShapeDtypeStruct

    halo, chosen, through, *direct = call(
        pick_kernel,
        "pick_rows",
        [shape((TILE, width), bf16), shape((slots, row_count), bf16)]
        + [shape((slots // 2, width), bf16)]
        + [shape((per_peer, width), bf16)] * (dom_size // 2),
        [features, send_rows],
        [pltpu.VMEM(features.shape, bf16), pltpu.VMEM(send_rows.shape, jnp.int32)],
        fetched=2,
    )
    through = swapped(through, 1, 0)
    prepared = call(
        functools.partial(prepare_kernel, per_peer),
        "prepare",
        [
            shape(out_grad.shape, bf16),
            shape(w_query.shape, bf16),
            shape(w_keyval.shape, bf16),
            shape((width, row_count + padded), bf16),
            shape((width, row_count), bf16),
            shape((width, row_count), bf16),
            shape((row_count + padded, 2 * width), bf16),
            shape((2 * width, row_count + padded), bf16),
            shape((2 * TILE, row_count), f32),
            shape((slots + padded, row_count), f32),
        ],
        [features, out_grad, w_query, w_keyval, w_out, virtual, local_nbr.T, expander.T],
        [
            pltpu.VMEM(features.shape, bf16),
            pltpu.VMEM(w_out.shape, bf16),
            pltpu.VMEM(virtual.shape, bf16),
            pltpu.VMEM(local_nbr.shape[::-1], jnp.int32),
            pltpu.VMEM(expander.shape[::-1], jnp.int32),
        ],
        fetched=8,
        flops=10 * row_count * width * width,
    )
    (through, halo), _ = lax.optimization_barrier(((through, halo), prepared[0]))
    arrived = handed_on(direct, through)
    halo = shifted(halo, "rows", 1)
    message, rider, *gradients = call(
        functools.partial(attend_kernel, nodes**-0.5, per_peer, dom_size),
        "attend",
        [
            shape((2 * width + padded, width), bf16),
            shape((padded, width), f32),
            shape((width, ext_rows), bf16),
            shape((width, row_count), bf16),
            shape((2 * width, ext_rows), bf16),
            shape((width, row_count), bf16),
        ],
        [*arrived, halo, *prepared],
        [
            pltpu.VMEM((slots, width), bf16),
            pltpu.VMEM((ext_rows, 2 * width), bf16),
            pltpu.VMEM((2 * width, ext_rows), bf16),
        ],
        flops=28 * ext_rows * width * width,
    )
    message = swapped(message, *CORES)
    own_feat, halo_feat, keep, *pairs = call(
        functools.partial(finish_kernel, nodes**-0.5),
        "finish",
        [shape((row_count, width), f32), shape((TILE, width), bf16), shape((2 * width, width), f32)]
        + [shape((2 * per_peer, width), bf16)] * (dom_size // 2),
        [*prepared[:3], *gradients],
        flops=6 * ext_rows * width * width,
    )

    keep, rider = added(keep, rounded(rider).astype(f32), {1: message})
    rider = rider[: -(-virt_rows // 8) * 8]
    pairs, _ = lax.optimization_barrier((pairs, keep))
    returned = [swapped(pairs[at], 2 * at, 0) for at in reversed(range(1, dom_size // 2))]
    keep, rider = scattered(keep, rider, square)
    keep, *returned[:-1] = lax.optimization_barrier((keep, *returned[:-1]))
    keep, rider = scattered(keep, rider, pair)
    (returned, halo_feat), _ = lax.optimization_barrier(((returned, halo_feat), keep))
    through = swapped(jnp.concatenate([x[per_peer:] for x in [pairs[0]] + returned[::-1]]), 1, 0)
    halo_back = shifted(halo_feat, "rows", -1)
    for mask in rest:
        message = swapped(with_rider(keep, rider), *mask)
        keep, rider = rounded(keep).astype(f32), rounded(rider).astype(f32)
        keep, rider = added(keep, rider, {1: message})
    (grad_features,) = call(
        return_kernel,
        "return_rows",
        [shape((row_count, width), f32)],
        [own_feat, chosen, halo_back, pairs[0], through, *returned],
    )

    held = rounded(keep)
    held = jnp.concatenate([held, swapped(held, *pair[0])], axis=0)
    held, grad_features = lax.optimization_barrier((held, grad_features))
    arrived = [swapped(held, *masks) for masks in partner_masks(square)[1:]]
    near = [held, *arrived]
    far = [swapped(part, *CORES) for part in near]
    grad_wq, grad_wkv, grad_wo = call(
        place_kernel,
        "place_sums",
        [shape((width, width), f32), shape((width, 2 * width), f32), shape((width, width), f32)],
        [*near, *far],
        [
            pltpu.VMEM((4 * width, width), bf16),
            pltpu.VMEM((4 * width, width), f32),
            pltpu.SemaphoreType.DMA((2 << len(pair + square),)),
        ],
        stored=True,
    )
    return grad_features, grad_wq, grad_wkv, grad_wo, rider[:virt_rows]


def solution(mesh):
    placed = (
        P(("dom", "rows"), None),
        P(("dom", "rows"), None),
        P(),
        P(),
        P(),
        P(),
        P(("dom", "rows"), None),
        P(("dom", "rows"), None),
        P(("dom", "rows"), None),
    )
    return jax.shard_map(
        shards,
        mesh=mesh,
        in_specs=placed,
        out_specs=(P(("dom", "rows"), None), P(), P(), P(), P()),
        check_vma=False,
    )
```

```python
import functools
import math

import jax
import jax.numpy as jnp
from jax import lax
from jax.experimental import pallas as pl
from jax.experimental.pallas import tpu as pltpu
from jax.sharding import PartitionSpec as P

HEADS = 8
TILE = 128
ROW_PACK = 16
NEGATIVE_FILL = -1e30
VMEM_BYTES = 24 * 1024 * 1024
LANES = 128


def f32_dot(left, right):
    return jnp.dot(left, right, preferred_element_type=jnp.float32)


def rows_contracted(left, right):
    return lax.dot_general(
        left, right, (((0,), (0,)), ((), ())), preferred_element_type=jnp.float32
    )


def times_transposed(left, right):
    return lax.dot_general(
        left, right, (((1,), (1,)), ((), ())), preferred_element_type=jnp.float32
    )


def rounded(value):
    return value.astype(jnp.bfloat16)


CORES = (0, 1)


def bits_of(size, first=1):
    return [1 << i for i in range(size.bit_length() - 1) if 1 << i >= first]


def exchange_plan():
    dom_size, rows_size = lax.axis_size("dom"), lax.axis_size("rows")
    square = [(1, 0), (0, 2)]
    rest = [(bit, 0) for bit in bits_of(dom_size, 2)] + [(0, bit) for bit in bits_of(rows_size, 4)]
    return square, rest


def partner_masks(block):
    masks = []
    for digit in range(1 << len(block)):
        chosen = [mask for i, mask in enumerate(block) if digit >> i & 1]
        masks.append((sum(mask[0] for mask in chosen), sum(mask[1] for mask in chosen)))
    return masks


def farthest_first(count):
    return sorted(range(1, count), key=lambda digit: (-digit.bit_count(), -digit))


def own_digit():
    square, _ = exchange_plan()
    digit = 0
    for i, (dom_mask, rows_mask) in enumerate(square):
        own = (lax.axis_index("dom") & dom_mask) | (lax.axis_index("rows") & rows_mask)
        digit += jnp.where(own != 0, 1 << i, 0)
    return digit


def swapped(block, dom_mask, rows_mask):
    dom_size, rows_size = lax.axis_size("dom"), lax.axis_size("rows")
    route = [
        (a * rows_size + b, (a ^ dom_mask) * rows_size + (b ^ rows_mask))
        for a in range(dom_size)
        for b in range(rows_size)
    ]
    return lax.ppermute(block, ("dom", "rows"), route)


def shifted(block, axis, distance):
    devices = range(lax.axis_size(axis))
    route = [((i - distance) % len(devices), i) for i in devices]
    return lax.ppermute(block, axis, route)


def paired_sum(terms):
    while len(terms) > 1:
        terms = [left + right for left, right in zip(terms[::2], terms[1::2])]
    return terms[0]


def with_rider(block, rider):
    return jnp.concatenate([rounded(block), rounded(rider)], axis=0)


def added(keep, rider, arrived):
    rows = keep.shape[0]
    riders = [rider] + [arrived[at][rows:].astype(jnp.float32) for at in sorted(arrived)]
    for block in arrived.values():
        keep = keep + block[:rows].astype(jnp.float32)
    return keep, paired_sum(riders)


def scattered(keep, rider, bits):
    masks = partner_masks(bits)
    rows = keep.shape[0] // len(masks)
    parts = [keep[at * rows : (at + 1) * rows] for at in range(len(masks))]
    messages = {at: with_rider(parts[at], rider) for at in farthest_first(len(masks))}
    arrived = {at: swapped(message, *masks[at]) for at, message in messages.items()}
    return added(parts[0], rounded(rider).astype(jnp.float32), arrived)


def handed_on(direct, through):
    rows = direct[0].shape[0]
    arrived = [direct[0], through]
    for at in reversed(range(1, len(direct))):
        message = jnp.concatenate([direct[at], through[at * rows : (at + 1) * rows]], axis=0)
        arrived.append(swapped(message, 2 * at, 0))
    return arrived


def listed_rows(send_ref, row_count):
    dom_size, per_peer = send_ref.shape
    slots = dom_size * per_peer
    slot = lax.broadcasted_iota(jnp.int32, (slots, per_peer), 0)
    place = lax.broadcasted_iota(jnp.int32, (slots, per_peer), 1)
    peer = (slot // per_peer) ^ lax.axis_index("dom")
    listed = jnp.zeros((slots, per_peer), jnp.int32)
    for at in range(dom_size):
        listed += jnp.where((peer == at) & (place == slot % per_peer), send_ref[at : at + 1, :], 0)
    column = jnp.sum(listed, axis=1, keepdims=True)
    rows = lax.broadcasted_iota(jnp.int32, (slots, row_count), 1)
    return jnp.where(column == rows, 1.0, 0.0).astype(jnp.bfloat16)


def fetch(pairs, sems):
    copies = [
        pltpu.make_async_copy(source, target, sems.at[at])
        for at, (source, target) in enumerate(pairs)
    ]
    for copy in copies:
        copy.start()
    return copies


def store_blocks(rows, through_ref, direct_refs):
    size = direct_refs[0].shape[0]
    for at, out_ref in enumerate(direct_refs):
        out_ref[...] = rows[2 * at * size : (2 * at + 1) * size]
        through_ref[at * size : (at + 1) * size] = rows[(2 * at + 1) * size : (2 * at + 2) * size]


def pick_kernel(feat_hbm, send_hbm, halo_ref, chosen_ref, through_ref, *refs):
    direct_refs, (feat_ref, send_ref, sems) = refs[:-3], refs[-3:]
    copies = fetch([(send_hbm, send_ref), (feat_hbm, feat_ref)], sems)
    copies[0].wait()
    chosen_ref[...] = listed_rows(send_ref, feat_ref.shape[0])
    copies[1].wait()
    halo_ref[...] = feat_ref[feat_ref.shape[0] - halo_ref.shape[0] :]
    store_blocks(rounded(f32_dot(chosen_ref[...], feat_ref[...])), through_ref, direct_refs)


def prepare_kernel(
    per_peer,
    feat_hbm,
    og_hbm,
    wq_hbm,
    wkv_hbm,
    wo_hbm,
    virt_hbm,
    nbr_hbm,
    exp_hbm,
    og_ref,
    wq_ref,
    wkv_ref,
    featt_ref,
    qt_ref,
    odt_ref,
    kv_ref,
    kvt_ref,
    local_bias_ref,
    far_bias_ref,
    feat_ref,
    wo_ref,
    virt_ref,
    nbr_ref,
    exp_ref,
    sems,
):
    nbr_copy, exp_copy, feat_copy, virt_copy, wq_copy, wkv_copy, og_copy, wo_copy = fetch(
        [
            (nbr_hbm, nbr_ref),
            (exp_hbm, exp_ref),
            (feat_hbm, feat_ref),
            (virt_hbm, virt_ref),
            (wq_hbm, wq_ref),
            (wkv_hbm, wkv_ref),
            (og_hbm, og_ref),
            (wo_hbm, wo_ref),
        ],
        sems,
    )
    row_count, width = feat_ref.shape
    window = local_bias_ref.shape[0]
    far = far_bias_ref.shape[0]
    virt_rows = virt_ref.shape[0]
    padded = kv_ref.shape[0] - row_count
    slots = far - padded
    scale = 1.0 / math.sqrt(width // HEADS)

    def multiplicity(key_rows, named):
        position = lax.broadcasted_iota(jnp.int32, (key_rows, row_count), 0)
        count = jnp.zeros((key_rows, row_count), jnp.float32)
        for at in range(named.shape[0]):
            count += jnp.where(named[at : at + 1, :] == position, 1.0, 0.0)
        return count

    nbr_copy.wait()
    local_bias_ref[...] = jnp.where(multiplicity(window, nbr_ref) > 0.0, 0.0, NEGATIVE_FILL)
    exp_copy.wait()
    expander = exp_ref[...]
    expander = ((expander // per_peer) ^ lax.axis_index("dom")) * per_peer + expander % per_peer
    named_times = multiplicity(slots, expander)
    slot_bias = jnp.full((slots, row_count), NEGATIVE_FILL, jnp.float32)
    for times in range(1, exp_ref.shape[0] + 1):
        slot_bias = jnp.where(named_times == float(times), math.log(times) / scale, slot_bias)
    far_bias_ref[:slots] = slot_bias
    virt_row = lax.broadcasted_iota(jnp.int32, (padded, row_count), 0)
    far_bias_ref[slots:] = jnp.where(virt_row < virt_rows, 0.0, NEGATIVE_FILL)

    feat_copy.wait()
    featt_ref[:, :row_count] = feat_ref[...].T
    virt_copy.wait()
    virt = jnp.concatenate(
        [virt_ref[...], jnp.zeros((padded - virt_rows, width), jnp.bfloat16)], axis=0
    )
    featt_ref[:, row_count:] = virt.T
    wq_copy.wait()
    qt_ref[...] = rounded(rows_contracted(wq_ref[...], featt_ref[:, :row_count]))
    wkv_copy.wait()
    kv_ref[:row_count] = rounded(f32_dot(feat_ref[...], wkv_ref[...]))
    kv_ref[row_count:] = rounded(f32_dot(virt, wkv_ref[...]))
    kvt_ref[...] = kv_ref[...].T
    og_copy.wait()
    wo_copy.wait()
    odt_ref[...] = rounded(times_transposed(wo_ref[...], og_ref[...]))


def attend_kernel(
    factor,
    per_peer,
    dom_size,
    *refs,
):
    count = dom_size // 2 + 1
    piece_refs, halo_ref, refs = refs[:count], refs[count], refs[count + 1 :]
    og_ref, wq_ref, wkv_ref, featt_ref, qt_ref, odt_ref, own_kv_ref, own_kvt_ref = refs[:8]
    local_bias_ref, far_bias_ref, send_ref, rider_ref = refs[8:12]
    extt_ref, gqt_ref, gkvt_ref, ot_ref, slot_ref, kv_ref, kvt_ref = refs[12:]
    width, row_count = qt_ref.shape
    tile = halo_ref.shape[0]
    tile_count = row_count // tile
    slots = dom_size * per_peer
    near = tile + row_count
    virt_at = near + slots
    head_dim = width // HEADS
    scale = 1.0 / math.sqrt(head_dim)

    kv_ref[tile:near] = own_kv_ref[:row_count]
    kv_ref[virt_at:] = own_kv_ref[row_count:]
    kvt_ref[:, tile:near] = own_kvt_ref[:, :row_count]
    kvt_ref[:, virt_at:] = own_kvt_ref[:, row_count:]
    extt_ref[:, tile:near] = featt_ref[:, :row_count]
    extt_ref[:, virt_at:] = featt_ref[:, row_count:]
    slot_ref[:per_peer] = piece_refs[0][...]
    slot_ref[per_peer : 2 * per_peer] = piece_refs[1][:per_peer]
    for at, piece_ref in enumerate(piece_refs[:1:-1], 1):
        slot_ref[2 * at * per_peer : (2 * at + 2) * per_peer] = piece_ref[...]
    for rows, source_ref in ((slice(0, tile), halo_ref), (slice(near, virt_at), slot_ref)):
        extt_ref[:, rows] = source_ref[...].T
        kv_ref[rows] = rounded(f32_dot(source_ref[...], wkv_ref[...]))
        kvt_ref[:, rows] = kv_ref[rows].T

    def tiles(of):
        return jnp.concatenate([of(t, slice(t * tile, (t + 1) * tile)) for t in range(tile_count)], 1)

    def bounds(head):
        low, high = head * head_dim, (head + 1) * head_dim
        return low, high, low // LANES * LANES, min(-(-high // LANES) * LANES, width)

    def products(head):
        low, high, first, last = bounds(head)
        column = lax.broadcasted_iota(jnp.int32, (last - first, row_count), 0) + first
        of_head = (column >= low) & (column < high)
        out = []
        for rows_ref, start in ((qt_ref, 0), (odt_ref, width)):
            operand = jnp.where(of_head, rows_ref[first:last, :], 0)
            every = f32_dot(kv_ref[:, start + first : start + last], operand)
            out.append(tiles(lambda t, lanes: every[t * tile : (t + 2) * tile, lanes]))
            out.append(every[near:])
        return out

    def weights(s_local, s_far, dp_local, dp_far):
        s_local += local_bias_ref[...]
        s_far += far_bias_ref[...]
        peak = jnp.maximum(
            jnp.max(s_local, axis=0, keepdims=True), jnp.max(s_far, axis=0, keepdims=True)
        )
        exponent_scale = scale * math.log2(math.e)
        e_local = jnp.exp2((s_local - peak) * exponent_scale)
        e_far = jnp.exp2((s_far - peak) * exponent_scale)
        total = jnp.sum(e_local, axis=0, keepdims=True) + jnp.sum(e_far, axis=0, keepdims=True)
        inverse = 1.0 / total
        p_local = e_local * inverse
        p_far = e_far * inverse
        delta = jnp.sum(p_local * dp_local, axis=0, keepdims=True) + jnp.sum(
            p_far * dp_far, axis=0, keepdims=True
        )
        ds_local = rounded(p_local * (dp_local - delta))
        ds_far = rounded(p_far * (dp_far - delta))
        return rounded(p_local), rounded(p_far), ds_local, ds_far

    def outputs(head, pb_local, pb_far, ds_local, ds_far):
        low, high, _, _ = bounds(head)

        def to_queries(start, local, beyond):
            rows = slice(start + low, start + high)
            near_part = tiles(
                lambda t, lanes: f32_dot(kvt_ref[rows, t * tile : (t + 2) * tile], local[:, lanes])
            )
            return near_part + f32_dot(kvt_ref[rows, near:], beyond)

        def to_keys(start, operand, local, beyond, factor):
            rows = slice(start + low, start + high)
            parts = []
            carried = None
            for t in range(tile_count):
                lanes = slice(t * tile, (t + 1) * tile)
                window = times_transposed(operand[:, lanes], local[:, lanes])
                previous = window[:, :tile]
                parts.append(previous if carried is None else previous + carried)
                carried = window[:, tile:]
            parts.append(carried)
            parts.append(times_transposed(operand, beyond))
            gathered = jnp.concatenate(parts, axis=1)
            gkvt_ref[rows] = rounded(gathered if factor is None else gathered * factor)

        ot_ref[low:high] = rounded(to_queries(width, pb_local, pb_far))
        gqt_ref[low:high] = rounded(to_queries(0, ds_local, ds_far) * scale)
        to_keys(0, qt_ref[low:high], ds_local, ds_far, scale)
        to_keys(width, odt_ref[low:high], pb_local, pb_far, None)

    coming = products(0)
    done = None
    for head in range(HEADS):
        now = coming
        if head + 1 < HEADS:
            coming = products(head + 1)
        if done is not None:
            outputs(head - 1, *done)
        done = weights(*now)
    outputs(HEADS - 1, *done)

    rider_ref[...] = f32_dot(wkv_ref[...], gkvt_ref[:, virt_at:]).T * factor
    weight_sums(
        1 - lax.axis_index("rows") % 2, send_ref, extt_ref, gqt_ref, gkvt_ref, ot_ref, og_ref, factor
    )
    send_ref[2 * width :] = rounded(rider_ref[...])


def weight_sums(core, out_ref, extt_ref, gqt_ref, gkvt_ref, ot_ref, og_ref, factor):
    width, row_count = gqt_ref.shape
    held = own_digit()
    square, _ = exchange_plan()
    rows = 2 * width >> len(square)

    def write(at, total):
        total = (total * factor).astype(out_ref.dtype)
        for start in range(0, width, rows):
            piece = (at * width + start) // rows
            offset = pl.multiple_of((piece ^ held) * rows, ROW_PACK)
            out_ref[pl.ds(offset, rows), :] = total[start : start + rows]

    @pl.when(core == 0)
    def _():
        own = slice(TILE, TILE + row_count)
        write(0, times_transposed(extt_ref[:, own], gqt_ref[...]))
        write(1, times_transposed(extt_ref[...], gkvt_ref[:width]))

    @pl.when(core == 1)
    def _():
        write(0, times_transposed(extt_ref[...], gkvt_ref[width:]))
        write(1, f32_dot(ot_ref[...], og_ref[...]))


def finish_kernel(factor, og_ref, wq_ref, wkv_ref, extt_ref, gqt_ref, gkvt_ref, ot_ref, *refs):
    gf_ref, halo_feat_ref, keep_ref = refs[:3]
    pair_refs = refs[3:]
    width, row_count = gqt_ref.shape
    near = TILE + row_count
    step = pair_refs[0].shape[0]
    slots = step * len(pair_refs)
    weight_sums(
        lax.axis_index("rows") % 2, keep_ref, extt_ref, gqt_ref, gkvt_ref, ot_ref, og_ref, factor
    )
    by_feature = f32_dot(wkv_ref[...], gkvt_ref[:, : near + slots])
    own = by_feature[:, TILE:near] + f32_dot(wq_ref[...], gqt_ref[...])
    gf_ref[...] = own.T
    halo_feat_ref[...] = rounded(by_feature[:, :TILE].T)
    slot_feat = rounded(by_feature[:, near:].T)
    for at, out_ref in enumerate(pair_refs):
        out_ref[...] = slot_feat[at * step : (at + 1) * step]


def place_kernel(*refs):
    part_refs, (gq_hbm, gkv_hbm, go_hbm, all_ref, out_ref, sems) = refs[:-6], refs[-6:]
    width = gq_hbm.shape[0]
    square, _ = exchange_plan()
    half = 1 << len(square)
    rows = 2 * width // half
    step = part_refs[0].shape[0]
    for at, part_ref in enumerate(part_refs):
        all_ref[at * step : (at + 1) * step] = part_ref[...]
    held = own_digit() + (lax.axis_index("rows") % 2) * half
    copies = []
    for at in range(2 * half):
        start = at * rows
        piece = slice(start, start + rows)
        offset = pl.multiple_of((held ^ at) * rows, ROW_PACK)
        out_ref[piece] = all_ref[pl.ds(offset, rows), :].astype(jnp.float32)
        rows_out = pl.ds(start % width, rows)
        which = start // width
        if which == 0:
            target = gq_hbm.at[rows_out]
        elif which == 3:
            target = go_hbm.at[rows_out]
        else:
            target = gkv_hbm.at[rows_out, pl.ds((which - 1) * width, width)]
        copies.append(pltpu.make_async_copy(out_ref.at[piece], target, sems.at[at]))
        copies[-1].start()
    for copy in copies:
        copy.wait()


def return_kernel(gf_ref, chosen_ref, halo_ref, own_ref, through_ref, *refs):
    far_refs, out_ref = refs[:-1], refs[-1]
    row_count = gf_ref.shape[0]
    tile = halo_ref.shape[0]
    per_peer = own_ref.shape[0] // 2
    returned = []
    for at, even_ref in enumerate([own_ref, *far_refs[::-1]]):
        returned += [even_ref[:per_peer], through_ref[at * per_peer : (at + 1) * per_peer]]
    total = gf_ref[...] + rows_contracted(chosen_ref[...], jnp.concatenate(returned, axis=0))
    out_ref[: row_count - tile] = total[: row_count - tile]
    out_ref[row_count - tile :] = total[row_count - tile :] + halo_ref[...].astype(jnp.float32)


def call(kernel, name, outs, args, scratch=(), fetched=0, flops=0, stored=False):
    spaces = [pltpu.HBM] * fetched
    spaces += [pltpu.VMEM] * (len(args) - len(spaces))
    moved = sum(x.size * x.dtype.itemsize for x in list(args) + list(outs))
    scratch = list(scratch)
    if fetched:
        scratch.append(pltpu.SemaphoreType.DMA((fetched,)))
    constrained = [
        pltpu.with_memory_space_constraint(x, pltpu.HBM) if space is pltpu.HBM else x
        for x, space in zip(args, spaces)
    ]
    return pl.pallas_call(
        kernel,
        out_shape=outs,
        in_specs=[pl.BlockSpec(memory_space=space) for space in spaces],
        out_specs=[pl.BlockSpec(memory_space=pl.ANY if stored else pltpu.VMEM)] * len(outs),
        scratch_shapes=scratch,
        compiler_params=pltpu.CompilerParams(vmem_limit_bytes=VMEM_BYTES),
        cost_estimate=pl.CostEstimate(flops=flops, bytes_accessed=moved, transcendentals=0),
        name=name,
    )(*constrained)


def shards(features, out_grad, w_query, w_keyval, w_out, virtual, local_nbr, expander, send_rows):
    row_count, width = features.shape
    dom_size, per_peer = send_rows.shape
    slots = dom_size * per_peer
    virt_rows = virtual.shape[0]
    padded = ROW_PACK * -(-virt_rows // ROW_PACK)
    ext_rows = TILE + row_count + slots + padded
    nodes = row_count * lax.axis_size("dom") * lax.axis_size("rows")
    square, rest = exchange_plan()
    bf16, f32 = jnp.bfloat16, jnp.float32
    shape = jax.ShapeDtypeStruct

    halo, chosen, through, *direct = call(
        pick_kernel,
        "pick_rows",
        [shape((TILE, width), bf16), shape((slots, row_count), bf16)]
        + [shape((slots // 2, width), bf16)]
        + [shape((per_peer, width), bf16)] * (dom_size // 2),
        [features, send_rows],
        [pltpu.VMEM(features.shape, bf16), pltpu.VMEM(send_rows.shape, jnp.int32)],
        fetched=2,
    )
    through = swapped(through, 1, 0)
    prepared = call(
        functools.partial(prepare_kernel, per_peer),
        "prepare",
        [
            shape(out_grad.shape, bf16),
            shape(w_query.shape, bf16),
            shape(w_keyval.shape, bf16),
            shape((width, row_count + padded), bf16),
            shape((width, row_count), bf16),
            shape((width, row_count), bf16),
            shape((row_count + padded, 2 * width), bf16),
            shape((2 * width, row_count + padded), bf16),
            shape((2 * TILE, row_count), f32),
            shape((slots + padded, row_count), f32),
        ],
        [features, out_grad, w_query, w_keyval, w_out, virtual, local_nbr.T, expander.T],
        [
            pltpu.VMEM(features.shape, bf16),
            pltpu.VMEM(w_out.shape, bf16),
            pltpu.VMEM(virtual.shape, bf16),
            pltpu.VMEM(local_nbr.shape[::-1], jnp.int32),
            pltpu.VMEM(expander.shape[::-1], jnp.int32),
        ],
        fetched=8,
        flops=10 * row_count * width * width,
    )
    (through, halo), _ = lax.optimization_barrier(((through, halo), prepared[0]))
    arrived = handed_on(direct, through)
    halo = shifted(halo, "rows", 1)
    message, rider, *gradients = call(
        functools.partial(attend_kernel, nodes**-0.5, per_peer, dom_size),
        "attend",
        [
            shape((2 * width + padded, width), bf16),
            shape((padded, width), f32),
            shape((width, ext_rows), bf16),
            shape((width, row_count), bf16),
            shape((2 * width, ext_rows), bf16),
            shape((width, row_count), bf16),
        ],
        [*arrived, halo, *prepared],
        [
            pltpu.VMEM((slots, width), bf16),
            pltpu.VMEM((ext_rows, 2 * width), bf16),
            pltpu.VMEM((2 * width, ext_rows), bf16),
        ],
        flops=28 * ext_rows * width * width,
    )
    message = swapped(message, *CORES)
    own_feat, halo_feat, keep, *pairs = call(
        functools.partial(finish_kernel, nodes**-0.5),
        "finish",
        [shape((row_count, width), f32), shape((TILE, width), bf16), shape((2 * width, width), f32)]
        + [shape((2 * per_peer, width), bf16)] * (dom_size // 2),
        [*prepared[:3], *gradients],
        flops=6 * ext_rows * width * width,
    )

    keep, rider = added(keep, rounded(rider).astype(f32), {1: message})
    rider = rider[: -(-virt_rows // 8) * 8]
    pairs, _ = lax.optimization_barrier((pairs, keep))
    returned = [swapped(pairs[at], 2 * at, 0) for at in reversed(range(1, dom_size // 2))]
    keep, rider = scattered(keep, rider, square)
    keep, *returned[:-1] = lax.optimization_barrier((keep, *returned[:-1]))
    for at, mask in enumerate(rest):
        message = swapped(with_rider(keep, rider), *mask)
        keep, rider = rounded(keep).astype(f32), rounded(rider).astype(f32)
        keep, rider = added(keep, rider, {1: message})
        if at == 0:
            (returned, halo_feat), _ = lax.optimization_barrier(((returned, halo_feat), keep))
            odd = [block[per_peer:] for block in [pairs[0]] + returned[::-1]]
            through = swapped(jnp.concatenate(odd, axis=0), 1, 0)
            halo_back = shifted(halo_feat, "rows", -1)
    (grad_features,) = call(
        return_kernel,
        "return_rows",
        [shape((row_count, width), f32)],
        [own_feat, chosen, halo_back, pairs[0], through, *returned],
    )

    held = rounded(keep)
    held, grad_features = lax.optimization_barrier((held, grad_features))
    arrived = [swapped(held, *masks) for masks in partner_masks(square)[1:]]
    near = [held, *arrived]
    far = [swapped(part, *CORES) for part in near]
    grad_wq, grad_wkv, grad_wo = call(
        place_kernel,
        "place_sums",
        [shape((width, width), f32), shape((width, 2 * width), f32), shape((width, width), f32)],
        [*near, *far],
        [
            pltpu.VMEM((4 * width, width), bf16),
            pltpu.VMEM((4 * width, width), f32),
            pltpu.SemaphoreType.DMA((2 << len(square),)),
        ],
        stored=True,
    )
    return grad_features, grad_wq, grad_wkv, grad_wo, rider[:virt_rows]


def solution(mesh):
    placed = (
        P(("dom", "rows"), None),
        P(("dom", "rows"), None),
        P(),
        P(),
        P(),
        P(),
        P(("dom", "rows"), None),
        P(("dom", "rows"), None),
        P(("dom", "rows"), None),
    )
    return jax.shard_map(
        shards,
        mesh=mesh,
        in_specs=placed,
        out_specs=(P(("dom", "rows"), None), P(), P(), P(), P()),
        check_vma=False,
    )
```

```python
import functools
import math

import jax
import jax.numpy as jnp
from jax import lax
from jax.experimental import pallas as pl
from jax.experimental.pallas import tpu as pltpu
from jax.sharding import PartitionSpec as P

HEADS = 8
TILE = 128
ROW_PACK = 16
NEGATIVE_FILL = -1e30
VMEM_BYTES = 24 * 1024 * 1024
LANES = 128


def f32_dot(left, right):
    return jnp.dot(left, right, preferred_element_type=jnp.float32)


def rows_contracted(left, right):
    return lax.dot_general(
        left, right, (((0,), (0,)), ((), ())), preferred_element_type=jnp.float32
    )


def times_transposed(left, right):
    return lax.dot_general(
        left, right, (((1,), (1,)), ((), ())), preferred_element_type=jnp.float32
    )


def rounded(value):
    return value.astype(jnp.bfloat16)


CORES = (0, 1)


def bits_of(size, first=1):
    return [1 << i for i in range(size.bit_length() - 1) if 1 << i >= first]


def exchange_plan():
    dom_size, rows_size = lax.axis_size("dom"), lax.axis_size("rows")
    pair, square = [(2, 0)], [(1, 0), (0, 2)]
    rest = [(bit, 0) for bit in bits_of(dom_size, 4)] + [(0, bit) for bit in bits_of(rows_size, 4)]
    return pair, square, rest


def partner_masks(block):
    masks = []
    for digit in range(1 << len(block)):
        chosen = [mask for i, mask in enumerate(block) if digit >> i & 1]
        masks.append((sum(mask[0] for mask in chosen), sum(mask[1] for mask in chosen)))
    return masks


def farthest_first(count):
    return sorted(range(1, count), key=lambda digit: (-digit.bit_count(), -digit))


def own_digit():
    pair, square, _ = exchange_plan()
    digit = 0
    for i, (dom_mask, rows_mask) in enumerate(pair + square):
        own = (lax.axis_index("dom") & dom_mask) | (lax.axis_index("rows") & rows_mask)
        digit += jnp.where(own != 0, 1 << i, 0)
    return digit


def swapped(block, dom_mask, rows_mask):
    dom_size, rows_size = lax.axis_size("dom"), lax.axis_size("rows")
    route = [
        (a * rows_size + b, (a ^ dom_mask) * rows_size + (b ^ rows_mask))
        for a in range(dom_size)
        for b in range(rows_size)
    ]
    return lax.ppermute(block, ("dom", "rows"), route)


def shifted(block, axis, distance):
    devices = range(lax.axis_size(axis))
    route = [((i - distance) % len(devices), i) for i in devices]
    return lax.ppermute(block, axis, route)


def paired_sum(terms):
    while len(terms) > 1:
        terms = [left + right for left, right in zip(terms[::2], terms[1::2])]
    return terms[0]


def with_rider(block, rider):
    return jnp.concatenate([rounded(block), rounded(rider)], axis=0)


def added(keep, rider, arrived):
    rows = keep.shape[0]
    riders = [rider] + [arrived[at][rows:].astype(jnp.float32) for at in sorted(arrived)]
    for block in arrived.values():
        keep = keep + block[:rows].astype(jnp.float32)
    return keep, paired_sum(riders)


def scattered(keep, rider, bits):
    masks = partner_masks(bits)
    rows = keep.shape[0] // len(masks)
    parts = [keep[at * rows : (at + 1) * rows] for at in range(len(masks))]
    messages = {at: with_rider(parts[at], rider) for at in farthest_first(len(masks))}
    arrived = {at: swapped(message, *masks[at]) for at, message in messages.items()}
    return added(parts[0], rounded(rider).astype(jnp.float32), arrived)


def handed_on(direct, through):
    rows = direct[0].shape[0]
    arrived = [direct[0], through]
    for at in reversed(range(1, len(direct))):
        message = jnp.concatenate([direct[at], through[at * rows : (at + 1) * rows]], axis=0)
        arrived.append(swapped(message, 2 * at, 0))
    return arrived


def listed_rows(send_ref, row_count):
    dom_size, per_peer = send_ref.shape
    slots = dom_size * per_peer
    slot = lax.broadcasted_iota(jnp.int32, (slots, per_peer), 0)
    place = lax.broadcasted_iota(jnp.int32, (slots, per_peer), 1)
    peer = (slot // per_peer) ^ lax.axis_index("dom")
    listed = jnp.zeros((slots, per_peer), jnp.int32)
    for at in range(dom_size):
        listed += jnp.where((peer == at) & (place == slot % per_peer), send_ref[at : at + 1, :], 0)
    column = jnp.sum(listed, axis=1, keepdims=True)
    rows = lax.broadcasted_iota(jnp.int32, (slots, row_count), 1)
    return jnp.where(column == rows, 1.0, 0.0).astype(jnp.bfloat16)


def fetch(pairs, sems):
    copies = [
        pltpu.make_async_copy(source, target, sems.at[at])
        for at, (source, target) in enumerate(pairs)
    ]
    for copy in copies:
        copy.start()
    return copies


def store_blocks(rows, through_ref, direct_refs):
    size = direct_refs[0].shape[0]
    for at, out_ref in enumerate(direct_refs):
        out_ref[...] = rows[2 * at * size : (2 * at + 1) * size]
        through_ref[at * size : (at + 1) * size] = rows[(2 * at + 1) * size : (2 * at + 2) * size]


def pick_kernel(feat_hbm, send_hbm, halo_ref, chosen_ref, through_ref, *refs):
    direct_refs, (feat_ref, send_ref, sems) = refs[:-3], refs[-3:]
    copies = fetch([(send_hbm, send_ref), (feat_hbm, feat_ref)], sems)
    copies[0].wait()
    chosen_ref[...] = listed_rows(send_ref, feat_ref.shape[0])
    copies[1].wait()
    halo_ref[...] = feat_ref[feat_ref.shape[0] - halo_ref.shape[0] :]
    store_blocks(rounded(f32_dot(chosen_ref[...], feat_ref[...])), through_ref, direct_refs)


def prepare_kernel(
    per_peer,
    feat_hbm,
    og_hbm,
    wq_hbm,
    wkv_hbm,
    wo_hbm,
    virt_hbm,
    nbr_hbm,
    exp_hbm,
    og_ref,
    wq_ref,
    wkv_ref,
    featt_ref,
    qt_ref,
    odt_ref,
    kv_ref,
    kvt_ref,
    local_bias_ref,
    far_bias_ref,
    feat_ref,
    wo_ref,
    virt_ref,
    nbr_ref,
    exp_ref,
    sems,
):
    nbr_copy, exp_copy, feat_copy, virt_copy, wq_copy, wkv_copy, og_copy, wo_copy = fetch(
        [
            (nbr_hbm, nbr_ref),
            (exp_hbm, exp_ref),
            (feat_hbm, feat_ref),
            (virt_hbm, virt_ref),
            (wq_hbm, wq_ref),
            (wkv_hbm, wkv_ref),
            (og_hbm, og_ref),
            (wo_hbm, wo_ref),
        ],
        sems,
    )
    row_count, width = feat_ref.shape
    window = local_bias_ref.shape[0]
    far = far_bias_ref.shape[0]
    virt_rows = virt_ref.shape[0]
    padded = kv_ref.shape[0] - row_count
    slots = far - padded
    scale = 1.0 / math.sqrt(width // HEADS)

    def multiplicity(key_rows, named):
        position = lax.broadcasted_iota(jnp.int32, (key_rows, row_count), 0)
        count = jnp.zeros((key_rows, row_count), jnp.float32)
        for at in range(named.shape[0]):
            count += jnp.where(named[at : at + 1, :] == position, 1.0, 0.0)
        return count

    nbr_copy.wait()
    local_bias_ref[...] = jnp.where(multiplicity(window, nbr_ref) > 0.0, 0.0, NEGATIVE_FILL)
    exp_copy.wait()
    expander = exp_ref[...]
    expander = ((expander // per_peer) ^ lax.axis_index("dom")) * per_peer + expander % per_peer
    named_times = multiplicity(slots, expander)
    slot_bias = jnp.full((slots, row_count), NEGATIVE_FILL, jnp.float32)
    for times in range(1, exp_ref.shape[0] + 1):
        slot_bias = jnp.where(named_times == float(times), math.log(times) / scale, slot_bias)
    far_bias_ref[:slots] = slot_bias
    virt_row = lax.broadcasted_iota(jnp.int32, (padded, row_count), 0)
    far_bias_ref[slots:] = jnp.where(virt_row < virt_rows, 0.0, NEGATIVE_FILL)

    feat_copy.wait()
    featt_ref[:, :row_count] = feat_ref[...].T
    virt_copy.wait()
    virt = jnp.concatenate(
        [virt_ref[...], jnp.zeros((padded - virt_rows, width), jnp.bfloat16)], axis=0
    )
    featt_ref[:, row_count:] = virt.T
    wq_copy.wait()
    qt_ref[...] = rounded(rows_contracted(wq_ref[...], featt_ref[:, :row_count]))
    wkv_copy.wait()
    kv_ref[:row_count] = rounded(f32_dot(feat_ref[...], wkv_ref[...]))
    kv_ref[row_count:] = rounded(f32_dot(virt, wkv_ref[...]))
    kvt_ref[...] = kv_ref[...].T
    og_copy.wait()
    wo_copy.wait()
    odt_ref[...] = rounded(times_transposed(wo_ref[...], og_ref[...]))


def attend_kernel(
    factor,
    per_peer,
    dom_size,
    *refs,
):
    count = dom_size // 2 + 1
    piece_refs, halo_ref, refs = refs[:count], refs[count], refs[count + 1 :]
    og_ref, wq_ref, wkv_ref, featt_ref, qt_ref, odt_ref, own_kv_ref, own_kvt_ref = refs[:8]
    local_bias_ref, far_bias_ref, send_ref, rider_ref = refs[8:12]
    extt_ref, gqt_ref, gkvt_ref, ot_ref, slot_ref, kv_ref, kvt_ref = refs[12:]
    width, row_count = qt_ref.shape
    tile = halo_ref.shape[0]
    tile_count = row_count // tile
    slots = dom_size * per_peer
    near = tile + row_count
    virt_at = near + slots
    head_dim = width // HEADS
    scale = 1.0 / math.sqrt(head_dim)

    kv_ref[tile:near] = own_kv_ref[:row_count]
    kv_ref[virt_at:] = own_kv_ref[row_count:]
    kvt_ref[:, tile:near] = own_kvt_ref[:, :row_count]
    kvt_ref[:, virt_at:] = own_kvt_ref[:, row_count:]
    extt_ref[:, tile:near] = featt_ref[:, :row_count]
    extt_ref[:, virt_at:] = featt_ref[:, row_count:]
    slot_ref[:per_peer] = piece_refs[0][...]
    slot_ref[per_peer : 2 * per_peer] = piece_refs[1][:per_peer]
    for at, piece_ref in enumerate(piece_refs[:1:-1], 1):
        slot_ref[2 * at * per_peer : (2 * at + 2) * per_peer] = piece_ref[...]
    for rows, source_ref in ((slice(0, tile), halo_ref), (slice(near, virt_at), slot_ref)):
        extt_ref[:, rows] = source_ref[...].T
        kv_ref[rows] = rounded(f32_dot(source_ref[...], wkv_ref[...]))
        kvt_ref[:, rows] = kv_ref[rows].T

    def tiles(of):
        return jnp.concatenate([of(t, slice(t * tile, (t + 1) * tile)) for t in range(tile_count)], 1)

    def bounds(head):
        low, high = head * head_dim, (head + 1) * head_dim
        return low, high, low // LANES * LANES, min(-(-high // LANES) * LANES, width)

    def products(head):
        low, high, first, last = bounds(head)
        column = lax.broadcasted_iota(jnp.int32, (last - first, row_count), 0) + first
        of_head = (column >= low) & (column < high)
        out = []
        for rows_ref, start in ((qt_ref, 0), (odt_ref, width)):
            operand = jnp.where(of_head, rows_ref[first:last, :], 0)
            every = f32_dot(kv_ref[:, start + first : start + last], operand)
            out.append(tiles(lambda t, lanes: every[t * tile : (t + 2) * tile, lanes]))
            out.append(every[near:])
        return out

    def weights(s_local, s_far, dp_local, dp_far):
        s_local += local_bias_ref[...]
        s_far += far_bias_ref[...]
        peak = jnp.maximum(
            jnp.max(s_local, axis=0, keepdims=True), jnp.max(s_far, axis=0, keepdims=True)
        )
        exponent_scale = scale * math.log2(math.e)
        e_local = jnp.exp2((s_local - peak) * exponent_scale)
        e_far = jnp.exp2((s_far - peak) * exponent_scale)
        total = jnp.sum(e_local, axis=0, keepdims=True) + jnp.sum(e_far, axis=0, keepdims=True)
        inverse = 1.0 / total
        p_local = e_local * inverse
        p_far = e_far * inverse
        delta = jnp.sum(p_local * dp_local, axis=0, keepdims=True) + jnp.sum(
            p_far * dp_far, axis=0, keepdims=True
        )
        ds_local = rounded(p_local * (dp_local - delta))
        ds_far = rounded(p_far * (dp_far - delta))
        return rounded(p_local), rounded(p_far), ds_local, ds_far

    def outputs(head, pb_local, pb_far, ds_local, ds_far):
        low, high, _, _ = bounds(head)

        def to_queries(start, local, beyond):
            rows = slice(start + low, start + high)
            near_part = tiles(
                lambda t, lanes: f32_dot(kvt_ref[rows, t * tile : (t + 2) * tile], local[:, lanes])
            )
            return near_part + f32_dot(kvt_ref[rows, near:], beyond)

        def to_keys(start, operand, local, beyond, factor):
            rows = slice(start + low, start + high)
            parts = []
            carried = None
            for t in range(tile_count):
                lanes = slice(t * tile, (t + 1) * tile)
                window = times_transposed(operand[:, lanes], local[:, lanes])
                previous = window[:, :tile]
                parts.append(previous if carried is None else previous + carried)
                carried = window[:, tile:]
            parts.append(carried)
            parts.append(times_transposed(operand, beyond))
            gathered = jnp.concatenate(parts, axis=1)
            gkvt_ref[rows] = rounded(gathered if factor is None else gathered * factor)

        ot_ref[low:high] = rounded(to_queries(width, pb_local, pb_far))
        gqt_ref[low:high] = rounded(to_queries(0, ds_local, ds_far) * scale)
        to_keys(0, qt_ref[low:high], ds_local, ds_far, scale)
        to_keys(width, odt_ref[low:high], pb_local, pb_far, None)

    coming = products(0)
    done = None
    for head in range(HEADS):
        now = coming
        if head + 1 < HEADS:
            coming = products(head + 1)
        if done is not None:
            outputs(head - 1, *done)
        done = weights(*now)
    outputs(HEADS - 1, *done)

    rider_ref[...] = f32_dot(wkv_ref[...], gkvt_ref[:, virt_at:]).T * factor
    weight_sums(
        1 - lax.axis_index("rows") % 2, send_ref, extt_ref, gqt_ref, gkvt_ref, ot_ref, og_ref, factor
    )
    send_ref[2 * width :] = rounded(rider_ref[...])


def weight_sums(core, out_ref, extt_ref, gqt_ref, gkvt_ref, ot_ref, og_ref, factor):
    width, row_count = gqt_ref.shape
    held = own_digit()
    pair, square, _ = exchange_plan()
    rows = 2 * width >> len(pair + square)

    def write(at, total):
        total = (total * factor).astype(out_ref.dtype)
        for start in range(0, width, rows):
            piece = (at * width + start) // rows
            offset = pl.multiple_of((piece ^ held) * rows, ROW_PACK)
            out_ref[pl.ds(offset, rows), :] = total[start : start + rows]

    @pl.when(core == 0)
    def _():
        own = slice(TILE, TILE + row_count)
        write(0, times_transposed(extt_ref[:, own], gqt_ref[...]))
        write(1, times_transposed(extt_ref[...], gkvt_ref[:width]))

    @pl.when(core == 1)
    def _():
        write(0, times_transposed(extt_ref[...], gkvt_ref[width:]))
        write(1, f32_dot(ot_ref[...], og_ref[...]))


def keep_kernel(factor, og_ref, extt_ref, gqt_ref, gkvt_ref, ot_ref, keep_ref):
    core = lax.axis_index("rows") % 2
    weight_sums(core, keep_ref, extt_ref, gqt_ref, gkvt_ref, ot_ref, og_ref, factor)


def finish_kernel(wq_ref, wkv_ref, gqt_ref, gkvt_ref, gf_ref, halo_feat_ref, *pair_refs):
    row_count = gqt_ref.shape[1]
    near = TILE + row_count
    step = pair_refs[0].shape[0]
    slots = step * len(pair_refs)
    by_feature = f32_dot(wkv_ref[...], gkvt_ref[:, : near + slots])
    slot_feat = rounded(by_feature[:, near:].T)
    for at, out_ref in enumerate(pair_refs):
        out_ref[...] = slot_feat[at * step : (at + 1) * step]
    own = by_feature[:, TILE:near] + f32_dot(wq_ref[...], gqt_ref[...])
    gf_ref[...] = own.T
    halo_feat_ref[...] = rounded(by_feature[:, :TILE].T)


def place_kernel(*refs):
    part_refs, (gq_hbm, gkv_hbm, go_hbm, all_ref, out_ref, sems) = refs[:-6], refs[-6:]
    width = gq_hbm.shape[0]
    pair, square, _ = exchange_plan()
    half = 1 << len(pair + square)
    rows = 2 * width // half
    step = part_refs[0].shape[0]
    for at, part_ref in enumerate(part_refs):
        all_ref[at * step : (at + 1) * step] = part_ref[...]
    held = own_digit() + (lax.axis_index("rows") % 2) * half
    copies = []
    for at in range(2 * half):
        start = at * rows
        piece = slice(start, start + rows)
        offset = pl.multiple_of((held ^ at) * rows, ROW_PACK)
        out_ref[piece] = all_ref[pl.ds(offset, rows), :].astype(jnp.float32)
        rows_out = pl.ds(start % width, rows)
        which = start // width
        if which == 0:
            target = gq_hbm.at[rows_out]
        elif which == 3:
            target = go_hbm.at[rows_out]
        else:
            target = gkv_hbm.at[rows_out, pl.ds((which - 1) * width, width)]
        copies.append(pltpu.make_async_copy(out_ref.at[piece], target, sems.at[at]))
        copies[-1].start()
    for copy in copies:
        copy.wait()


def return_kernel(gf_ref, chosen_ref, halo_ref, own_ref, through_ref, *refs):
    far_refs, out_ref = refs[:-1], refs[-1]
    row_count = gf_ref.shape[0]
    tile = halo_ref.shape[0]
    per_peer = own_ref.shape[0] // 2
    returned = []
    for at, even_ref in enumerate([own_ref, *far_refs[::-1]]):
        returned += [even_ref[:per_peer], through_ref[at * per_peer : (at + 1) * per_peer]]
    total = gf_ref[...] + rows_contracted(chosen_ref[...], jnp.concatenate(returned, axis=0))
    out_ref[: row_count - tile] = total[: row_count - tile]
    out_ref[row_count - tile :] = total[row_count - tile :] + halo_ref[...].astype(jnp.float32)


def call(kernel, name, outs, args, scratch=(), fetched=0, flops=0, stored=False):
    spaces = [pltpu.HBM] * fetched
    spaces += [pltpu.VMEM] * (len(args) - len(spaces))
    moved = sum(x.size * x.dtype.itemsize for x in list(args) + list(outs))
    scratch = list(scratch)
    if fetched:
        scratch.append(pltpu.SemaphoreType.DMA((fetched,)))
    constrained = [
        pltpu.with_memory_space_constraint(x, pltpu.HBM) if space is pltpu.HBM else x
        for x, space in zip(args, spaces)
    ]
    return pl.pallas_call(
        kernel,
        out_shape=outs,
        in_specs=[pl.BlockSpec(memory_space=space) for space in spaces],
        out_specs=[pl.BlockSpec(memory_space=pl.ANY if stored else pltpu.VMEM)] * len(outs),
        scratch_shapes=scratch,
        compiler_params=pltpu.CompilerParams(vmem_limit_bytes=VMEM_BYTES),
        cost_estimate=pl.CostEstimate(flops=flops, bytes_accessed=moved, transcendentals=0),
        name=name,
    )(*constrained)


def shards(features, out_grad, w_query, w_keyval, w_out, virtual, local_nbr, expander, send_rows):
    row_count, width = features.shape
    dom_size, per_peer = send_rows.shape
    slots = dom_size * per_peer
    virt_rows = virtual.shape[0]
    padded = ROW_PACK * -(-virt_rows // ROW_PACK)
    ext_rows = TILE + row_count + slots + padded
    nodes = row_count * lax.axis_size("dom") * lax.axis_size("rows")
    pair, square, rest = exchange_plan()
    bf16, f32 = jnp.bfloat16, jnp.float32
    shape = jax.ShapeDtypeStruct

    halo, chosen, through, *direct = call(
        pick_kernel,
        "pick_rows",
        [shape((TILE, width), bf16), shape((slots, row_count), bf16)]
        + [shape((slots // 2, width), bf16)]
        + [shape((per_peer, width), bf16)] * (dom_size // 2),
        [features, send_rows],
        [pltpu.VMEM(features.shape, bf16), pltpu.VMEM(send_rows.shape, jnp.int32)],
        fetched=2,
    )
    through = swapped(through, 1, 0)
    prepared = call(
        functools.partial(prepare_kernel, per_peer),
        "prepare",
        [
            shape(out_grad.shape, bf16),
            shape(w_query.shape, bf16),
            shape(w_keyval.shape, bf16),
            shape((width, row_count + padded), bf16),
            shape((width, row_count), bf16),
            shape((width, row_count), bf16),
            shape((row_count + padded, 2 * width), bf16),
            shape((2 * width, row_count + padded), bf16),
            shape((2 * TILE, row_count), f32),
            shape((slots + padded, row_count), f32),
        ],
        [features, out_grad, w_query, w_keyval, w_out, virtual, local_nbr.T, expander.T],
        [
            pltpu.VMEM(features.shape, bf16),
            pltpu.VMEM(w_out.shape, bf16),
            pltpu.VMEM(virtual.shape, bf16),
            pltpu.VMEM(local_nbr.shape[::-1], jnp.int32),
            pltpu.VMEM(expander.shape[::-1], jnp.int32),
        ],
        fetched=8,
        flops=10 * row_count * width * width,
    )
    (through, halo), _ = lax.optimization_barrier(((through, halo), prepared[0]))
    arrived = handed_on(direct, through)
    halo = shifted(halo, "rows", 1)
    message, rider, *gradients = call(
        functools.partial(attend_kernel, nodes**-0.5, per_peer, dom_size),
        "attend",
        [
            shape((2 * width + padded, width), bf16),
            shape((padded, width), f32),
            shape((width, ext_rows), bf16),
            shape((width, row_count), bf16),
            shape((2 * width, ext_rows), bf16),
            shape((width, row_count), bf16),
        ],
        [*arrived, halo, *prepared],
        [
            pltpu.VMEM((slots, width), bf16),
            pltpu.VMEM((ext_rows, 2 * width), bf16),
            pltpu.VMEM((2 * width, ext_rows), bf16),
        ],
        flops=28 * ext_rows * width * width,
    )
    order = [*farthest_first(4), 0]
    step = width // 2
    parts = {at: message[at * step : (at + 1) * step + (padded if at == 3 else 0)] for at in order}
    parts = {at: swapped(part, *CORES) for at, part in parts.items()}
    (keep,) = call(
        functools.partial(keep_kernel, nodes**-0.5),
        "keep",
        [shape((2 * width, width), f32)],
        [prepared[0], *gradients],
        flops=3 * ext_rows * width * width,
    )
    rider = rounded(rider).astype(f32) + parts[3][step:].astype(f32)
    rider = rider[: -(-virt_rows // 8) * 8]
    keep = {at: keep[at * step : (at + 1) * step] + parts[at][:step].astype(f32) for at in order}

    masks = partner_masks(square)
    messages = {at: with_rider(keep[at], rider) for at in order[:-1]}
    gradients, _ = lax.optimization_barrier((gradients, list(messages.values())))
    arrived = {at: swapped(message, *masks[at]) for at, message in messages.items()}
    own_feat, halo_feat, *pairs = call(
        finish_kernel,
        "finish",
        [shape((row_count, width), f32), shape((TILE, width), bf16)]
        + [shape((2 * per_peer, width), bf16)] * (dom_size // 2),
        [*prepared[1:3], gradients[1], gradients[2]],
        flops=3 * ext_rows * width * width,
    )
    returned = [swapped(pairs[at], 2 * at, 0) for at in reversed(range(1, dom_size // 2))]
    keep, rider = added(keep[0], rounded(rider).astype(f32), arrived)
    keep, *returned[:-1] = lax.optimization_barrier((keep, *returned[:-1]))
    keep, rider = scattered(keep, rider, pair)
    (returned, halo_feat), _ = lax.optimization_barrier(((returned, halo_feat), keep))
    through = swapped(jnp.concatenate([x[per_peer:] for x in [pairs[0]] + returned[::-1]]), 1, 0)
    halo_back = shifted(halo_feat, "rows", -1)
    for mask in rest:
        message = swapped(with_rider(keep, rider), *mask)
        keep, rider = rounded(keep).astype(f32), rounded(rider).astype(f32)
        keep, rider = added(keep, rider, {1: message})
    (grad_features,) = call(
        return_kernel,
        "return_rows",
        [shape((row_count, width), f32)],
        [own_feat, chosen, halo_back, pairs[0], through, *returned],
    )

    held = rounded(keep)
    held = jnp.concatenate([held, swapped(held, *pair[0])], axis=0)
    held, grad_features = lax.optimization_barrier((held, grad_features))
    arrived = [swapped(held, *masks) for masks in partner_masks(square)[1:]]
    near = [held, *arrived]
    far = [swapped(part, *CORES) for part in near]
    grad_wq, grad_wkv, grad_wo = call(
        place_kernel,
        "place_sums",
        [shape((width, width), f32), shape((width, 2 * width), f32), shape((width, width), f32)],
        [*near, *far],
        [
            pltpu.VMEM((4 * width, width), bf16),
            pltpu.VMEM((4 * width, width), f32),
            pltpu.SemaphoreType.DMA((2 << len(pair + square),)),
        ],
        stored=True,
    )
    return grad_features, grad_wq, grad_wkv, grad_wo, rider[:virt_rows]


def solution(mesh):
    placed = (
        P(("dom", "rows"), None),
        P(("dom", "rows"), None),
        P(),
        P(),
        P(),
        P(),
        P(("dom", "rows"), None),
        P(("dom", "rows"), None),
        P(("dom", "rows"), None),
    )
    return jax.shard_map(
        shards,
        mesh=mesh,
        in_specs=placed,
        out_specs=(P(("dom", "rows"), None), P(), P(), P(), P()),
        check_vma=False,
    )
```

```python
import functools
import math

import jax
import jax.numpy as jnp
from jax import lax
from jax.experimental import pallas as pl
from jax.experimental.pallas import tpu as pltpu
from jax.sharding import PartitionSpec as P

HEADS = 8
TILE = 128
ROW_PACK = 16
NEGATIVE_FILL = -1e30
VMEM_BYTES = 24 * 1024 * 1024
LANES = 128


def f32_dot(left, right):
    return jnp.dot(left, right, preferred_element_type=jnp.float32)


def rows_contracted(left, right):
    return lax.dot_general(
        left, right, (((0,), (0,)), ((), ())), preferred_element_type=jnp.float32
    )


def times_transposed(left, right):
    return lax.dot_general(
        left, right, (((1,), (1,)), ((), ())), preferred_element_type=jnp.float32
    )


def rounded(value):
    return value.astype(jnp.bfloat16)


CORES = (0, 1)


def bits_of(size, first=1):
    return [1 << i for i in range(size.bit_length() - 1) if 1 << i >= first]


def exchange_plan():
    dom_size, rows_size = lax.axis_size("dom"), lax.axis_size("rows")
    pair, square = [(2, 0)], [(1, 0), (0, 2)]
    rest = [(bit, 0) for bit in bits_of(dom_size, 4)] + [(0, bit) for bit in bits_of(rows_size, 4)]
    return pair, square, rest


def partner_masks(block):
    masks = []
    for digit in range(1 << len(block)):
        chosen = [mask for i, mask in enumerate(block) if digit >> i & 1]
        masks.append((sum(mask[0] for mask in chosen), sum(mask[1] for mask in chosen)))
    return masks


def farthest_first(count):
    return sorted(range(1, count), key=lambda digit: (-digit.bit_count(), -digit))


def own_digit():
    pair, square, _ = exchange_plan()
    digit = 0
    for i, (dom_mask, rows_mask) in enumerate(pair + square):
        own = (lax.axis_index("dom") & dom_mask) | (lax.axis_index("rows") & rows_mask)
        digit += jnp.where(own != 0, 1 << i, 0)
    return digit


def swapped(block, dom_mask, rows_mask):
    dom_size, rows_size = lax.axis_size("dom"), lax.axis_size("rows")
    route = [
        (a * rows_size + b, (a ^ dom_mask) * rows_size + (b ^ rows_mask))
        for a in range(dom_size)
        for b in range(rows_size)
    ]
    return lax.ppermute(block, ("dom", "rows"), route)


def shifted(block, axis, distance):
    devices = range(lax.axis_size(axis))
    route = [((i - distance) % len(devices), i) for i in devices]
    return lax.ppermute(block, axis, route)


def paired_sum(terms):
    while len(terms) > 1:
        terms = [left + right for left, right in zip(terms[::2], terms[1::2])]
    return terms[0]


def with_rider(block, rider):
    return jnp.concatenate([rounded(block), rounded(rider)], axis=0)


def added(keep, rider, arrived):
    rows = keep.shape[0]
    riders = [rider] + [arrived[at][rows:].astype(jnp.float32) for at in sorted(arrived)]
    for block in arrived.values():
        keep = keep + block[:rows].astype(jnp.float32)
    return keep, paired_sum(riders)


def scattered(keep, rider, bits):
    masks = partner_masks(bits)
    rows = keep.shape[0] // len(masks)
    parts = [keep[at * rows : (at + 1) * rows] for at in range(len(masks))]
    messages = {at: with_rider(parts[at], rider) for at in farthest_first(len(masks))}
    arrived = {at: swapped(message, *masks[at]) for at, message in messages.items()}
    return added(parts[0], rounded(rider).astype(jnp.float32), arrived)


def handed_on(direct, through):
    rows = direct[0].shape[0]
    arrived = [direct[0], through]
    for at in reversed(range(1, len(direct))):
        message = jnp.concatenate([direct[at], through[at * rows : (at + 1) * rows]], axis=0)
        arrived.append(swapped(message, 2 * at, 0))
    return arrived


def listed_rows(send_ref, row_count):
    dom_size, per_peer = send_ref.shape
    slots = dom_size * per_peer
    slot = lax.broadcasted_iota(jnp.int32, (slots, per_peer), 0)
    place = lax.broadcasted_iota(jnp.int32, (slots, per_peer), 1)
    peer = (slot // per_peer) ^ lax.axis_index("dom")
    listed = jnp.zeros((slots, per_peer), jnp.int32)
    for at in range(dom_size):
        listed += jnp.where((peer == at) & (place == slot % per_peer), send_ref[at : at + 1, :], 0)
    column = jnp.sum(listed, axis=1, keepdims=True)
    rows = lax.broadcasted_iota(jnp.int32, (slots, row_count), 1)
    return jnp.where(column == rows, 1.0, 0.0).astype(jnp.bfloat16)


def fetch(pairs, sems):
    copies = [
        pltpu.make_async_copy(source, target, sems.at[at])
        for at, (source, target) in enumerate(pairs)
    ]
    for copy in copies:
        copy.start()
    return copies


def store_blocks(rows, through_ref, direct_refs):
    size = direct_refs[0].shape[0]
    for at, out_ref in enumerate(direct_refs):
        out_ref[...] = rows[2 * at * size : (2 * at + 1) * size]
        through_ref[at * size : (at + 1) * size] = rows[(2 * at + 1) * size : (2 * at + 2) * size]


def pick_kernel(feat_hbm, send_hbm, halo_ref, chosen_ref, through_ref, *refs):
    direct_refs, (feat_ref, send_ref, sems) = refs[:-3], refs[-3:]
    copies = fetch([(send_hbm, send_ref), (feat_hbm, feat_ref)], sems)
    copies[0].wait()
    chosen_ref[...] = listed_rows(send_ref, feat_ref.shape[0])
    copies[1].wait()
    halo_ref[...] = feat_ref[feat_ref.shape[0] - halo_ref.shape[0] :]
    store_blocks(rounded(f32_dot(chosen_ref[...], feat_ref[...])), through_ref, direct_refs)


def prepare_kernel(
    per_peer,
    feat_hbm,
    og_hbm,
    wq_hbm,
    wkv_hbm,
    wo_hbm,
    virt_hbm,
    nbr_hbm,
    exp_hbm,
    og_ref,
    wq_ref,
    wkv_ref,
    featt_ref,
    qt_ref,
    odt_ref,
    kv_ref,
    kvt_ref,
    local_bias_ref,
    far_bias_ref,
    feat_ref,
    wo_ref,
    virt_ref,
    nbr_ref,
    exp_ref,
    sems,
):
    nbr_copy, exp_copy, feat_copy, virt_copy, wq_copy, wkv_copy, og_copy, wo_copy = fetch(
        [
            (nbr_hbm, nbr_ref),
            (exp_hbm, exp_ref),
            (feat_hbm, feat_ref),
            (virt_hbm, virt_ref),
            (wq_hbm, wq_ref),
            (wkv_hbm, wkv_ref),
            (og_hbm, og_ref),
            (wo_hbm, wo_ref),
        ],
        sems,
    )
    row_count, width = feat_ref.shape
    window = local_bias_ref.shape[0]
    far = far_bias_ref.shape[0]
    virt_rows = virt_ref.shape[0]
    padded = kv_ref.shape[0] - row_count
    slots = far - padded
    scale = 1.0 / math.sqrt(width // HEADS)

    def multiplicity(key_rows, named):
        position = lax.broadcasted_iota(jnp.int32, (key_rows, row_count), 0)
        count = jnp.zeros((key_rows, row_count), jnp.float32)
        for at in range(named.shape[0]):
            count += jnp.where(named[at : at + 1, :] == position, 1.0, 0.0)
        return count

    nbr_copy.wait()
    local_bias_ref[...] = jnp.where(multiplicity(window, nbr_ref) > 0.0, 0.0, NEGATIVE_FILL)
    exp_copy.wait()
    expander = exp_ref[...]
    expander = ((expander // per_peer) ^ lax.axis_index("dom")) * per_peer + expander % per_peer
    named_times = multiplicity(slots, expander)
    slot_bias = jnp.full((slots, row_count), NEGATIVE_FILL, jnp.float32)
    for times in range(1, exp_ref.shape[0] + 1):
        slot_bias = jnp.where(named_times == float(times), math.log(times) / scale, slot_bias)
    far_bias_ref[:slots] = slot_bias
    virt_row = lax.broadcasted_iota(jnp.int32, (padded, row_count), 0)
    far_bias_ref[slots:] = jnp.where(virt_row < virt_rows, 0.0, NEGATIVE_FILL)

    feat_copy.wait()
    featt_ref[:, :row_count] = feat_ref[...].T
    virt_copy.wait()
    virt = jnp.concatenate(
        [virt_ref[...], jnp.zeros((padded - virt_rows, width), jnp.bfloat16)], axis=0
    )
    featt_ref[:, row_count:] = virt.T
    wq_copy.wait()
    qt_ref[...] = rounded(rows_contracted(wq_ref[...], featt_ref[:, :row_count]))
    wkv_copy.wait()
    kv_ref[:row_count] = rounded(f32_dot(feat_ref[...], wkv_ref[...]))
    kv_ref[row_count:] = rounded(f32_dot(virt, wkv_ref[...]))
    kvt_ref[...] = kv_ref[...].T
    og_copy.wait()
    wo_copy.wait()
    odt_ref[...] = rounded(times_transposed(wo_ref[...], og_ref[...]))


def attend_kernel(
    factor,
    per_peer,
    dom_size,
    *refs,
):
    count = dom_size // 2 + 1
    piece_refs, halo_ref, refs = refs[:count], refs[count], refs[count + 1 :]
    og_ref, wq_ref, wkv_ref, featt_ref, qt_ref, odt_ref, own_kv_ref, own_kvt_ref = refs[:8]
    local_bias_ref, far_bias_ref, send_ref, rider_ref = refs[8:12]
    extt_ref, gqt_ref, gkvt_ref, ot_ref, slot_ref, kv_ref, kvt_ref = refs[12:]
    width, row_count = qt_ref.shape
    tile = halo_ref.shape[0]
    tile_count = row_count // tile
    slots = dom_size * per_peer
    near = tile + row_count
    virt_at = near + slots
    head_dim = width // HEADS
    scale = 1.0 / math.sqrt(head_dim)

    kv_ref[tile:near] = own_kv_ref[:row_count]
    kv_ref[virt_at:] = own_kv_ref[row_count:]
    kvt_ref[:, tile:near] = own_kvt_ref[:, :row_count]
    kvt_ref[:, virt_at:] = own_kvt_ref[:, row_count:]
    extt_ref[:, tile:near] = featt_ref[:, :row_count]
    extt_ref[:, virt_at:] = featt_ref[:, row_count:]
    slot_ref[:per_peer] = piece_refs[0][...]
    slot_ref[per_peer : 2 * per_peer] = piece_refs[1][:per_peer]
    for at, piece_ref in enumerate(piece_refs[:1:-1], 1):
        slot_ref[2 * at * per_peer : (2 * at + 2) * per_peer] = piece_ref[...]
    for rows, source_ref in ((slice(0, tile), halo_ref), (slice(near, virt_at), slot_ref)):
        extt_ref[:, rows] = source_ref[...].T
        kv_ref[rows] = rounded(f32_dot(source_ref[...], wkv_ref[...]))
        kvt_ref[:, rows] = kv_ref[rows].T

    def tiles(of):
        return jnp.concatenate([of(t, slice(t * tile, (t + 1) * tile)) for t in range(tile_count)], 1)

    def bounds(head):
        low, high = head * head_dim, (head + 1) * head_dim
        return low, high, low // LANES * LANES, min(-(-high // LANES) * LANES, width)

    def products(head):
        low, high, first, last = bounds(head)
        column = lax.broadcasted_iota(jnp.int32, (last - first, row_count), 0) + first
        of_head = (column >= low) & (column < high)
        out = []
        for rows_ref, start in ((qt_ref, 0), (odt_ref, width)):
            operand = jnp.where(of_head, rows_ref[first:last, :], 0)
            every = f32_dot(kv_ref[:, start + first : start + last], operand)
            out.append(tiles(lambda t, lanes: every[t * tile : (t + 2) * tile, lanes]))
            out.append(every[near:])
        return out

    def weights(s_local, s_far, dp_local, dp_far):
        s_local += local_bias_ref[...]
        s_far += far_bias_ref[...]
        peak = jnp.maximum(
            jnp.max(s_local, axis=0, keepdims=True), jnp.max(s_far, axis=0, keepdims=True)
        )
        exponent_scale = scale * math.log2(math.e)
        e_local = jnp.exp2((s_local - peak) * exponent_scale)
        e_far = jnp.exp2((s_far - peak) * exponent_scale)
        total = jnp.sum(e_local, axis=0, keepdims=True) + jnp.sum(e_far, axis=0, keepdims=True)
        inverse = 1.0 / total
        p_local = e_local * inverse
        p_far = e_far * inverse
        delta = jnp.sum(p_local * dp_local, axis=0, keepdims=True) + jnp.sum(
            p_far * dp_far, axis=0, keepdims=True
        )
        ds_local = rounded(p_local * (dp_local - delta))
        ds_far = rounded(p_far * (dp_far - delta))
        return rounded(p_local), rounded(p_far), ds_local, ds_far

    def outputs(head, pb_local, pb_far, ds_local, ds_far):
        low, high, _, _ = bounds(head)

        def to_queries(start, local, beyond):
            rows = slice(start + low, start + high)
            near_part = tiles(
                lambda t, lanes: f32_dot(kvt_ref[rows, t * tile : (t + 2) * tile], local[:, lanes])
            )
            return near_part + f32_dot(kvt_ref[rows, near:], beyond)

        def to_keys(start, operand, local, beyond, factor):
            rows = slice(start + low, start + high)
            parts = []
            carried = None
            for t in range(tile_count):
                lanes = slice(t * tile, (t + 1) * tile)
                window = times_transposed(operand[:, lanes], local[:, lanes])
                previous = window[:, :tile]
                parts.append(previous if carried is None else previous + carried)
                carried = window[:, tile:]
            parts.append(carried)
            parts.append(times_transposed(operand, beyond))
            gathered = jnp.concatenate(parts, axis=1)
            gkvt_ref[rows] = rounded(gathered if factor is None else gathered * factor)

        ot_ref[low:high] = rounded(to_queries(width, pb_local, pb_far))
        gqt_ref[low:high] = rounded(to_queries(0, ds_local, ds_far) * scale)
        to_keys(0, qt_ref[low:high], ds_local, ds_far, scale)
        to_keys(width, odt_ref[low:high], pb_local, pb_far, None)

    coming = products(0)
    done = None
    for head in range(HEADS):
        now = coming
        if head + 1 < HEADS:
            coming = products(head + 1)
        if done is not None:
            outputs(head - 1, *done)
        done = weights(*now)
    outputs(HEADS - 1, *done)

    rider_ref[...] = f32_dot(wkv_ref[...], gkvt_ref[:, virt_at:]).T * factor
    weight_sums(
        1 - lax.axis_index("rows") % 2, send_ref, extt_ref, gqt_ref, gkvt_ref, ot_ref, og_ref, factor
    )
    send_ref[2 * width :] = rounded(rider_ref[...])


def weight_sums(core, out_ref, extt_ref, gqt_ref, gkvt_ref, ot_ref, og_ref, factor):
    width, row_count = gqt_ref.shape
    held = own_digit()
    pair, square, _ = exchange_plan()
    rows = 2 * width >> len(pair + square)

    def write(at, total):
        total = (total * factor).astype(out_ref.dtype)
        for start in range(0, width, rows):
            piece = (at * width + start) // rows
            offset = pl.multiple_of((piece ^ held) * rows, ROW_PACK)
            out_ref[pl.ds(offset, rows), :] = total[start : start + rows]

    @pl.when(core == 0)
    def _():
        own = slice(TILE, TILE + row_count)
        write(0, times_transposed(extt_ref[:, own], gqt_ref[...]))
        write(1, times_transposed(extt_ref[...], gkvt_ref[:width]))

    @pl.when(core == 1)
    def _():
        write(0, times_transposed(extt_ref[...], gkvt_ref[width:]))
        write(1, f32_dot(ot_ref[...], og_ref[...]))


def finish_kernel(factor, og_ref, wq_ref, wkv_ref, extt_ref, gqt_ref, gkvt_ref, ot_ref, *refs):
    gf_ref, halo_feat_ref, keep_ref = refs[:3]
    pair_refs = refs[3:]
    width, row_count = gqt_ref.shape
    near = TILE + row_count
    step = pair_refs[0].shape[0]
    slots = step * len(pair_refs)
    weight_sums(
        lax.axis_index("rows") % 2, keep_ref, extt_ref, gqt_ref, gkvt_ref, ot_ref, og_ref, factor
    )
    by_feature = f32_dot(wkv_ref[...], gkvt_ref[:, : near + slots])
    own = by_feature[:, TILE:near] + f32_dot(wq_ref[...], gqt_ref[...])
    gf_ref[...] = own.T
    halo_feat_ref[...] = rounded(by_feature[:, :TILE].T)
    slot_feat = rounded(by_feature[:, near:].T)
    for at, out_ref in enumerate(pair_refs):
        out_ref[...] = slot_feat[at * step : (at + 1) * step]


def place_kernel(*refs):
    part_refs, (gq_hbm, gkv_hbm, go_hbm, all_ref, out_ref, sems) = refs[:-6], refs[-6:]
    width = gq_hbm.shape[0]
    pair, square, _ = exchange_plan()
    half = 1 << len(pair + square)
    rows = 2 * width // half
    step = part_refs[0].shape[0]
    for at, part_ref in enumerate(part_refs):
        all_ref[at * step : (at + 1) * step] = part_ref[...]
    held = own_digit() + (lax.axis_index("rows") % 2) * half
    copies = []
    for at in range(2 * half):
        start = at * rows
        piece = slice(start, start + rows)
        offset = pl.multiple_of((held ^ at) * rows, ROW_PACK)
        out_ref[piece] = all_ref[pl.ds(offset, rows), :].astype(jnp.float32)
        rows_out = pl.ds(start % width, rows)
        which = start // width
        if which == 0:
            target = gq_hbm.at[rows_out]
        elif which == 3:
            target = go_hbm.at[rows_out]
        else:
            target = gkv_hbm.at[rows_out, pl.ds((which - 1) * width, width)]
        copies.append(pltpu.make_async_copy(out_ref.at[piece], target, sems.at[at]))
        copies[-1].start()
    for copy in copies:
        copy.wait()


def return_kernel(gf_ref, chosen_ref, halo_ref, own_ref, through_ref, *refs):
    far_refs, out_ref = refs[:-1], refs[-1]
    row_count = gf_ref.shape[0]
    tile = halo_ref.shape[0]
    per_peer = own_ref.shape[0] // 2
    returned = []
    for at, even_ref in enumerate([own_ref, *far_refs[::-1]]):
        returned += [even_ref[:per_peer], through_ref[at * per_peer : (at + 1) * per_peer]]
    total = gf_ref[...] + rows_contracted(chosen_ref[...], jnp.concatenate(returned, axis=0))
    out_ref[: row_count - tile] = total[: row_count - tile]
    out_ref[row_count - tile :] = total[row_count - tile :] + halo_ref[...].astype(jnp.float32)


def call(kernel, name, outs, args, scratch=(), fetched=0, flops=0, stored=False):
    spaces = [pltpu.HBM] * fetched
    spaces += [pltpu.VMEM] * (len(args) - len(spaces))
    moved = sum(x.size * x.dtype.itemsize for x in list(args) + list(outs))
    scratch = list(scratch)
    if fetched:
        scratch.append(pltpu.SemaphoreType.DMA((fetched,)))
    constrained = [
        pltpu.with_memory_space_constraint(x, pltpu.HBM) if space is pltpu.HBM else x
        for x, space in zip(args, spaces)
    ]
    return pl.pallas_call(
        kernel,
        out_shape=outs,
        in_specs=[pl.BlockSpec(memory_space=space) for space in spaces],
        out_specs=[pl.BlockSpec(memory_space=pl.ANY if stored else pltpu.VMEM)] * len(outs),
        scratch_shapes=scratch,
        compiler_params=pltpu.CompilerParams(vmem_limit_bytes=VMEM_BYTES),
        cost_estimate=pl.CostEstimate(flops=flops, bytes_accessed=moved, transcendentals=0),
        name=name,
    )(*constrained)


def shards(features, out_grad, w_query, w_keyval, w_out, virtual, local_nbr, expander, send_rows):
    row_count, width = features.shape
    dom_size, per_peer = send_rows.shape
    slots = dom_size * per_peer
    virt_rows = virtual.shape[0]
    padded = ROW_PACK * -(-virt_rows // ROW_PACK)
    ext_rows = TILE + row_count + slots + padded
    nodes = row_count * lax.axis_size("dom") * lax.axis_size("rows")
    pair, square, rest = exchange_plan()
    bf16, f32 = jnp.bfloat16, jnp.float32
    shape = jax.ShapeDtypeStruct

    halo, chosen, through, *direct = call(
        pick_kernel,
        "pick_rows",
        [shape((TILE, width), bf16), shape((slots, row_count), bf16)]
        + [shape((slots // 2, width), bf16)]
        + [shape((per_peer, width), bf16)] * (dom_size // 2),
        [features, send_rows],
        [pltpu.VMEM(features.shape, bf16), pltpu.VMEM(send_rows.shape, jnp.int32)],
        fetched=2,
    )
    through = swapped(through, 1, 0)
    prepared = call(
        functools.partial(prepare_kernel, per_peer),
        "prepare",
        [
            shape(out_grad.shape, bf16),
            shape(w_query.shape, bf16),
            shape(w_keyval.shape, bf16),
            shape((width, row_count + padded), bf16),
            shape((width, row_count), bf16),
            shape((width, row_count), bf16),
            shape((row_count + padded, 2 * width), bf16),
            shape((2 * width, row_count + padded), bf16),
            shape((2 * TILE, row_count), f32),
            shape((slots + padded, row_count), f32),
        ],
        [features, out_grad, w_query, w_keyval, w_out, virtual, local_nbr.T, expander.T],
        [
            pltpu.VMEM(features.shape, bf16),
            pltpu.VMEM(w_out.shape, bf16),
            pltpu.VMEM(virtual.shape, bf16),
            pltpu.VMEM(local_nbr.shape[::-1], jnp.int32),
            pltpu.VMEM(expander.shape[::-1], jnp.int32),
        ],
        fetched=8,
        flops=10 * row_count * width * width,
    )
    (through, halo), _ = lax.optimization_barrier(((through, halo), prepared[0]))
    arrived = handed_on(direct, through)
    halo = shifted(halo, "rows", 1)
    message, rider, *gradients = call(
        functools.partial(attend_kernel, nodes**-0.5, per_peer, dom_size),
        "attend",
        [
            shape((2 * width + padded, width), bf16),
            shape((padded, width), f32),
            shape((width, ext_rows), bf16),
            shape((width, row_count), bf16),
            shape((2 * width, ext_rows), bf16),
            shape((width, row_count), bf16),
        ],
        [*arrived, halo, *prepared],
        [
            pltpu.VMEM((slots, width), bf16),
            pltpu.VMEM((ext_rows, 2 * width), bf16),
            pltpu.VMEM((2 * width, ext_rows), bf16),
        ],
        flops=28 * ext_rows * width * width,
    )
    message = swapped(message, *CORES)
    own_feat, halo_feat, keep, *pairs = call(
        functools.partial(finish_kernel, nodes**-0.5),
        "finish",
        [shape((row_count, width), f32), shape((TILE, width), bf16), shape((2 * width, width), f32)]
        + [shape((2 * per_peer, width), bf16)] * (dom_size // 2),
        [*prepared[:3], *gradients],
        flops=6 * ext_rows * width * width,
    )

    keep, rider = added(keep, rounded(rider).astype(f32), {1: message})
    rider = rider[: -(-virt_rows // 8) * 8]
    pairs, _ = lax.optimization_barrier((pairs, keep))
    returned = [swapped(pairs[at], 2 * at, 0) for at in reversed(range(2, dom_size // 2))]
    keep, rider = scattered(keep, rider, square)
    keep, *returned = lax.optimization_barrier((keep, *returned))
    keep, rider = scattered(keep, rider, pair)
    (nearest, halo_feat), _ = lax.optimization_barrier(((pairs[1], halo_feat), keep))
    returned.append(swapped(nearest, 2, 0))
    halo_back = shifted(halo_feat, "rows", -1)
    for mask in rest:
        message = swapped(with_rider(keep, rider), *mask)
        keep, rider = rounded(keep).astype(f32), rounded(rider).astype(f32)
        keep, rider = added(keep, rider, {1: message})

    held = rounded(keep)
    held, returned, halo_back = lax.optimization_barrier((held, returned, halo_back))
    odd = [block[per_peer:] for block in [pairs[0]] + returned[::-1]]
    through = swapped(jnp.concatenate(odd, axis=0), 1, 0)
    held = jnp.concatenate([held, swapped(held, *pair[0])], axis=0)
    held, through = lax.optimization_barrier((held, through))
    (grad_features,) = call(
        return_kernel,
        "return_rows",
        [shape((row_count, width), f32)],
        [own_feat, chosen, halo_back, pairs[0], through, *returned],
    )
    arrived = [swapped(held, *masks) for masks in partner_masks(square)[1:]]
    arrived, _ = lax.optimization_barrier((arrived, grad_features))
    near = [held, *arrived]
    far = [swapped(part, *CORES) for part in near]
    grad_wq, grad_wkv, grad_wo = call(
        place_kernel,
        "place_sums",
        [shape((width, width), f32), shape((width, 2 * width), f32), shape((width, width), f32)],
        [*near, *far],
        [
            pltpu.VMEM((4 * width, width), bf16),
            pltpu.VMEM((4 * width, width), f32),
            pltpu.SemaphoreType.DMA((2 << len(pair + square),)),
        ],
        stored=True,
    )
    return grad_features, grad_wq, grad_wkv, grad_wo, rider[:virt_rows]


def solution(mesh):
    placed = (
        P(("dom", "rows"), None),
        P(("dom", "rows"), None),
        P(),
        P(),
        P(),
        P(),
        P(("dom", "rows"), None),
        P(("dom", "rows"), None),
        P(("dom", "rows"), None),
    )
    return jax.shard_map(
        shards,
        mesh=mesh,
        in_specs=placed,
        out_specs=(P(("dom", "rows"), None), P(), P(), P(), P()),
        check_vma=False,
    )
```

```python
import functools
import math

import jax
import jax.numpy as jnp
from jax import lax
from jax.experimental import pallas as pl
from jax.experimental.pallas import tpu as pltpu
from jax.sharding import PartitionSpec as P

HEADS = 8
TILE = 128
ROW_PACK = 16
NEGATIVE_FILL = -1e30
VMEM_BYTES = 24 * 1024 * 1024
LANES = 128


def f32_dot(left, right):
    return jnp.dot(left, right, preferred_element_type=jnp.float32)


def rows_contracted(left, right):
    return lax.dot_general(
        left, right, (((0,), (0,)), ((), ())), preferred_element_type=jnp.float32
    )


def times_transposed(left, right):
    return lax.dot_general(
        left, right, (((1,), (1,)), ((), ())), preferred_element_type=jnp.float32
    )


def rounded(value):
    return value.astype(jnp.bfloat16)


CORES = (0, 1)


def bits_of(size, first=1):
    return [1 << i for i in range(size.bit_length() - 1) if 1 << i >= first]


def exchange_plan():
    dom_size, rows_size = lax.axis_size("dom"), lax.axis_size("rows")
    pair, square = [(2, 0)], [(1, 0), (0, 2)]
    rest = [(bit, 0) for bit in bits_of(dom_size, 4)] + [(0, bit) for bit in bits_of(rows_size, 4)]
    return pair, square, rest


def partner_masks(block):
    masks = []
    for digit in range(1 << len(block)):
        chosen = [mask for i, mask in enumerate(block) if digit >> i & 1]
        masks.append((sum(mask[0] for mask in chosen), sum(mask[1] for mask in chosen)))
    return masks


def farthest_first(count):
    return sorted(range(1, count), key=lambda digit: (-digit.bit_count(), -digit))


def own_digit():
    pair, square, _ = exchange_plan()
    digit = 0
    for i, (dom_mask, rows_mask) in enumerate(pair + square):
        own = (lax.axis_index("dom") & dom_mask) | (lax.axis_index("rows") & rows_mask)
        digit += jnp.where(own != 0, 1 << i, 0)
    return digit


def swapped(block, dom_mask, rows_mask):
    dom_size, rows_size = lax.axis_size("dom"), lax.axis_size("rows")
    route = [
        (a * rows_size + b, (a ^ dom_mask) * rows_size + (b ^ rows_mask))
        for a in range(dom_size)
        for b in range(rows_size)
    ]
    return lax.ppermute(block, ("dom", "rows"), route)


def shifted(block, axis, distance):
    devices = range(lax.axis_size(axis))
    route = [((i - distance) % len(devices), i) for i in devices]
    return lax.ppermute(block, axis, route)


def paired_sum(terms):
    while len(terms) > 1:
        terms = [left + right for left, right in zip(terms[::2], terms[1::2])]
    return terms[0]


def with_rider(block, rider):
    return jnp.concatenate([rounded(block), rounded(rider)], axis=0)


def added(keep, rider, arrived):
    rows = keep.shape[0]
    riders = [rider] + [arrived[at][rows:].astype(jnp.float32) for at in sorted(arrived)]
    for block in arrived.values():
        keep = keep + block[:rows].astype(jnp.float32)
    return keep, paired_sum(riders)


def scattered(keep, rider, bits):
    masks = partner_masks(bits)
    rows = keep.shape[0] // len(masks)
    parts = [keep[at * rows : (at + 1) * rows] for at in range(len(masks))]
    messages = {at: with_rider(parts[at], rider) for at in farthest_first(len(masks))}
    arrived = {at: swapped(message, *masks[at]) for at, message in messages.items()}
    return added(parts[0], rounded(rider).astype(jnp.float32), arrived)


def handed_on(direct, through):
    rows = direct[0].shape[0]
    arrived = [direct[0], through]
    for at in reversed(range(1, len(direct))):
        message = jnp.concatenate([direct[at], through[at * rows : (at + 1) * rows]], axis=0)
        arrived.append(swapped(message, 2 * at, 0))
    return arrived


def listed_rows(send_ref, row_count):
    dom_size, per_peer = send_ref.shape
    slots = dom_size * per_peer
    slot = lax.broadcasted_iota(jnp.int32, (slots, per_peer), 0)
    place = lax.broadcasted_iota(jnp.int32, (slots, per_peer), 1)
    peer = (slot // per_peer) ^ lax.axis_index("dom")
    listed = jnp.zeros((slots, per_peer), jnp.int32)
    for at in range(dom_size):
        listed += jnp.where((peer == at) & (place == slot % per_peer), send_ref[at : at + 1, :], 0)
    column = jnp.sum(listed, axis=1, keepdims=True)
    rows = lax.broadcasted_iota(jnp.int32, (slots, row_count), 1)
    return jnp.where(column == rows, 1.0, 0.0).astype(jnp.bfloat16)


def fetch(pairs, sems):
    copies = [
        pltpu.make_async_copy(source, target, sems.at[at])
        for at, (source, target) in enumerate(pairs)
    ]
    for copy in copies:
        copy.start()
    return copies


def store_blocks(rows, through_ref, direct_refs):
    size = direct_refs[0].shape[0]
    for at, out_ref in enumerate(direct_refs):
        out_ref[...] = rows[2 * at * size : (2 * at + 1) * size]
        through_ref[at * size : (at + 1) * size] = rows[(2 * at + 1) * size : (2 * at + 2) * size]


def pick_kernel(feat_hbm, send_hbm, halo_ref, chosen_ref, through_ref, *refs):
    direct_refs, (feat_ref, send_ref, sems) = refs[:-3], refs[-3:]
    copies = fetch([(send_hbm, send_ref), (feat_hbm, feat_ref)], sems)
    copies[0].wait()
    chosen_ref[...] = listed_rows(send_ref, feat_ref.shape[0])
    copies[1].wait()
    halo_ref[...] = feat_ref[feat_ref.shape[0] - halo_ref.shape[0] :]
    store_blocks(rounded(f32_dot(chosen_ref[...], feat_ref[...])), through_ref, direct_refs)


def prepare_kernel(
    per_peer,
    feat_hbm,
    og_hbm,
    wq_hbm,
    wkv_hbm,
    wo_hbm,
    virt_hbm,
    nbr_hbm,
    exp_hbm,
    og_ref,
    wq_ref,
    wkv_ref,
    featt_ref,
    qt_ref,
    odt_ref,
    kv_ref,
    kvt_ref,
    local_bias_ref,
    far_bias_ref,
    feat_ref,
    wo_ref,
    virt_ref,
    nbr_ref,
    exp_ref,
    sems,
):
    nbr_copy, exp_copy, feat_copy, virt_copy, wq_copy, wkv_copy, og_copy, wo_copy = fetch(
        [
            (nbr_hbm, nbr_ref),
            (exp_hbm, exp_ref),
            (feat_hbm, feat_ref),
            (virt_hbm, virt_ref),
            (wq_hbm, wq_ref),
            (wkv_hbm, wkv_ref),
            (og_hbm, og_ref),
            (wo_hbm, wo_ref),
        ],
        sems,
    )
    row_count, width = feat_ref.shape
    window = local_bias_ref.shape[0]
    far = far_bias_ref.shape[0]
    virt_rows = virt_ref.shape[0]
    padded = kv_ref.shape[0] - row_count
    slots = far - padded
    scale = 1.0 / math.sqrt(width // HEADS)

    def multiplicity(key_rows, named):
        position = lax.broadcasted_iota(jnp.int32, (key_rows, row_count), 0)
        count = jnp.zeros((key_rows, row_count), jnp.float32)
        for at in range(named.shape[0]):
            count += jnp.where(named[at : at + 1, :] == position, 1.0, 0.0)
        return count

    nbr_copy.wait()
    local_bias_ref[...] = jnp.where(multiplicity(window, nbr_ref) > 0.0, 0.0, NEGATIVE_FILL)
    exp_copy.wait()
    expander = exp_ref[...]
    expander = ((expander // per_peer) ^ lax.axis_index("dom")) * per_peer + expander % per_peer
    named_times = multiplicity(slots, expander)
    slot_bias = jnp.full((slots, row_count), NEGATIVE_FILL, jnp.float32)
    for times in range(1, exp_ref.shape[0] + 1):
        slot_bias = jnp.where(named_times == float(times), math.log(times) / scale, slot_bias)
    far_bias_ref[:slots] = slot_bias
    virt_row = lax.broadcasted_iota(jnp.int32, (padded, row_count), 0)
    far_bias_ref[slots:] = jnp.where(virt_row < virt_rows, 0.0, NEGATIVE_FILL)

    feat_copy.wait()
    featt_ref[:, :row_count] = feat_ref[...].T
    virt_copy.wait()
    virt = jnp.concatenate(
        [virt_ref[...], jnp.zeros((padded - virt_rows, width), jnp.bfloat16)], axis=0
    )
    featt_ref[:, row_count:] = virt.T
    wq_copy.wait()
    qt_ref[...] = rounded(rows_contracted(wq_ref[...], featt_ref[:, :row_count]))
    wkv_copy.wait()
    kv_ref[:row_count] = rounded(f32_dot(feat_ref[...], wkv_ref[...]))
    kv_ref[row_count:] = rounded(f32_dot(virt, wkv_ref[...]))
    kvt_ref[...] = kv_ref[...].T
    og_copy.wait()
    wo_copy.wait()
    odt_ref[...] = rounded(times_transposed(wo_ref[...], og_ref[...]))


def attend_kernel(
    factor,
    per_peer,
    dom_size,
    *refs,
):
    count = dom_size // 2 + 1
    piece_refs, halo_ref, refs = refs[:count], refs[count], refs[count + 1 :]
    og_ref, wq_ref, wkv_ref, featt_ref, qt_ref, odt_ref, own_kv_ref, own_kvt_ref = refs[:8]
    local_bias_ref, far_bias_ref, send_ref, rider_ref = refs[8:12]
    extt_ref, gqt_ref, gkvt_ref, ot_ref, slot_ref, kv_ref, kvt_ref = refs[12:]
    width, row_count = qt_ref.shape
    tile = halo_ref.shape[0]
    tile_count = row_count // tile
    slots = dom_size * per_peer
    near = tile + row_count
    virt_at = near + slots
    head_dim = width // HEADS
    scale = 1.0 / math.sqrt(head_dim)

    kv_ref[tile:near] = own_kv_ref[:row_count]
    kv_ref[virt_at:] = own_kv_ref[row_count:]
    kvt_ref[:, tile:near] = own_kvt_ref[:, :row_count]
    kvt_ref[:, virt_at:] = own_kvt_ref[:, row_count:]
    extt_ref[:, tile:near] = featt_ref[:, :row_count]
    extt_ref[:, virt_at:] = featt_ref[:, row_count:]
    slot_ref[:per_peer] = piece_refs[0][...]
    slot_ref[per_peer : 2 * per_peer] = piece_refs[1][:per_peer]
    for at, piece_ref in enumerate(piece_refs[:1:-1], 1):
        slot_ref[2 * at * per_peer : (2 * at + 2) * per_peer] = piece_ref[...]
    for rows, source_ref in ((slice(0, tile), halo_ref), (slice(near, virt_at), slot_ref)):
        extt_ref[:, rows] = source_ref[...].T
        kv_ref[rows] = rounded(f32_dot(source_ref[...], wkv_ref[...]))
        kvt_ref[:, rows] = kv_ref[rows].T

    def tiles(of):
        return jnp.concatenate([of(t, slice(t * tile, (t + 1) * tile)) for t in range(tile_count)], 1)

    def bounds(head):
        low, high = head * head_dim, (head + 1) * head_dim
        return low, high, low // LANES * LANES, min(-(-high // LANES) * LANES, width)

    def product(head, rows_ref, start):
        low, high, first, last = bounds(head)
        column = lax.broadcasted_iota(jnp.int32, (last - first, row_count), 0) + first
        of_head = (column >= low) & (column < high)
        operand = jnp.where(of_head, rows_ref[first:last, :], 0)
        every = f32_dot(kv_ref[:, start + first : start + last], operand)
        return tiles(lambda t, lanes: every[t * tile : (t + 2) * tile, lanes]), every[near:]

    def scores(head):
        return product(head, qt_ref, 0)

    def dprobs(head):
        return product(head, odt_ref, width)

    def to_queries(head, start, local, beyond):
        low, high, _, _ = bounds(head)
        rows = slice(start + low, start + high)
        near_part = tiles(
            lambda t, lanes: f32_dot(kvt_ref[rows, t * tile : (t + 2) * tile], local[:, lanes])
        )
        return near_part + f32_dot(kvt_ref[rows, near:], beyond)

    def to_keys(head, start, rows_ref, local, beyond, factor):
        low, high, _, _ = bounds(head)
        operand = rows_ref[low:high]
        parts = []
        carried = None
        for t in range(tile_count):
            lanes = slice(t * tile, (t + 1) * tile)
            window = times_transposed(operand[:, lanes], local[:, lanes])
            previous = window[:, :tile]
            parts.append(previous if carried is None else previous + carried)
            carried = window[:, tile:]
        parts.append(carried)
        parts.append(times_transposed(operand, beyond))
        gathered = jnp.concatenate(parts, axis=1)
        gkvt_ref[start + low : start + high] = rounded(
            gathered if factor is None else gathered * factor
        )

    def step(head, given, done):
        if head < HEADS:
            (s_local, s_far), (dp_local, dp_far) = given
            s_local += local_bias_ref[...]
            s_far += far_bias_ref[...]
            peak = jnp.maximum(
                jnp.max(s_local, axis=0, keepdims=True), jnp.max(s_far, axis=0, keepdims=True)
            )
        if done:
            low, high, _, _ = bounds(head - 1)
            pb_before, ds_before = done
            ot_ref[low:high] = rounded(to_queries(head - 1, width, *pb_before))
        if head < HEADS:
            exponent_scale = scale * math.log2(math.e)
            e_local = jnp.exp2((s_local - peak) * exponent_scale)
            e_far = jnp.exp2((s_far - peak) * exponent_scale)
            total = jnp.sum(e_local, axis=0, keepdims=True) + jnp.sum(e_far, axis=0, keepdims=True)
            inverse = 1.0 / total
        coming_scores = scores(head + 1) if head + 1 < HEADS else None
        if done:
            gqt_ref[low:high] = rounded(to_queries(head - 1, 0, *ds_before) * scale)
        if head < HEADS:
            p_local = e_local * inverse
            p_far = e_far * inverse
            delta = jnp.sum(p_local * dp_local, axis=0, keepdims=True) + jnp.sum(
                p_far * dp_far, axis=0, keepdims=True
            )
            pb = rounded(p_local), rounded(p_far)
        coming_dprobs = dprobs(head + 1) if head + 1 < HEADS else None
        if done:
            to_keys(head - 1, width, odt_ref, *pb_before, None)
        if head < HEADS:
            ds = rounded(p_local * (dp_local - delta)), rounded(p_far * (dp_far - delta))
        if done:
            to_keys(head - 1, 0, qt_ref, *ds_before, scale)
        return (coming_scores, coming_dprobs), (pb, ds) if head < HEADS else None

    given, done = (scores(0), dprobs(0)), None
    for head in range(HEADS + 1):
        given, done = step(head, given, done)

    rider_ref[...] = f32_dot(wkv_ref[...], gkvt_ref[:, virt_at:]).T * factor
    weight_sums(
        1 - lax.axis_index("rows") % 2, send_ref, extt_ref, gqt_ref, gkvt_ref, ot_ref, og_ref, factor
    )
    send_ref[2 * width :] = rounded(rider_ref[...])


def weight_sums(core, out_ref, extt_ref, gqt_ref, gkvt_ref, ot_ref, og_ref, factor):
    width, row_count = gqt_ref.shape
    held = own_digit()
    pair, square, _ = exchange_plan()
    rows = 2 * width >> len(pair + square)

    def write(at, total):
        total = (total * factor).astype(out_ref.dtype)
        for start in range(0, width, rows):
            piece = (at * width + start) // rows
            offset = pl.multiple_of((piece ^ held) * rows, ROW_PACK)
            out_ref[pl.ds(offset, rows), :] = total[start : start + rows]

    @pl.when(core == 0)
    def _():
        own = slice(TILE, TILE + row_count)
        write(0, times_transposed(extt_ref[:, own], gqt_ref[...]))
        write(1, times_transposed(extt_ref[...], gkvt_ref[:width]))

    @pl.when(core == 1)
    def _():
        write(0, times_transposed(extt_ref[...], gkvt_ref[width:]))
        write(1, f32_dot(ot_ref[...], og_ref[...]))


def finish_kernel(factor, og_ref, wq_ref, wkv_ref, extt_ref, gqt_ref, gkvt_ref, ot_ref, *refs):
    gf_ref, halo_feat_ref, keep_ref = refs[:3]
    pair_refs = refs[3:]
    width, row_count = gqt_ref.shape
    near = TILE + row_count
    step = pair_refs[0].shape[0]
    slots = step * len(pair_refs)
    weight_sums(
        lax.axis_index("rows") % 2, keep_ref, extt_ref, gqt_ref, gkvt_ref, ot_ref, og_ref, factor
    )
    by_feature = f32_dot(wkv_ref[...], gkvt_ref[:, : near + slots])
    own = by_feature[:, TILE:near] + f32_dot(wq_ref[...], gqt_ref[...])
    gf_ref[...] = own.T
    halo_feat_ref[...] = rounded(by_feature[:, :TILE].T)
    slot_feat = rounded(by_feature[:, near:].T)
    for at, out_ref in enumerate(pair_refs):
        out_ref[...] = slot_feat[at * step : (at + 1) * step]


def place_kernel(*refs):
    part_refs, (gq_hbm, gkv_hbm, go_hbm, all_ref, out_ref, sems) = refs[:-6], refs[-6:]
    width = gq_hbm.shape[0]
    pair, square, _ = exchange_plan()
    half = 1 << len(pair + square)
    rows = 2 * width // half
    step = part_refs[0].shape[0]
    for at, part_ref in enumerate(part_refs):
        all_ref[at * step : (at + 1) * step] = part_ref[...]
    held = own_digit() + (lax.axis_index("rows") % 2) * half
    copies = []
    for at in range(2 * half):
        start = at * rows
        piece = slice(start, start + rows)
        offset = pl.multiple_of((held ^ at) * rows, ROW_PACK)
        out_ref[piece] = all_ref[pl.ds(offset, rows), :].astype(jnp.float32)
        rows_out = pl.ds(start % width, rows)
        which = start // width
        if which == 0:
            target = gq_hbm.at[rows_out]
        elif which == 3:
            target = go_hbm.at[rows_out]
        else:
            target = gkv_hbm.at[rows_out, pl.ds((which - 1) * width, width)]
        copies.append(pltpu.make_async_copy(out_ref.at[piece], target, sems.at[at]))
        copies[-1].start()
    for copy in copies:
        copy.wait()


def return_kernel(gf_ref, chosen_ref, halo_ref, own_ref, through_ref, *refs):
    far_refs, out_ref = refs[:-1], refs[-1]
    row_count = gf_ref.shape[0]
    tile = halo_ref.shape[0]
    per_peer = own_ref.shape[0] // 2
    returned = []
    for at, even_ref in enumerate([own_ref, *far_refs[::-1]]):
        returned += [even_ref[:per_peer], through_ref[at * per_peer : (at + 1) * per_peer]]
    total = gf_ref[...] + rows_contracted(chosen_ref[...], jnp.concatenate(returned, axis=0))
    out_ref[: row_count - tile] = total[: row_count - tile]
    out_ref[row_count - tile :] = total[row_count - tile :] + halo_ref[...].astype(jnp.float32)


def call(kernel, name, outs, args, scratch=(), fetched=0, flops=0, stored=False):
    spaces = [pltpu.HBM] * fetched
    spaces += [pltpu.VMEM] * (len(args) - len(spaces))
    moved = sum(x.size * x.dtype.itemsize for x in list(args) + list(outs))
    scratch = list(scratch)
    if fetched:
        scratch.append(pltpu.SemaphoreType.DMA((fetched,)))
    constrained = [
        pltpu.with_memory_space_constraint(x, pltpu.HBM) if space is pltpu.HBM else x
        for x, space in zip(args, spaces)
    ]
    return pl.pallas_call(
        kernel,
        out_shape=outs,
        in_specs=[pl.BlockSpec(memory_space=space) for space in spaces],
        out_specs=[pl.BlockSpec(memory_space=pl.ANY if stored else pltpu.VMEM)] * len(outs),
        scratch_shapes=scratch,
        compiler_params=pltpu.CompilerParams(vmem_limit_bytes=VMEM_BYTES),
        cost_estimate=pl.CostEstimate(flops=flops, bytes_accessed=moved, transcendentals=0),
        name=name,
    )(*constrained)


def shards(features, out_grad, w_query, w_keyval, w_out, virtual, local_nbr, expander, send_rows):
    row_count, width = features.shape
    dom_size, per_peer = send_rows.shape
    slots = dom_size * per_peer
    virt_rows = virtual.shape[0]
    padded = ROW_PACK * -(-virt_rows // ROW_PACK)
    ext_rows = TILE + row_count + slots + padded
    nodes = row_count * lax.axis_size("dom") * lax.axis_size("rows")
    pair, square, rest = exchange_plan()
    bf16, f32 = jnp.bfloat16, jnp.float32
    shape = jax.ShapeDtypeStruct

    halo, chosen, through, *direct = call(
        pick_kernel,
        "pick_rows",
        [shape((TILE, width), bf16), shape((slots, row_count), bf16)]
        + [shape((slots // 2, width), bf16)]
        + [shape((per_peer, width), bf16)] * (dom_size // 2),
        [features, send_rows],
        [pltpu.VMEM(features.shape, bf16), pltpu.VMEM(send_rows.shape, jnp.int32)],
        fetched=2,
    )
    through = swapped(through, 1, 0)
    prepared = call(
        functools.partial(prepare_kernel, per_peer),
        "prepare",
        [
            shape(out_grad.shape, bf16),
            shape(w_query.shape, bf16),
            shape(w_keyval.shape, bf16),
            shape((width, row_count + padded), bf16),
            shape((width, row_count), bf16),
            shape((width, row_count), bf16),
            shape((row_count + padded, 2 * width), bf16),
            shape((2 * width, row_count + padded), bf16),
            shape((2 * TILE, row_count), f32),
            shape((slots + padded, row_count), f32),
        ],
        [features, out_grad, w_query, w_keyval, w_out, virtual, local_nbr.T, expander.T],
        [
            pltpu.VMEM(features.shape, bf16),
            pltpu.VMEM(w_out.shape, bf16),
            pltpu.VMEM(virtual.shape, bf16),
            pltpu.VMEM(local_nbr.shape[::-1], jnp.int32),
            pltpu.VMEM(expander.shape[::-1], jnp.int32),
        ],
        fetched=8,
        flops=10 * row_count * width * width,
    )
    (through, halo), _ = lax.optimization_barrier(((through, halo), prepared[0]))
    arrived = handed_on(direct, through)
    halo = shifted(halo, "rows", 1)
    message, rider, *gradients = call(
        functools.partial(attend_kernel, nodes**-0.5, per_peer, dom_size),
        "attend",
        [
            shape((2 * width + padded, width), bf16),
            shape((padded, width), f32),
            shape((width, ext_rows), bf16),
            shape((width, row_count), bf16),
            shape((2 * width, ext_rows), bf16),
            shape((width, row_count), bf16),
        ],
        [*arrived, halo, *prepared],
        [
            pltpu.VMEM((slots, width), bf16),
            pltpu.VMEM((ext_rows, 2 * width), bf16),
            pltpu.VMEM((2 * width, ext_rows), bf16),
        ],
        flops=28 * ext_rows * width * width,
    )
    message = swapped(message, *CORES)
    own_feat, halo_feat, keep, *pairs = call(
        functools.partial(finish_kernel, nodes**-0.5),
        "finish",
        [shape((row_count, width), f32), shape((TILE, width), bf16), shape((2 * width, width), f32)]
        + [shape((2 * per_peer, width), bf16)] * (dom_size // 2),
        [*prepared[:3], *gradients],
        flops=6 * ext_rows * width * width,
    )

    keep, rider = added(keep, rounded(rider).astype(f32), {1: message})
    rider = rider[: -(-virt_rows // 8) * 8]
    pairs, _ = lax.optimization_barrier((pairs, keep))
    returned = [swapped(pairs[at], 2 * at, 0) for at in reversed(range(1, dom_size // 2))]
    keep, rider = scattered(keep, rider, square)
    keep, *returned[:-1] = lax.optimization_barrier((keep, *returned[:-1]))
    keep, rider = scattered(keep, rider, pair)
    (returned, halo_feat), _ = lax.optimization_barrier(((returned, halo_feat), keep))
    through = swapped(jnp.concatenate([x[per_peer:] for x in [pairs[0]] + returned[::-1]]), 1, 0)
    halo_back = shifted(halo_feat, "rows", -1)
    for mask in rest:
        message = swapped(with_rider(keep, rider), *mask)
        keep, rider = rounded(keep).astype(f32), rounded(rider).astype(f32)
        keep, rider = added(keep, rider, {1: message})
    (grad_features,) = call(
        return_kernel,
        "return_rows",
        [shape((row_count, width), f32)],
        [own_feat, chosen, halo_back, pairs[0], through, *returned],
    )

    held = rounded(keep)
    held = jnp.concatenate([held, swapped(held, *pair[0])], axis=0)
    held, grad_features = lax.optimization_barrier((held, grad_features))
    arrived = [swapped(held, *masks) for masks in partner_masks(square)[1:]]
    near = [held, *arrived]
    far = [swapped(part, *CORES) for part in near]
    grad_wq, grad_wkv, grad_wo = call(
        place_kernel,
        "place_sums",
        [shape((width, width), f32), shape((width, 2 * width), f32), shape((width, width), f32)],
        [*near, *far],
        [
            pltpu.VMEM((4 * width, width), bf16),
            pltpu.VMEM((4 * width, width), f32),
            pltpu.SemaphoreType.DMA((2 << len(pair + square),)),
        ],
        stored=True,
    )
    return grad_features, grad_wq, grad_wkv, grad_wo, rider[:virt_rows]


def solution(mesh):
    placed = (
        P(("dom", "rows"), None),
        P(("dom", "rows"), None),
        P(),
        P(),
        P(),
        P(),
        P(("dom", "rows"), None),
        P(("dom", "rows"), None),
        P(("dom", "rows"), None),
    )
    return jax.shard_map(
        shards,
        mesh=mesh,
        in_specs=placed,
        out_specs=(P(("dom", "rows"), None), P(), P(), P(), P()),
        check_vma=False,
    )
```

```python
import functools
import math

import jax
import jax.numpy as jnp
from jax import lax
from jax.experimental import pallas as pl
from jax.experimental.pallas import tpu as pltpu
from jax.sharding import PartitionSpec as P

HEADS = 8
TILE = 128
ROW_PACK = 16
NEGATIVE_FILL = -1e30
VMEM_BYTES = 24 * 1024 * 1024
LANES = 128


def f32_dot(left, right):
    return jnp.dot(left, right, preferred_element_type=jnp.float32)


def rows_contracted(left, right):
    return lax.dot_general(
        left, right, (((0,), (0,)), ((), ())), preferred_element_type=jnp.float32
    )


def times_transposed(left, right):
    return lax.dot_general(
        left, right, (((1,), (1,)), ((), ())), preferred_element_type=jnp.float32
    )


def rounded(value):
    return value.astype(jnp.bfloat16)


CORES = (0, 1)


def bits_of(size, first=1):
    return [1 << i for i in range(size.bit_length() - 1) if 1 << i >= first]


def exchange_plan():
    dom_size, rows_size = lax.axis_size("dom"), lax.axis_size("rows")
    pair, square = [(2, 0)], [(1, 0), (0, 2)]
    rest = [(bit, 0) for bit in bits_of(dom_size, 4)] + [(0, bit) for bit in bits_of(rows_size, 4)]
    return pair, square, rest


def partner_masks(block):
    masks = []
    for digit in range(1 << len(block)):
        chosen = [mask for i, mask in enumerate(block) if digit >> i & 1]
        masks.append((sum(mask[0] for mask in chosen), sum(mask[1] for mask in chosen)))
    return masks


def farthest_first(count):
    return sorted(range(1, count), key=lambda digit: (-digit.bit_count(), -digit))


def own_digit():
    pair, square, _ = exchange_plan()
    digit = 0
    for i, (dom_mask, rows_mask) in enumerate(pair + square):
        own = (lax.axis_index("dom") & dom_mask) | (lax.axis_index("rows") & rows_mask)
        digit += jnp.where(own != 0, 1 << i, 0)
    return digit


def swapped(block, dom_mask, rows_mask):
    dom_size, rows_size = lax.axis_size("dom"), lax.axis_size("rows")
    route = [
        (a * rows_size + b, (a ^ dom_mask) * rows_size + (b ^ rows_mask))
        for a in range(dom_size)
        for b in range(rows_size)
    ]
    return lax.ppermute(block, ("dom", "rows"), route)


def shifted(block, axis, distance):
    devices = range(lax.axis_size(axis))
    route = [((i - distance) % len(devices), i) for i in devices]
    return lax.ppermute(block, axis, route)


def paired_sum(terms):
    while len(terms) > 1:
        terms = [left + right for left, right in zip(terms[::2], terms[1::2])]
    return terms[0]


def with_rider(block, rider):
    return jnp.concatenate([rounded(block), rounded(rider)], axis=0)


def added(keep, rider, arrived):
    rows = keep.shape[0]
    riders = [rider] + [arrived[at][rows:].astype(jnp.float32) for at in sorted(arrived)]
    for block in arrived.values():
        keep = keep + block[:rows].astype(jnp.float32)
    return keep, paired_sum(riders)


def scattered(keep, rider, bits):
    masks = partner_masks(bits)
    rows = keep.shape[0] // len(masks)
    parts = [keep[at * rows : (at + 1) * rows] for at in range(len(masks))]
    messages = {at: with_rider(parts[at], rider) for at in farthest_first(len(masks))}
    arrived = {at: swapped(message, *masks[at]) for at, message in messages.items()}
    return added(parts[0], rounded(rider).astype(jnp.float32), arrived)


def handed_on(direct, through):
    rows = direct[0].shape[0]
    arrived = [direct[0], through]
    for at in reversed(range(1, len(direct))):
        message = jnp.concatenate([direct[at], through[at * rows : (at + 1) * rows]], axis=0)
        arrived.append(swapped(message, 2 * at, 0))
    return arrived


def listed_rows(send_ref, row_count):
    dom_size, per_peer = send_ref.shape
    slots = dom_size * per_peer
    slot = lax.broadcasted_iota(jnp.int32, (slots, per_peer), 0)
    place = lax.broadcasted_iota(jnp.int32, (slots, per_peer), 1)
    peer = (slot // per_peer) ^ lax.axis_index("dom")
    listed = jnp.zeros((slots, per_peer), jnp.int32)
    for at in range(dom_size):
        listed += jnp.where((peer == at) & (place == slot % per_peer), send_ref[at : at + 1, :], 0)
    column = jnp.sum(listed, axis=1, keepdims=True)
    rows = lax.broadcasted_iota(jnp.int32, (slots, row_count), 1)
    return jnp.where(column == rows, 1.0, 0.0).astype(jnp.bfloat16)


def fetch(pairs, sems):
    copies = [
        pltpu.make_async_copy(source, target, sems.at[at])
        for at, (source, target) in enumerate(pairs)
    ]
    for copy in copies:
        copy.start()
    return copies


def store_blocks(rows, through_ref, direct_refs):
    size = direct_refs[0].shape[0]
    for at, out_ref in enumerate(direct_refs):
        out_ref[...] = rows[2 * at * size : (2 * at + 1) * size]
        through_ref[at * size : (at + 1) * size] = rows[(2 * at + 1) * size : (2 * at + 2) * size]


def pick_kernel(feat_hbm, send_hbm, halo_ref, chosen_ref, through_ref, *refs):
    direct_refs, (feat_ref, send_ref, sems) = refs[:-3], refs[-3:]
    copies = fetch([(send_hbm, send_ref), (feat_hbm, feat_ref)], sems)
    copies[0].wait()
    chosen_ref[...] = listed_rows(send_ref, feat_ref.shape[0])
    copies[1].wait()
    halo_ref[...] = feat_ref[feat_ref.shape[0] - halo_ref.shape[0] :]
    store_blocks(rounded(f32_dot(chosen_ref[...], feat_ref[...])), through_ref, direct_refs)


def prepare_kernel(
    per_peer,
    feat_hbm,
    og_hbm,
    wq_hbm,
    wkv_hbm,
    wo_hbm,
    virt_hbm,
    nbr_hbm,
    exp_hbm,
    og_ref,
    wq_ref,
    wkv_ref,
    featt_ref,
    qt_ref,
    odt_ref,
    q_ref,
    od_ref,
    kv_ref,
    kvt_ref,
    local_bias_ref,
    far_bias_ref,
    feat_ref,
    wo_ref,
    virt_ref,
    nbr_ref,
    exp_ref,
    sems,
):
    nbr_copy, exp_copy, feat_copy, virt_copy, wq_copy, wkv_copy, og_copy, wo_copy = fetch(
        [
            (nbr_hbm, nbr_ref),
            (exp_hbm, exp_ref),
            (feat_hbm, feat_ref),
            (virt_hbm, virt_ref),
            (wq_hbm, wq_ref),
            (wkv_hbm, wkv_ref),
            (og_hbm, og_ref),
            (wo_hbm, wo_ref),
        ],
        sems,
    )
    row_count, width = feat_ref.shape
    window = local_bias_ref.shape[0]
    far = far_bias_ref.shape[0]
    virt_rows = virt_ref.shape[0]
    padded = kv_ref.shape[0] - row_count
    slots = far - padded
    scale = 1.0 / math.sqrt(width // HEADS)

    def multiplicity(key_rows, named):
        position = lax.broadcasted_iota(jnp.int32, (key_rows, row_count), 0)
        count = jnp.zeros((key_rows, row_count), jnp.float32)
        for at in range(named.shape[0]):
            count += jnp.where(named[at : at + 1, :] == position, 1.0, 0.0)
        return count

    nbr_copy.wait()
    local_bias_ref[...] = jnp.where(multiplicity(window, nbr_ref) > 0.0, 0.0, NEGATIVE_FILL)
    exp_copy.wait()
    expander = exp_ref[...]
    expander = ((expander // per_peer) ^ lax.axis_index("dom")) * per_peer + expander % per_peer
    named_times = multiplicity(slots, expander)
    slot_bias = jnp.full((slots, row_count), NEGATIVE_FILL, jnp.float32)
    for times in range(1, exp_ref.shape[0] + 1):
        slot_bias = jnp.where(named_times == float(times), math.log(times) / scale, slot_bias)
    far_bias_ref[:slots] = slot_bias
    virt_row = lax.broadcasted_iota(jnp.int32, (padded, row_count), 0)
    far_bias_ref[slots:] = jnp.where(virt_row < virt_rows, 0.0, NEGATIVE_FILL)

    feat_copy.wait()
    featt_ref[:, :row_count] = feat_ref[...].T
    virt_copy.wait()
    virt = jnp.concatenate(
        [virt_ref[...], jnp.zeros((padded - virt_rows, width), jnp.bfloat16)], axis=0
    )
    featt_ref[:, row_count:] = virt.T
    wq_copy.wait()
    qt_ref[...] = rounded(rows_contracted(wq_ref[...], featt_ref[:, :row_count]))
    wkv_copy.wait()
    kv_ref[:row_count] = rounded(f32_dot(feat_ref[...], wkv_ref[...]))
    kv_ref[row_count:] = rounded(f32_dot(virt, wkv_ref[...]))
    kvt_ref[...] = kv_ref[...].T
    og_copy.wait()
    wo_copy.wait()
    odt_ref[...] = rounded(times_transposed(wo_ref[...], og_ref[...]))
    q_ref[...] = qt_ref[...].T
    od_ref[...] = odt_ref[...].T


def attend_kernel(
    factor,
    per_peer,
    dom_size,
    *refs,
):
    count = dom_size // 2 + 1
    piece_refs, halo_ref, refs = refs[:count], refs[count], refs[count + 1 :]
    og_ref, wq_ref, wkv_ref, featt_ref, qt_ref, odt_ref, q_ref, od_ref = refs[:8]
    own_kv_ref, own_kvt_ref, local_bias_ref, far_bias_ref, send_ref, rider_ref = refs[8:14]
    extt_ref, gqt_ref, gkv_ref, ot_ref, slot_ref, kv_ref, kvt_ref, sum_ref = refs[14:]
    width, row_count = qt_ref.shape
    tile = halo_ref.shape[0]
    tile_count = row_count // tile
    slots = dom_size * per_peer
    near = tile + row_count
    virt_at = near + slots
    head_dim = width // HEADS
    scale = 1.0 / math.sqrt(head_dim)

    kv_ref[tile:near] = own_kv_ref[:row_count]
    kv_ref[virt_at:] = own_kv_ref[row_count:]
    kvt_ref[:, tile:near] = own_kvt_ref[:, :row_count]
    kvt_ref[:, virt_at:] = own_kvt_ref[:, row_count:]
    extt_ref[:, tile:near] = featt_ref[:, :row_count]
    extt_ref[:, virt_at:] = featt_ref[:, row_count:]
    slot_ref[:per_peer] = piece_refs[0][...]
    slot_ref[per_peer : 2 * per_peer] = piece_refs[1][:per_peer]
    for at, piece_ref in enumerate(piece_refs[:1:-1], 1):
        slot_ref[2 * at * per_peer : (2 * at + 2) * per_peer] = piece_ref[...]
    for rows, source_ref in ((slice(0, tile), halo_ref), (slice(near, virt_at), slot_ref)):
        extt_ref[:, rows] = source_ref[...].T
        kv_ref[rows] = rounded(f32_dot(source_ref[...], wkv_ref[...]))
        kvt_ref[:, rows] = kv_ref[rows].T

    def tiles(of):
        return jnp.concatenate([of(t, slice(t * tile, (t + 1) * tile)) for t in range(tile_count)], 1)

    def bounds(head):
        low, high = head * head_dim, (head + 1) * head_dim
        return low, high, low // LANES * LANES, min(-(-high // LANES) * LANES, width)

    def products(head):
        low, high, first, last = bounds(head)
        column = lax.broadcasted_iota(jnp.int32, (last - first, row_count), 0) + first
        of_head = (column >= low) & (column < high)
        out = []
        for rows_ref, start in ((qt_ref, 0), (odt_ref, width)):
            operand = jnp.where(of_head, rows_ref[first:last, :], 0)
            every = f32_dot(kv_ref[:, start + first : start + last], operand)
            out.append(tiles(lambda t, lanes: every[t * tile : (t + 2) * tile, lanes]))
            out.append(every[near:])
        return out

    def weights(s_local, s_far, dp_local, dp_far):
        s_local += local_bias_ref[...]
        s_far += far_bias_ref[...]
        peak = jnp.maximum(
            jnp.max(s_local, axis=0, keepdims=True), jnp.max(s_far, axis=0, keepdims=True)
        )
        exponent_scale = scale * math.log2(math.e)
        e_local = jnp.exp2((s_local - peak) * exponent_scale)
        e_far = jnp.exp2((s_far - peak) * exponent_scale)
        total = jnp.sum(e_local, axis=0, keepdims=True) + jnp.sum(e_far, axis=0, keepdims=True)
        inverse = 1.0 / total
        p_local = e_local * inverse
        p_far = e_far * inverse
        delta = jnp.sum(p_local * dp_local, axis=0, keepdims=True) + jnp.sum(
            p_far * dp_far, axis=0, keepdims=True
        )
        ds_local = rounded(p_local * (dp_local - delta))
        ds_far = rounded(p_far * (dp_far - delta))
        return rounded(p_local), rounded(p_far), ds_local, ds_far

    def outputs(head, pb_local, pb_far, ds_local, ds_far):
        low, high, first, last = bounds(head)

        def to_queries(start, local, beyond):
            rows = slice(start + low, start + high)
            near_part = tiles(
                lambda t, lanes: f32_dot(kvt_ref[rows, t * tile : (t + 2) * tile], local[:, lanes])
            )
            return near_part + f32_dot(kvt_ref[rows, near:], beyond)

        def to_keys(start, rows_ref, local, beyond):
            column = lax.broadcasted_iota(jnp.int32, (row_count, last - first), 1) + first
            of_head = (column >= low) & (column < high)
            operand = jnp.where(of_head, rows_ref[:, first:last], 0)
            columns = slice(start + first, start + last)
            for t in range(tile_count):
                lanes = slice(t * tile, (t + 1) * tile)
                sum_ref[t * tile : (t + 2) * tile, columns] += f32_dot(local[:, lanes], operand[lanes])
            sum_ref[near:, columns] += f32_dot(beyond, operand)

        ot_ref[low:high] = rounded(to_queries(width, pb_local, pb_far))
        gqt_ref[low:high] = rounded(to_queries(0, ds_local, ds_far) * scale)
        to_keys(0, q_ref, ds_local, ds_far)
        to_keys(width, od_ref, pb_local, pb_far)

    sum_ref[...] = jnp.zeros_like(sum_ref)

    coming = products(0)
    done = None
    for head in range(HEADS):
        now = coming
        if head + 1 < HEADS:
            coming = products(head + 1)
        if done is not None:
            outputs(head - 1, *done)
        done = weights(*now)
    outputs(HEADS - 1, *done)

    gkv_ref[:, :width] = rounded(sum_ref[:, :width] * scale)
    gkv_ref[:, width:] = rounded(sum_ref[:, width:])
    rider_ref[...] = times_transposed(gkv_ref[virt_at:], wkv_ref[...]) * factor
    weight_sums(
        1 - lax.axis_index("rows") % 2, send_ref, extt_ref, gqt_ref, gkv_ref, ot_ref, og_ref, factor
    )
    send_ref[2 * width :] = rounded(rider_ref[...])


def weight_sums(core, out_ref, extt_ref, gqt_ref, gkv_ref, ot_ref, og_ref, factor):
    width, row_count = gqt_ref.shape
    held = own_digit()
    pair, square, _ = exchange_plan()
    rows = 2 * width >> len(pair + square)

    def write(at, total):
        total = (total * factor).astype(out_ref.dtype)
        for start in range(0, width, rows):
            piece = (at * width + start) // rows
            offset = pl.multiple_of((piece ^ held) * rows, ROW_PACK)
            out_ref[pl.ds(offset, rows), :] = total[start : start + rows]

    @pl.when(core == 0)
    def _():
        own = slice(TILE, TILE + row_count)
        write(0, times_transposed(extt_ref[:, own], gqt_ref[...]))
        write(1, f32_dot(extt_ref[...], gkv_ref[:, :width]))

    @pl.when(core == 1)
    def _():
        write(0, f32_dot(extt_ref[...], gkv_ref[:, width:]))
        write(1, f32_dot(ot_ref[...], og_ref[...]))


def finish_kernel(factor, og_ref, wq_ref, wkv_ref, extt_ref, gqt_ref, gkv_ref, ot_ref, *refs):
    gf_ref, halo_feat_ref, keep_ref = refs[:3]
    pair_refs = refs[3:]
    width, row_count = gqt_ref.shape
    near = TILE + row_count
    step = pair_refs[0].shape[0]
    slots = step * len(pair_refs)
    weight_sums(
        lax.axis_index("rows") % 2, keep_ref, extt_ref, gqt_ref, gkv_ref, ot_ref, og_ref, factor
    )
    rows = times_transposed(gkv_ref[: near + slots], wkv_ref[...])
    gf_ref[...] = rows[TILE:near] + times_transposed(gqt_ref[...].T, wq_ref[...])
    halo_feat_ref[...] = rounded(rows[:TILE])
    for at, out_ref in enumerate(pair_refs):
        out_ref[...] = rounded(rows[near + at * step : near + (at + 1) * step])


def place_kernel(*refs):
    part_refs, (gq_hbm, gkv_hbm, go_hbm, all_ref, out_ref, sems) = refs[:-6], refs[-6:]
    width = gq_hbm.shape[0]
    pair, square, _ = exchange_plan()
    half = 1 << len(pair + square)
    rows = 2 * width // half
    step = part_refs[0].shape[0]
    for at, part_ref in enumerate(part_refs):
        all_ref[at * step : (at + 1) * step] = part_ref[...]
    held = own_digit() + (lax.axis_index("rows") % 2) * half
    copies = []
    for at in range(2 * half):
        start = at * rows
        piece = slice(start, start + rows)
        offset = pl.multiple_of((held ^ at) * rows, ROW_PACK)
        out_ref[piece] = all_ref[pl.ds(offset, rows), :].astype(jnp.float32)
        rows_out = pl.ds(start % width, rows)
        which = start // width
        if which == 0:
            target = gq_hbm.at[rows_out]
        elif which == 3:
            target = go_hbm.at[rows_out]
        else:
            target = gkv_hbm.at[rows_out, pl.ds((which - 1) * width, width)]
        copies.append(pltpu.make_async_copy(out_ref.at[piece], target, sems.at[at]))
        copies[-1].start()
    for copy in copies:
        copy.wait()


def return_kernel(gf_ref, chosen_ref, halo_ref, own_ref, through_ref, *refs):
    far_refs, out_ref = refs[:-1], refs[-1]
    row_count = gf_ref.shape[0]
    tile = halo_ref.shape[0]
    per_peer = own_ref.shape[0] // 2
    returned = []
    for at, even_ref in enumerate([own_ref, *far_refs[::-1]]):
        returned += [even_ref[:per_peer], through_ref[at * per_peer : (at + 1) * per_peer]]
    total = gf_ref[...] + rows_contracted(chosen_ref[...], jnp.concatenate(returned, axis=0))
    out_ref[: row_count - tile] = total[: row_count - tile]
    out_ref[row_count - tile :] = total[row_count - tile :] + halo_ref[...].astype(jnp.float32)


def call(kernel, name, outs, args, scratch=(), fetched=0, flops=0, stored=False):
    spaces = [pltpu.HBM] * fetched
    spaces += [pltpu.VMEM] * (len(args) - len(spaces))
    moved = sum(x.size * x.dtype.itemsize for x in list(args) + list(outs))
    scratch = list(scratch)
    if fetched:
        scratch.append(pltpu.SemaphoreType.DMA((fetched,)))
    constrained = [
        pltpu.with_memory_space_constraint(x, pltpu.HBM) if space is pltpu.HBM else x
        for x, space in zip(args, spaces)
    ]
    return pl.pallas_call(
        kernel,
        out_shape=outs,
        in_specs=[pl.BlockSpec(memory_space=space) for space in spaces],
        out_specs=[pl.BlockSpec(memory_space=pl.ANY if stored else pltpu.VMEM)] * len(outs),
        scratch_shapes=scratch,
        compiler_params=pltpu.CompilerParams(vmem_limit_bytes=VMEM_BYTES),
        cost_estimate=pl.CostEstimate(flops=flops, bytes_accessed=moved, transcendentals=0),
        name=name,
    )(*constrained)


def shards(features, out_grad, w_query, w_keyval, w_out, virtual, local_nbr, expander, send_rows):
    row_count, width = features.shape
    dom_size, per_peer = send_rows.shape
    slots = dom_size * per_peer
    virt_rows = virtual.shape[0]
    padded = ROW_PACK * -(-virt_rows // ROW_PACK)
    ext_rows = TILE + row_count + slots + padded
    nodes = row_count * lax.axis_size("dom") * lax.axis_size("rows")
    pair, square, rest = exchange_plan()
    bf16, f32 = jnp.bfloat16, jnp.float32
    shape = jax.ShapeDtypeStruct

    halo, chosen, through, *direct = call(
        pick_kernel,
        "pick_rows",
        [shape((TILE, width), bf16), shape((slots, row_count), bf16)]
        + [shape((slots // 2, width), bf16)]
        + [shape((per_peer, width), bf16)] * (dom_size // 2),
        [features, send_rows],
        [pltpu.VMEM(features.shape, bf16), pltpu.VMEM(send_rows.shape, jnp.int32)],
        fetched=2,
    )
    through = swapped(through, 1, 0)
    prepared = call(
        functools.partial(prepare_kernel, per_peer),
        "prepare",
        [
            shape(out_grad.shape, bf16),
            shape(w_query.shape, bf16),
            shape(w_keyval.shape, bf16),
            shape((width, row_count + padded), bf16),
            shape((width, row_count), bf16),
            shape((width, row_count), bf16),
            shape((row_count, width), bf16),
            shape((row_count, width), bf16),
            shape((row_count + padded, 2 * width), bf16),
            shape((2 * width, row_count + padded), bf16),
            shape((2 * TILE, row_count), f32),
            shape((slots + padded, row_count), f32),
        ],
        [features, out_grad, w_query, w_keyval, w_out, virtual, local_nbr.T, expander.T],
        [
            pltpu.VMEM(features.shape, bf16),
            pltpu.VMEM(w_out.shape, bf16),
            pltpu.VMEM(virtual.shape, bf16),
            pltpu.VMEM(local_nbr.shape[::-1], jnp.int32),
            pltpu.VMEM(expander.shape[::-1], jnp.int32),
        ],
        fetched=8,
        flops=10 * row_count * width * width,
    )
    (through, halo), _ = lax.optimization_barrier(((through, halo), prepared[0]))
    arrived = handed_on(direct, through)
    halo = shifted(halo, "rows", 1)
    message, rider, *gradients = call(
        functools.partial(attend_kernel, nodes**-0.5, per_peer, dom_size),
        "attend",
        [
            shape((2 * width + padded, width), bf16),
            shape((padded, width), f32),
            shape((width, ext_rows), bf16),
            shape((width, row_count), bf16),
            shape((ext_rows, 2 * width), bf16),
            shape((width, row_count), bf16),
        ],
        [*arrived, halo, *prepared],
        [
            pltpu.VMEM((slots, width), bf16),
            pltpu.VMEM((ext_rows, 2 * width), bf16),
            pltpu.VMEM((2 * width, ext_rows), bf16),
            pltpu.VMEM((ext_rows, 2 * width), f32),
        ],
        flops=28 * ext_rows * width * width,
    )
    message = swapped(message, *CORES)
    own_feat, halo_feat, keep, *pairs = call(
        functools.partial(finish_kernel, nodes**-0.5),
        "finish",
        [shape((row_count, width), f32), shape((TILE, width), bf16), shape((2 * width, width), f32)]
        + [shape((2 * per_peer, width), bf16)] * (dom_size // 2),
        [*prepared[:3], *gradients],
        flops=6 * ext_rows * width * width,
    )

    keep, rider = added(keep, rounded(rider).astype(f32), {1: message})
    rider = rider[: -(-virt_rows // 8) * 8]
    pairs, _ = lax.optimization_barrier((pairs, keep))
    returned = [swapped(pairs[at], 2 * at, 0) for at in reversed(range(1, dom_size // 2))]
    keep, rider = scattered(keep, rider, square)
    keep, *returned[:-1] = lax.optimization_barrier((keep, *returned[:-1]))
    keep, rider = scattered(keep, rider, pair)
    (returned, halo_feat), _ = lax.optimization_barrier(((returned, halo_feat), keep))
    through = swapped(jnp.concatenate([x[per_peer:] for x in [pairs[0]] + returned[::-1]]), 1, 0)
    halo_back = shifted(halo_feat, "rows", -1)
    for mask in rest:
        message = swapped(with_rider(keep, rider), *mask)
        keep, rider = rounded(keep).astype(f32), rounded(rider).astype(f32)
        keep, rider = added(keep, rider, {1: message})
    (grad_features,) = call(
        return_kernel,
        "return_rows",
        [shape((row_count, width), f32)],
        [own_feat, chosen, halo_back, pairs[0], through, *returned],
    )

    held = rounded(keep)
    held = jnp.concatenate([held, swapped(held, *pair[0])], axis=0)
    held, grad_features = lax.optimization_barrier((held, grad_features))
    arrived = [swapped(held, *masks) for masks in partner_masks(square)[1:]]
    near = [held, *arrived]
    far = [swapped(part, *CORES) for part in near]
    grad_wq, grad_wkv, grad_wo = call(
        place_kernel,
        "place_sums",
        [shape((width, width), f32), shape((width, 2 * width), f32), shape((width, width), f32)],
        [*near, *far],
        [
            pltpu.VMEM((4 * width, width), bf16),
            pltpu.VMEM((4 * width, width), f32),
            pltpu.SemaphoreType.DMA((2 << len(pair + square),)),
        ],
        stored=True,
    )
    return grad_features, grad_wq, grad_wkv, grad_wo, rider[:virt_rows]


def solution(mesh):
    placed = (
        P(("dom", "rows"), None),
        P(("dom", "rows"), None),
        P(),
        P(),
        P(),
        P(),
        P(("dom", "rows"), None),
        P(("dom", "rows"), None),
        P(("dom", "rows"), None),
    )
    return jax.shard_map(
        shards,
        mesh=mesh,
        in_specs=placed,
        out_specs=(P(("dom", "rows"), None), P(), P(), P(), P()),
        check_vma=False,
    )
```

```python
import functools
import math

import jax
import jax.numpy as jnp
from jax import lax
from jax.experimental import pallas as pl
from jax.experimental.pallas import tpu as pltpu
from jax.sharding import PartitionSpec as P

HEADS = 8
TILE = 128
ROW_PACK = 16
NEGATIVE_FILL = -1e30
VMEM_BYTES = 24 * 1024 * 1024
LANES = 128


def f32_dot(left, right):
    return jnp.dot(left, right, preferred_element_type=jnp.float32)


def rows_contracted(left, right):
    return lax.dot_general(
        left, right, (((0,), (0,)), ((), ())), preferred_element_type=jnp.float32
    )


def times_transposed(left, right):
    return lax.dot_general(
        left, right, (((1,), (1,)), ((), ())), preferred_element_type=jnp.float32
    )


def rounded(value):
    return value.astype(jnp.bfloat16)


CORES = (0, 1)


def bits_of(size, first=1):
    return [1 << i for i in range(size.bit_length() - 1) if 1 << i >= first]


def exchange_plan():
    dom_size, rows_size = lax.axis_size("dom"), lax.axis_size("rows")
    pair, square = [(2, 0)], [(1, 0), (0, 2)]
    rest = [(bit, 0) for bit in bits_of(dom_size, 4)] + [(0, bit) for bit in bits_of(rows_size, 4)]
    return pair, square, rest


def partner_masks(block):
    masks = []
    for digit in range(1 << len(block)):
        chosen = [mask for i, mask in enumerate(block) if digit >> i & 1]
        masks.append((sum(mask[0] for mask in chosen), sum(mask[1] for mask in chosen)))
    return masks


def farthest_first(count):
    return sorted(range(1, count), key=lambda digit: (-digit.bit_count(), -digit))


def own_digit():
    pair, square, _ = exchange_plan()
    digit = 0
    for i, (dom_mask, rows_mask) in enumerate(pair + square):
        own = (lax.axis_index("dom") & dom_mask) | (lax.axis_index("rows") & rows_mask)
        digit += jnp.where(own != 0, 1 << i, 0)
    return digit


def swapped(block, dom_mask, rows_mask):
    dom_size, rows_size = lax.axis_size("dom"), lax.axis_size("rows")
    route = [
        (a * rows_size + b, (a ^ dom_mask) * rows_size + (b ^ rows_mask))
        for a in range(dom_size)
        for b in range(rows_size)
    ]
    return lax.ppermute(block, ("dom", "rows"), route)


def shifted(block, axis, distance):
    devices = range(lax.axis_size(axis))
    route = [((i - distance) % len(devices), i) for i in devices]
    return lax.ppermute(block, axis, route)


def paired_sum(terms):
    while len(terms) > 1:
        terms = [left + right for left, right in zip(terms[::2], terms[1::2])]
    return terms[0]


def with_rider(block, rider):
    return jnp.concatenate([rounded(block), rounded(rider)], axis=0)


def added(keep, rider, arrived):
    rows = keep.shape[0]
    riders = [rider] + [arrived[at][rows:].astype(jnp.float32) for at in sorted(arrived)]
    for block in arrived.values():
        keep = keep + block[:rows].astype(jnp.float32)
    return keep, paired_sum(riders)


def scattered(keep, rider, bits):
    masks = partner_masks(bits)
    rows = keep.shape[0] // len(masks)
    parts = [keep[at * rows : (at + 1) * rows] for at in range(len(masks))]
    messages = {at: with_rider(parts[at], rider) for at in farthest_first(len(masks))}
    arrived = {at: swapped(message, *masks[at]) for at, message in messages.items()}
    return added(parts[0], rounded(rider).astype(jnp.float32), arrived)


def handed_on(direct, through):
    rows = direct[0].shape[0]
    arrived = [direct[0], through]
    for at in reversed(range(1, len(direct))):
        message = jnp.concatenate([direct[at], through[at * rows : (at + 1) * rows]], axis=0)
        arrived.append(swapped(message, 2 * at, 0))
    return arrived


def listed_rows(send_ref, row_count):
    dom_size, per_peer = send_ref.shape
    slots = dom_size * per_peer
    slot = lax.broadcasted_iota(jnp.int32, (slots, per_peer), 0)
    place = lax.broadcasted_iota(jnp.int32, (slots, per_peer), 1)
    peer = (slot // per_peer) ^ lax.axis_index("dom")
    listed = jnp.zeros((slots, per_peer), jnp.int32)
    for at in range(dom_size):
        listed += jnp.where((peer == at) & (place == slot % per_peer), send_ref[at : at + 1, :], 0)
    column = jnp.sum(listed, axis=1, keepdims=True)
    rows = lax.broadcasted_iota(jnp.int32, (slots, row_count), 1)
    return jnp.where(column == rows, 1.0, 0.0).astype(jnp.bfloat16)


def fetch(pairs, sems):
    copies = [
        pltpu.make_async_copy(source, target, sems.at[at])
        for at, (source, target) in enumerate(pairs)
    ]
    for copy in copies:
        copy.start()
    return copies


def store_blocks(rows, through_ref, direct_refs):
    size = direct_refs[0].shape[0]
    for at, out_ref in enumerate(direct_refs):
        out_ref[...] = rows[2 * at * size : (2 * at + 1) * size]
        through_ref[at * size : (at + 1) * size] = rows[(2 * at + 1) * size : (2 * at + 2) * size]


def pick_kernel(feat_hbm, send_hbm, halo_ref, chosen_ref, through_ref, *refs):
    direct_refs, (feat_ref, send_ref, sems) = refs[:-3], refs[-3:]
    copies = fetch([(send_hbm, send_ref), (feat_hbm, feat_ref)], sems)
    copies[0].wait()
    chosen_ref[...] = listed_rows(send_ref, feat_ref.shape[0])
    copies[1].wait()
    halo_ref[...] = feat_ref[feat_ref.shape[0] - halo_ref.shape[0] :]
    store_blocks(rounded(f32_dot(chosen_ref[...], feat_ref[...])), through_ref, direct_refs)


def prepare_kernel(
    per_peer,
    feat_hbm,
    og_hbm,
    wq_hbm,
    wkv_hbm,
    wo_hbm,
    virt_hbm,
    nbr_hbm,
    exp_hbm,
    og_ref,
    wq_ref,
    wkv_ref,
    featt_ref,
    qt_ref,
    odt_ref,
    kv_ref,
    kvt_ref,
    local_bias_ref,
    far_bias_ref,
    feat_ref,
    wo_ref,
    virt_ref,
    nbr_ref,
    exp_ref,
    sems,
):
    nbr_copy, exp_copy, feat_copy, virt_copy, wq_copy, wkv_copy, og_copy, wo_copy = fetch(
        [
            (nbr_hbm, nbr_ref),
            (exp_hbm, exp_ref),
            (feat_hbm, feat_ref),
            (virt_hbm, virt_ref),
            (wq_hbm, wq_ref),
            (wkv_hbm, wkv_ref),
            (og_hbm, og_ref),
            (wo_hbm, wo_ref),
        ],
        sems,
    )
    row_count, width = feat_ref.shape
    window = local_bias_ref.shape[0]
    far = far_bias_ref.shape[0]
    virt_rows = virt_ref.shape[0]
    padded = kv_ref.shape[0] - row_count
    slots = far - padded
    scale = 1.0 / math.sqrt(width // HEADS)

    def multiplicity(key_rows, named):
        position = lax.broadcasted_iota(jnp.int32, (key_rows, row_count), 0)
        count = jnp.zeros((key_rows, row_count), jnp.float32)
        for at in range(named.shape[0]):
            count += jnp.where(named[at : at + 1, :] == position, 1.0, 0.0)
        return count

    nbr_copy.wait()
    local_bias_ref[...] = jnp.where(multiplicity(window, nbr_ref) > 0.0, 0.0, NEGATIVE_FILL)
    exp_copy.wait()
    expander = exp_ref[...]
    expander = ((expander // per_peer) ^ lax.axis_index("dom")) * per_peer + expander % per_peer
    named_times = multiplicity(slots, expander)
    slot_bias = jnp.full((slots, row_count), NEGATIVE_FILL, jnp.float32)
    for times in range(1, exp_ref.shape[0] + 1):
        slot_bias = jnp.where(named_times == float(times), math.log(times) / scale, slot_bias)
    far_bias_ref[:slots] = slot_bias
    virt_row = lax.broadcasted_iota(jnp.int32, (padded, row_count), 0)
    far_bias_ref[slots:] = jnp.where(virt_row < virt_rows, 0.0, NEGATIVE_FILL)

    feat_copy.wait()
    featt_ref[:, :row_count] = feat_ref[...].T
    virt_copy.wait()
    virt = jnp.concatenate(
        [virt_ref[...], jnp.zeros((padded - virt_rows, width), jnp.bfloat16)], axis=0
    )
    featt_ref[:, row_count:] = virt.T
    wq_copy.wait()
    qt_ref[...] = rounded(rows_contracted(wq_ref[...], featt_ref[:, :row_count]))
    wkv_copy.wait()
    kv_ref[:row_count] = rounded(f32_dot(feat_ref[...], wkv_ref[...]))
    kv_ref[row_count:] = rounded(f32_dot(virt, wkv_ref[...]))
    kvt_ref[...] = kv_ref[...].T
    og_copy.wait()
    wo_copy.wait()
    odt_ref[...] = rounded(times_transposed(wo_ref[...], og_ref[...]))


def attend_kernel(
    factor,
    per_peer,
    dom_size,
    *refs,
):
    count = dom_size // 2 + 1
    piece_refs, halo_ref, refs = refs[:count], refs[count], refs[count + 1 :]
    og_ref, wq_ref, wkv_ref, featt_ref, qt_ref, odt_ref, own_kv_ref, own_kvt_ref = refs[:8]
    local_bias_ref, far_bias_ref, send_ref, rider_ref = refs[8:12]
    extt_ref, gqt_ref, gkvt_ref, ot_ref, slot_ref, kv_ref, kvt_ref = refs[12:]
    width, row_count = qt_ref.shape
    tile = halo_ref.shape[0]
    tile_count = row_count // tile
    slots = dom_size * per_peer
    near = tile + row_count
    virt_at = near + slots
    head_dim = width // HEADS
    scale = 1.0 / math.sqrt(head_dim)

    kv_ref[tile:near] = own_kv_ref[:row_count]
    kv_ref[virt_at:] = own_kv_ref[row_count:]
    kvt_ref[:, tile:near] = own_kvt_ref[:, :row_count]
    kvt_ref[:, virt_at:] = own_kvt_ref[:, row_count:]
    extt_ref[:, tile:near] = featt_ref[:, :row_count]
    extt_ref[:, virt_at:] = featt_ref[:, row_count:]
    slot_ref[:per_peer] = piece_refs[0][...]
    slot_ref[per_peer : 2 * per_peer] = piece_refs[1][:per_peer]
    for at, piece_ref in enumerate(piece_refs[:1:-1], 1):
        slot_ref[2 * at * per_peer : (2 * at + 2) * per_peer] = piece_ref[...]
    for rows, source_ref in ((slice(0, tile), halo_ref), (slice(near, virt_at), slot_ref)):
        extt_ref[:, rows] = source_ref[...].T
        kv_ref[rows] = rounded(f32_dot(source_ref[...], wkv_ref[...]))
        kvt_ref[:, rows] = kv_ref[rows].T

    def tiles(of):
        return jnp.concatenate([of(t, slice(t * tile, (t + 1) * tile)) for t in range(tile_count)], 1)

    def bounds(head):
        low, high = head * head_dim, (head + 1) * head_dim
        return low, high, low // LANES * LANES, min(-(-high // LANES) * LANES, width)

    def products(head):
        low, high, first, last = bounds(head)
        column = lax.broadcasted_iota(jnp.int32, (last - first, row_count), 0) + first
        of_head = (column >= low) & (column < high)
        out = []
        for rows_ref, start in ((qt_ref, 0), (odt_ref, width)):
            operand = jnp.where(of_head, rows_ref[first:last, :], 0)
            every = f32_dot(kv_ref[:, start + first : start + last], operand)
            out.append(tiles(lambda t, lanes: every[t * tile : (t + 2) * tile, lanes]))
            out.append(every[near:])
        return out

    def weights(s_local, s_far, dp_local, dp_far):
        s_local += local_bias_ref[...]
        s_far += far_bias_ref[...]
        peak = jnp.maximum(
            jnp.max(s_local, axis=0, keepdims=True), jnp.max(s_far, axis=0, keepdims=True)
        )
        exponent_scale = scale * math.log2(math.e)
        e_local = jnp.exp2((s_local - peak) * exponent_scale)
        e_far = jnp.exp2((s_far - peak) * exponent_scale)
        total = jnp.sum(e_local, axis=0, keepdims=True) + jnp.sum(e_far, axis=0, keepdims=True)
        inverse = 1.0 / total
        delta = inverse * (
            jnp.sum(e_local * dp_local, axis=0, keepdims=True)
            + jnp.sum(e_far * dp_far, axis=0, keepdims=True)
        )
        p_local = e_local * inverse
        p_far = e_far * inverse
        ds_local = rounded(p_local * (dp_local - delta))
        ds_far = rounded(p_far * (dp_far - delta))
        return rounded(p_local), rounded(p_far), ds_local, ds_far

    def outputs(head, pb_local, pb_far, ds_local, ds_far):
        low, high, _, _ = bounds(head)

        def to_queries(start, local, beyond):
            rows = slice(start + low, start + high)
            near_part = tiles(
                lambda t, lanes: f32_dot(kvt_ref[rows, t * tile : (t + 2) * tile], local[:, lanes])
            )
            return near_part + f32_dot(kvt_ref[rows, near:], beyond)

        def to_keys(start, operand, local, beyond, factor):
            rows = slice(start + low, start + high)
            parts = []
            carried = None
            for t in range(tile_count):
                lanes = slice(t * tile, (t + 1) * tile)
                window = times_transposed(operand[:, lanes], local[:, lanes])
                previous = window[:, :tile]
                parts.append(previous if carried is None else previous + carried)
                carried = window[:, tile:]
            parts.append(carried)
            parts.append(times_transposed(operand, beyond))
            gathered = jnp.concatenate(parts, axis=1)
            gkvt_ref[rows] = rounded(gathered if factor is None else gathered * factor)

        ot_ref[low:high] = rounded(to_queries(width, pb_local, pb_far))
        gqt_ref[low:high] = rounded(to_queries(0, ds_local, ds_far) * scale)
        to_keys(0, qt_ref[low:high], ds_local, ds_far, scale)
        to_keys(width, odt_ref[low:high], pb_local, pb_far, None)

    coming = products(0)
    done = None
    for head in range(HEADS):
        now = coming
        if head + 1 < HEADS:
            coming = products(head + 1)
        if done is not None:
            outputs(head - 1, *done)
        done = weights(*now)
    outputs(HEADS - 1, *done)

    rider_ref[...] = f32_dot(wkv_ref[...], gkvt_ref[:, virt_at:]).T * factor
    weight_sums(
        1 - lax.axis_index("rows") % 2, send_ref, extt_ref, gqt_ref, gkvt_ref, ot_ref, og_ref, factor
    )
    send_ref[2 * width :] = rounded(rider_ref[...])


def weight_sums(core, out_ref, extt_ref, gqt_ref, gkvt_ref, ot_ref, og_ref, factor):
    width, row_count = gqt_ref.shape
    held = own_digit()
    pair, square, _ = exchange_plan()
    rows = 2 * width >> len(pair + square)

    def write(at, total):
        total = (total * factor).astype(out_ref.dtype)
        for start in range(0, width, rows):
            piece = (at * width + start) // rows
            offset = pl.multiple_of((piece ^ held) * rows, ROW_PACK)
            out_ref[pl.ds(offset, rows), :] = total[start : start + rows]

    @pl.when(core == 0)
    def _():
        own = slice(TILE, TILE + row_count)
        write(0, times_transposed(extt_ref[:, own], gqt_ref[...]))
        write(1, times_transposed(extt_ref[...], gkvt_ref[:width]))

    @pl.when(core == 1)
    def _():
        write(0, times_transposed(extt_ref[...], gkvt_ref[width:]))
        write(1, f32_dot(ot_ref[...], og_ref[...]))


def finish_kernel(factor, og_ref, wq_ref, wkv_ref, extt_ref, gqt_ref, gkvt_ref, ot_ref, *refs):
    gf_ref, halo_feat_ref, keep_ref = refs[:3]
    pair_refs = refs[3:]
    width, row_count = gqt_ref.shape
    near = TILE + row_count
    step = pair_refs[0].shape[0]
    slots = step * len(pair_refs)
    weight_sums(
        lax.axis_index("rows") % 2, keep_ref, extt_ref, gqt_ref, gkvt_ref, ot_ref, og_ref, factor
    )
    by_feature = f32_dot(wkv_ref[...], gkvt_ref[:, : near + slots])
    own = by_feature[:, TILE:near] + f32_dot(wq_ref[...], gqt_ref[...])
    gf_ref[...] = own.T
    halo_feat_ref[...] = rounded(by_feature[:, :TILE].T)
    slot_feat = rounded(by_feature[:, near:].T)
    for at, out_ref in enumerate(pair_refs):
        out_ref[...] = slot_feat[at * step : (at + 1) * step]


def place_kernel(*refs):
    part_refs, (gq_hbm, gkv_hbm, go_hbm, all_ref, out_ref, sems) = refs[:-6], refs[-6:]
    width = gq_hbm.shape[0]
    pair, square, _ = exchange_plan()
    half = 1 << len(pair + square)
    rows = 2 * width // half
    step = part_refs[0].shape[0]
    for at, part_ref in enumerate(part_refs):
        all_ref[at * step : (at + 1) * step] = part_ref[...]
    held = own_digit() + (lax.axis_index("rows") % 2) * half
    copies = []
    for at in range(2 * half):
        start = at * rows
        piece = slice(start, start + rows)
        offset = pl.multiple_of((held ^ at) * rows, ROW_PACK)
        out_ref[piece] = all_ref[pl.ds(offset, rows), :].astype(jnp.float32)
        rows_out = pl.ds(start % width, rows)
        which = start // width
        if which == 0:
            target = gq_hbm.at[rows_out]
        elif which == 3:
            target = go_hbm.at[rows_out]
        else:
            target = gkv_hbm.at[rows_out, pl.ds((which - 1) * width, width)]
        copies.append(pltpu.make_async_copy(out_ref.at[piece], target, sems.at[at]))
        copies[-1].start()
    for copy in copies:
        copy.wait()


def return_kernel(gf_ref, chosen_ref, halo_ref, own_ref, through_ref, *refs):
    far_refs, out_ref = refs[:-1], refs[-1]
    row_count = gf_ref.shape[0]
    tile = halo_ref.shape[0]
    per_peer = own_ref.shape[0] // 2
    returned = []
    for at, even_ref in enumerate([own_ref, *far_refs[::-1]]):
        returned += [even_ref[:per_peer], through_ref[at * per_peer : (at + 1) * per_peer]]
    total = gf_ref[...] + rows_contracted(chosen_ref[...], jnp.concatenate(returned, axis=0))
    out_ref[: row_count - tile] = total[: row_count - tile]
    out_ref[row_count - tile :] = total[row_count - tile :] + halo_ref[...].astype(jnp.float32)


def call(kernel, name, outs, args, scratch=(), fetched=0, flops=0, stored=False):
    spaces = [pltpu.HBM] * fetched
    spaces += [pltpu.VMEM] * (len(args) - len(spaces))
    moved = sum(x.size * x.dtype.itemsize for x in list(args) + list(outs))
    scratch = list(scratch)
    if fetched:
        scratch.append(pltpu.SemaphoreType.DMA((fetched,)))
    constrained = [
        pltpu.with_memory_space_constraint(x, pltpu.HBM) if space is pltpu.HBM else x
        for x, space in zip(args, spaces)
    ]
    return pl.pallas_call(
        kernel,
        out_shape=outs,
        in_specs=[pl.BlockSpec(memory_space=space) for space in spaces],
        out_specs=[pl.BlockSpec(memory_space=pl.ANY if stored else pltpu.VMEM)] * len(outs),
        scratch_shapes=scratch,
        compiler_params=pltpu.CompilerParams(vmem_limit_bytes=VMEM_BYTES),
        cost_estimate=pl.CostEstimate(flops=flops, bytes_accessed=moved, transcendentals=0),
        name=name,
    )(*constrained)


def shards(features, out_grad, w_query, w_keyval, w_out, virtual, local_nbr, expander, send_rows):
    row_count, width = features.shape
    dom_size, per_peer = send_rows.shape
    slots = dom_size * per_peer
    virt_rows = virtual.shape[0]
    padded = ROW_PACK * -(-virt_rows // ROW_PACK)
    ext_rows = TILE + row_count + slots + padded
    nodes = row_count * lax.axis_size("dom") * lax.axis_size("rows")
    pair, square, rest = exchange_plan()
    bf16, f32 = jnp.bfloat16, jnp.float32
    shape = jax.ShapeDtypeStruct

    halo, chosen, through, *direct = call(
        pick_kernel,
        "pick_rows",
        [shape((TILE, width), bf16), shape((slots, row_count), bf16)]
        + [shape((slots // 2, width), bf16)]
        + [shape((per_peer, width), bf16)] * (dom_size // 2),
        [features, send_rows],
        [pltpu.VMEM(features.shape, bf16), pltpu.VMEM(send_rows.shape, jnp.int32)],
        fetched=2,
    )
    through = swapped(through, 1, 0)
    prepared = call(
        functools.partial(prepare_kernel, per_peer),
        "prepare",
        [
            shape(out_grad.shape, bf16),
            shape(w_query.shape, bf16),
            shape(w_keyval.shape, bf16),
            shape((width, row_count + padded), bf16),
            shape((width, row_count), bf16),
            shape((width, row_count), bf16),
            shape((row_count + padded, 2 * width), bf16),
            shape((2 * width, row_count + padded), bf16),
            shape((2 * TILE, row_count), f32),
            shape((slots + padded, row_count), f32),
        ],
        [features, out_grad, w_query, w_keyval, w_out, virtual, local_nbr.T, expander.T],
        [
            pltpu.VMEM(features.shape, bf16),
            pltpu.VMEM(w_out.shape, bf16),
            pltpu.VMEM(virtual.shape, bf16),
            pltpu.VMEM(local_nbr.shape[::-1], jnp.int32),
            pltpu.VMEM(expander.shape[::-1], jnp.int32),
        ],
        fetched=8,
        flops=10 * row_count * width * width,
    )
    (through, halo), _ = lax.optimization_barrier(((through, halo), prepared[0]))
    arrived = handed_on(direct, through)
    halo = shifted(halo, "rows", 1)
    message, rider, *gradients = call(
        functools.partial(attend_kernel, nodes**-0.5, per_peer, dom_size),
        "attend",
        [
            shape((2 * width + padded, width), bf16),
            shape((padded, width), f32),
            shape((width, ext_rows), bf16),
            shape((width, row_count), bf16),
            shape((2 * width, ext_rows), bf16),
            shape((width, row_count), bf16),
        ],
        [*arrived, halo, *prepared],
        [
            pltpu.VMEM((slots, width), bf16),
            pltpu.VMEM((ext_rows, 2 * width), bf16),
            pltpu.VMEM((2 * width, ext_rows), bf16),
        ],
        flops=28 * ext_rows * width * width,
    )
    message = swapped(message, *CORES)
    own_feat, halo_feat, keep, *pairs = call(
        functools.partial(finish_kernel, nodes**-0.5),
        "finish",
        [shape((row_count, width), f32), shape((TILE, width), bf16), shape((2 * width, width), f32)]
        + [shape((2 * per_peer, width), bf16)] * (dom_size // 2),
        [*prepared[:3], *gradients],
        flops=6 * ext_rows * width * width,
    )

    keep, rider = added(keep, rounded(rider).astype(f32), {1: message})
    rider = rider[: -(-virt_rows // 8) * 8]
    pairs, _ = lax.optimization_barrier((pairs, keep))
    returned = [swapped(pairs[at], 2 * at, 0) for at in reversed(range(1, dom_size // 2))]
    keep, rider = scattered(keep, rider, square)
    keep, *returned[:-1] = lax.optimization_barrier((keep, *returned[:-1]))
    keep, rider = scattered(keep, rider, pair)
    (returned, halo_feat), _ = lax.optimization_barrier(((returned, halo_feat), keep))
    through = swapped(jnp.concatenate([x[per_peer:] for x in [pairs[0]] + returned[::-1]]), 1, 0)
    halo_back = shifted(halo_feat, "rows", -1)
    for mask in rest:
        message = swapped(with_rider(keep, rider), *mask)
        keep, rider = rounded(keep).astype(f32), rounded(rider).astype(f32)
        keep, rider = added(keep, rider, {1: message})
    (grad_features,) = call(
        return_kernel,
        "return_rows",
        [shape((row_count, width), f32)],
        [own_feat, chosen, halo_back, pairs[0], through, *returned],
    )

    held = rounded(keep)
    held = jnp.concatenate([held, swapped(held, *pair[0])], axis=0)
    held, grad_features = lax.optimization_barrier((held, grad_features))
    arrived = [swapped(held, *masks) for masks in partner_masks(square)[1:]]
    near = [held, *arrived]
    far = [swapped(part, *CORES) for part in near]
    grad_wq, grad_wkv, grad_wo = call(
        place_kernel,
        "place_sums",
        [shape((width, width), f32), shape((width, 2 * width), f32), shape((width, width), f32)],
        [*near, *far],
        [
            pltpu.VMEM((4 * width, width), bf16),
            pltpu.VMEM((4 * width, width), f32),
            pltpu.SemaphoreType.DMA((2 << len(pair + square),)),
        ],
        stored=True,
    )
    return grad_features, grad_wq, grad_wkv, grad_wo, rider[:virt_rows]


def solution(mesh):
    placed = (
        P(("dom", "rows"), None),
        P(("dom", "rows"), None),
        P(),
        P(),
        P(),
        P(),
        P(("dom", "rows"), None),
        P(("dom", "rows"), None),
        P(("dom", "rows"), None),
    )
    return jax.shard_map(
        shards,
        mesh=mesh,
        in_specs=placed,
        out_specs=(P(("dom", "rows"), None), P(), P(), P(), P()),
        check_vma=False,
    )
```

```python
import functools
import math

import jax
import jax.numpy as jnp
from jax import lax
from jax.experimental import pallas as pl
from jax.experimental.pallas import tpu as pltpu
from jax.sharding import PartitionSpec as P

HEADS = 8
TILE = 128
ROW_PACK = 16
NEGATIVE_FILL = -1e30
VMEM_BYTES = 24 * 1024 * 1024
LANES = 128


def f32_dot(left, right):
    return jnp.dot(left, right, preferred_element_type=jnp.float32)


def rows_contracted(left, right):
    return lax.dot_general(
        left, right, (((0,), (0,)), ((), ())), preferred_element_type=jnp.float32
    )


def times_transposed(left, right):
    return lax.dot_general(
        left, right, (((1,), (1,)), ((), ())), preferred_element_type=jnp.float32
    )


def rounded(value):
    return value.astype(jnp.bfloat16)


CORES = (0, 1)


def bits_of(size, first=1):
    return [1 << i for i in range(size.bit_length() - 1) if 1 << i >= first]


def exchange_plan():
    dom_size, rows_size = lax.axis_size("dom"), lax.axis_size("rows")
    pair, square = [(2, 0)], [(1, 0), (0, 2)]
    rest = [(bit, 0) for bit in bits_of(dom_size, 4)] + [(0, bit) for bit in bits_of(rows_size, 4)]
    return pair, square, rest


def partner_masks(block):
    masks = []
    for digit in range(1 << len(block)):
        chosen = [mask for i, mask in enumerate(block) if digit >> i & 1]
        masks.append((sum(mask[0] for mask in chosen), sum(mask[1] for mask in chosen)))
    return masks


def farthest_first(count):
    return sorted(range(1, count), key=lambda digit: (-digit.bit_count(), -digit))


def own_digit():
    pair, square, _ = exchange_plan()
    digit = 0
    for i, (dom_mask, rows_mask) in enumerate(pair + square):
        own = (lax.axis_index("dom") & dom_mask) | (lax.axis_index("rows") & rows_mask)
        digit += jnp.where(own != 0, 1 << i, 0)
    return digit


def swapped(block, dom_mask, rows_mask):
    dom_size, rows_size = lax.axis_size("dom"), lax.axis_size("rows")
    route = [
        (a * rows_size + b, (a ^ dom_mask) * rows_size + (b ^ rows_mask))
        for a in range(dom_size)
        for b in range(rows_size)
    ]
    return lax.ppermute(block, ("dom", "rows"), route)


def shifted(block, axis, distance):
    devices = range(lax.axis_size(axis))
    route = [((i - distance) % len(devices), i) for i in devices]
    return lax.ppermute(block, axis, route)


def paired_sum(terms):
    while len(terms) > 1:
        terms = [left + right for left, right in zip(terms[::2], terms[1::2])]
    return terms[0]


def with_rider(block, rider):
    return jnp.concatenate([rounded(block), rounded(rider)], axis=0)


def added(keep, rider, arrived):
    rows = keep.shape[0]
    riders = [rider] + [arrived[at][rows:].astype(jnp.float32) for at in sorted(arrived)]
    for block in arrived.values():
        keep = keep + block[:rows].astype(jnp.float32)
    return keep, paired_sum(riders)


def scattered(keep, rider, bits):
    masks = partner_masks(bits)
    rows = keep.shape[0] // len(masks)
    parts = [keep[at * rows : (at + 1) * rows] for at in range(len(masks))]
    messages = {at: with_rider(parts[at], rider) for at in farthest_first(len(masks))}
    arrived = {at: swapped(message, *masks[at]) for at, message in messages.items()}
    return added(parts[0], rounded(rider).astype(jnp.float32), arrived)


def handed_on(direct, through):
    rows = direct[0].shape[0]
    arrived = [direct[0], through]
    for at in reversed(range(1, len(direct))):
        message = jnp.concatenate([direct[at], through[at * rows : (at + 1) * rows]], axis=0)
        arrived.append(swapped(message, 2 * at, 0))
    return arrived


def listed_rows(send_ref, row_count):
    dom_size, per_peer = send_ref.shape
    slots = dom_size * per_peer
    slot = lax.broadcasted_iota(jnp.int32, (slots, per_peer), 0)
    place = lax.broadcasted_iota(jnp.int32, (slots, per_peer), 1)
    peer = (slot // per_peer) ^ lax.axis_index("dom")
    listed = jnp.zeros((slots, per_peer), jnp.int32)
    for at in range(dom_size):
        listed += jnp.where((peer == at) & (place == slot % per_peer), send_ref[at : at + 1, :], 0)
    column = jnp.sum(listed, axis=1, keepdims=True)
    rows = lax.broadcasted_iota(jnp.int32, (slots, row_count), 1)
    return jnp.where(column == rows, 1.0, 0.0).astype(jnp.bfloat16)


def fetch(pairs, sems):
    copies = [
        pltpu.make_async_copy(source, target, sems.at[at])
        for at, (source, target) in enumerate(pairs)
    ]
    for copy in copies:
        copy.start()
    return copies


def store_blocks(rows, through_ref, direct_refs):
    size = direct_refs[0].shape[0]
    for at, out_ref in enumerate(direct_refs):
        out_ref[...] = rows[2 * at * size : (2 * at + 1) * size]
        through_ref[at * size : (at + 1) * size] = rows[(2 * at + 1) * size : (2 * at + 2) * size]


def pick_kernel(feat_hbm, send_hbm, halo_ref, chosen_ref, through_ref, *refs):
    direct_refs, (feat_ref, send_ref, sems) = refs[:-3], refs[-3:]
    copies = fetch([(send_hbm, send_ref), (feat_hbm, feat_ref)], sems)
    copies[0].wait()
    chosen_ref[...] = listed_rows(send_ref, feat_ref.shape[0])
    copies[1].wait()
    halo_ref[...] = feat_ref[feat_ref.shape[0] - halo_ref.shape[0] :]
    store_blocks(rounded(f32_dot(chosen_ref[...], feat_ref[...])), through_ref, direct_refs)


def prepare_kernel(
    per_peer,
    feat_hbm,
    og_hbm,
    wq_hbm,
    wkv_hbm,
    wo_hbm,
    virt_hbm,
    nbr_hbm,
    exp_hbm,
    og_ref,
    wq_ref,
    wkv_ref,
    featt_ref,
    qt_ref,
    odt_ref,
    kv_ref,
    kvt_ref,
    local_bias_ref,
    far_bias_ref,
    feat_ref,
    wo_ref,
    virt_ref,
    nbr_ref,
    exp_ref,
    sems,
):
    nbr_copy, exp_copy, feat_copy, virt_copy, wq_copy, wkv_copy, og_copy, wo_copy = fetch(
        [
            (nbr_hbm, nbr_ref),
            (exp_hbm, exp_ref),
            (feat_hbm, feat_ref),
            (virt_hbm, virt_ref),
            (wq_hbm, wq_ref),
            (wkv_hbm, wkv_ref),
            (og_hbm, og_ref),
            (wo_hbm, wo_ref),
        ],
        sems,
    )
    row_count, width = feat_ref.shape
    window = local_bias_ref.shape[0]
    far = far_bias_ref.shape[0]
    virt_rows = virt_ref.shape[0]
    padded = kv_ref.shape[0] - row_count
    slots = far - padded
    scale = 1.0 / math.sqrt(width // HEADS)

    def multiplicity(key_rows, named):
        position = lax.broadcasted_iota(jnp.int32, (key_rows, row_count), 0)
        count = jnp.zeros((key_rows, row_count), jnp.float32)
        for at in range(named.shape[0]):
            count += jnp.where(named[at : at + 1, :] == position, 1.0, 0.0)
        return count

    nbr_copy.wait()
    local_bias_ref[...] = jnp.where(multiplicity(window, nbr_ref) > 0.0, 0.0, NEGATIVE_FILL)
    exp_copy.wait()
    expander = exp_ref[...]
    expander = ((expander // per_peer) ^ lax.axis_index("dom")) * per_peer + expander % per_peer
    named_times = multiplicity(slots, expander)
    slot_bias = jnp.full((slots, row_count), NEGATIVE_FILL, jnp.float32)
    for times in range(1, exp_ref.shape[0] + 1):
        slot_bias = jnp.where(named_times == float(times), math.log(times) / scale, slot_bias)
    far_bias_ref[:slots] = slot_bias
    virt_row = lax.broadcasted_iota(jnp.int32, (padded, row_count), 0)
    far_bias_ref[slots:] = jnp.where(virt_row < virt_rows, 0.0, NEGATIVE_FILL)

    feat_copy.wait()
    featt_ref[:, :row_count] = feat_ref[...].T
    virt_copy.wait()
    virt = jnp.concatenate(
        [virt_ref[...], jnp.zeros((padded - virt_rows, width), jnp.bfloat16)], axis=0
    )
    featt_ref[:, row_count:] = virt.T
    wq_copy.wait()
    qt_ref[...] = rounded(rows_contracted(wq_ref[...], featt_ref[:, :row_count]))
    wkv_copy.wait()
    kv_ref[:row_count] = rounded(f32_dot(feat_ref[...], wkv_ref[...]))
    kv_ref[row_count:] = rounded(f32_dot(virt, wkv_ref[...]))
    kvt_ref[...] = kv_ref[...].T
    og_copy.wait()
    wo_copy.wait()
    odt_ref[...] = rounded(times_transposed(wo_ref[...], og_ref[...]))


def attend_kernel(
    factor,
    per_peer,
    dom_size,
    *refs,
):
    count = dom_size // 2 + 1
    piece_refs, halo_ref, refs = refs[:count], refs[count], refs[count + 1 :]
    og_ref, wq_ref, wkv_ref, featt_ref, qt_ref, odt_ref, own_kv_ref, own_kvt_ref = refs[:8]
    local_bias_ref, far_bias_ref, send_ref, rider_ref = refs[8:12]
    extt_ref, gqt_ref, gkvt_ref, ot_ref, slot_ref, kv_ref, kvt_ref = refs[12:]
    width, row_count = qt_ref.shape
    tile = halo_ref.shape[0]
    tile_count = row_count // tile
    slots = dom_size * per_peer
    near = tile + row_count
    virt_at = near + slots
    head_dim = width // HEADS
    scale = 1.0 / math.sqrt(head_dim)

    kv_ref[tile:near] = own_kv_ref[:row_count]
    kv_ref[virt_at:] = own_kv_ref[row_count:]
    kvt_ref[:, tile:near] = own_kvt_ref[:, :row_count]
    kvt_ref[:, virt_at:] = own_kvt_ref[:, row_count:]
    extt_ref[:, tile:near] = featt_ref[:, :row_count]
    extt_ref[:, virt_at:] = featt_ref[:, row_count:]
    slot_ref[:per_peer] = piece_refs[0][...]
    slot_ref[per_peer : 2 * per_peer] = piece_refs[1][:per_peer]
    for at, piece_ref in enumerate(piece_refs[:1:-1], 1):
        slot_ref[2 * at * per_peer : (2 * at + 2) * per_peer] = piece_ref[...]
    for rows, source_ref in ((slice(0, tile), halo_ref), (slice(near, virt_at), slot_ref)):
        extt_ref[:, rows] = source_ref[...].T
        kv_ref[rows] = rounded(f32_dot(source_ref[...], wkv_ref[...]))
        kvt_ref[:, rows] = kv_ref[rows].T

    def tiles(of):
        return jnp.concatenate([of(t, slice(t * tile, (t + 1) * tile)) for t in range(tile_count)], 1)

    def bounds(head):
        low, high = head * head_dim, (head + 1) * head_dim
        return low, high, low // LANES * LANES, min(-(-high // LANES) * LANES, width)

    def products(head):
        low, high, first, last = bounds(head)
        column = lax.broadcasted_iota(jnp.int32, (last - first, row_count), 0) + first
        of_head = (column >= low) & (column < high)
        out = []
        for rows_ref, start in ((qt_ref, 0), (odt_ref, width)):
            operand = jnp.where(of_head, rows_ref[first:last, :], 0)
            every = f32_dot(kv_ref[:, start + first : start + last], operand)
            out.append(tiles(lambda t, lanes: every[t * tile : (t + 2) * tile, lanes]))
            out.append(every[near:])
        return out

    def weights(s_local, s_far, dp_local, dp_far):
        s_local += local_bias_ref[...]
        s_far += far_bias_ref[...]
        peak = jnp.maximum(
            jnp.max(s_local, axis=0, keepdims=True), jnp.max(s_far, axis=0, keepdims=True)
        )
        exponent_scale = scale * math.log2(math.e)
        e_local = jnp.exp2((s_local - peak) * exponent_scale)
        e_far = jnp.exp2((s_far - peak) * exponent_scale)
        total = jnp.sum(e_local, axis=0, keepdims=True) + jnp.sum(e_far, axis=0, keepdims=True)
        inverse = 1.0 / total
        p_local = e_local * inverse
        p_far = e_far * inverse
        delta = jnp.sum(p_local * dp_local, axis=0, keepdims=True) + jnp.sum(
            p_far * dp_far, axis=0, keepdims=True
        )
        ds_local = rounded(p_local * (dp_local - delta))
        ds_far = rounded(p_far * (dp_far - delta))
        return rounded(p_local), rounded(p_far), ds_local, ds_far

    def outputs(head, pb_local, pb_far, ds_local, ds_far):
        low, high, _, _ = bounds(head)

        def to_queries(start, local, beyond):
            rows = slice(start + low, start + high)
            near_part = tiles(
                lambda t, lanes: f32_dot(kvt_ref[rows, t * tile : (t + 2) * tile], local[:, lanes])
            )
            return near_part + f32_dot(kvt_ref[rows, near:], beyond)

        def to_keys(start, operand, local, beyond, factor):
            rows = slice(start + low, start + high)
            parts = []
            carried = None
            for t in range(tile_count):
                lanes = slice(t * tile, (t + 1) * tile)
                window = times_transposed(operand[:, lanes], local[:, lanes])
                previous = window[:, :tile]
                parts.append(previous if carried is None else previous + carried)
                carried = window[:, tile:]
            parts.append(carried)
            parts.append(times_transposed(operand, beyond))
            gathered = jnp.concatenate(parts, axis=1)
            gkvt_ref[rows] = rounded(gathered if factor is None else gathered * factor)

        ot_ref[low:high] = rounded(to_queries(width, pb_local, pb_far))
        gqt_ref[low:high] = rounded(to_queries(0, ds_local, ds_far) * scale)
        to_keys(0, qt_ref[low:high], ds_local, ds_far, scale)
        to_keys(width, odt_ref[low:high], pb_local, pb_far, None)

    coming = products(0)
    done = None
    for head in range(HEADS):
        now = coming
        if head + 1 < HEADS:
            coming = products(head + 1)
        if done is not None:
            outputs(head - 1, *done)
        done = weights(*now)
    outputs(HEADS - 1, *done)

    rider_ref[...] = f32_dot(wkv_ref[...], gkvt_ref[:, virt_at:]).T * factor
    weight_sums(
        1 - lax.axis_index("rows") % 2, send_ref, extt_ref, gqt_ref, gkvt_ref, ot_ref, og_ref, factor
    )
    send_ref[2 * width :] = rounded(rider_ref[...])


def weight_sums(core, out_ref, extt_ref, gqt_ref, gkvt_ref, ot_ref, og_ref, factor):
    width, row_count = gqt_ref.shape
    held = own_digit()
    pair, square, _ = exchange_plan()
    rows = 2 * width >> len(pair + square)

    def write(at, total):
        total = (total * factor).astype(out_ref.dtype)
        for start in range(0, width, rows):
            piece = (at * width + start) // rows
            offset = pl.multiple_of((piece ^ held) * rows, ROW_PACK)
            out_ref[pl.ds(offset, rows), :] = total[start : start + rows]

    @pl.when(core == 0)
    def _():
        own = slice(TILE, TILE + row_count)
        write(0, times_transposed(extt_ref[:, own], gqt_ref[...]))
        write(1, times_transposed(extt_ref[...], gkvt_ref[:width]))

    @pl.when(core == 1)
    def _():
        write(0, times_transposed(extt_ref[...], gkvt_ref[width:]))
        write(1, f32_dot(ot_ref[...], og_ref[...]))


def finish_kernel(factor, og_ref, wq_ref, wkv_ref, extt_ref, gqt_ref, gkvt_ref, ot_ref, *refs):
    gf_ref, halo_feat_ref, keep_ref = refs[:3]
    pair_refs = refs[3:]
    width, row_count = gqt_ref.shape
    near = TILE + row_count
    step = pair_refs[0].shape[0]
    slots = step * len(pair_refs)
    weight_sums(
        lax.axis_index("rows") % 2, keep_ref, extt_ref, gqt_ref, gkvt_ref, ot_ref, og_ref, factor
    )
    by_feature = f32_dot(wkv_ref[...], gkvt_ref[:, : near + slots])
    own = by_feature[:, TILE:near] + f32_dot(wq_ref[...], gqt_ref[...])
    gf_ref[...] = own.T
    halo_feat_ref[...] = rounded(by_feature[:, :TILE].T)
    slot_feat = rounded(by_feature[:, near:].T)
    for at, out_ref in enumerate(pair_refs):
        out_ref[...] = slot_feat[at * step : (at + 1) * step]


def place_kernel(*refs):
    part_refs, (gq_hbm, gkv_hbm, go_hbm, all_ref, out_ref, sems) = refs[:-6], refs[-6:]
    width = gq_hbm.shape[0]
    pair, square, _ = exchange_plan()
    half = 1 << len(pair + square)
    rows = 2 * width // half
    step = part_refs[0].shape[0]
    for at, part_ref in enumerate(part_refs):
        all_ref[at * step : (at + 1) * step] = part_ref[...]
    held = own_digit() + (lax.axis_index("rows") % 2) * half
    copies = []
    for at in range(2 * half):
        start = at * rows
        piece = slice(start, start + rows)
        offset = pl.multiple_of((held ^ at) * rows, ROW_PACK)
        out_ref[piece] = all_ref[pl.ds(offset, rows), :].astype(jnp.float32)
        rows_out = pl.ds(start % width, rows)
        which = start // width
        if which == 0:
            target = gq_hbm.at[rows_out]
        elif which == 3:
            target = go_hbm.at[rows_out]
        else:
            target = gkv_hbm.at[rows_out, pl.ds((which - 1) * width, width)]
        copies.append(pltpu.make_async_copy(out_ref.at[piece], target, sems.at[at]))
        copies[-1].start()
    for copy in copies:
        copy.wait()


def return_kernel(gf_ref, chosen_ref, halo_ref, own_ref, through_ref, *refs):
    far_refs, out_ref = refs[:-1], refs[-1]
    row_count = gf_ref.shape[0]
    tile = halo_ref.shape[0]
    per_peer = own_ref.shape[0] // 2
    returned = []
    for at, even_ref in enumerate([own_ref, *far_refs[::-1]]):
        returned += [even_ref[:per_peer], through_ref[at * per_peer : (at + 1) * per_peer]]
    total = gf_ref[...] + rows_contracted(chosen_ref[...], jnp.concatenate(returned, axis=0))
    out_ref[: row_count - tile] = total[: row_count - tile]
    out_ref[row_count - tile :] = total[row_count - tile :] + halo_ref[...].astype(jnp.float32)


def call(kernel, name, outs, args, scratch=(), fetched=0, flops=0, stored=False):
    spaces = [pltpu.HBM] * fetched
    spaces += [pltpu.VMEM] * (len(args) - len(spaces))
    moved = sum(x.size * x.dtype.itemsize for x in list(args) + list(outs))
    scratch = list(scratch)
    if fetched:
        scratch.append(pltpu.SemaphoreType.DMA((fetched,)))
    constrained = [
        pltpu.with_memory_space_constraint(x, pltpu.HBM) if space is pltpu.HBM else x
        for x, space in zip(args, spaces)
    ]
    return pl.pallas_call(
        kernel,
        out_shape=outs,
        in_specs=[pl.BlockSpec(memory_space=space) for space in spaces],
        out_specs=[pl.BlockSpec(memory_space=pl.ANY if stored else pltpu.VMEM)] * len(outs),
        scratch_shapes=scratch,
        compiler_params=pltpu.CompilerParams(vmem_limit_bytes=VMEM_BYTES),
        cost_estimate=pl.CostEstimate(flops=flops, bytes_accessed=moved, transcendentals=0),
        name=name,
    )(*constrained)


def shards(features, out_grad, w_query, w_keyval, w_out, virtual, local_nbr, expander, send_rows):
    row_count, width = features.shape
    dom_size, per_peer = send_rows.shape
    slots = dom_size * per_peer
    virt_rows = virtual.shape[0]
    padded = ROW_PACK * -(-virt_rows // ROW_PACK)
    ext_rows = TILE + row_count + slots + padded
    nodes = row_count * lax.axis_size("dom") * lax.axis_size("rows")
    pair, square, rest = exchange_plan()
    bf16, f32 = jnp.bfloat16, jnp.float32
    shape = jax.ShapeDtypeStruct

    halo, chosen, through, *direct = call(
        pick_kernel,
        "pick_rows",
        [shape((TILE, width), bf16), shape((slots, row_count), bf16)]
        + [shape((slots // 2, width), bf16)]
        + [shape((per_peer, width), bf16)] * (dom_size // 2),
        [features, send_rows],
        [pltpu.VMEM(features.shape, bf16), pltpu.VMEM(send_rows.shape, jnp.int32)],
        fetched=2,
    )
    through = swapped(through, 1, 0)
    prepared = call(
        functools.partial(prepare_kernel, per_peer),
        "prepare",
        [
            shape(out_grad.shape, bf16),
            shape(w_query.shape, bf16),
            shape(w_keyval.shape, bf16),
            shape((width, row_count + padded), bf16),
            shape((width, row_count), bf16),
            shape((width, row_count), bf16),
            shape((row_count + padded, 2 * width), bf16),
            shape((2 * width, row_count + padded), bf16),
            shape((2 * TILE, row_count), f32),
            shape((slots + padded, row_count), f32),
        ],
        [features, out_grad, w_query, w_keyval, w_out, virtual, local_nbr.T, expander.T],
        [
            pltpu.VMEM(features.shape, bf16),
            pltpu.VMEM(w_out.shape, bf16),
            pltpu.VMEM(virtual.shape, bf16),
            pltpu.VMEM(local_nbr.shape[::-1], jnp.int32),
            pltpu.VMEM(expander.shape[::-1], jnp.int32),
        ],
        fetched=8,
        flops=10 * row_count * width * width,
    )
    (through, halo), _ = lax.optimization_barrier(((through, halo), prepared[0]))
    arrived = handed_on(direct, through)
    halo = shifted(halo, "rows", 1)
    message, rider, *gradients = call(
        functools.partial(attend_kernel, nodes**-0.5, per_peer, dom_size),
        "attend",
        [
            shape((2 * width + padded, width), bf16),
            shape((padded, width), f32),
            shape((width, ext_rows), bf16),
            shape((width, row_count), bf16),
            shape((2 * width, ext_rows), bf16),
            shape((width, row_count), bf16),
        ],
        [*arrived, halo, *prepared],
        [
            pltpu.VMEM((slots, width), bf16),
            pltpu.VMEM((ext_rows, 2 * width), bf16),
            pltpu.VMEM((2 * width, ext_rows), bf16),
        ],
        flops=28 * ext_rows * width * width,
    )
    message = swapped(message, *CORES)
    own_feat, halo_feat, keep, *pairs = call(
        functools.partial(finish_kernel, nodes**-0.5),
        "finish",
        [shape((row_count, width), f32), shape((TILE, width), bf16), shape((2 * width, width), f32)]
        + [shape((2 * per_peer, width), bf16)] * (dom_size // 2),
        [*prepared[:3], *gradients],
        flops=6 * ext_rows * width * width,
    )

    keep, rider = added(keep, rounded(rider).astype(f32), {1: message})
    rider = rider[: -(-virt_rows // 8) * 8]
    pairs, _ = lax.optimization_barrier((pairs, keep))
    returned = [swapped(pairs[at], 2 * at, 0) for at in reversed(range(1, dom_size // 2))]
    keep, rider = scattered(keep, rider, square)
    keep, *returned[:-1] = lax.optimization_barrier((keep, *returned[:-1]))
    keep, rider = scattered(keep, rider, pair)
    for at, mask in enumerate(rest):
        message = with_rider(keep, rider)
        if at == 0:
            (last, halo_feat), _ = lax.optimization_barrier(((returned[-1], halo_feat), message))
            halo_back = shifted(halo_feat, "rows", -1)
        message = swapped(message, *mask)
        keep, rider = rounded(keep).astype(f32), rounded(rider).astype(f32)
        keep, rider = added(keep, rider, {1: message})
    returned[-1] = last
    odd = [block[per_peer:] for block in [pairs[0]] + returned[::-1]]
    through = swapped(jnp.concatenate(odd, axis=0), 1, 0)
    (grad_features,) = call(
        return_kernel,
        "return_rows",
        [shape((row_count, width), f32)],
        [own_feat, chosen, halo_back, pairs[0], through, *returned],
    )

    held = rounded(keep)
    held = jnp.concatenate([held, swapped(held, *pair[0])], axis=0)
    held, grad_features = lax.optimization_barrier((held, grad_features))
    arrived = [swapped(held, *masks) for masks in partner_masks(square)[1:]]
    near = [held, *arrived]
    far = [swapped(part, *CORES) for part in near]
    grad_wq, grad_wkv, grad_wo = call(
        place_kernel,
        "place_sums",
        [shape((width, width), f32), shape((width, 2 * width), f32), shape((width, width), f32)],
        [*near, *far],
        [
            pltpu.VMEM((4 * width, width), bf16),
            pltpu.VMEM((4 * width, width), f32),
            pltpu.SemaphoreType.DMA((2 << len(pair + square),)),
        ],
        stored=True,
    )
    return grad_features, grad_wq, grad_wkv, grad_wo, rider[:virt_rows]


def solution(mesh):
    placed = (
        P(("dom", "rows"), None),
        P(("dom", "rows"), None),
        P(),
        P(),
        P(),
        P(),
        P(("dom", "rows"), None),
        P(("dom", "rows"), None),
        P(("dom", "rows"), None),
    )
    return jax.shard_map(
        shards,
        mesh=mesh,
        in_specs=placed,
        out_specs=(P(("dom", "rows"), None), P(), P(), P(), P()),
        check_vma=False,
    )
```
